32 devices in a mesh: groups: 2 (over x), shell: 16 (over z, y, core).
Axes of the slice: x: 2, y: 2, z: 4, core: 2. Of those that a mesh axis runs over, the one named last changes fastest.
Arguments:
- panels: bfloat16 [256, 32, 256], P(('groups', 'shell')), parts along dimension 0, may hold values from -6 to 6
- block_pairs: int32 [256, 2], P(('groups', 'shell')), parts along dimension 0, may hold values from 0 to 255, as said below
- block_count: int32 [32], P(('groups', 'shell')), parts along dimension 0, may hold values from 1 to 8, 64 in all
- shell_size: int32 [512], P('groups'), parts along dimension 0, may hold values from 1 to 16, 2560 in all
- occ_coef: bfloat16 [5120, 256], P(('groups', 'shell')), parts along dimension 0, may hold values from -4 to 4
- vir_coef: bfloat16 [5120, 2304], P(('groups', 'shell')), parts along dimension 0, may hold values from -0.125 to 0.125
Outputs:
- mo_vectors: bfloat16 [64, 256, 2304], P(('groups', 'shell')), parts along dimension 0
The draws below stay inside these ranges and needn't reach their ends.
There are 2 independent parts, one for each index of `groups`. The reference program is written for one: setup_inputs(seed, part) draws one part's arguments, and reference() takes and returns one part's arrays. A program takes and returns all parts, laid end to end along the dimension named above; each array names one. Nothing has to cross between parts.
Inputs may be any that keep to these rules, and one draw needn't show every extreme that they name: `block_pairs`: no (row, column) pair of shell blocks appears twice among the slots. `block_count`: the counts of all devices sum to 64. `shell_size`: the sizes sum to 2560.
All inputs are finite; a program needn't handle non-finite values.
Results may differ from the reference program's by a relative error of at most 0.0049.
Values may be sent and summed in bfloat16 or wider, within the bound.
No kernel may reach another device: no remote copies, remote signals or barrier semaphores. Data moves between devices by JAX's collectives and lax.ppermute only.
A program may use at most 192 MiB of HBM per device.

```python
import math
import jax
import jax.numpy as jnp
import numpy as np
from jax import lax

EDGE = 16
NBF = 2560
NSH = 256
NOCC = 256
NVIR = 2304
BLK_DEV = 8
VEC_DEV = 2
VECS = 32
SLOTS = 128
LIVE = 64
N_SHELL = 16


def draw_block_pairs(key, part):
    key = jax.random.fold_in(key, 11)
    picked = jax.random.permutation(key, NSH * NSH)[:SLOTS]
    return jnp.stack([picked // NSH, picked % NSH], axis=1).astype(jnp.int32)


def block_levels(stream_key, dims, shards, least, top_value):
    loudness = 1.0
    for axis_at, blocks in shards:
        steps = jax.random.uniform(jax.random.fold_in(jax.random.fold_in(stream_key, 6), axis_at), (blocks,), jnp.float32, least / len(shards), top_value / len(shards))
        loudness = loudness * jnp.repeat(jnp.exp(steps), dims[axis_at] // blocks).reshape((-1,) + (1,) * (len(dims) - 1 - axis_at))
    return loudness


def split_up(number_of, total, bound, lean):
    weights = [(1 << 20) // math.isqrt(grade ** lean) + 1 for grade in range(2, number_of + 1)]
    spare, counts = total - bound - (number_of - 1), [1] * (number_of - 1)
    while spare > 0:
        candidates = [i for i in range(number_of - 1) if counts[i] < bound]
        mass, remaining = sum([weights[i] for i in candidates]), spare
        for i in candidates:
            extra = min(bound - counts[i], max(1, remaining * weights[i] // mass), spare)
            counts[i] = counts[i] + extra
            spare = spare - extra
    return np.array([bound] + counts)


def uneven(rng, number_of, total, bound, skew):
    if number_of == 2:
        one = jax.random.randint(rng, (), max(1, total - bound), min(bound, total - 1) + 1)
        return jnp.stack([one, total - one])
    sizes = jnp.asarray(split_up(number_of, total, bound, skew), jnp.int32)
    pairs = (number_of - 1) // 2
    donor, sink = sizes[1:1 + 2 * pairs:2], sizes[2:2 + 2 * pairs:2]
    slack = jnp.minimum(donor - 1, bound - sink)
    shifted = jax.random.randint(jax.random.fold_in(rng, 1), (pairs,), 0, 1 << 20) % (slack + 1)
    sizes = sizes.at[1:1 + 2 * pairs:2].set(donor - shifted).at[2:2 + 2 * pairs:2].set(sink + shifted)
    return sizes[jax.random.permutation(jax.random.fold_in(rng, 2), number_of)]


def scatter_about(own_key, dims, spread, reach, shards=(), held_as=jnp.bfloat16):
    drawn = spread * jax.random.normal(own_key, dims, jnp.float32)
    if shards:
        drawn = drawn * block_levels(own_key, dims, shards, -0.22, 0.18)
    return jnp.clip(drawn, -reach, reach).astype(held_as)


def setup_inputs(seed: int = 0, part: int = 0) -> dict:
    arg_keys = jax.random.split(jax.random.key(seed), 7)
    part_splits = jax.random.split(jax.random.fold_in(arg_keys[6], part), 7)
    return {
        "panels": scatter_about(part_splits[0], (SLOTS, VECS, EDGE * EDGE), 1.0, 6.0, ((0, 16),)),
        "block_pairs": draw_block_pairs(jax.random.fold_in(jax.random.fold_in(arg_keys[6], part), 71), part),
        "block_count": uneven(part_splits[2], N_SHELL, LIVE, BLK_DEV, 2).astype(jnp.int32),
        "shell_size": uneven(part_splits[3], NSH, NBF, EDGE, 1).astype(jnp.int32),
        "occ_coef": scatter_about(part_splits[4], (NBF, NOCC), (10 * LIVE // NSH) ** -0.5, 4.0, ((0, 16),)),
        "vir_coef": scatter_about(part_splits[5], (NBF, NVIR), NBF ** -0.5, 0.125, ((0, 16),)),
    }


def occupied_blocks(occ_coef, starts, shell_size):
    offsets = jnp.arange(EDGE, dtype=jnp.int32)
    rows = jnp.minimum(starts[:, None] + offsets[None, :], occ_coef.shape[0] - 1).astype(jnp.int32)
    inside = offsets[None, :] < shell_size[:, None]
    return jnp.where(inside[:, :, None], occ_coef[rows], jnp.zeros((), occ_coef.dtype))


def reference(panels, block_pairs, block_count, shell_size, occ_coef, vir_coef):
    slot_total = panels.shape[0]
    vec_total = panels.shape[1]
    nbf_here = occ_coef.shape[0]
    starts = (jnp.cumsum(shell_size) - shell_size).astype(jnp.int32)
    occ_blocks = occupied_blocks(occ_coef, starts, shell_size)
    position = jnp.arange(slot_total, dtype=jnp.int32)
    live = (position % BLK_DEV) < block_count[position // BLK_DEV]
    offsets = jnp.arange(EDGE, dtype=jnp.int32)
    col_shell = block_pairs[:, 1]
    column_ok = live[:, None] & (offsets[None, :] < shell_size[col_shell][:, None])
    columns = jnp.minimum(starts[col_shell][:, None] + offsets[None, :], nbf_here - 1).astype(jnp.int32)
    group_size = math.gcd(512, slot_total)
    turns = slot_total // group_size
    width_vec = VEC_DEV
    stacks = panels.reshape(slot_total, vec_total // width_vec, width_vec, EDGE, EDGE).transpose(1, 0, 2, 3, 4)

    def one_stack(stack):
        def advance(total, turn):
            first = turn * group_size
            block = lax.dynamic_slice_in_dim(stack, first, group_size, 0)
            okay = lax.dynamic_slice_in_dim(column_ok, first, group_size, 0)
            block = jnp.where(okay[:, None, None, :], block, jnp.zeros((), block.dtype)).astype(jnp.float32)
            row_shell = lax.dynamic_slice_in_dim(block_pairs[:, 0], first, group_size, 0)
            coefs = occ_blocks[row_shell].astype(jnp.float32)
            piece = jnp.einsum('kmi,kvmn->vikn', coefs, block).reshape(width_vec, NOCC, group_size * EDGE)
            where_to = lax.dynamic_slice_in_dim(columns, first, group_size, 0).reshape(-1)
            return total.at[:, :, where_to].add(piece), None

        start_total = jnp.zeros((width_vec, NOCC, nbf_here), jnp.float32)
        half, _ = lax.scan(advance, start_total, jnp.arange(turns, dtype=jnp.int32))
        half_round = half.astype(jnp.bfloat16)
        result = jnp.einsum('vin,na->via', half_round.astype(jnp.float32), vir_coef.astype(jnp.float32))
        return result.astype(jnp.bfloat16)

    mapped = lax.map(one_stack, stacks)
    return mapped.reshape(vec_total, NOCC, vir_coef.shape[1])
```

```python
import functools
import math

import jax
import jax.numpy as jnp
from jax import lax
from jax.experimental import pallas as pl
from jax.experimental.pallas import tpu as pltpu
from jax.sharding import PartitionSpec as P

EDGE = 16
NOCC = 256
BLK_DEV = 8
LIVE_DEV = 4
CAP = 160
Z, Y, CORES = 4, 2, 2
F32 = jnp.float32
BF16 = jnp.bfloat16


def padded_rows(matrix, starts, shell_size):
    offsets = jnp.arange(EDGE, dtype=jnp.int32)
    rows = jnp.minimum(starts[:, None] + offsets[None, :], matrix.shape[0] - 1)
    inside = offsets[None, :] < shell_size[:, None]
    return jnp.where(inside[:, :, None], matrix[rows], jnp.zeros((), matrix.dtype))


def half_transform(slot_rows, pairs, keep, occ_blocks):
    count = slot_rows.shape[0]
    vecs_here = slot_rows.shape[1]
    shells = occ_blocks.shape[0]
    group_size = math.gcd(512, count)
    turns = count // group_size
    shaped = slot_rows.reshape(count, vecs_here, EDGE, EDGE)

    def advance(total, turn):
        first = turn * group_size
        block = lax.dynamic_slice_in_dim(shaped, first, group_size, 0)
        okay = lax.dynamic_slice_in_dim(keep, first, group_size, 0)
        block = jnp.where(okay[:, None, None, None], block, jnp.zeros((), block.dtype))
        row_shell = lax.dynamic_slice_in_dim(pairs[:, 0], first, group_size, 0)
        col_shell = lax.dynamic_slice_in_dim(pairs[:, 1], first, group_size, 0)
        coefs = occ_blocks[row_shell]
        piece = jnp.einsum("kmi,kvmn->kvin", coefs, block, preferred_element_type=jnp.float32)
        return (total.at[col_shell].add(piece), None)

    start_total = jnp.zeros((shells, vecs_here, NOCC, EDGE), jnp.float32)
    half, _ = lax.scan(advance, start_total, jnp.arange(turns, dtype=jnp.int32))
    return half


def long_way(panels, block_pairs, block_count, shell_size, occ_coef, vir_coef):
    all_pairs, all_counts = (
        lax.all_gather(block_pairs, "shell", axis=0, tiled=True),
        lax.all_gather(block_count, "shell", axis=0, tiled=True),
    )
    turned = lax.all_to_all(panels, "shell", split_axis=1, concat_axis=0, tiled=True)
    occ_full = lax.all_gather(occ_coef, "shell", axis=0, tiled=True)
    starts = jnp.cumsum(shell_size) - shell_size
    occ_blocks = padded_rows(occ_full, starts, shell_size)
    slot_total = turned.shape[0]
    position = jnp.arange(slot_total, dtype=jnp.int32)
    live = position % BLK_DEV < all_counts[position // BLK_DEV]
    half = half_transform(turned, all_pairs, live, occ_blocks)
    hidden = half.astype(jnp.bfloat16)
    vir_full = lax.all_gather(vir_coef, "shell", axis=0, tiled=True)
    vir_blocks = padded_rows(vir_full, starts, shell_size)
    result = jnp.einsum("svin,sna->via", hidden, vir_blocks, preferred_element_type=jnp.float32)
    return result.astype(jnp.bfloat16)


def iota(shape, dim):
    return lax.broadcasted_iota(jnp.int32, shape, dim)


def column_of(row, mask):
    return jnp.sum(jnp.where(mask, row, 0.0), axis=1, keepdims=True)


def row_of(column, mask):
    return jnp.sum(jnp.where(mask, column, 0.0), axis=0, keepdims=True)


def one_hots(ids, shells):
    lanes = iota(ids.shape, 1).astype(F32)
    return jnp.concatenate(
        [(ids == lanes + 128.0 * k).astype(F32) for k in range(shells // 128)], axis=1
    )


def shell_table(col_hot, size_row, windows, rows):
    shells = size_row.shape[1]
    sub, lane = iota((shells, shells), 0), iota((shells, shells), 1)
    used_row = jnp.max(col_hot, axis=0, keepdims=True)
    before, same = lane < sub, lane == sub
    starts = column_of(size_row, before)
    ahead = column_of(size_row * used_row, before)
    size = column_of(size_row, same)
    used = column_of(used_row, same)
    edge = (iota((shells, 128), 1) * rows).astype(F32)
    reach = used * jnp.clip(edge - starts, 0.0, size)
    before_window = jnp.sum(reach, axis=0, keepdims=True)
    return starts, size, used, ahead, before_window


def lane_value(row, index):
    return jnp.sum(jnp.where(iota(row.shape, 1) == index, row, 0.0), axis=1, keepdims=True)


def pick_kernel(windows, rows, got_ref, size_ref, own_ref, other_ref, out_ref, over_ref):
    shells = size_ref.shape[1]
    here = rows // 2
    me = lax.axis_index("shell")
    core = lax.rem(me, 2)
    window = lax.div(me, 2)
    got = got_ref[...].astype(F32)
    slots = got.shape[0] * BLK_DEV
    ids = got[:, 2 * BLK_DEV :, :].reshape(slots, 256)
    col_hot = one_hots(ids[:, :128], shells)
    size_row = size_ref[...].astype(F32)
    starts, size, used, ahead, before_window = shell_table(col_hot, size_row, windows, rows)
    lanes = iota(before_window.shape, 1)
    after = jnp.sum(
        used * jnp.clip(((iota((shells, 128), 1) + 1) * rows).astype(F32) - starts, 0.0, size), axis=0, keepdims=True
    )
    most = jnp.max(jnp.where(lanes < windows, after - before_window, 0.0))
    over_ref[0] = jnp.where(most > CAP, 1, 0).astype(jnp.int32)
    base = lane_value(before_window, window)

    def chosen(first):
        where = (iota((shells, 256), 1) + first).astype(F32) - starts
        inside = (used > 0.0) & (where >= 0.0) & (where < size)
        place = jnp.sum(jnp.where(inside, ahead + where + 1.0, 0.0), axis=0, keepdims=True)
        place = jnp.where(place > 0.0, place - 1.0 - base, -1.0)
        hot = place == iota((CAP, 256), 0).astype(F32)
        return jnp.where(hot, 1.0, 0.0).astype(BF16)[:, :here]

    mine = chosen(window * rows + core * here)
    theirs = chosen(window * rows + (1 - core) * here)
    width = out_ref.shape[1]
    own = own_ref[:, pl.ds(pl.multiple_of(core * width, 128), width)]
    total = jnp.dot(mine, own, preferred_element_type=F32)
    total += jnp.dot(theirs, other_ref[...], preferred_element_type=F32)
    out_ref[...] = total.astype(BF16)


def half_kernel(windows, rows, got_ref, size_ref, occ_ref, out_ref, total_ref):
    shells = size_ref.shape[1]
    nbf = occ_ref.shape[0]
    sources = got_ref.shape[0]
    got = got_ref[...].astype(F32)
    slots = sources * BLK_DEV
    ids = got[:, 2 * BLK_DEV :, :].reshape(slots, 256)
    col_hot = one_hots(ids[:, :128], shells)
    live = jnp.sum(col_hot, axis=1, keepdims=True)
    row_hot = one_hots(ids[:, 128:], shells) * live
    size_row = size_ref[...].astype(F32)
    starts, size, used, ahead, before_window = shell_table(col_hot, size_row, windows, rows)
    sub, lane = iota((shells, shells), 0), iota((shells, shells), 1)
    starts_row = row_of(starts, sub == lane)
    ahead_row = row_of(ahead, sub == lane)

    def of_slot(hot, row):
        return jnp.sum(hot * row, axis=1, keepdims=True)

    def spread(column):
        wide = jnp.broadcast_to(column, (slots, 128)).reshape(slots, 1, 128)
        return jnp.broadcast_to(wide, (slots, EDGE, 128)).reshape(slots * EDGE, 128)

    step = (iota((slots * EDGE, 128), 0) % EDGE).astype(F32)
    first, length, skip = (spread(of_slot(col_hot, r)) for r in (starts_row, size_row, ahead_row))
    place = skip + step
    for w in range(1, windows):
        shift = CAP - (lane_value(before_window, w) - lane_value(before_window, w - 1))
        place += jnp.where(first + step >= float(rows * w), shift, 0.0)
    place = jnp.where(step < length, place, -1.0)
    first_r, length_r = (spread(of_slot(row_hot, r)) for r in (starts_row, size_row))
    where_r = jnp.where(step < length_r, first_r + step, -1.0)

    span = 2 * BLK_DEV * EDGE
    width = out_ref.shape[1]
    s_in, l_in = iota((span, span), 0), iota((span, span), 1)
    keep_m = (l_in // EDGE) == (s_in % EDGE)
    fold = jnp.where((s_in % EDGE) == (l_in % EDGE), 1.0, 0.0).astype(BF16)
    same_slot = (s_in // EDGE) == (l_in // EDGE)
    for g in range(slots * EDGE // span):
        at = slice(g * span, (g + 1) * span)
        r_hot = where_r[at, :1] == iota((span, nbf), 1).astype(F32)
        occ_rows = jnp.dot(jnp.where(r_hot, 1.0, 0.0).astype(BF16), occ_ref[...], preferred_element_type=F32)
        occ_rows = occ_rows.astype(BF16)
        c_hot = place[at, :1] == iota((span, width), 1).astype(F32)
        c_hot = jnp.where(c_hot, 1.0, 0.0).astype(BF16)
        for p in range(2):
            block = got[2 * g : 2 * g + 2, p * BLK_DEV : (p + 1) * BLK_DEV, :].reshape(16, 1, span)
            block = jnp.broadcast_to(block, (16, EDGE, span)).reshape(span, span)
            block = jnp.where(keep_m, block, 0.0).astype(BF16)
            diag = jnp.dot(block, fold, preferred_element_type=F32)
            diag = jnp.where(same_slot, diag, 0.0).astype(BF16)
            placed = jnp.dot(diag, c_hot, preferred_element_type=F32).astype(BF16)
            piece = lax.dot_general(occ_rows, placed, (((0,), (0,)), ((), ())), preferred_element_type=F32)
            rows_p = slice(p * NOCC, (p + 1) * NOCC)
            if g == 0:
                total_ref[rows_p, :] = piece
            else:
                total_ref[rows_p, :] += piece
    out_ref[...] = total_ref[...].astype(BF16)


def last_kernel(count, order_ref, half_ref, *refs):
    pieces, (out_ref, all_ref, sems) = refs[: 2 * count], refs[2 * count :]
    width = pieces[0].shape[1]
    core = order_ref[count]

    def copies():
        for k, piece in enumerate(pieces):
            w = order_ref[k % count]
            half = core if k < count else 1 - core
            yield pltpu.make_async_copy(
                piece,
                all_ref.at[half, pl.ds(pl.multiple_of(w * CAP, 16), CAP), :],
                sems.at[k],
            )

    @pl.when(pl.program_id(0) == 0)
    def _():
        for copy in copies():
            copy.start()
        for copy in copies():
            copy.wait()

    tile = out_ref.shape[2]
    j = pl.program_id(0)
    per = width // tile
    right = all_ref[lax.div(j, per), :, pl.ds(pl.multiple_of(lax.rem(j, per) * tile, 128), tile)]
    for p in range(2):
        out_ref[p] = jnp.dot(half_ref[p * NOCC : (p + 1) * NOCC, :], right, preferred_element_type=F32).astype(BF16)


VMEM = pl.BlockSpec(memory_space=pltpu.VMEM)
SMEM = pl.BlockSpec(memory_space=pltpu.SMEM)
ANY = pl.BlockSpec(memory_space=pl.ANY)


def short_way(panels, block_pairs, block_count, shell_size, occ_coef, vir_coef):
    n = lax.axis_size("shell")
    windows = n // CORES
    here, nvir = vir_coef.shape
    rows = CORES * here
    width = nvir // CORES
    me = lax.axis_index("shell")
    core = me % 2
    y = (me // 2) % 2
    z = me // 4

    def swap(array, bit):
        return lax.ppermute(array, "shell", [(i, i ^ bit) for i in range(n)])

    def along_z(array, s):
        return lax.ppermute(array, "shell", [(i, (i + 4 * s) % n) for i in range(n)])

    other = swap(lax.dynamic_slice_in_dim(vir_coef, (1 - core) * width, width, 1), 1)
    keep = jnp.arange(BLK_DEV, dtype=jnp.int32) < block_count[0]
    cols = jnp.where(keep, block_pairs[:, 1], -1).astype(BF16)
    ids = jnp.concatenate(
        [jnp.broadcast_to(v[:, None], (BLK_DEV, 128)) for v in (cols, block_pairs[:, 0].astype(BF16))], axis=1
    )
    send = panels.transpose(1, 0, 2).reshape(n, 2 * BLK_DEV, EDGE * EDGE)
    send = jnp.concatenate([send, jnp.broadcast_to(ids, (n,) + ids.shape)], axis=1)
    got = lax.all_to_all(send, "shell", split_axis=0, concat_axis=0, tiled=True)
    occ_full = lax.all_gather(occ_coef, "shell", axis=0, tiled=True)
    size_row = shell_size.reshape(1, -1)

    mine, over = pl.pallas_call(
        functools.partial(pick_kernel, windows, rows),
        out_shape=(jax.ShapeDtypeStruct((CAP, width), BF16), jax.ShapeDtypeStruct((1,), jnp.int32)),
        in_specs=[VMEM] * 4,
        out_specs=(VMEM, SMEM),
        compiler_params=pltpu.CompilerParams(vmem_limit_bytes=32 << 20),
        cost_estimate=pl.CostEstimate(flops=10**8, bytes_accessed=2 * 10**6, transcendentals=0),
        name="pick_rows",
    )(got, size_row, vir_coef, other)

    near = [mine] + [along_z(mine, s) for s in range(1, Z)]
    pieces, order = [], []
    for s, piece in enumerate(near):
        for dy in range(Y):
            pieces.append(piece if dy == 0 else swap(piece, 2))
            order.append(((z - s) % Z) * Y + (y ^ dy))
    far = [swap(piece, 1) for piece in pieces]
    order = jnp.stack(order + [core]).astype(jnp.int32)

    half = pl.pallas_call(
        functools.partial(half_kernel, windows, rows),
        out_shape=jax.ShapeDtypeStruct((2 * NOCC, windows * CAP), BF16),
        in_specs=[VMEM] * 3,
        out_specs=VMEM,
        scratch_shapes=[
            pltpu.VMEM((2 * NOCC, windows * CAP), F32),
        ],
        compiler_params=pltpu.CompilerParams(vmem_limit_bytes=48 << 20),
        cost_estimate=pl.CostEstimate(flops=8 * 10**9, bytes_accessed=4 * 10**6, transcendentals=0),
        name="half_transform",
    )(got, size_row, occ_full)

    tile = width // 3
    count = len(pieces)
    out = pl.pallas_call(
        functools.partial(last_kernel, count),
        out_shape=jax.ShapeDtypeStruct((2, NOCC, nvir), BF16),
        grid_spec=pltpu.PrefetchScalarGridSpec(
            num_scalar_prefetch=1,
            grid=(nvir // tile,),
            in_specs=[pl.BlockSpec((2 * NOCC, windows * CAP), lambda j, o: (0, 0))] + [ANY] * (2 * count),
            out_specs=pl.BlockSpec((2, NOCC, tile), lambda j, o: (0, 0, j)),
            scratch_shapes=[
                pltpu.VMEM((CORES, windows * CAP, width), BF16),
                pltpu.SemaphoreType.DMA((2 * count,)),
            ],
        ),
        compiler_params=pltpu.CompilerParams(vmem_limit_bytes=48 << 20),
        cost_estimate=pl.CostEstimate(flops=3 * 10**9, bytes_accessed=10**7, transcendentals=0),
        name="last_product",
    )(order, half, *pieces, *far)
    return out, over[0]


def per_device(*args):
    n = lax.axis_size("shell")
    here, nvir = args[5].shape
    sparse = LIVE_DEV * n * EDGE < n * here
    if not (sparse and n == Z * Y * CORES and here <= 256 and here % 16 == 0 and nvir % 768 == 0):
        return long_way(*args)
    out, over = short_way(*args)

    def again(carry):
        over, _ = carry
        over, *held = lax.optimization_barrier((over, *args))
        return over - 1, long_way(*held)

    return lax.while_loop(lambda carry: carry[0] > 0, again, (over, out))[1]


def solution(mesh):
    placed = (
        P(("groups", "shell"), None, None),
        P(("groups", "shell"), None),
        P(("groups", "shell")),
        P("groups"),
        P(("groups", "shell"), None),
        P(("groups", "shell"), None),
    )
    return jax.shard_map(
        per_device,
        mesh=mesh,
        in_specs=placed,
        out_specs=P(("groups", "shell"), None, None),
        check_vma=False,
    )
```

```python
import functools
import math

import jax
import jax.numpy as jnp
from jax import lax
from jax.experimental import pallas as pl
from jax.experimental.pallas import tpu as pltpu
from jax.sharding import PartitionSpec as P

EDGE = 16
NOCC = 256
BLK_DEV = 8
LIVE_DEV = 4
CAP = 160
Z, Y, CORES = 4, 2, 2
F32 = jnp.float32
BF16 = jnp.bfloat16


def padded_rows(matrix, starts, shell_size):
    offsets = jnp.arange(EDGE, dtype=jnp.int32)
    rows = jnp.minimum(starts[:, None] + offsets[None, :], matrix.shape[0] - 1)
    inside = offsets[None, :] < shell_size[:, None]
    return jnp.where(inside[:, :, None], matrix[rows], jnp.zeros((), matrix.dtype))


def half_transform(slot_rows, pairs, keep, occ_blocks):
    count = slot_rows.shape[0]
    vecs_here = slot_rows.shape[1]
    shells = occ_blocks.shape[0]
    group_size = math.gcd(512, count)
    turns = count // group_size
    shaped = slot_rows.reshape(count, vecs_here, EDGE, EDGE)

    def advance(total, turn):
        first = turn * group_size
        block = lax.dynamic_slice_in_dim(shaped, first, group_size, 0)
        okay = lax.dynamic_slice_in_dim(keep, first, group_size, 0)
        block = jnp.where(okay[:, None, None, None], block, jnp.zeros((), block.dtype))
        row_shell = lax.dynamic_slice_in_dim(pairs[:, 0], first, group_size, 0)
        col_shell = lax.dynamic_slice_in_dim(pairs[:, 1], first, group_size, 0)
        coefs = occ_blocks[row_shell]
        piece = jnp.einsum("kmi,kvmn->kvin", coefs, block, preferred_element_type=jnp.float32)
        return (total.at[col_shell].add(piece), None)

    start_total = jnp.zeros((shells, vecs_here, NOCC, EDGE), jnp.float32)
    half, _ = lax.scan(advance, start_total, jnp.arange(turns, dtype=jnp.int32))
    return half


def long_way(panels, block_pairs, block_count, shell_size, occ_coef, vir_coef):
    all_pairs, all_counts = (
        lax.all_gather(block_pairs, "shell", axis=0, tiled=True),
        lax.all_gather(block_count, "shell", axis=0, tiled=True),
    )
    turned = lax.all_to_all(panels, "shell", split_axis=1, concat_axis=0, tiled=True)
    occ_full = lax.all_gather(occ_coef, "shell", axis=0, tiled=True)
    starts = jnp.cumsum(shell_size) - shell_size
    occ_blocks = padded_rows(occ_full, starts, shell_size)
    slot_total = turned.shape[0]
    position = jnp.arange(slot_total, dtype=jnp.int32)
    live = position % BLK_DEV < all_counts[position // BLK_DEV]
    half = half_transform(turned, all_pairs, live, occ_blocks)
    hidden = half.astype(jnp.bfloat16)
    vir_full = lax.all_gather(vir_coef, "shell", axis=0, tiled=True)
    vir_blocks = padded_rows(vir_full, starts, shell_size)
    result = jnp.einsum("svin,sna->via", hidden, vir_blocks, preferred_element_type=jnp.float32)
    return result.astype(jnp.bfloat16)


def iota(shape, dim):
    return lax.broadcasted_iota(jnp.int32, shape, dim)


def column_of(row, mask):
    return jnp.sum(jnp.where(mask, row, 0.0), axis=1, keepdims=True)


def row_of(column, mask):
    return jnp.sum(jnp.where(mask, column, 0.0), axis=0, keepdims=True)


def one_hots(ids, shells):
    lanes = iota(ids.shape, 1)
    return jnp.concatenate(
        [(ids == lanes + 128 * k).astype(F32) for k in range(shells // 128)], axis=1
    )


def shell_table(col_hot, size_row, rows):
    shells = size_row.shape[1]
    sub, lane = iota((shells, shells), 0), iota((shells, shells), 1)
    used_row = jnp.max(col_hot, axis=0, keepdims=True)
    before, same = lane < sub, lane == sub
    starts = column_of(size_row, before)
    ahead = column_of(size_row * used_row, before)
    size = column_of(size_row, same)
    used = column_of(used_row, same)
    edge = (iota((shells, 128), 1) * rows).astype(F32)
    reach = used * jnp.clip(edge - starts, 0.0, size)
    before_window = jnp.sum(reach, axis=0, keepdims=True)
    return starts, size, used, ahead, before_window


def lane_value(row, index):
    return jnp.sum(jnp.where(iota(row.shape, 1) == index, row, 0.0), axis=1, keepdims=True)


def pick_kernel(windows, rows, code_ref, size_ref, own_ref, other_ref, out_ref, over_ref):
    shells = size_ref.shape[1]
    here = rows // 2
    me = lax.axis_index("shell")
    core = lax.rem(me, 2)
    window = lax.div(me, 2)
    code = code_ref[...].reshape(-1, 128)
    col_hot = one_hots(jnp.where(code < 0, -1, code % shells), shells)
    size_row = size_ref[...].astype(F32)
    starts, size, used, ahead, before_window = shell_table(col_hot, size_row, rows)
    lanes = iota(before_window.shape, 1)
    after = jnp.sum(
        used * jnp.clip(((iota((shells, 128), 1) + 1) * rows).astype(F32) - starts, 0.0, size), axis=0, keepdims=True
    )
    most = jnp.max(jnp.where(lanes < windows, after - before_window, 0.0))
    over_ref[0] = jnp.where(most > CAP, 1, 0).astype(jnp.int32)
    base = lane_value(before_window, window)

    def chosen(first):
        where = (iota((shells, 256), 1) + first).astype(F32) - starts
        inside = (used > 0.0) & (where >= 0.0) & (where < size)
        place = jnp.sum(jnp.where(inside, ahead + where + 1.0, 0.0), axis=0, keepdims=True)
        place = jnp.where(place > 0.0, place - 1.0 - base, -1.0)
        hot = place == iota((CAP, 256), 0).astype(F32)
        return jnp.where(hot, 1.0, 0.0).astype(BF16)[:, :here]

    mine = chosen(window * rows + core * here)
    theirs = chosen(window * rows + (1 - core) * here)
    width = out_ref.shape[1]
    own = own_ref[:, pl.ds(pl.multiple_of(core * width, 128), width)]
    total = jnp.dot(mine, own, preferred_element_type=F32)
    total += jnp.dot(theirs, other_ref[...], preferred_element_type=F32)
    out_ref[...] = total.astype(BF16)


def half_kernel(windows, rows, code_ref, got_ref, size_ref, *refs):
    parts, (out_ref, total_ref, occ_ref, sems) = refs[:4], refs[4:]
    me = lax.axis_index("shell")
    core, y, z = lax.rem(me, 2), lax.rem(lax.div(me, 2), 2), lax.div(me, 4)
    here = rows // 2
    copies = []
    for dc in range(CORES):
        for dy in range(Y):
            for s in range(Z):
                source = (lax.rem(z - s + Z, Z) * Y + lax.rem(y + dy, Y)) * CORES + lax.rem(core + dc, CORES)
                copies.append(
                    pltpu.make_async_copy(
                        parts[dc * Y + dy].at[pl.ds(s * here, here), :],
                        occ_ref.at[pl.ds(pl.multiple_of(source * here, 16), here), :],
                        sems.at[len(copies)],
                    )
                )
    for copy in copies:
        copy.start()

    shells = size_ref.shape[1]
    nbf = occ_ref.shape[0]
    code = code_ref[...].reshape(-1, 128)
    slots = code.shape[0]
    kept = LIVE_DEV * (slots // BLK_DEV)
    cols = one_hots(jnp.where(code < 0, -1, code % shells), shells)
    rws = one_hots(jnp.where(code < 0, -1, code // shells), shells)
    alive = (code >= 0).astype(F32)
    sub, lane = iota((slots, slots), 0), iota((slots, slots), 1)
    rank = row_of(alive, sub < lane)
    alive_row = row_of(alive, sub == lane)
    take = (rank == iota((kept, slots), 0).astype(F32)) & (alive_row > 0.0)
    take = jnp.where(take, 1.0, 0.0).astype(BF16)

    def taken(array):
        return jnp.dot(take, array.astype(BF16), preferred_element_type=F32)

    col_hot, row_hot = taken(cols), taken(rws)
    size_row = size_ref[...].astype(F32)
    starts, size, used, ahead, before_window = shell_table(col_hot, size_row, rows)
    sub, lane = iota((shells, shells), 0), iota((shells, shells), 1)
    starts_row = row_of(starts, sub == lane)
    ahead_row = row_of(ahead, sub == lane)

    def spread(hot, row):
        column = jnp.sum(hot * row, axis=1, keepdims=True)
        wide = jnp.broadcast_to(column, (kept, 128)).reshape(kept, 1, 128)
        return jnp.broadcast_to(wide, (kept, EDGE, 128)).reshape(kept * EDGE, 128)

    step = (iota((kept * EDGE, 128), 0) % EDGE).astype(F32)
    first, length, skip = (spread(col_hot, r) for r in (starts_row, size_row, ahead_row))
    place = skip + step
    for w in range(1, windows):
        shift = CAP - (lane_value(before_window, w) - lane_value(before_window, w - 1))
        place += jnp.where(first + step >= float(rows * w), shift, 0.0)
    place = jnp.where(step < length, place, -1.0)
    first_r, length_r = (spread(row_hot, r) for r in (starts_row, size_row))
    where_r = jnp.where(step < length_r, first_r + step, -1.0)

    span = 16 * EDGE
    width = out_ref.shape[1]
    s_in, l_in = iota((span, span), 0), iota((span, span), 1)
    keep_m = (l_in // EDGE) == (s_in % EDGE)
    fold = jnp.where((s_in % EDGE) == (l_in % EDGE), 1.0, 0.0).astype(BF16)
    same_slot = (s_in // EDGE) == (l_in // EDGE)
    got = got_ref[...].astype(F32)
    blocks = [taken(got[:, p * BLK_DEV : (p + 1) * BLK_DEV, :].reshape(slots, span)) for p in range(2)]
    for copy in copies:
        copy.wait()
    for g in range(kept // 16):
        at = slice(g * span, (g + 1) * span)
        r_hot = where_r[at, :1] == iota((span, nbf), 1).astype(F32)
        occ_rows = jnp.dot(jnp.where(r_hot, 1.0, 0.0).astype(BF16), occ_ref[...], preferred_element_type=F32)
        occ_rows = occ_rows.astype(BF16)
        c_hot = place[at, :1] == iota((span, width), 1).astype(F32)
        c_hot = jnp.where(c_hot, 1.0, 0.0).astype(BF16)
        for p in range(2):
            block = blocks[p][g * 16 : (g + 1) * 16].reshape(16, 1, span)
            block = jnp.broadcast_to(block, (16, EDGE, span)).reshape(span, span)
            block = jnp.where(keep_m, block, 0.0).astype(BF16)
            diag = jnp.dot(block, fold, preferred_element_type=F32)
            diag = jnp.where(same_slot, diag, 0.0).astype(BF16)
            placed = jnp.dot(diag, c_hot, preferred_element_type=F32).astype(BF16)
            piece = lax.dot_general(occ_rows, placed, (((0,), (0,)), ((), ())), preferred_element_type=F32)
            rows_p = slice(p * NOCC, (p + 1) * NOCC)
            if g == 0:
                total_ref[rows_p, :] = piece
            else:
                total_ref[rows_p, :] += piece
    out_ref[...] = total_ref[...].astype(BF16)


def last_kernel(count, order_ref, half_ref, *refs):
    pieces, (out_ref, all_ref, sems) = refs[: 2 * count], refs[2 * count :]
    width = pieces[0].shape[1]
    tile = out_ref.shape[2]
    per = width // tile
    core = order_ref[count]
    j = pl.program_id(0)

    def copies(far):
        for k in range(count):
            yield pltpu.make_async_copy(
                pieces[far * count + k],
                all_ref.at[far, pl.ds(pl.multiple_of(order_ref[k] * CAP, 16), CAP), :],
                sems.at[far * count + k],
            )

    @pl.when(j == 0)
    def _():
        for far in range(2):
            for copy in copies(far):
                copy.start()

    for far in range(2):

        @pl.when(j == far * per)
        def _():
            for copy in copies(far):
                copy.wait()

    right = all_ref[lax.div(j, per), :, pl.ds(pl.multiple_of(lax.rem(j, per) * tile, 128), tile)]
    for p in range(2):
        out_ref[p] = jnp.dot(half_ref[p * NOCC : (p + 1) * NOCC, :], right, preferred_element_type=F32).astype(BF16)


VMEM = pl.BlockSpec(memory_space=pltpu.VMEM)
SMEM = pl.BlockSpec(memory_space=pltpu.SMEM)
ANY = pl.BlockSpec(memory_space=pl.ANY)


def short_way(panels, block_pairs, block_count, shell_size, occ_coef, vir_coef):
    n = lax.axis_size("shell")
    windows = n // CORES
    here, nvir = vir_coef.shape
    rows = CORES * here
    width = nvir // CORES
    shells = shell_size.shape[0]
    me = lax.axis_index("shell")
    core = me % 2
    y = (me // 2) % 2
    z = me // 4

    def swap(array, bit):
        return lax.ppermute(array, "shell", [(i, i ^ bit) for i in range(n)])

    def along_z(array, s):
        return lax.ppermute(array, "shell", [(i, (i + 4 * s) % n) for i in range(n)])

    def between(array, steps):
        return lax.ppermute(array, "shell", [(4 * a + k, 4 * b + k) for a, b in steps for k in range(4)])

    keep = jnp.arange(BLK_DEV, dtype=jnp.int32) < block_count[0]
    code = jnp.where(keep, block_pairs[:, 1] + shells * block_pairs[:, 0], -1)
    code = jnp.broadcast_to(code[None, :, None], (n, BLK_DEV, 128))
    code = lax.all_to_all(code, "shell", split_axis=0, concat_axis=0, tiled=True)
    other = swap(lax.dynamic_slice_in_dim(vir_coef, (1 - core) * width, width, 1), 1)
    size_row = shell_size.reshape(1, -1)

    mine, over = pl.pallas_call(
        functools.partial(pick_kernel, windows, rows),
        out_shape=(jax.ShapeDtypeStruct((CAP, width), BF16), jax.ShapeDtypeStruct((1,), jnp.int32)),
        in_specs=[VMEM] * 4,
        out_specs=(VMEM, SMEM),
        compiler_params=pltpu.CompilerParams(vmem_limit_bytes=32 << 20),
        cost_estimate=pl.CostEstimate(flops=10**8, bytes_accessed=2 * 10**6, transcendentals=0),
        name="pick_rows",
    )(code, size_row, vir_coef, other)

    near = (z == 1) | (z == 2)
    pair = between(mine, [(0, 1), (1, 0), (2, 3), (3, 2)])
    middle = between(mine, [(1, 2), (2, 1)])
    middle_far = between(pair, [(1, 2), (2, 1)])
    outward = between(middle, [(1, 0), (2, 3)])
    outward_far = between(middle_far, [(1, 0), (2, 3)])
    columns = [mine, pair, jnp.where(near, middle, outward), jnp.where(near, middle_far, outward_far)]
    sources = [z, z ^ 1, jnp.where(z < 2, 2, 1), jnp.where(z < 2, 3, 0)]
    swapped = [swap(piece, 2) for piece in columns]

    line = jnp.concatenate([occ_coef] + [along_z(occ_coef, s) for s in range(1, Z)], axis=0)
    plane = [line, swap(line, 2)]
    plane += [swap(part, 1) for part in plane]

    send = panels.transpose(1, 0, 2).reshape(n, 2 * BLK_DEV, EDGE * EDGE)
    send, _ = lax.optimization_barrier((send, mine))
    got = lax.all_to_all(send, "shell", split_axis=0, concat_axis=0, tiled=True)

    half = pl.pallas_call(
        functools.partial(half_kernel, windows, rows),
        out_shape=jax.ShapeDtypeStruct((2 * NOCC, windows * CAP), BF16),
        in_specs=[VMEM] * 3 + [ANY] * 4,
        out_specs=VMEM,
        scratch_shapes=[
            pltpu.VMEM((2 * NOCC, windows * CAP), F32),
            pltpu.VMEM((n * here, NOCC), BF16),
            pltpu.SemaphoreType.DMA((n,)),
        ],
        compiler_params=pltpu.CompilerParams(vmem_limit_bytes=32 << 20),
        cost_estimate=pl.CostEstimate(flops=8 * 10**9, bytes_accessed=4 * 10**6, transcendentals=0),
        name="half_transform",
    )(code, got, size_row, *plane)

    swapped[3], half = lax.optimization_barrier((swapped[3], half))
    pieces, order = [], []
    for k in range(Z):
        pieces += [columns[k], swapped[k]]
        order += [sources[k] * Y + y, sources[k] * Y + (y ^ 1)]
    far = [swap(piece, 1) for piece in pieces]
    order = jnp.stack(order + [core]).astype(jnp.int32)

    tile = width // 3
    count = len(pieces)
    out = pl.pallas_call(
        functools.partial(last_kernel, count),
        out_shape=jax.ShapeDtypeStruct((2, NOCC, nvir), BF16),
        grid_spec=pltpu.PrefetchScalarGridSpec(
            num_scalar_prefetch=1,
            grid=(nvir // tile,),
            in_specs=[VMEM] + [ANY] * (2 * count),
            out_specs=pl.BlockSpec((2, NOCC, tile), lambda j, o: (0, 0, (j + 3 * o[count]) % 6)),
            scratch_shapes=[
                pltpu.VMEM((CORES, windows * CAP, width), BF16),
                pltpu.SemaphoreType.DMA((2 * count,)),
            ],
        ),
        compiler_params=pltpu.CompilerParams(vmem_limit_bytes=32 << 20),
        cost_estimate=pl.CostEstimate(flops=3 * 10**9, bytes_accessed=10**7, transcendentals=0),
        name="last_product",
    )(order, half, *pieces, *far)
    return out, over[0]


def per_device(*args):
    n = lax.axis_size("shell")
    here, nvir = args[5].shape
    sparse = LIVE_DEV * n * EDGE < n * here
    if not (sparse and n == Z * Y * CORES and here <= 256 and here % 16 == 0 and nvir % 768 == 0):
        return long_way(*args)
    out, over = short_way(*args)

    def again(carry):
        over, _ = carry
        over, *held = lax.optimization_barrier((over, *args))
        return over - 1, long_way(*held)

    return lax.while_loop(lambda carry: carry[0] > 0, again, (over, out))[1]


def solution(mesh):
    placed = (
        P(("groups", "shell"), None, None),
        P(("groups", "shell"), None),
        P(("groups", "shell")),
        P("groups"),
        P(("groups", "shell"), None),
        P(("groups", "shell"), None),
    )
    return jax.shard_map(
        per_device,
        mesh=mesh,
        in_specs=placed,
        out_specs=P(("groups", "shell"), None, None),
        check_vma=False,
    )
```

```python
import functools
import math

import jax
import jax.numpy as jnp
from jax import lax
from jax.experimental import pallas as pl
from jax.experimental.pallas import tpu as pltpu
from jax.sharding import PartitionSpec as P

EDGE = 16
NOCC = 256
BLK_DEV = 8
LIVE_DEV = 4
CAP = 128
Z, Y, CORES = 4, 2, 2
F32 = jnp.float32
BF16 = jnp.bfloat16


def padded_rows(matrix, starts, shell_size):
    offsets = jnp.arange(EDGE, dtype=jnp.int32)
    rows = jnp.minimum(starts[:, None] + offsets[None, :], matrix.shape[0] - 1)
    inside = offsets[None, :] < shell_size[:, None]
    return jnp.where(inside[:, :, None], matrix[rows], jnp.zeros((), matrix.dtype))


def half_transform(slot_rows, pairs, keep, occ_blocks):
    count = slot_rows.shape[0]
    vecs_here = slot_rows.shape[1]
    shells = occ_blocks.shape[0]
    group_size = math.gcd(512, count)
    turns = count // group_size
    shaped = slot_rows.reshape(count, vecs_here, EDGE, EDGE)

    def advance(total, turn):
        first = turn * group_size
        block = lax.dynamic_slice_in_dim(shaped, first, group_size, 0)
        okay = lax.dynamic_slice_in_dim(keep, first, group_size, 0)
        block = jnp.where(okay[:, None, None, None], block, jnp.zeros((), block.dtype))
        row_shell = lax.dynamic_slice_in_dim(pairs[:, 0], first, group_size, 0)
        col_shell = lax.dynamic_slice_in_dim(pairs[:, 1], first, group_size, 0)
        coefs = occ_blocks[row_shell]
        piece = jnp.einsum("kmi,kvmn->kvin", coefs, block, preferred_element_type=jnp.float32)
        return (total.at[col_shell].add(piece), None)

    start_total = jnp.zeros((shells, vecs_here, NOCC, EDGE), jnp.float32)
    half, _ = lax.scan(advance, start_total, jnp.arange(turns, dtype=jnp.int32))
    return half


def long_way(turned, pairs, live, shell_size, occ_coef, vir_coef):
    occ_full = lax.all_gather(occ_coef, "shell", axis=0, tiled=True)
    starts = jnp.cumsum(shell_size) - shell_size
    occ_blocks = padded_rows(occ_full, starts, shell_size)
    half = half_transform(turned, pairs, live, occ_blocks)
    hidden = half.astype(jnp.bfloat16)
    vir_full = lax.all_gather(vir_coef, "shell", axis=0, tiled=True)
    vir_blocks = padded_rows(vir_full, starts, shell_size)
    result = jnp.einsum("svin,sna->via", hidden, vir_blocks, preferred_element_type=jnp.float32)
    return result.astype(jnp.bfloat16)


def from_start(panels, block_pairs, block_count, *rest):
    pairs = lax.all_gather(block_pairs, "shell", axis=0, tiled=True)
    counts = lax.all_gather(block_count, "shell", axis=0, tiled=True)
    turned = lax.all_to_all(panels, "shell", split_axis=1, concat_axis=0, tiled=True)
    position = jnp.arange(turned.shape[0], dtype=jnp.int32)
    live = position % BLK_DEV < counts[position // BLK_DEV]
    return long_way(turned, pairs, live, *rest)


def iota(shape, dim):
    return lax.broadcasted_iota(jnp.int32, shape, dim)


def column_of(row, mask):
    return jnp.sum(jnp.where(mask, row, 0.0), axis=1, keepdims=True)


def row_of(column, mask):
    return jnp.sum(jnp.where(mask, column, 0.0), axis=0, keepdims=True)


def zero_one(mask):
    return jnp.where(mask, 1.0, 0.0)


def lane_value(row, index):
    return jnp.sum(jnp.where(iota(row.shape, 1) == index, row, 0.0), axis=1, keepdims=True)


def one_hots(ids, shells):
    lanes = iota(ids.shape, 1).astype(F32)
    return jnp.concatenate([zero_one(ids == lanes + 128.0 * k) for k in range(shells // 128)], axis=1)


def slot_hots(got, shells):
    ids = got[:, 2 * BLK_DEV :, :].reshape(-1, 256)
    return one_hots(ids[:, :128], shells), one_hots(ids[:, 128:], shells)


class Shells:
    def __init__(self, size_row):
        shells = size_row.shape[1]
        sub, lane = iota((shells, shells), 0), iota((shells, shells), 1)
        self.before, self.same = lane < sub, lane == sub
        self.starts = column_of(size_row, self.before)
        self.size = column_of(size_row, self.same)
        self.odd = self.starts - 2.0 * jnp.floor(self.starts * 0.5)


class Used:
    def __init__(self, shells, hot, window):
        self.used = column_of(jnp.max(hot, axis=0, keepdims=True), shells.same)
        self.extra, self.ahead, self.edges = [], [], []
        edge = (iota((hot.shape[1], 128), 1) * window).astype(F32)
        reach = jnp.clip(edge - shells.starts, 0.0, shells.size)
        for parity in range(2):
            extra = 1.0 - shells.odd if parity == 0 else shells.odd
            count = self.used * jnp.floor((shells.size + extra) * 0.5)
            count_row = row_of(count, shells.same)
            self.extra.append(extra)
            self.ahead.append(column_of(count_row, shells.before))
            self.edges.append(jnp.sum(self.used * jnp.floor((reach + extra) * 0.5), axis=0, keepdims=True))


def pack_kernel(pairs_ref, count_ref, panels_ref, vir_ref, occ_ref, send_ref, *outs):
    me = lax.axis_index("shell")
    core, y = lax.rem(me, 2), lax.rem(lax.div(me, 2), 2)
    here, nvir = vir_ref.shape
    width, thin = nvir // CORES, occ_ref.shape[1] // CORES
    for dy in range(2):
        parity = lax.rem(y + dy, 2)
        pick = zero_one(iota((here // 2, here), 1) == 2 * iota((here // 2, here), 0) + parity).astype(BF16)
        for dc in range(2):
            half = lax.rem(core + dc, 2)
            out = outs[2 * dy + dc]
            part = vir_ref[:, pl.ds(pl.multiple_of(half * width, 128), width)]
            out[:, :width] = jnp.dot(pick, part, preferred_element_type=F32).astype(BF16)
            part = occ_ref[:, pl.ds(pl.multiple_of(half * thin, 128), thin)]
            out[:, width:] = jnp.dot(pick, part, preferred_element_type=F32).astype(BF16)
    n = send_ref.shape[0]
    turned = jnp.swapaxes(panels_ref[...].astype(F32), 0, 1)
    send_ref[:, : 2 * BLK_DEV, :] = turned.reshape(n, 2 * BLK_DEV, EDGE * EDGE).astype(BF16)
    slot, lane = iota((BLK_DEV, 256), 0), iota((BLK_DEV, 256), 1)
    ids = jnp.zeros((BLK_DEV, 256), jnp.int32)
    for g in range(BLK_DEV):
        ids = jnp.where(slot == g, jnp.where(lane < 128, pairs_ref[g, 1], pairs_ref[g, 0]), ids)
    ids = jnp.where(slot < count_ref[0], ids, -1).astype(F32)
    send_ref[:, 2 * BLK_DEV :, :] = jnp.broadcast_to(ids[None], (n, BLK_DEV, 256)).astype(BF16)


def pick_kernel(here, got_ref, size_ref, *refs):
    sources, (out_ref, over_ref) = refs[:4], refs[4:]
    me = lax.axis_index("shell")
    core, y, z = lax.rem(me, 2), lax.rem(lax.div(me, 2), 2), lax.div(me, 4)
    window = CORES * Y * here
    shell_count = size_ref.shape[1]
    got = got_ref[...].astype(F32)
    shells = Shells(size_ref[...].astype(F32))
    lists = [Used(shells, hot, window) for hot in slot_hots(got, shell_count)]
    most = jnp.zeros((1, 1), F32)
    lane = iota((1, 128), 1)
    for chosen in lists:
        for edges in chosen.edges:
            later = jnp.concatenate([edges[:, 1:], edges[:, :1]], axis=1)
            most = jnp.maximum(most, jnp.max(jnp.where(lane < Z, later - edges, 0.0), axis=1, keepdims=True))
    over_ref[0] = jnp.where(jnp.max(most) > CAP, 1, 0).astype(jnp.int32)

    width = vir_width = out_ref.shape[1] - 128
    even = y == 0
    totals = [jnp.zeros((CAP, width), F32), jnp.zeros((CAP, 128), F32)]
    columns = [slice(0, vir_width), slice(vir_width, vir_width + 128)]
    extra = jnp.where(even, lists[0].extra[0], lists[0].extra[1])
    for k, source in enumerate(sources):
        device = 4 * z + 2 * lax.rem(y + k // 2, 2) + lax.rem(core + k % 2, 2)
        row = (2 * iota((shell_count, 128), 1) + device * here + y).astype(F32)
        where = row - shells.starts
        inside = (where >= 0.0) & (where < shells.size)
        within = jnp.floor((where + extra) * 0.5)
        for chosen, total, column in zip(lists, range(2), columns):
            ahead = jnp.where(even, chosen.ahead[0], chosen.ahead[1])
            base = lane_value(jnp.where(even, chosen.edges[0], chosen.edges[1]), z)
            place = jnp.where(inside & (chosen.used > 0.0), ahead + within + 1.0, 0.0)
            place = jnp.sum(place, axis=0, keepdims=True)
            place = jnp.where(place > 0.0, place - 1.0 - base, -1.0)
            hot = zero_one(place == iota((CAP, 128), 0).astype(F32)).astype(BF16)
            totals[total] += jnp.dot(
                hot[:, : here // 2], source[:, column], preferred_element_type=F32
            )
    for total, column in zip(totals, columns):
        out_ref[:, column] = total.astype(BF16)


def place_kernel(here, got_ref, size_ref, rows_ref, placed_ref):
    window = CORES * Y * here
    shell_count = size_ref.shape[1]
    got = got_ref[...].astype(F32)
    size_row = size_ref[...].astype(F32)
    shells = Shells(size_row)
    hots = slot_hots(got, shell_count)
    lists = [Used(shells, hot, window) for hot in hots]
    slots = hots[0].shape[0]
    kept = LIVE_DEV * (slots // BLK_DEV)
    alive = jnp.broadcast_to(jnp.sum(hots[0], axis=1, keepdims=True), (slots, slots))
    sub, lane = iota((slots, slots), 0), iota((slots, slots), 1)
    rank = row_of(alive, sub < lane)
    alive_row = row_of(alive, sub == lane)
    take = (rank == iota((kept, slots), 0).astype(F32)) & (alive_row > 0.0)
    take = zero_one(take).astype(BF16)

    def taken(array):
        return jnp.dot(take, array.astype(BF16), preferred_element_type=F32)

    def spread(hot, column):
        value = jnp.sum(hot * row_of(column, shells.same), axis=1, keepdims=True)
        wide = jnp.broadcast_to(value, (kept, 128)).reshape(kept, 1, 128)
        return jnp.broadcast_to(wide, (kept, EDGE, 128)).reshape(kept * EDGE, 128)

    at = iota((kept * EDGE, 128), 0) % EDGE
    step = at.astype(F32)

    def places(hot, chosen):
        hot = taken(hot)
        first, length = spread(hot, shells.starts), spread(hot, shells.size)
        row = first + step
        odd = (row - 2.0 * jnp.floor(row * 0.5)) > 0.0
        place = jnp.where(odd, spread(hot, chosen.ahead[1]) + CAP, spread(hot, chosen.ahead[0]))
        place += jnp.floor(step * 0.5)
        for w in range(1, Z):
            gap = [2.0 * CAP - (lane_value(e, w) - lane_value(e, w - 1)) for e in chosen.edges]
            place += jnp.where(row >= float(window * w), jnp.where(odd, gap[1], gap[0]), 0.0)
        return jnp.where(step < length, place, -1.0)[:, :1]

    place_c, place_r = places(hots[0], lists[0]), places(hots[1], lists[1])
    span = 16 * EDGE
    width = rows_ref.shape[1]
    s_in, l_in = iota((span, span), 0), iota((span, span), 1)
    keep_m = (l_in // EDGE) == (s_in % EDGE)
    fold = zero_one((s_in % EDGE) == (l_in % EDGE)).astype(BF16)
    same_slot = (s_in // EDGE) == (l_in // EDGE)
    blocks = [taken(got[:, p * BLK_DEV : (p + 1) * BLK_DEV, :].reshape(slots, span)) for p in range(2)]
    lanes = iota((span, width), 1).astype(F32)
    for g in range(kept // 16):
        rows = slice(g * span, (g + 1) * span)
        rows_ref[rows, :] = zero_one(place_r[rows] == lanes).astype(BF16)
        c_hot = zero_one(place_c[rows] == lanes).astype(BF16)
        for p in range(2):
            block = blocks[p][g * 16 : (g + 1) * 16].reshape(16, 1, span)
            block = jnp.broadcast_to(block, (16, EDGE, span)).reshape(span, span)
            block = jnp.where(keep_m, block, 0.0).astype(BF16)
            diag = jnp.dot(block, fold, preferred_element_type=F32)
            diag = jnp.where(same_slot, diag, 0.0).astype(BF16)
            placed_ref[p, rows, :] = jnp.dot(diag, c_hot, preferred_element_type=F32).astype(BF16)


def last_kernel(count, me_ref, rows_ref, placed_ref, *refs):
    pieces, (out_ref, vir_ref, occ_ref, half_ref, sems) = refs[: 2 * count], refs[2 * count :]
    width = vir_ref.shape[2]
    tile = out_ref.shape[2]
    per = width // tile
    core = lax.rem(me_ref[0], CORES)
    chip = lax.div(me_ref[0], CORES)
    j = pl.program_id(0)

    def copies(far, part):
        for k in range(count):
            rows = pl.ds(pl.multiple_of((chip ^ k) * CAP, CAP), CAP)
            columns = pl.ds(0, width) if part == 0 else pl.ds(width, 128)
            target = vir_ref.at[far, rows, :] if part == 0 else occ_ref.at[far, rows, :]
            yield pltpu.make_async_copy(
                pieces[far * count + k].at[:, columns], target, sems.at[(2 * far + part) * count + k]
            )

    @pl.when(j == 0)
    def _():
        for far, part in ((0, 1), (1, 1), (0, 0), (1, 0)):
            for copy in copies(far, part):
                copy.start()
        for far in range(2):
            for copy in copies(far, 1):
                copy.wait()
        parts = [
            jnp.dot(rows_ref[...], occ_ref[far], preferred_element_type=F32).astype(BF16) for far in range(2)
        ]
        for far in range(2):
            half = jnp.where(far == 0, core, 1 - core)
            for p in range(2):
                piece = lax.dot_general(
                    parts[far], placed_ref[p], (((0,), (0,)), ((), ())), preferred_element_type=F32
                )
                start = pl.multiple_of(p * NOCC + half * 128, 128)
                half_ref[pl.ds(start, 128), :] = piece.astype(BF16)

    for far in range(2):

        @pl.when(j == far * per)
        def _():
            for copy in copies(far, 0):
                copy.wait()

    right = vir_ref[lax.div(j, per), :, pl.ds(pl.multiple_of(lax.rem(j, per) * tile, 128), tile)]
    for p in range(2):
        out_ref[p] = jnp.dot(half_ref[p * NOCC : (p + 1) * NOCC, :], right, preferred_element_type=F32).astype(BF16)


VMEM = pl.BlockSpec(memory_space=pltpu.VMEM)
SMEM = pl.BlockSpec(memory_space=pltpu.SMEM)
ANY = pl.BlockSpec(memory_space=pl.ANY)


def shape(*dims, dtype=BF16):
    return jax.ShapeDtypeStruct(dims, dtype)


def params(mib):
    return pltpu.CompilerParams(vmem_limit_bytes=mib << 20)


def cost(flops, nbytes):
    return pl.CostEstimate(flops=int(flops), bytes_accessed=int(nbytes), transcendentals=0)


def short_way(panels, block_pairs, block_count, shell_size, occ_coef, vir_coef):
    n = lax.axis_size("shell")
    here, nvir = vir_coef.shape
    width = nvir // CORES
    packed = width + NOCC // CORES
    room = Z * Y * CAP
    me = lax.axis_index("shell")
    size_row = shell_size.reshape(1, -1)

    def swap(array, bit):
        return lax.ppermute(array, "shell", [(i, i ^ bit) for i in range(n)])

    send, keep, to_core, to_y, to_both = pl.pallas_call(
        pack_kernel,
        out_shape=[shape(n, 3 * BLK_DEV, EDGE * EDGE)] + [shape(here // 2, packed)] * 4,
        in_specs=[SMEM] * 2 + [VMEM] * 3,
        out_specs=[VMEM] * 5,
        compiler_params=params(32),
        cost_estimate=cost(3e8, 3e6),
        name="pack_rows",
    )(block_pairs, block_count, panels, vir_coef, occ_coef)
    fresh = [keep, swap(to_core, 1), swap(to_y, 2), swap(to_both, 3)]
    got = lax.all_to_all(send, "shell", split_axis=0, concat_axis=0, tiled=True)

    mine, over = pl.pallas_call(
        functools.partial(pick_kernel, here),
        out_shape=(shape(CAP, packed), shape(1, dtype=jnp.int32)),
        in_specs=[VMEM] * 6,
        out_specs=(VMEM, SMEM),
        compiler_params=params(32),
        cost_estimate=cost(3e8, 2e6),
        name="pick_rows",
    )(got, size_row, *fresh)

    across, beside, mine_y = swap(mine, 8), swap(mine, 4), swap(mine, 2)
    beside, mine_y, got_late = lax.optimization_barrier((beside, mine_y, got))
    beside_y = swap(beside, 2)

    rows, placed = pl.pallas_call(
        functools.partial(place_kernel, here),
        out_shape=(shape(LIVE_DEV * n * EDGE, room), shape(2, LIVE_DEV * n * EDGE, room)),
        in_specs=[VMEM] * 2,
        out_specs=(VMEM, VMEM),
        compiler_params=params(32),
        cost_estimate=cost(4e9, 8e6),
        name="place_panels",
    )(got_late, size_row)

    across, beside_y, rows, placed = lax.optimization_barrier((across, beside_y, rows, placed))
    corner, across_y = swap(across, 4), swap(across, 2)
    corner, across_y = lax.optimization_barrier((corner, across_y))
    corner_y = swap(corner, 2)
    pieces = [mine, mine_y, beside, beside_y, across, across_y, corner, corner_y]
    far = [swap(piece, 1) for piece in pieces]

    tile = width // 3
    count = len(pieces)
    out = pl.pallas_call(
        functools.partial(last_kernel, count),
        out_shape=shape(2, NOCC, nvir),
        grid_spec=pltpu.PrefetchScalarGridSpec(
            num_scalar_prefetch=1,
            grid=(nvir // tile,),
            in_specs=[VMEM] * 2 + [ANY] * (2 * count),
            out_specs=pl.BlockSpec((2, NOCC, tile), lambda j, o: (0, 0, (j + 3 * (o[0] % 2)) % 6)),
            scratch_shapes=[
                pltpu.VMEM((CORES, room, width), BF16),
                pltpu.VMEM((CORES, room, 128), BF16),
                pltpu.VMEM((2 * NOCC, room), BF16),
                pltpu.SemaphoreType.DMA((4 * count,)),
            ],
        ),
        compiler_params=params(32),
        cost_estimate=cost(4e9, 1e7),
        name="last_product",
    )(me.reshape(1), rows, placed, *pieces, *far)
    return out, over[0], got


def per_device(*args):
    n = lax.axis_size("shell")
    here, nvir = args[5].shape
    sparse = LIVE_DEV * n * EDGE < n * here
    if not (sparse and n == Z * Y * CORES and here <= 256 and here % 16 == 0 and nvir % 768 == 0):
        return from_start(*args)
    out, over, got = short_way(*args)

    def again(carry):
        over, _ = carry
        over, got_now, *held = lax.optimization_barrier((over, got, *args[3:]))
        turned = got_now[:, : 2 * BLK_DEV].reshape(n, 2, BLK_DEV, EDGE * EDGE).swapaxes(1, 2)
        turned = turned.reshape(n * BLK_DEV, 2, EDGE * EDGE)
        ids = got_now[:, 2 * BLK_DEV :].reshape(n * BLK_DEV, 256)
        pairs = jnp.stack([ids[:, 128], ids[:, 0]], axis=1).astype(jnp.int32)
        return over - 1, long_way(turned, jnp.maximum(pairs, 0), pairs[:, 1] >= 0, *held)

    return lax.while_loop(lambda carry: carry[0] > 0, again, (over, out))[1]


def solution(mesh):
    placed = (
        P(("groups", "shell"), None, None),
        P(("groups", "shell"), None),
        P(("groups", "shell")),
        P("groups"),
        P(("groups", "shell"), None),
        P(("groups", "shell"), None),
    )
    return jax.shard_map(
        per_device,
        mesh=mesh,
        in_specs=placed,
        out_specs=P(("groups", "shell"), None, None),
        check_vma=False,
    )
```

```python
import functools
import math

import jax
import jax.numpy as jnp
from jax import lax
from jax.experimental import pallas as pl
from jax.experimental.pallas import tpu as pltpu
from jax.sharding import PartitionSpec as P

EDGE = 16
NOCC = 256
BLK_DEV = 8
LIVE_DEV = 4
CAP = 128
Z, Y, CORES = 4, 2, 2
F32 = jnp.float32
BF16 = jnp.bfloat16


def padded_rows(matrix, starts, shell_size):
    offsets = jnp.arange(EDGE, dtype=jnp.int32)
    rows = jnp.minimum(starts[:, None] + offsets[None, :], matrix.shape[0] - 1)
    inside = offsets[None, :] < shell_size[:, None]
    return jnp.where(inside[:, :, None], matrix[rows], jnp.zeros((), matrix.dtype))


def half_transform(slot_rows, pairs, keep, occ_blocks):
    count = slot_rows.shape[0]
    vecs_here = slot_rows.shape[1]
    shells = occ_blocks.shape[0]
    group_size = math.gcd(512, count)
    turns = count // group_size
    shaped = slot_rows.reshape(count, vecs_here, EDGE, EDGE)

    def advance(total, turn):
        first = turn * group_size
        block = lax.dynamic_slice_in_dim(shaped, first, group_size, 0)
        okay = lax.dynamic_slice_in_dim(keep, first, group_size, 0)
        block = jnp.where(okay[:, None, None, None], block, jnp.zeros((), block.dtype))
        row_shell = lax.dynamic_slice_in_dim(pairs[:, 0], first, group_size, 0)
        col_shell = lax.dynamic_slice_in_dim(pairs[:, 1], first, group_size, 0)
        coefs = occ_blocks[row_shell]
        piece = jnp.einsum("kmi,kvmn->kvin", coefs, block, preferred_element_type=jnp.float32)
        return (total.at[col_shell].add(piece), None)

    start_total = jnp.zeros((shells, vecs_here, NOCC, EDGE), jnp.float32)
    half, _ = lax.scan(advance, start_total, jnp.arange(turns, dtype=jnp.int32))
    return half


def long_way(turned, pairs, live, shell_size, occ_coef, vir_coef):
    occ_full = lax.all_gather(occ_coef, "shell", axis=0, tiled=True)
    starts = jnp.cumsum(shell_size) - shell_size
    occ_blocks = padded_rows(occ_full, starts, shell_size)
    half = half_transform(turned, pairs, live, occ_blocks)
    hidden = half.astype(jnp.bfloat16)
    vir_full = lax.all_gather(vir_coef, "shell", axis=0, tiled=True)
    vir_blocks = padded_rows(vir_full, starts, shell_size)
    result = jnp.einsum("svin,sna->via", hidden, vir_blocks, preferred_element_type=jnp.float32)
    return result.astype(jnp.bfloat16)


def from_start(panels, block_pairs, block_count, *rest):
    pairs = lax.all_gather(block_pairs, "shell", axis=0, tiled=True)
    counts = lax.all_gather(block_count, "shell", axis=0, tiled=True)
    turned = lax.all_to_all(panels, "shell", split_axis=1, concat_axis=0, tiled=True)
    position = jnp.arange(turned.shape[0], dtype=jnp.int32)
    live = position % BLK_DEV < counts[position // BLK_DEV]
    return long_way(turned, pairs, live, *rest)


def iota(shape, dim):
    return lax.broadcasted_iota(jnp.int32, shape, dim)


def column_of(row, mask):
    return jnp.sum(jnp.where(mask, row, 0.0), axis=1, keepdims=True)


def row_of(column, mask):
    return jnp.sum(jnp.where(mask, column, 0.0), axis=0, keepdims=True)


def zero_one(mask):
    return jnp.where(mask, 1.0, 0.0)


def lane_value(row, index):
    return jnp.sum(jnp.where(iota(row.shape, 1) == index, row, 0.0), axis=1, keepdims=True)


def one_hots(ids, shells):
    lanes = iota(ids.shape, 1).astype(F32)
    return jnp.concatenate([zero_one(ids == lanes + 128.0 * k) for k in range(shells // 128)], axis=1)


def slot_hots(code, shells):
    code = code.reshape(-1, 128)
    kept = code >= 0
    columns = jnp.where(kept, code % shells, -1).astype(F32)
    return one_hots(columns, shells), one_hots(jnp.where(kept, code // shells, -1).astype(F32), shells)


class Shells:
    def __init__(self, size_row):
        shells = size_row.shape[1]
        sub, lane = iota((shells, shells), 0), iota((shells, shells), 1)
        self.before, self.same = lane < sub, lane == sub
        self.starts = column_of(size_row, self.before)
        self.size = column_of(size_row, self.same)
        self.odd = self.starts - 2.0 * jnp.floor(self.starts * 0.5)


class Used:
    def __init__(self, shells, hot, window):
        self.used = column_of(jnp.max(hot, axis=0, keepdims=True), shells.same)
        self.extra, self.ahead, self.edges = [], [], []
        edge = (iota((hot.shape[1], 128), 1) * window).astype(F32)
        reach = jnp.clip(edge - shells.starts, 0.0, shells.size)
        for parity in range(2):
            extra = 1.0 - shells.odd if parity == 0 else shells.odd
            count = self.used * jnp.floor((shells.size + extra) * 0.5)
            count_row = row_of(count, shells.same)
            self.extra.append(extra)
            self.ahead.append(column_of(count_row, shells.before))
            self.edges.append(jnp.sum(self.used * jnp.floor((reach + extra) * 0.5), axis=0, keepdims=True))


def pack_kernel(shells, pairs_ref, count_ref, vir_ref, occ_ref, code_ref, *outs):
    me = lax.axis_index("shell")
    core, y = lax.rem(me, 2), lax.rem(lax.div(me, 2), 2)
    here, nvir = vir_ref.shape
    width, thin = nvir // CORES, occ_ref.shape[1] // CORES
    for dy in range(2):
        parity = lax.rem(y + dy, 2)
        pick = zero_one(iota((here // 2, here), 1) == 2 * iota((here // 2, here), 0) + parity).astype(BF16)
        for dc in range(2):
            half = lax.rem(core + dc, 2)
            out = outs[2 * dy + dc]
            part = vir_ref[:, pl.ds(pl.multiple_of(half * width, 128), width)]
            out[:, :width] = jnp.dot(pick, part, preferred_element_type=F32).astype(BF16)
            part = occ_ref[:, pl.ds(pl.multiple_of(half * thin, 128), thin)]
            out[:, width:] = jnp.dot(pick, part, preferred_element_type=F32).astype(BF16)
    code = pairs_ref[1:2, :] + shells * pairs_ref[0:1, :]
    code = jnp.where(iota((1, BLK_DEV), 1) < count_ref[...], code, -1).astype(F32)
    square = (BLK_DEV, BLK_DEV)
    code = column_of(code, iota(square, 0) == iota(square, 1)).astype(jnp.int32)
    code_ref[...] = jnp.broadcast_to(jnp.broadcast_to(code, (BLK_DEV, 128))[None], code_ref.shape)


def send_kernel(panels_ref, send_ref):
    turned = jnp.swapaxes(panels_ref[...].astype(F32), 0, 1)
    send_ref[...] = turned.reshape(send_ref.shape).astype(BF16)


def pick_kernel(here, code_ref, size_ref, *refs):
    sources, (out_ref, over_ref) = refs[:4], refs[4:]
    me = lax.axis_index("shell")
    core, y, z = lax.rem(me, 2), lax.rem(lax.div(me, 2), 2), lax.div(me, 4)
    window = CORES * Y * here
    shell_count = size_ref.shape[1]
    shells = Shells(size_ref[...].astype(F32))
    lists = [Used(shells, hot, window) for hot in slot_hots(code_ref[...], shell_count)]
    most = jnp.zeros((1, 1), F32)
    lane = iota((1, 128), 1)
    for chosen in lists:
        for edges in chosen.edges:
            later = jnp.concatenate([edges[:, 1:], edges[:, :1]], axis=1)
            most = jnp.maximum(most, jnp.max(jnp.where(lane < Z, later - edges, 0.0), axis=1, keepdims=True))
    over_ref[0] = jnp.where(jnp.max(most) > CAP, 1, 0).astype(jnp.int32)

    width = vir_width = out_ref.shape[1] - 128
    even = y == 0
    totals = [jnp.zeros((CAP, width), F32), jnp.zeros((CAP, 128), F32)]
    columns = [slice(0, vir_width), slice(vir_width, vir_width + 128)]
    extra = jnp.where(even, lists[0].extra[0], lists[0].extra[1])
    for k, source in enumerate(sources):
        device = 4 * z + 2 * lax.rem(y + k // 2, 2) + lax.rem(core + k % 2, 2)
        row = (2 * iota((shell_count, 128), 1) + device * here + y).astype(F32)
        where = row - shells.starts
        inside = (where >= 0.0) & (where < shells.size)
        within = jnp.floor((where + extra) * 0.5)
        for chosen, total, column in zip(lists, range(2), columns):
            ahead = jnp.where(even, chosen.ahead[0], chosen.ahead[1])
            base = lane_value(jnp.where(even, chosen.edges[0], chosen.edges[1]), z)
            place = jnp.where(inside & (chosen.used > 0.0), ahead + within + 1.0, 0.0)
            place = jnp.sum(place, axis=0, keepdims=True)
            place = jnp.where(place > 0.0, place - 1.0 - base, -1.0)
            hot = zero_one(place == iota((CAP, 128), 0).astype(F32)).astype(BF16)
            totals[total] += jnp.dot(
                hot[:, : here // 2], source[:, column], preferred_element_type=F32
            )
    for total, column in zip(totals, columns):
        out_ref[:, column] = total.astype(BF16)


def place_kernel(here, code_ref, got_ref, size_ref, rows_ref, placed_ref):
    chip = lax.div(lax.axis_index("shell"), CORES)
    window = CORES * Y * here
    shell_count = size_ref.shape[1]
    got = got_ref[...].astype(F32)
    size_row = size_ref[...].astype(F32)
    shells = Shells(size_row)
    hots = slot_hots(code_ref[...], shell_count)
    lists = [Used(shells, hot, window) for hot in hots]
    slots = hots[0].shape[0]
    kept = LIVE_DEV * (slots // BLK_DEV)
    alive = jnp.broadcast_to(jnp.sum(hots[0], axis=1, keepdims=True), (slots, slots))
    sub, lane = iota((slots, slots), 0), iota((slots, slots), 1)
    rank = row_of(alive, sub < lane)
    alive_row = row_of(alive, sub == lane)
    take = (rank == iota((kept, slots), 0).astype(F32)) & (alive_row > 0.0)
    take = zero_one(take).astype(BF16)

    def taken(array):
        return jnp.dot(take, array.astype(BF16), preferred_element_type=F32)

    def spread(hot, column):
        value = jnp.sum(hot * row_of(column, shells.same), axis=1, keepdims=True)
        wide = jnp.broadcast_to(value, (kept, 128)).reshape(kept, 1, 128)
        return jnp.broadcast_to(wide, (kept, EDGE, 128)).reshape(kept * EDGE, 128)

    at = iota((kept * EDGE, 128), 0) % EDGE
    step = at.astype(F32)

    def places(hot, chosen):
        hot = taken(hot)
        first, length = spread(hot, shells.starts), spread(hot, shells.size)
        row = first + step
        odd = (row - 2.0 * jnp.floor(row * 0.5)) > 0.0
        place = jnp.where(odd, spread(hot, chosen.ahead[1]), spread(hot, chosen.ahead[0]))
        place += jnp.floor(step * 0.5)
        offsets = [
            [((w * Y + k) ^ chip).astype(F32) * CAP - lane_value(e, w) for w in range(Z)]
            for k, e in enumerate(chosen.edges)
        ]
        offset = jnp.where(odd, offsets[1][0], offsets[0][0])
        for w in range(1, Z):
            offset = jnp.where(row >= float(window * w), jnp.where(odd, offsets[1][w], offsets[0][w]), offset)
        return jnp.where(step < length, place + offset, -1.0)[:, :1]

    place_c, place_r = places(hots[0], lists[0]), places(hots[1], lists[1])
    span = 16 * EDGE
    width = rows_ref.shape[1]
    s_in, l_in = iota((span, span), 0), iota((span, span), 1)
    keep_m = (l_in // EDGE) == (s_in % EDGE)
    fold = zero_one((s_in % EDGE) == (l_in % EDGE)).astype(BF16)
    same_slot = (s_in // EDGE) == (l_in // EDGE)
    blocks = [taken(got[:, p * BLK_DEV : (p + 1) * BLK_DEV, :].reshape(slots, span)) for p in range(2)]
    lanes = iota((span, width), 1).astype(F32)
    for g in range(kept // 16):
        rows = slice(g * span, (g + 1) * span)
        rows_ref[rows, :] = zero_one(place_r[rows] == lanes).astype(BF16)
        c_hot = zero_one(place_c[rows] == lanes).astype(BF16)
        for p in range(2):
            block = blocks[p][g * 16 : (g + 1) * 16].reshape(16, 1, span)
            block = jnp.broadcast_to(block, (16, EDGE, span)).reshape(span, span)
            block = jnp.where(keep_m, block, 0.0).astype(BF16)
            diag = jnp.dot(block, fold, preferred_element_type=F32)
            diag = jnp.where(same_slot, diag, 0.0).astype(BF16)
            placed_ref[p, rows, :] = jnp.dot(diag, c_hot, preferred_element_type=F32).astype(BF16)


def last_kernel(count, me_ref, rows_ref, placed_ref, *refs):
    pieces, (out_ref, parts_ref, half_ref) = refs[: 2 * count], refs[2 * count :]
    sides = [pieces[:count], pieces[count:]]
    width = pieces[0].shape[1] - 128
    tile = out_ref.shape[2]
    per = width // tile
    core = lax.rem(me_ref[0], CORES)
    j = pl.program_id(0)

    @pl.when(j == 0)
    def _():
        for far, side in enumerate(sides):
            occ = jnp.concatenate([piece[:, width:] for piece in side], axis=0)
            part = jnp.dot(rows_ref[...], occ, preferred_element_type=F32).astype(BF16)
            half = lax.rem(core + far, CORES)
            parts_ref[:, pl.ds(pl.multiple_of(half * 128, 128), 128)] = part
        for p in range(2):
            piece = lax.dot_general(
                parts_ref[...], placed_ref[p], (((0,), (0,)), ((), ())), preferred_element_type=F32
            )
            half_ref[p * NOCC : (p + 1) * NOCC, :] = piece.astype(BF16)

    for far, side in enumerate(sides):

        @pl.when(lax.div(j, per) == far)
        def _():
            columns = pl.ds(pl.multiple_of(lax.rem(j, per) * tile, 128), tile)
            right = jnp.concatenate([piece[:, columns] for piece in side], axis=0)
            for p in range(2):
                left = half_ref[p * NOCC : (p + 1) * NOCC, :]
                out_ref[p] = jnp.dot(left, right, preferred_element_type=F32).astype(BF16)


VMEM = pl.BlockSpec(memory_space=pltpu.VMEM)
SMEM = pl.BlockSpec(memory_space=pltpu.SMEM)


def shape(*dims, dtype=BF16):
    return jax.ShapeDtypeStruct(dims, dtype)


def params(mib):
    return pltpu.CompilerParams(vmem_limit_bytes=mib << 20)


def cost(flops, nbytes):
    return pl.CostEstimate(flops=int(flops), bytes_accessed=int(nbytes), transcendentals=0)


def short_way(panels, block_pairs, block_count, shell_size, occ_coef, vir_coef):
    n = lax.axis_size("shell")
    here, nvir = vir_coef.shape
    width = nvir // CORES
    packed = width + NOCC // CORES
    room = Z * Y * CAP
    me = lax.axis_index("shell")
    size_row = shell_size.reshape(1, -1)

    def swap(array, bit):
        return lax.ppermute(array, "shell", [(i, i ^ bit) for i in range(n)])

    code, keep, to_core, to_y, to_both = pl.pallas_call(
        functools.partial(pack_kernel, size_row.shape[1]),
        out_shape=[shape(n, BLK_DEV, 128, dtype=jnp.int32)] + [shape(here // 2, packed)] * 4,
        in_specs=[VMEM] * 4,
        out_specs=[VMEM] * 5,
        compiler_params=params(12),
        cost_estimate=cost(3e8, 3e6),
        name="pack_rows",
    )(block_pairs.T, block_count.reshape(1, 1), vir_coef, occ_coef)
    fresh = [keep, swap(to_core, 1), swap(to_y, 2), swap(to_both, 3)]
    code = lax.all_to_all(code, "shell", split_axis=0, concat_axis=0, tiled=True)

    mine, over = pl.pallas_call(
        functools.partial(pick_kernel, here),
        out_shape=(shape(CAP, packed), shape(1, dtype=jnp.int32)),
        in_specs=[VMEM] * 6,
        out_specs=(VMEM, SMEM),
        compiler_params=params(12),
        cost_estimate=cost(3e8, 2e6),
        name="pick_rows",
    )(code, size_row, *fresh)

    panels, mine_again = lax.optimization_barrier((panels, mine))
    send = pl.pallas_call(
        send_kernel,
        out_shape=shape(n, 2 * BLK_DEV, EDGE * EDGE),
        in_specs=[VMEM],
        out_specs=VMEM,
        compiler_params=params(12),
        cost_estimate=cost(1e6, 3e5),
        name="turn_panels",
    )(panels)
    got = lax.all_to_all(send, "shell", split_axis=0, concat_axis=0, tiled=True)

    across, beside, mine_y = swap(mine, 8), swap(mine, 4), swap(mine, 2)
    beside, mine_y, got_late = lax.optimization_barrier((beside, mine_y, got))
    beside_y = swap(beside, 2)

    rows, placed = pl.pallas_call(
        functools.partial(place_kernel, here),
        out_shape=(shape(LIVE_DEV * n * EDGE, room), shape(2, LIVE_DEV * n * EDGE, room)),
        in_specs=[VMEM] * 3,
        out_specs=(VMEM, VMEM),
        compiler_params=params(20),
        cost_estimate=cost(4e9, 8e6),
        name="place_panels",
    )(code, got_late, size_row)

    across, beside_y, rows, placed = lax.optimization_barrier((across, beside_y, rows, placed))
    corner, across_y = swap(across, 4), swap(across, 2)
    corner, across_y = lax.optimization_barrier((corner, across_y))
    corner_y = swap(corner, 2)
    pieces = [mine, mine_y, beside, beside_y, across, across_y, corner, corner_y]
    far = [swap(piece, 1) for piece in pieces]

    tile = width // 3
    count = len(pieces)
    out = pl.pallas_call(
        functools.partial(last_kernel, count),
        out_shape=shape(2, NOCC, nvir),
        grid_spec=pltpu.PrefetchScalarGridSpec(
            num_scalar_prefetch=1,
            grid=(nvir // tile,),
            in_specs=[VMEM] * (2 + 2 * count),
            out_specs=pl.BlockSpec((2, NOCC, tile), lambda j, o: (0, 0, (j + 3 * (o[0] % 2)) % 6)),
            scratch_shapes=[pltpu.VMEM((LIVE_DEV * n * EDGE, NOCC), BF16), pltpu.VMEM((2 * NOCC, room), BF16)],
        ),
        compiler_params=params(24),
        cost_estimate=cost(4e9, 1e7),
        name="last_product",
    )(me.reshape(1), rows, placed, *pieces, *far)
    return out, over[0], code, got


def per_device(*args):
    n = lax.axis_size("shell")
    here, nvir = args[5].shape
    shells = args[3].shape[0]
    sparse = LIVE_DEV * n * EDGE < n * here
    if not (sparse and n == Z * Y * CORES and here <= 256 and here % 16 == 0 and nvir % 768 == 0):
        return from_start(*args)
    out, over, code, got = short_way(*args)

    def again(carry):
        over, _ = carry
        over, code_now, turned, *held = lax.optimization_barrier((over, code, got, *args[3:]))
        turned = turned.reshape(n, 2, BLK_DEV, EDGE * EDGE).swapaxes(1, 2).reshape(n * BLK_DEV, 2, EDGE * EDGE)
        code_now = jnp.max(code_now, axis=2).reshape(n * BLK_DEV)
        ids = jnp.maximum(code_now, 0)
        pairs = jnp.stack([ids // shells, ids % shells], axis=1)
        return over - 1, long_way(turned, pairs, code_now >= 0, *held)

    return lax.while_loop(lambda carry: carry[0] > 0, again, (over, out))[1]


def solution(mesh):
    placed = (
        P(("groups", "shell"), None, None),
        P(("groups", "shell"), None),
        P(("groups", "shell")),
        P("groups"),
        P(("groups", "shell"), None),
        P(("groups", "shell"), None),
    )
    return jax.shard_map(
        per_device,
        mesh=mesh,
        in_specs=placed,
        out_specs=P(("groups", "shell"), None, None),
        check_vma=False,
    )
```

```python
import functools
import math

import jax
import jax.numpy as jnp
from jax import lax
from jax.experimental import pallas as pl
from jax.experimental.pallas import tpu as pltpu
from jax.sharding import PartitionSpec as P

EDGE = 16
NOCC = 256
BLK_DEV = 8
LIVE_DEV = 4
CAP = 128
Z, Y, CORES = 4, 2, 2
F32 = jnp.float32
BF16 = jnp.bfloat16


def padded_rows(matrix, starts, shell_size):
    offsets = jnp.arange(EDGE, dtype=jnp.int32)
    rows = jnp.minimum(starts[:, None] + offsets[None, :], matrix.shape[0] - 1)
    inside = offsets[None, :] < shell_size[:, None]
    return jnp.where(inside[:, :, None], matrix[rows], jnp.zeros((), matrix.dtype))


def half_transform(slot_rows, pairs, keep, occ_blocks):
    count = slot_rows.shape[0]
    vecs_here = slot_rows.shape[1]
    shells = occ_blocks.shape[0]
    group_size = math.gcd(512, count)
    turns = count // group_size
    shaped = slot_rows.reshape(count, vecs_here, EDGE, EDGE)

    def advance(total, turn):
        first = turn * group_size
        block = lax.dynamic_slice_in_dim(shaped, first, group_size, 0)
        okay = lax.dynamic_slice_in_dim(keep, first, group_size, 0)
        block = jnp.where(okay[:, None, None, None], block, jnp.zeros((), block.dtype))
        row_shell = lax.dynamic_slice_in_dim(pairs[:, 0], first, group_size, 0)
        col_shell = lax.dynamic_slice_in_dim(pairs[:, 1], first, group_size, 0)
        coefs = occ_blocks[row_shell]
        piece = jnp.einsum("kmi,kvmn->kvin", coefs, block, preferred_element_type=jnp.float32)
        return (total.at[col_shell].add(piece), None)

    start_total = jnp.zeros((shells, vecs_here, NOCC, EDGE), jnp.float32)
    half, _ = lax.scan(advance, start_total, jnp.arange(turns, dtype=jnp.int32))
    return half


def long_way(turned, pairs, live, shell_size, occ_coef, vir_coef):
    occ_full = lax.all_gather(occ_coef, "shell", axis=0, tiled=True)
    starts = jnp.cumsum(shell_size) - shell_size
    occ_blocks = padded_rows(occ_full, starts, shell_size)
    half = half_transform(turned, pairs, live, occ_blocks)
    hidden = half.astype(jnp.bfloat16)
    vir_full = lax.all_gather(vir_coef, "shell", axis=0, tiled=True)
    vir_blocks = padded_rows(vir_full, starts, shell_size)
    result = jnp.einsum("svin,sna->via", hidden, vir_blocks, preferred_element_type=jnp.float32)
    return result.astype(jnp.bfloat16)


def from_start(panels, block_pairs, block_count, *rest):
    pairs = lax.all_gather(block_pairs, "shell", axis=0, tiled=True)
    counts = lax.all_gather(block_count, "shell", axis=0, tiled=True)
    turned = lax.all_to_all(panels, "shell", split_axis=1, concat_axis=0, tiled=True)
    position = jnp.arange(turned.shape[0], dtype=jnp.int32)
    live = position % BLK_DEV < counts[position // BLK_DEV]
    return long_way(turned, pairs, live, *rest)


def iota(shape, dim):
    return lax.broadcasted_iota(jnp.int32, shape, dim)


def column_of(row, mask):
    return jnp.sum(jnp.where(mask, row, 0.0), axis=1, keepdims=True)


def row_of(column, mask):
    return jnp.sum(jnp.where(mask, column, 0.0), axis=0, keepdims=True)


def zero_one(mask):
    return jnp.where(mask, 1.0, 0.0)


def lane_value(row, index):
    return jnp.sum(jnp.where(iota(row.shape, 1) == index, row, 0.0), axis=1, keepdims=True)


def one_hots(ids, shells):
    lanes = iota(ids.shape, 1).astype(F32)
    return jnp.concatenate([zero_one(ids == lanes + 128.0 * k) for k in range(shells // 128)], axis=1)


def slot_hots(code, shells):
    code = code.reshape(-1, 128)
    kept = code >= 0
    columns = jnp.where(kept, code % shells, -1).astype(F32)
    return one_hots(columns, shells), one_hots(jnp.where(kept, code // shells, -1).astype(F32), shells)


class Shells:
    def __init__(self, size_row):
        shells = size_row.shape[1]
        sub, lane = iota((shells, shells), 0), iota((shells, shells), 1)
        self.before, self.same = lane < sub, lane == sub
        self.starts = column_of(size_row, self.before)
        self.size = column_of(size_row, self.same)
        self.odd = self.starts - 2.0 * jnp.floor(self.starts * 0.5)


class Used:
    def __init__(self, shells, hot, window):
        self.used = column_of(jnp.max(hot, axis=0, keepdims=True), shells.same)
        self.extra, self.ahead, self.edges = [], [], []
        edge = (iota((hot.shape[1], 128), 1) * window).astype(F32)
        reach = jnp.clip(edge - shells.starts, 0.0, shells.size)
        for parity in range(2):
            extra = 1.0 - shells.odd if parity == 0 else shells.odd
            count = self.used * jnp.floor((shells.size + extra) * 0.5)
            count_row = row_of(count, shells.same)
            self.extra.append(extra)
            self.ahead.append(column_of(count_row, shells.before))
            self.edges.append(jnp.sum(self.used * jnp.floor((reach + extra) * 0.5), axis=0, keepdims=True))


def pack_kernel(shells, pairs_any, count_any, vir_ref, occ_ref, code_ref, *refs):
    outs, (pairs_ref, count_ref, sems) = refs[:4], refs[4:]
    copies = [
        pltpu.make_async_copy(pairs_any, pairs_ref, sems.at[0]),
        pltpu.make_async_copy(count_any, count_ref, sems.at[1]),
    ]
    for copy in copies:
        copy.start()
    me = lax.axis_index("shell")
    core, y = lax.rem(me, 2), lax.rem(lax.div(me, 2), 2)
    here, nvir = vir_ref.shape
    width, thin = nvir // CORES, occ_ref.shape[1] // CORES
    for dy in range(2):
        parity = lax.rem(y + dy, 2)
        pick = zero_one(iota((here // 2, here), 1) == 2 * iota((here // 2, here), 0) + parity).astype(BF16)
        for dc in range(2):
            half = lax.rem(core + dc, 2)
            out = outs[2 * dy + dc]
            part = vir_ref[:, pl.ds(pl.multiple_of(half * width, 128), width)]
            out[:, :width] = jnp.dot(pick, part, preferred_element_type=F32).astype(BF16)
            part = occ_ref[:, pl.ds(pl.multiple_of(half * thin, 128), thin)]
            out[:, width:] = jnp.dot(pick, part, preferred_element_type=F32).astype(BF16)
    for copy in copies:
        copy.wait()
    code = pairs_ref[1:2, :] + shells * pairs_ref[0:1, :]
    code = jnp.where(iota((1, BLK_DEV), 1) < count_ref[...], code, -1).astype(F32)
    square = (BLK_DEV, BLK_DEV)
    code = column_of(code, iota(square, 0) == iota(square, 1)).astype(jnp.int32)
    code_ref[...] = jnp.broadcast_to(jnp.broadcast_to(code, (BLK_DEV, 128))[None], code_ref.shape)


def send_kernel(panels_ref, send_ref):
    turned = jnp.swapaxes(panels_ref[...].astype(F32), 0, 1)
    send_ref[...] = turned.reshape(send_ref.shape).astype(BF16)


def pick_kernel(here, code_ref, size_ref, *refs):
    sources, (out_ref, over_ref) = refs[:4], refs[4:]
    me = lax.axis_index("shell")
    core, y, z = lax.rem(me, 2), lax.rem(lax.div(me, 2), 2), lax.div(me, 4)
    window = CORES * Y * here
    shell_count = size_ref.shape[1]
    shells = Shells(size_ref[...].astype(F32))
    lists = [Used(shells, hot, window) for hot in slot_hots(code_ref[...], shell_count)]
    most = jnp.zeros((1, 1), F32)
    lane = iota((1, 128), 1)
    for chosen in lists:
        for edges in chosen.edges:
            later = jnp.concatenate([edges[:, 1:], edges[:, :1]], axis=1)
            most = jnp.maximum(most, jnp.max(jnp.where(lane < Z, later - edges, 0.0), axis=1, keepdims=True))
    over_ref[0] = jnp.where(jnp.max(most) > CAP, 1, 0).astype(jnp.int32)

    width = vir_width = out_ref.shape[1] - 128
    even = y == 0
    totals = [jnp.zeros((CAP, width), F32), jnp.zeros((CAP, 128), F32)]
    columns = [slice(0, vir_width), slice(vir_width, vir_width + 128)]
    extra = jnp.where(even, lists[0].extra[0], lists[0].extra[1])
    for k, source in enumerate(sources):
        device = 4 * z + 2 * lax.rem(y + k // 2, 2) + lax.rem(core + k % 2, 2)
        row = (2 * iota((shell_count, 128), 1) + device * here + y).astype(F32)
        where = row - shells.starts
        inside = (where >= 0.0) & (where < shells.size)
        within = jnp.floor((where + extra) * 0.5)
        for chosen, total, column in zip(lists, range(2), columns):
            ahead = jnp.where(even, chosen.ahead[0], chosen.ahead[1])
            base = lane_value(jnp.where(even, chosen.edges[0], chosen.edges[1]), z)
            place = jnp.where(inside & (chosen.used > 0.0), ahead + within + 1.0, 0.0)
            place = jnp.sum(place, axis=0, keepdims=True)
            place = jnp.where(place > 0.0, place - 1.0 - base, -1.0)
            hot = zero_one(place == iota((CAP, 128), 0).astype(F32)).astype(BF16)
            totals[total] += jnp.dot(
                hot[:, : here // 2], source[:, column], preferred_element_type=F32
            )
    for total, column in zip(totals, columns):
        out_ref[:, column] = total.astype(BF16)


def place_kernel(here, code_ref, got_ref, size_ref, rows_ref, placed_ref):
    chip = lax.div(lax.axis_index("shell"), CORES)
    window = CORES * Y * here
    shell_count = size_ref.shape[1]
    got = got_ref[...].astype(F32)
    size_row = size_ref[...].astype(F32)
    shells = Shells(size_row)
    hots = slot_hots(code_ref[...], shell_count)
    lists = [Used(shells, hot, window) for hot in hots]
    slots = hots[0].shape[0]
    kept = LIVE_DEV * (slots // BLK_DEV)
    alive = jnp.broadcast_to(jnp.sum(hots[0], axis=1, keepdims=True), (slots, slots))
    sub, lane = iota((slots, slots), 0), iota((slots, slots), 1)
    rank = row_of(alive, sub < lane)
    alive_row = row_of(alive, sub == lane)
    take = (rank == iota((kept, slots), 0).astype(F32)) & (alive_row > 0.0)
    take = zero_one(take).astype(BF16)

    def taken(array):
        return jnp.dot(take, array.astype(BF16), preferred_element_type=F32)

    def spread(hot, column):
        value = jnp.sum(hot * row_of(column, shells.same), axis=1, keepdims=True)
        wide = jnp.broadcast_to(value, (kept, 128)).reshape(kept, 1, 128)
        return jnp.broadcast_to(wide, (kept, EDGE, 128)).reshape(kept * EDGE, 128)

    at = iota((kept * EDGE, 128), 0) % EDGE
    step = at.astype(F32)

    def places(hot, chosen):
        hot = taken(hot)
        first, length = spread(hot, shells.starts), spread(hot, shells.size)
        row = first + step
        odd = (row - 2.0 * jnp.floor(row * 0.5)) > 0.0
        place = jnp.where(odd, spread(hot, chosen.ahead[1]), spread(hot, chosen.ahead[0]))
        place += jnp.floor(step * 0.5)
        offsets = [
            [((w * Y + k) ^ chip).astype(F32) * CAP - lane_value(e, w) for w in range(Z)]
            for k, e in enumerate(chosen.edges)
        ]
        offset = jnp.where(odd, offsets[1][0], offsets[0][0])
        for w in range(1, Z):
            offset = jnp.where(row >= float(window * w), jnp.where(odd, offsets[1][w], offsets[0][w]), offset)
        return jnp.where(step < length, place + offset, -1.0)[:, :1]

    place_c, place_r = places(hots[0], lists[0]), places(hots[1], lists[1])
    span = 16 * EDGE
    width = rows_ref.shape[1]
    s_in, l_in = iota((span, span), 0), iota((span, span), 1)
    keep_m = (l_in // EDGE) == (s_in % EDGE)
    fold = zero_one((s_in % EDGE) == (l_in % EDGE)).astype(BF16)
    same_slot = (s_in // EDGE) == (l_in // EDGE)
    blocks = [taken(got[:, p * BLK_DEV : (p + 1) * BLK_DEV, :].reshape(slots, span)) for p in range(2)]
    lanes = iota((span, width), 1).astype(F32)
    for g in range(kept // 16):
        rows = slice(g * span, (g + 1) * span)
        rows_ref[rows, :] = zero_one(place_r[rows] == lanes).astype(BF16)
        c_hot = zero_one(place_c[rows] == lanes).astype(BF16)
        for p in range(2):
            block = blocks[p][g * 16 : (g + 1) * 16].reshape(16, 1, span)
            block = jnp.broadcast_to(block, (16, EDGE, span)).reshape(span, span)
            block = jnp.where(keep_m, block, 0.0).astype(BF16)
            diag = jnp.dot(block, fold, preferred_element_type=F32)
            diag = jnp.where(same_slot, diag, 0.0).astype(BF16)
            placed_ref[p, rows, :] = jnp.dot(diag, c_hot, preferred_element_type=F32).astype(BF16)


def last_kernel(count, me_ref, rows_ref, placed_ref, *refs):
    pieces, (out_ref, occ_ref, half_ref) = refs[: 2 * count], refs[2 * count :]
    sides = [pieces[:count], pieces[count:]]
    width = pieces[0].shape[1] - 128
    tile = out_ref.shape[2]
    per = width // tile
    core = lax.rem(me_ref[0], CORES)
    j = pl.program_id(0)

    @pl.when(j == 0)
    def _():
        for far, side in enumerate(sides):
            occ = jnp.concatenate([piece[:, width:] for piece in side], axis=0)
            half = lax.rem(core + far, CORES)
            occ_ref[:, pl.ds(pl.multiple_of(half * 128, 128), 128)] = occ
        part = jnp.dot(rows_ref[...], occ_ref[...], preferred_element_type=F32)
        part = part.T.astype(BF16)
        for p in range(2):
            piece = jnp.dot(part, placed_ref[p], preferred_element_type=F32)
            half_ref[p * NOCC : (p + 1) * NOCC, :] = piece.astype(BF16)

    for far, side in enumerate(sides):

        @pl.when(lax.div(j, per) == far)
        def _():
            columns = pl.ds(pl.multiple_of(lax.rem(j, per) * tile, 128), tile)
            right = jnp.concatenate([piece[:, columns] for piece in side], axis=0)
            total = jnp.dot(half_ref[...], right, preferred_element_type=F32).astype(BF16)
            out_ref[...] = total.reshape(out_ref.shape)


VMEM = pl.BlockSpec(memory_space=pltpu.VMEM)
SMEM = pl.BlockSpec(memory_space=pltpu.SMEM)
HBM = pl.BlockSpec(memory_space=pltpu.HBM)


def shape(*dims, dtype=BF16):
    return jax.ShapeDtypeStruct(dims, dtype)


def params(mib):
    return pltpu.CompilerParams(vmem_limit_bytes=mib << 20)


def cost(flops, nbytes):
    return pl.CostEstimate(flops=int(flops), bytes_accessed=int(nbytes), transcendentals=0)


def short_way(panels, block_pairs, block_count, shell_size, occ_coef, vir_coef):
    n = lax.axis_size("shell")
    here, nvir = vir_coef.shape
    width = nvir // CORES
    packed = width + NOCC // CORES
    room = Z * Y * CAP
    me = lax.axis_index("shell")
    size_row = shell_size.reshape(1, -1)

    def swap(array, bit):
        return lax.ppermute(array, "shell", [(i, i ^ bit) for i in range(n)])

    code, keep, to_core, to_y, to_both = pl.pallas_call(
        functools.partial(pack_kernel, size_row.shape[1]),
        out_shape=[shape(n, BLK_DEV, 128, dtype=jnp.int32)] + [shape(here // 2, packed)] * 4,
        in_specs=[HBM] * 2 + [VMEM] * 2,
        out_specs=[VMEM] * 5,
        scratch_shapes=[
            pltpu.VMEM((2, BLK_DEV), jnp.int32),
            pltpu.VMEM((1, 1), jnp.int32),
            pltpu.SemaphoreType.DMA((2,)),
        ],
        compiler_params=params(12),
        cost_estimate=cost(3e8, 3e6),
        name="pack_rows",
    )(block_pairs.T, block_count.reshape(1, 1), vir_coef, occ_coef)
    to_y, to_both, to_core = swap(to_y, 2), swap(to_both, 3), swap(to_core, 1)
    code = lax.all_to_all(code, "shell", split_axis=0, concat_axis=0, tiled=True)

    mine, over = pl.pallas_call(
        functools.partial(pick_kernel, here),
        out_shape=(shape(CAP, packed), shape(1, dtype=jnp.int32)),
        in_specs=[VMEM] * 6,
        out_specs=(VMEM, SMEM),
        compiler_params=params(12),
        cost_estimate=cost(3e8, 2e6),
        name="pick_rows",
    )(code, size_row, keep, to_core, to_y, to_both)

    across, beside, mine_y = swap(mine, 8), swap(mine, 4), swap(mine, 2)
    beside, mine_y, panels = lax.optimization_barrier((beside, mine_y, panels))
    beside_y = swap(beside, 2)
    send = pl.pallas_call(
        send_kernel,
        out_shape=shape(n, 2 * BLK_DEV, EDGE * EDGE),
        in_specs=[VMEM],
        out_specs=VMEM,
        compiler_params=params(12),
        cost_estimate=cost(1e6, 3e5),
        name="turn_panels",
    )(panels)
    got = lax.all_to_all(send, "shell", split_axis=0, concat_axis=0, tiled=True)


    far = [swap(mine, 1), swap(mine_y, 1), swap(beside, 1)]
    across, beside_y, got, *far = lax.optimization_barrier((across, beside_y, got, *far))
    corner, across_y = swap(across, 4), swap(across, 2)
    far += [swap(beside_y, 1), swap(across, 1)]
    corner, across_y, got, *far = lax.optimization_barrier((corner, across_y, got, *far))
    corner_y = swap(corner, 2)
    rows, placed = pl.pallas_call(
        functools.partial(place_kernel, here),
        out_shape=(shape(LIVE_DEV * n * EDGE, room), shape(2, LIVE_DEV * n * EDGE, room)),
        in_specs=[VMEM] * 3,
        out_specs=(VMEM, VMEM),
        compiler_params=params(20),
        cost_estimate=cost(4e9, 8e6),
        name="place_panels",
    )(code, got, size_row)

    far += [swap(across_y, 1), swap(corner, 1)]
    corner_y, rows, placed, *far = lax.optimization_barrier((corner_y, rows, placed, *far))
    far.append(swap(corner_y, 1))
    pieces = [mine, mine_y, beside, beside_y, across, across_y, corner, corner_y]

    tile = width // 3
    count = len(pieces)
    out = pl.pallas_call(
        functools.partial(last_kernel, count),
        out_shape=shape(2, NOCC, nvir),
        grid_spec=pltpu.PrefetchScalarGridSpec(
            num_scalar_prefetch=1,
            grid=(nvir // tile,),
            in_specs=[VMEM] * (2 + 2 * count),
            out_specs=pl.BlockSpec((2, NOCC, tile), lambda j, o: (0, 0, (j + 3 * (o[0] % 2)) % 6)),
            scratch_shapes=[pltpu.VMEM((room, NOCC), BF16), pltpu.VMEM((2 * NOCC, room), BF16)],
        ),
        compiler_params=params(24),
        cost_estimate=cost(4e9, 1e7),
        name="last_product",
    )(me.reshape(1), rows, placed, *pieces, *far)
    return out, over[0], code, got


def per_device(*args):
    n = lax.axis_size("shell")
    here, nvir = args[5].shape
    shells = args[3].shape[0]
    sparse = LIVE_DEV * n * EDGE < n * here
    if not (sparse and n == Z * Y * CORES and here <= 256 and here % 16 == 0 and nvir % 768 == 0):
        return from_start(*args)
    out, over, code, got = short_way(*args)

    def again(carry):
        over, _ = carry
        over, code_now, turned, *held = lax.optimization_barrier((over, code, got, *args[3:]))
        turned = turned.reshape(n, 2, BLK_DEV, EDGE * EDGE).swapaxes(1, 2).reshape(n * BLK_DEV, 2, EDGE * EDGE)
        code_now = jnp.max(code_now, axis=2).reshape(n * BLK_DEV)
        ids = jnp.maximum(code_now, 0)
        pairs = jnp.stack([ids // shells, ids % shells], axis=1)
        return over - 1, long_way(turned, pairs, code_now >= 0, *held)

    return lax.while_loop(lambda carry: carry[0] > 0, again, (over, out))[1]


def solution(mesh):
    placed = (
        P(("groups", "shell"), None, None),
        P(("groups", "shell"), None),
        P(("groups", "shell")),
        P("groups"),
        P(("groups", "shell"), None),
        P(("groups", "shell"), None),
    )
    return jax.shard_map(
        per_device,
        mesh=mesh,
        in_specs=placed,
        out_specs=P(("groups", "shell"), None, None),
        check_vma=False,
    )
```

```python
import functools
import math

import jax
import jax.numpy as jnp
from jax import lax
from jax.experimental import pallas as pl
from jax.experimental.pallas import tpu as pltpu
from jax.sharding import PartitionSpec as P

EDGE = 16
NOCC = 256
BLK_DEV = 8
LIVE_DEV = 4
CAP = 128
Z, Y, CORES = 4, 2, 2
F32 = jnp.float32
BF16 = jnp.bfloat16


def padded_rows(matrix, starts, shell_size):
    offsets = jnp.arange(EDGE, dtype=jnp.int32)
    rows = jnp.minimum(starts[:, None] + offsets[None, :], matrix.shape[0] - 1)
    inside = offsets[None, :] < shell_size[:, None]
    return jnp.where(inside[:, :, None], matrix[rows], jnp.zeros((), matrix.dtype))


def half_transform(slot_rows, pairs, keep, occ_blocks):
    count = slot_rows.shape[0]
    vecs_here = slot_rows.shape[1]
    shells = occ_blocks.shape[0]
    group_size = math.gcd(512, count)
    turns = count // group_size
    shaped = slot_rows.reshape(count, vecs_here, EDGE, EDGE)

    def advance(total, turn):
        first = turn * group_size
        block = lax.dynamic_slice_in_dim(shaped, first, group_size, 0)
        okay = lax.dynamic_slice_in_dim(keep, first, group_size, 0)
        block = jnp.where(okay[:, None, None, None], block, jnp.zeros((), block.dtype))
        row_shell = lax.dynamic_slice_in_dim(pairs[:, 0], first, group_size, 0)
        col_shell = lax.dynamic_slice_in_dim(pairs[:, 1], first, group_size, 0)
        coefs = occ_blocks[row_shell]
        piece = jnp.einsum("kmi,kvmn->kvin", coefs, block, preferred_element_type=jnp.float32)
        return (total.at[col_shell].add(piece), None)

    start_total = jnp.zeros((shells, vecs_here, NOCC, EDGE), jnp.float32)
    half, _ = lax.scan(advance, start_total, jnp.arange(turns, dtype=jnp.int32))
    return half


def long_way(turned, pairs, live, shell_size, occ_coef, vir_coef):
    occ_full = lax.all_gather(occ_coef, "shell", axis=0, tiled=True)
    starts = jnp.cumsum(shell_size) - shell_size
    occ_blocks = padded_rows(occ_full, starts, shell_size)
    half = half_transform(turned, pairs, live, occ_blocks)
    hidden = half.astype(jnp.bfloat16)
    vir_full = lax.all_gather(vir_coef, "shell", axis=0, tiled=True)
    vir_blocks = padded_rows(vir_full, starts, shell_size)
    result = jnp.einsum("svin,sna->via", hidden, vir_blocks, preferred_element_type=jnp.float32)
    return result.astype(jnp.bfloat16)


def from_start(panels, block_pairs, block_count, *rest):
    pairs = lax.all_gather(block_pairs, "shell", axis=0, tiled=True)
    counts = lax.all_gather(block_count, "shell", axis=0, tiled=True)
    turned = lax.all_to_all(panels, "shell", split_axis=1, concat_axis=0, tiled=True)
    position = jnp.arange(turned.shape[0], dtype=jnp.int32)
    live = position % BLK_DEV < counts[position // BLK_DEV]
    return long_way(turned, pairs, live, *rest)


def iota(shape, dim):
    return lax.broadcasted_iota(jnp.int32, shape, dim)


def column_of(row, mask):
    return jnp.sum(jnp.where(mask, row, 0.0), axis=1, keepdims=True)


def row_of(column, mask):
    return jnp.sum(jnp.where(mask, column, 0.0), axis=0, keepdims=True)


def zero_one(mask):
    return jnp.where(mask, 1.0, 0.0)


def lane_value(row, index):
    return jnp.sum(jnp.where(iota(row.shape, 1) == index, row, 0.0), axis=1, keepdims=True)


def one_hots(ids, shells):
    lanes = iota(ids.shape, 1).astype(F32)
    return jnp.concatenate([zero_one(ids == lanes + 128.0 * k) for k in range(shells // 128)], axis=1)


def slot_hots(code, shells):
    code = code.reshape(-1, 128)
    kept = code >= 0
    columns = jnp.where(kept, code % shells, -1).astype(F32)
    return one_hots(columns, shells), one_hots(jnp.where(kept, code // shells, -1).astype(F32), shells)


class Shells:
    def __init__(self, size_row):
        shells = size_row.shape[1]
        sub, lane = iota((shells, shells), 0), iota((shells, shells), 1)
        self.before, self.same = lane < sub, lane == sub
        self.starts = column_of(size_row, self.before)
        self.size = column_of(size_row, self.same)
        self.odd = self.starts - 2.0 * jnp.floor(self.starts * 0.5)


class Used:
    def __init__(self, shells, hot, window):
        self.used = column_of(jnp.max(hot, axis=0, keepdims=True), shells.same)
        self.extra, self.ahead, self.edges = [], [], []
        edge = (iota((hot.shape[1], 128), 1) * window).astype(F32)
        reach = jnp.clip(edge - shells.starts, 0.0, shells.size)
        for parity in range(2):
            extra = 1.0 - shells.odd if parity == 0 else shells.odd
            count = self.used * jnp.floor((shells.size + extra) * 0.5)
            count_row = row_of(count, shells.same)
            self.extra.append(extra)
            self.ahead.append(column_of(count_row, shells.before))
            self.edges.append(jnp.sum(self.used * jnp.floor((reach + extra) * 0.5), axis=0, keepdims=True))


def pack_kernel(shells, pairs_any, count_any, vir_ref, occ_ref, code_ref, *refs):
    outs, (pairs_ref, count_ref, sems) = refs[:4], refs[4:]
    copies = [
        pltpu.make_async_copy(pairs_any, pairs_ref, sems.at[0]),
        pltpu.make_async_copy(count_any, count_ref, sems.at[1]),
    ]
    for copy in copies:
        copy.start()
    me = lax.axis_index("shell")
    core, y = lax.rem(me, 2), lax.rem(lax.div(me, 2), 2)
    here, nvir = vir_ref.shape
    width, thin = nvir // CORES, occ_ref.shape[1] // CORES
    for dy in range(2):
        parity = lax.rem(y + dy, 2)
        pick = zero_one(iota((here // 2, here), 1) == 2 * iota((here // 2, here), 0) + parity).astype(BF16)
        for dc in range(2):
            half = lax.rem(core + dc, 2)
            out = outs[2 * dy + dc]
            part = vir_ref[:, pl.ds(pl.multiple_of(half * width, 128), width)]
            out[:, :width] = jnp.dot(pick, part, preferred_element_type=F32).astype(BF16)
            part = occ_ref[:, pl.ds(pl.multiple_of(half * thin, 128), thin)]
            out[:, width:] = jnp.dot(pick, part, preferred_element_type=F32).astype(BF16)
    for copy in copies:
        copy.wait()
    code = pairs_ref[1:2, :] + shells * pairs_ref[0:1, :]
    code = jnp.where(iota((1, BLK_DEV), 1) < count_ref[...], code, -1).astype(F32)
    square = (BLK_DEV, BLK_DEV)
    code = column_of(code, iota(square, 0) == iota(square, 1)).astype(jnp.int32)
    code_ref[...] = jnp.broadcast_to(jnp.broadcast_to(code, (BLK_DEV, 128))[None], code_ref.shape)


def send_kernel(panels_ref, send_ref):
    turned = jnp.swapaxes(panels_ref[...].astype(F32), 0, 1)
    send_ref[...] = turned.reshape(send_ref.shape).astype(BF16)


def pick_kernel(here, code_ref, size_ref, *refs):
    sources, (out_ref, over_ref) = refs[:4], refs[4:]
    me = lax.axis_index("shell")
    core, y, z = lax.rem(me, 2), lax.rem(lax.div(me, 2), 2), lax.div(me, 4)
    window = CORES * Y * here
    shell_count = size_ref.shape[1]
    shells = Shells(size_ref[...].astype(F32))
    lists = [Used(shells, hot, window) for hot in slot_hots(code_ref[...], shell_count)]
    most = jnp.zeros((1, 1), F32)
    lane = iota((1, 128), 1)
    for chosen in lists:
        for edges in chosen.edges:
            later = jnp.concatenate([edges[:, 1:], edges[:, :1]], axis=1)
            most = jnp.maximum(most, jnp.max(jnp.where(lane < Z, later - edges, 0.0), axis=1, keepdims=True))
    over_ref[0] = jnp.where(jnp.max(most) > CAP, 1, 0).astype(jnp.int32)

    width = out_ref.shape[1] - 128
    even = y == 0
    totals = [jnp.zeros((CAP, width), F32), jnp.zeros((CAP, 128), F32)]
    columns = [slice(0, width), slice(width, width + 128)]
    extra = jnp.where(even, lists[0].extra[0], lists[0].extra[1])
    for k, source in enumerate(sources):
        device = 4 * z + 2 * lax.rem(y + k // 2, 2) + lax.rem(core + k % 2, 2)
        row = (2 * iota((shell_count, 128), 1) + device * here + y).astype(F32)
        where = row - shells.starts
        inside = (where >= 0.0) & (where < shells.size)
        within = jnp.floor((where + extra) * 0.5)
        for chosen, total, column in zip(lists, range(2), columns):
            ahead = jnp.where(even, chosen.ahead[0], chosen.ahead[1])
            base = lane_value(jnp.where(even, chosen.edges[0], chosen.edges[1]), z)
            place = jnp.where(inside & (chosen.used > 0.0), ahead + within + 1.0, 0.0)
            place = jnp.sum(place, axis=0, keepdims=True)
            place = jnp.where(place > 0.0, place - 1.0 - base, -1.0)
            hot = zero_one(place == iota((CAP, 128), 0).astype(F32)).astype(BF16)
            totals[total] += jnp.dot(
                hot[:, : here // 2], source[:, column], preferred_element_type=F32
            )
    for total, column in zip(totals, columns):
        out_ref[:, column] = total.astype(BF16)


def slot_of(window, chip):
    z = lax.div(chip, Y)
    slot = window ^ chip
    inner = (z == 1) | (z == 2)
    return jnp.where(inner & (slot >= 2 * Y), slot ^ Y, slot)


def half_kernel(here, code_ref, got_ref, size_ref, *refs):
    count = (len(refs) - 4) // 2
    pieces, (half_ref, late_ref, occ_ref, sems) = refs[: 2 * count], refs[2 * count :]
    me = lax.axis_index("shell")
    core, chip = lax.rem(me, CORES), lax.div(me, CORES)
    width = pieces[0].shape[1] - 128
    copies = []
    for far in range(2):
        half = lax.rem(core + far, CORES)
        for k in range(count):
            at = far * count + k
            target = occ_ref.at[pl.ds(k * CAP, CAP), pl.ds(pl.multiple_of(half * 128, 128), 128)]
            copies.append(pltpu.make_async_copy(pieces[at].at[:, pl.ds(width, 128)], target, sems.at[at]))
    for copy in copies:
        copy.start()
    occ_ref[count * CAP :, :] = jnp.zeros((occ_ref.shape[0] - count * CAP, occ_ref.shape[1]), BF16)
    window = CORES * Y * here
    shell_count = size_ref.shape[1]
    got = got_ref[...].astype(F32)
    size_row = size_ref[...].astype(F32)
    shells = Shells(size_row)
    hots = slot_hots(code_ref[...], shell_count)
    lists = [Used(shells, hot, window) for hot in hots]
    slots = hots[0].shape[0]
    kept = LIVE_DEV * (slots // BLK_DEV)
    alive = jnp.broadcast_to(jnp.sum(hots[0], axis=1, keepdims=True), (slots, slots))
    sub, lane = iota((slots, slots), 0), iota((slots, slots), 1)
    rank = row_of(alive, sub < lane)
    alive_row = row_of(alive, sub == lane)
    take = (rank == iota((kept, slots), 0).astype(F32)) & (alive_row > 0.0)
    take = zero_one(take).astype(BF16)

    def taken(array):
        return jnp.dot(take, array.astype(BF16), preferred_element_type=F32)

    def spread(hot, column):
        value = jnp.sum(hot * row_of(column, shells.same), axis=1, keepdims=True)
        wide = jnp.broadcast_to(value, (kept, 128)).reshape(kept, 1, 128)
        return jnp.broadcast_to(wide, (kept, EDGE, 128)).reshape(kept * EDGE, 128)

    at = iota((kept * EDGE, 128), 0) % EDGE
    step = at.astype(F32)

    def places(hot, chosen):
        hot = taken(hot)
        first, length = spread(hot, shells.starts), spread(hot, shells.size)
        row = first + step
        odd = (row - 2.0 * jnp.floor(row * 0.5)) > 0.0
        place = jnp.where(odd, spread(hot, chosen.ahead[1]), spread(hot, chosen.ahead[0]))
        place += jnp.floor(step * 0.5)
        offsets = [
            [slot_of(w * Y + k, chip).astype(F32) * CAP - lane_value(e, w) for w in range(Z)]
            for k, e in enumerate(chosen.edges)
        ]
        offset = jnp.where(odd, offsets[1][0], offsets[0][0])
        for w in range(1, Z):
            offset = jnp.where(row >= float(window * w), jnp.where(odd, offsets[1][w], offsets[0][w]), offset)
        return jnp.where(step < length, place + offset, -1.0)[:, :1]

    place_c, place_r = places(hots[0], lists[0]), places(hots[1], lists[1])
    span = 16 * EDGE
    width = half_ref.shape[1]
    s_in, l_in = iota((span, span), 0), iota((span, span), 1)
    keep_m = (l_in // EDGE) == (s_in % EDGE)
    fold = zero_one((s_in % EDGE) == (l_in % EDGE)).astype(BF16)
    same_slot = (s_in // EDGE) == (l_in // EDGE)
    blocks = [taken(got[:, p * BLK_DEV : (p + 1) * BLK_DEV, :].reshape(slots, span)) for p in range(2)]
    lanes = iota((span, width), 1).astype(F32)
    for copy in copies:
        copy.wait()
    occ = occ_ref[...]
    late = []
    for g in range(kept // 16):
        rows = slice(g * span, (g + 1) * span)
        r_hot = zero_one(place_r[rows] == lanes).astype(BF16)
        c_hot = zero_one(place_c[rows] == lanes).astype(BF16)
        part = jnp.dot(r_hot, occ, preferred_element_type=F32).T.astype(BF16)
        for p in range(2):
            block = blocks[p][g * 16 : (g + 1) * 16].reshape(16, 1, span)
            block = jnp.broadcast_to(block, (16, EDGE, span)).reshape(span, span)
            block = jnp.where(keep_m, block, 0.0).astype(BF16)
            diag = jnp.dot(block, fold, preferred_element_type=F32)
            diag = jnp.where(same_slot, diag, 0.0).astype(BF16)
            placed = jnp.dot(diag, c_hot, preferred_element_type=F32).astype(BF16)
            piece = jnp.dot(part, placed, preferred_element_type=F32)
            rows_p = slice(p * NOCC, (p + 1) * NOCC)
            rows_l = slice(p * CAP, (p + 1) * CAP)
            later = jnp.dot(r_hot[:, count * CAP :].T, placed, preferred_element_type=F32)
            if g == 0:
                half_ref[rows_p, :] = piece
                late.append(later)
            else:
                half_ref[rows_p, :] += piece
                late[p] += later
    for p in range(2):
        late_ref[p * CAP : (p + 1) * CAP, :] = late[p].astype(BF16)


def last_kernel(count, me_ref, part_ref, late_ref, *refs):
    pieces, (out_ref, right_ref, occ_ref, half_ref, sems) = refs[: 2 * count], refs[2 * count :]
    tile = out_ref.shape[2]
    width = right_ref.shape[2]
    per = width // tile
    core = lax.rem(me_ref[0], CORES)
    j = pl.program_id(0)

    def occ_copies():
        for far in range(2):
            half = lax.rem(core + far, CORES)
            target = occ_ref.at[:, pl.ds(pl.multiple_of(half * 128, 128), 128)]
            source = pieces[far * count + count - 1].at[:, pl.ds(width, 128)]
            yield pltpu.make_async_copy(source, target, sems.at[2 * count + far])

    def copies(far):
        for k in range(count):
            at = far * count + k
            target = right_ref.at[far, pl.ds(k * CAP, CAP), :]
            yield pltpu.make_async_copy(pieces[at].at[:, pl.ds(0, width)], target, sems.at[at])

    @pl.when(j == 0)
    def _():
        for copy in (*occ_copies(), *copies(0), *copies(1)):
            copy.start()
        for copy in occ_copies():
            copy.wait()
        occ = occ_ref[...].T
        for p in range(2):
            rows = slice(p * NOCC, (p + 1) * NOCC)
            late = jnp.dot(occ, late_ref[p * CAP : (p + 1) * CAP, :], preferred_element_type=F32)
            half_ref[rows, :] = (part_ref[rows, :] + late).astype(BF16)

    for far in range(2):

        @pl.when(j == far * per)
        def _():
            for copy in copies(far):
                copy.wait()

    right = right_ref[lax.div(j, per), :, pl.ds(pl.multiple_of(lax.rem(j, per) * tile, 128), tile)]
    total = jnp.dot(half_ref[...], right, preferred_element_type=F32).astype(BF16)
    out_ref[...] = total.reshape(out_ref.shape)


VMEM = pl.BlockSpec(memory_space=pltpu.VMEM)
SMEM = pl.BlockSpec(memory_space=pltpu.SMEM)
HBM = pl.BlockSpec(memory_space=pltpu.HBM)
ANY = pl.BlockSpec(memory_space=pl.ANY)


def shape(*dims, dtype=BF16):
    return jax.ShapeDtypeStruct(dims, dtype)


def params(mib):
    return pltpu.CompilerParams(vmem_limit_bytes=mib << 20)


def cost(flops, nbytes):
    return pl.CostEstimate(flops=int(flops), bytes_accessed=int(nbytes), transcendentals=0)


def short_way(panels, block_pairs, block_count, shell_size, occ_coef, vir_coef):
    n = lax.axis_size("shell")
    here, nvir = vir_coef.shape
    width = nvir // CORES
    packed = width + NOCC // CORES
    room = Z * Y * CAP
    me = lax.axis_index("shell")
    size_row = shell_size.reshape(1, -1)

    def swap(array, bit):
        return lax.ppermute(array, "shell", [(i, i ^ bit) for i in range(n)])

    code, keep, to_core, to_y, to_both = pl.pallas_call(
        functools.partial(pack_kernel, size_row.shape[1]),
        out_shape=[shape(n, BLK_DEV, 128, dtype=jnp.int32)] + [shape(here // 2, packed)] * 4,
        in_specs=[HBM] * 2 + [VMEM] * 2,
        out_specs=[VMEM] * 5,
        scratch_shapes=[
            pltpu.VMEM((2, BLK_DEV), jnp.int32),
            pltpu.VMEM((1, 1), jnp.int32),
            pltpu.SemaphoreType.DMA((2,)),
        ],
        compiler_params=params(12),
        cost_estimate=cost(3e8, 3e6),
        name="pack_rows",
    )(block_pairs.T, block_count.reshape(1, 1), vir_coef, occ_coef)
    to_y, to_both, to_core = swap(to_y, 2), swap(to_both, 3), swap(to_core, 1)
    code = lax.all_to_all(code, "shell", split_axis=0, concat_axis=0, tiled=True)

    mine, over = pl.pallas_call(
        functools.partial(pick_kernel, here),
        out_shape=(shape(CAP, packed), shape(1, dtype=jnp.int32)),
        in_specs=[VMEM] * 6,
        out_specs=(VMEM, SMEM),
        compiler_params=params(12),
        cost_estimate=cost(3e8, 2e6),
        name="pick_rows",
    )(code, size_row, keep, to_core, to_y, to_both)

    z = me // (Y * CORES)
    inner = (z == 1) | (z == 2)
    ends, middle, outward = [(0, 1), (1, 0), (2, 3), (3, 2)], [(1, 2), (2, 1)], [(1, 0), (2, 3)]

    def hop(array, steps):
        return lax.ppermute(array, "shell", [(4 * a + k, 4 * b + k) for a, b in steps for k in range(4)])

    beside, across, mine_y = hop(mine, ends), hop(mine, middle), swap(mine, 2)
    beside, across, mine_y = lax.optimization_barrier((beside, across, mine_y))

    corner, across_out, beside_y = hop(beside, middle), hop(across, outward), swap(beside, 2)
    far = [swap(mine, 1), swap(mine_y, 1), swap(beside, 1)]
    corner, across_out, beside_y, panels, *far = lax.optimization_barrier(
        (corner, across_out, beside_y, panels, *far)
    )

    across = jnp.where(inner, across, across_out)
    corner_out, across_y = hop(corner, outward), swap(across, 2)
    far += [swap(beside_y, 1), swap(across, 1)]
    send = pl.pallas_call(
        send_kernel,
        out_shape=shape(n, 2 * BLK_DEV, EDGE * EDGE),
        in_specs=[VMEM],
        out_specs=VMEM,
        compiler_params=params(12),
        cost_estimate=cost(1e6, 3e5),
        name="turn_panels",
    )(panels)
    got = lax.all_to_all(send, "shell", split_axis=0, concat_axis=0, tiled=True)
    corner_out, across_y, got, *far = lax.optimization_barrier((corner_out, across_y, got, *far))

    corner = jnp.where(inner, corner, corner_out)
    corner_y = swap(corner, 2)
    far += [swap(across_y, 1), swap(corner, 1)]
    near = [mine, mine_y, beside, beside_y, across, across_y, corner]
    count = len(near)
    half, late = pl.pallas_call(
        functools.partial(half_kernel, here),
        out_shape=(shape(2 * NOCC, room, dtype=F32), shape(2 * CAP, room)),
        grid=(1,),
        in_specs=[VMEM] * 3 + [ANY] * (2 * count),
        out_specs=(
            pl.BlockSpec((2 * NOCC, room), lambda i: (0, 0)),
            pl.BlockSpec((2 * CAP, room), lambda i: (0, 0)),
        ),
        scratch_shapes=[pltpu.VMEM((room, NOCC), BF16), pltpu.SemaphoreType.DMA((2 * count,))],
        compiler_params=params(24),
        cost_estimate=cost(4e9, 8e6),
        name="half_transform",
    )(code, got, size_row, *near, *far)
    corner_y, half, late = lax.optimization_barrier((corner_y, half, late))
    near.append(corner_y)
    far.append(swap(corner_y, 1))

    count = len(near)
    tile = width // 3
    out = pl.pallas_call(
        functools.partial(last_kernel, count),
        out_shape=shape(2, NOCC, nvir),
        grid_spec=pltpu.PrefetchScalarGridSpec(
            num_scalar_prefetch=1,
            grid=(nvir // tile,),
            in_specs=[
                pl.BlockSpec((2 * NOCC, room), lambda j, o: (0, 0)),
                pl.BlockSpec((2 * CAP, room), lambda j, o: (0, 0)),
            ]
            + [ANY] * (2 * count),
            out_specs=pl.BlockSpec((2, NOCC, tile), lambda j, o: (0, 0, (j + 3 * (o[0] % 2)) % 6)),
            scratch_shapes=[
                pltpu.VMEM((CORES, room, width), BF16),
                pltpu.VMEM((CAP, NOCC), BF16),
                pltpu.VMEM((2 * NOCC, room), BF16),
                pltpu.SemaphoreType.DMA((2 * count + 2,)),
            ],
        ),
        compiler_params=params(24),
        cost_estimate=cost(3e9, 1e7),
        name="last_product",
    )(me.reshape(1), half, late, *near, *far)
    return out, over[0], code, got


def per_device(*args):
    n = lax.axis_size("shell")
    here, nvir = args[5].shape
    shells = args[3].shape[0]
    sparse = LIVE_DEV * n * EDGE < n * here
    if not (sparse and n == Z * Y * CORES and here <= 256 and here % 16 == 0 and nvir % 768 == 0):
        return from_start(*args)
    out, over, code, got = short_way(*args)

    def again(carry):
        over, _ = carry
        over, code_now, turned, *held = lax.optimization_barrier((over, code, got, *args[3:]))
        turned = turned.reshape(n, 2, BLK_DEV, EDGE * EDGE).swapaxes(1, 2).reshape(n * BLK_DEV, 2, EDGE * EDGE)
        code_now = jnp.max(code_now, axis=2).reshape(n * BLK_DEV)
        ids = jnp.maximum(code_now, 0)
        pairs = jnp.stack([ids // shells, ids % shells], axis=1)
        return over - 1, long_way(turned, pairs, code_now >= 0, *held)

    return lax.while_loop(lambda carry: carry[0] > 0, again, (over, out))[1]


def solution(mesh):
    placed = (
        P(("groups", "shell"), None, None),
        P(("groups", "shell"), None),
        P(("groups", "shell")),
        P("groups"),
        P(("groups", "shell"), None),
        P(("groups", "shell"), None),
    )
    return jax.shard_map(
        per_device,
        mesh=mesh,
        in_specs=placed,
        out_specs=P(("groups", "shell"), None, None),
        check_vma=False,
    )
```

```python
import functools
import math

import jax
import jax.numpy as jnp
from jax import lax
from jax.experimental import pallas as pl
from jax.experimental.pallas import tpu as pltpu
from jax.sharding import PartitionSpec as P

EDGE = 16
NOCC = 256
BLK_DEV = 8
LIVE_DEV = 4
CAP = 128
Z, Y, CORES = 4, 2, 2
F32 = jnp.float32
BF16 = jnp.bfloat16


def padded_rows(matrix, starts, shell_size):
    offsets = jnp.arange(EDGE, dtype=jnp.int32)
    rows = jnp.minimum(starts[:, None] + offsets[None, :], matrix.shape[0] - 1)
    inside = offsets[None, :] < shell_size[:, None]
    return jnp.where(inside[:, :, None], matrix[rows], jnp.zeros((), matrix.dtype))


def half_transform(slot_rows, pairs, keep, occ_blocks):
    count = slot_rows.shape[0]
    vecs_here = slot_rows.shape[1]
    shells = occ_blocks.shape[0]
    group_size = math.gcd(512, count)
    turns = count // group_size
    shaped = slot_rows.reshape(count, vecs_here, EDGE, EDGE)

    def advance(total, turn):
        first = turn * group_size
        block = lax.dynamic_slice_in_dim(shaped, first, group_size, 0)
        okay = lax.dynamic_slice_in_dim(keep, first, group_size, 0)
        block = jnp.where(okay[:, None, None, None], block, jnp.zeros((), block.dtype))
        row_shell = lax.dynamic_slice_in_dim(pairs[:, 0], first, group_size, 0)
        col_shell = lax.dynamic_slice_in_dim(pairs[:, 1], first, group_size, 0)
        coefs = occ_blocks[row_shell]
        piece = jnp.einsum("kmi,kvmn->kvin", coefs, block, preferred_element_type=jnp.float32)
        return (total.at[col_shell].add(piece), None)

    start_total = jnp.zeros((shells, vecs_here, NOCC, EDGE), jnp.float32)
    half, _ = lax.scan(advance, start_total, jnp.arange(turns, dtype=jnp.int32))
    return half


def long_way(turned, pairs, live, shell_size, occ_coef, vir_coef):
    occ_full = lax.all_gather(occ_coef, "shell", axis=0, tiled=True)
    starts = jnp.cumsum(shell_size) - shell_size
    occ_blocks = padded_rows(occ_full, starts, shell_size)
    half = half_transform(turned, pairs, live, occ_blocks)
    hidden = half.astype(jnp.bfloat16)
    vir_full = lax.all_gather(vir_coef, "shell", axis=0, tiled=True)
    vir_blocks = padded_rows(vir_full, starts, shell_size)
    result = jnp.einsum("svin,sna->via", hidden, vir_blocks, preferred_element_type=jnp.float32)
    return result.astype(jnp.bfloat16)


def from_start(panels, block_pairs, block_count, *rest):
    pairs = lax.all_gather(block_pairs, "shell", axis=0, tiled=True)
    counts = lax.all_gather(block_count, "shell", axis=0, tiled=True)
    turned = lax.all_to_all(panels, "shell", split_axis=1, concat_axis=0, tiled=True)
    position = jnp.arange(turned.shape[0], dtype=jnp.int32)
    live = position % BLK_DEV < counts[position // BLK_DEV]
    return long_way(turned, pairs, live, *rest)


def iota(shape, dim):
    return lax.broadcasted_iota(jnp.int32, shape, dim)


def column_of(row, mask):
    return jnp.sum(jnp.where(mask, row, 0.0), axis=1, keepdims=True)


def row_of(column, mask):
    return jnp.sum(jnp.where(mask, column, 0.0), axis=0, keepdims=True)


def zero_one(mask):
    return jnp.where(mask, 1.0, 0.0)


def lane_value(row, index):
    return jnp.sum(jnp.where(iota(row.shape, 1) == index, row, 0.0), axis=1, keepdims=True)


def one_hots(ids, shells):
    lanes = iota(ids.shape, 1).astype(F32)
    return jnp.concatenate([zero_one(ids == lanes + 128.0 * k) for k in range(shells // 128)], axis=1)


def slot_hots(got, shells):
    ids = got[:, 2 * BLK_DEV :, :].reshape(-1, 256)
    return one_hots(ids[:, :128], shells), one_hots(ids[:, 128:], shells)


class Shells:
    def __init__(self, size_row):
        shells = size_row.shape[1]
        sub, lane = iota((shells, shells), 0), iota((shells, shells), 1)
        self.before, self.same = lane < sub, lane == sub
        self.starts = column_of(size_row, self.before)
        self.size = column_of(size_row, self.same)
        self.odd = self.starts - 2.0 * jnp.floor(self.starts * 0.5)


class Used:
    def __init__(self, shells, hot, window):
        self.used = column_of(jnp.max(hot, axis=0, keepdims=True), shells.same)
        self.extra, self.ahead, self.edges = [], [], []
        edge = (iota((hot.shape[1], 128), 1) * window).astype(F32)
        reach = jnp.clip(edge - shells.starts, 0.0, shells.size)
        for parity in range(2):
            extra = 1.0 - shells.odd if parity == 0 else shells.odd
            count = self.used * jnp.floor((shells.size + extra) * 0.5)
            count_row = row_of(count, shells.same)
            self.extra.append(extra)
            self.ahead.append(column_of(count_row, shells.before))
            self.edges.append(jnp.sum(self.used * jnp.floor((reach + extra) * 0.5), axis=0, keepdims=True))


def pack_kernel(vir_ref, occ_ref, *outs):
    me = lax.axis_index("shell")
    core, y = lax.rem(me, 2), lax.rem(lax.div(me, 2), 2)
    here, nvir = vir_ref.shape
    width, thin = nvir // CORES, occ_ref.shape[1] // CORES
    for dy in range(2):
        parity = lax.rem(y + dy, 2)
        pick = zero_one(iota((here // 2, here), 1) == 2 * iota((here // 2, here), 0) + parity).astype(BF16)
        for dc in range(2):
            half = lax.rem(core + dc, 2)
            out = outs[2 * dy + dc]
            part = vir_ref[:, pl.ds(pl.multiple_of(half * width, 128), width)]
            out[:, :width] = jnp.dot(pick, part, preferred_element_type=F32).astype(BF16)
            part = occ_ref[:, pl.ds(pl.multiple_of(half * thin, 128), thin)]
            out[:, width:] = jnp.dot(pick, part, preferred_element_type=F32).astype(BF16)


def send_kernel(pairs_ref, count_ref, panels_ref, send_ref):
    n = send_ref.shape[0]
    turned = jnp.swapaxes(panels_ref[...].astype(F32), 0, 1)
    send_ref[:, : 2 * BLK_DEV, :] = turned.reshape(n, 2 * BLK_DEV, EDGE * EDGE).astype(BF16)
    kept = iota((1, BLK_DEV), 1) < count_ref[...]
    square = (BLK_DEV, BLK_DEV)
    same = iota(square, 0) == iota(square, 1)
    wide = (BLK_DEV, 128)
    columns, rows = (
        jnp.broadcast_to(column_of(jnp.where(kept, pairs_ref[k : k + 1, :], -1).astype(F32), same), wide)
        for k in (1, 0)
    )
    ids = jnp.concatenate([columns, rows], axis=1)
    send_ref[:, 2 * BLK_DEV :, :] = jnp.broadcast_to(ids[None], (n, BLK_DEV, 256)).astype(BF16)


def pick_kernel(here, got_ref, size_ref, *refs):
    sources, (out_ref, over_ref) = refs[:4], refs[4:]
    me = lax.axis_index("shell")
    core, y, z = lax.rem(me, 2), lax.rem(lax.div(me, 2), 2), lax.div(me, 4)
    window = CORES * Y * here
    shell_count = size_ref.shape[1]
    shells = Shells(size_ref[...].astype(F32))
    lists = [Used(shells, hot, window) for hot in slot_hots(got_ref[...].astype(F32), shell_count)]
    most = jnp.zeros((1, 1), F32)
    lane = iota((1, 128), 1)
    for chosen in lists:
        for edges in chosen.edges:
            later = jnp.concatenate([edges[:, 1:], edges[:, :1]], axis=1)
            most = jnp.maximum(most, jnp.max(jnp.where(lane < Z, later - edges, 0.0), axis=1, keepdims=True))
    over_ref[0] = jnp.where(jnp.max(most) > CAP, 1, 0).astype(jnp.int32)

    width = out_ref.shape[1] - 128
    even = y == 0
    totals = [jnp.zeros((CAP, width), F32), jnp.zeros((CAP, 128), F32)]
    columns = [slice(0, width), slice(width, width + 128)]
    extra = jnp.where(even, lists[0].extra[0], lists[0].extra[1])
    for k, source in enumerate(sources):
        device = 4 * z + 2 * lax.rem(y + k // 2, 2) + lax.rem(core + k % 2, 2)
        row = (2 * iota((shell_count, 128), 1) + device * here + y).astype(F32)
        where = row - shells.starts
        inside = (where >= 0.0) & (where < shells.size)
        within = jnp.floor((where + extra) * 0.5)
        for chosen, total, column in zip(lists, range(2), columns):
            ahead = jnp.where(even, chosen.ahead[0], chosen.ahead[1])
            base = lane_value(jnp.where(even, chosen.edges[0], chosen.edges[1]), z)
            place = jnp.where(inside & (chosen.used > 0.0), ahead + within + 1.0, 0.0)
            place = jnp.sum(place, axis=0, keepdims=True)
            place = jnp.where(place > 0.0, place - 1.0 - base, -1.0)
            hot = zero_one(place == iota((CAP, 128), 0).astype(F32)).astype(BF16)
            totals[total] += jnp.dot(
                hot[:, : here // 2], source[:, column], preferred_element_type=F32
            )
    for total, column in zip(totals, columns):
        out_ref[:, column] = total.astype(BF16)


def half_kernel(here, got_ref, size_ref, *refs):
    count = (len(refs) - 4) // 2
    pieces, (half_ref, late_ref, occ_ref, sems) = refs[: 2 * count], refs[2 * count :]
    me = lax.axis_index("shell")
    core, chip = lax.rem(me, CORES), lax.div(me, CORES)
    width = pieces[0].shape[1] - 128
    copies = []
    for far in range(2):
        half = lax.rem(core + far, CORES)
        for k in range(count):
            at = far * count + k
            target = occ_ref.at[pl.ds(k * CAP, CAP), pl.ds(pl.multiple_of(half * 128, 128), 128)]
            copies.append(pltpu.make_async_copy(pieces[at].at[:, pl.ds(width, 128)], target, sems.at[at]))
    for copy in copies:
        copy.start()
    occ_ref[count * CAP :, :] = jnp.zeros((occ_ref.shape[0] - count * CAP, occ_ref.shape[1]), BF16)
    window = CORES * Y * here
    shell_count = size_ref.shape[1]
    got = got_ref[...].astype(F32)
    size_row = size_ref[...].astype(F32)
    shells = Shells(size_row)
    got = got_ref[...].astype(F32)
    hots = slot_hots(got, shell_count)
    lists = [Used(shells, hot, window) for hot in hots]
    slots = hots[0].shape[0]
    kept = LIVE_DEV * (slots // BLK_DEV)
    alive = jnp.broadcast_to(jnp.sum(hots[0], axis=1, keepdims=True), (slots, slots))
    sub, lane = iota((slots, slots), 0), iota((slots, slots), 1)
    rank = row_of(alive, sub < lane)
    alive_row = row_of(alive, sub == lane)
    take = (rank == iota((kept, slots), 0).astype(F32)) & (alive_row > 0.0)
    take = zero_one(take).astype(BF16)

    def taken(array):
        return jnp.dot(take, array.astype(BF16), preferred_element_type=F32)

    def spread(hot, column):
        value = jnp.sum(hot * row_of(column, shells.same), axis=1, keepdims=True)
        wide = jnp.broadcast_to(value, (kept, 128)).reshape(kept, 1, 128)
        return jnp.broadcast_to(wide, (kept, EDGE, 128)).reshape(kept * EDGE, 128)

    at = iota((kept * EDGE, 128), 0) % EDGE
    step = at.astype(F32)

    def places(hot, chosen):
        hot = taken(hot)
        first, length = spread(hot, shells.starts), spread(hot, shells.size)
        row = first + step
        odd = (row - 2.0 * jnp.floor(row * 0.5)) > 0.0
        place = jnp.where(odd, spread(hot, chosen.ahead[1]), spread(hot, chosen.ahead[0]))
        place += jnp.floor(step * 0.5)
        offsets = [
            [((w * Y + k) ^ chip).astype(F32) * CAP - lane_value(e, w) for w in range(Z)]
            for k, e in enumerate(chosen.edges)
        ]
        offset = jnp.where(odd, offsets[1][0], offsets[0][0])
        for w in range(1, Z):
            offset = jnp.where(row >= float(window * w), jnp.where(odd, offsets[1][w], offsets[0][w]), offset)
        return jnp.where(step < length, place + offset, -1.0)[:, :1]

    place_c, place_r = places(hots[0], lists[0]), places(hots[1], lists[1])
    span = 16 * EDGE
    width = half_ref.shape[1]
    s_in, l_in = iota((span, span), 0), iota((span, span), 1)
    keep_m = (l_in // EDGE) == (s_in % EDGE)
    fold = zero_one((s_in % EDGE) == (l_in % EDGE)).astype(BF16)
    same_slot = (s_in // EDGE) == (l_in // EDGE)
    blocks = [taken(got[:, p * BLK_DEV : (p + 1) * BLK_DEV, :].reshape(slots, span)) for p in range(2)]
    lanes = iota((span, width), 1).astype(F32)
    for copy in copies:
        copy.wait()
    occ = occ_ref[...]
    late = []
    for g in range(kept // 16):
        rows = slice(g * span, (g + 1) * span)
        r_hot = zero_one(place_r[rows] == lanes).astype(BF16)
        c_hot = zero_one(place_c[rows] == lanes).astype(BF16)
        part = jnp.dot(r_hot, occ, preferred_element_type=F32).T.astype(BF16)
        for p in range(2):
            block = blocks[p][g * 16 : (g + 1) * 16].reshape(16, 1, span)
            block = jnp.broadcast_to(block, (16, EDGE, span)).reshape(span, span)
            block = jnp.where(keep_m, block, 0.0).astype(BF16)
            diag = jnp.dot(block, fold, preferred_element_type=F32)
            diag = jnp.where(same_slot, diag, 0.0).astype(BF16)
            placed = jnp.dot(diag, c_hot, preferred_element_type=F32).astype(BF16)
            piece = jnp.dot(part, placed, preferred_element_type=F32)
            rows_p = slice(p * NOCC, (p + 1) * NOCC)
            rows_l = slice(p * CAP, (p + 1) * CAP)
            later = jnp.dot(r_hot[:, count * CAP :].T, placed, preferred_element_type=F32)
            if g == 0:
                half_ref[rows_p, :] = piece
                late.append(later)
            else:
                half_ref[rows_p, :] += piece
                late[p] += later
    for p in range(2):
        late_ref[p * CAP : (p + 1) * CAP, :] = late[p].astype(BF16)


def last_kernel(count, me_ref, part_ref, late_ref, *refs):
    pieces, (out_ref, right_ref, occ_ref, half_ref, sems) = refs[: 2 * count], refs[2 * count :]
    tile = out_ref.shape[2]
    width = right_ref.shape[2]
    per = width // tile
    core = lax.rem(me_ref[0], CORES)
    j = pl.program_id(0)

    def occ_copies():
        for far in range(2):
            half = lax.rem(core + far, CORES)
            target = occ_ref.at[:, pl.ds(pl.multiple_of(half * 128, 128), 128)]
            source = pieces[far * count + count - 1].at[:, pl.ds(width, 128)]
            yield pltpu.make_async_copy(source, target, sems.at[2 * count + far])

    def copies(far):
        for k in range(count):
            at = far * count + k
            target = right_ref.at[far, pl.ds(k * CAP, CAP), :]
            yield pltpu.make_async_copy(pieces[at].at[:, pl.ds(0, width)], target, sems.at[at])

    @pl.when(j == 0)
    def _():
        for copy in (*occ_copies(), *copies(0), *copies(1)):
            copy.start()
        for copy in occ_copies():
            copy.wait()
        occ = occ_ref[...].T
        for p in range(2):
            rows = slice(p * NOCC, (p + 1) * NOCC)
            late = jnp.dot(occ, late_ref[p * CAP : (p + 1) * CAP, :], preferred_element_type=F32)
            half_ref[rows, :] = (part_ref[rows, :] + late).astype(BF16)

    for far in range(2):

        @pl.when(j == far * per)
        def _():
            for copy in copies(far):
                copy.wait()

    right = right_ref[lax.div(j, per), :, pl.ds(pl.multiple_of(lax.rem(j, per) * tile, 128), tile)]
    total = jnp.dot(half_ref[...], right, preferred_element_type=F32).astype(BF16)
    out_ref[...] = total.reshape(out_ref.shape)


VMEM = pl.BlockSpec(memory_space=pltpu.VMEM)
SMEM = pl.BlockSpec(memory_space=pltpu.SMEM)
ANY = pl.BlockSpec(memory_space=pl.ANY)


def shape(*dims, dtype=BF16):
    return jax.ShapeDtypeStruct(dims, dtype)


def params(mib):
    return pltpu.CompilerParams(vmem_limit_bytes=mib << 20)


def cost(flops, nbytes):
    return pl.CostEstimate(flops=int(flops), bytes_accessed=int(nbytes), transcendentals=0)


def short_way(panels, block_pairs, block_count, shell_size, occ_coef, vir_coef):
    n = lax.axis_size("shell")
    here, nvir = vir_coef.shape
    width = nvir // CORES
    packed = width + NOCC // CORES
    room = Z * Y * CAP
    me = lax.axis_index("shell")
    size_row = shell_size.reshape(1, -1)

    def swap(array, bit):
        return lax.ppermute(array, "shell", [(i, i ^ bit) for i in range(n)])

    keep, to_core, to_y, to_both = pl.pallas_call(
        pack_kernel,
        out_shape=[shape(here // 2, packed)] * 4,
        in_specs=[VMEM] * 2,
        out_specs=[VMEM] * 4,
        compiler_params=params(12),
        cost_estimate=cost(3e8, 3e6),
        name="pack_rows",
    )(vir_coef, occ_coef)
    to_y, to_both, to_core = swap(to_y, 2), swap(to_both, 3), swap(to_core, 1)
    send = pl.pallas_call(
        send_kernel,
        out_shape=shape(n, 3 * BLK_DEV, EDGE * EDGE),
        in_specs=[VMEM] * 3,
        out_specs=VMEM,
        compiler_params=params(12),
        cost_estimate=cost(1e6, 5e5),
        name="pack_panels",
    )(block_pairs.T, block_count.reshape(1, 1), panels)
    got = lax.all_to_all(send, "shell", split_axis=0, concat_axis=0, tiled=True)

    mine, over = pl.pallas_call(
        functools.partial(pick_kernel, here),
        out_shape=(shape(CAP, packed), shape(1, dtype=jnp.int32)),
        in_specs=[VMEM] * 6,
        out_specs=(VMEM, SMEM),
        compiler_params=params(12),
        cost_estimate=cost(3e8, 2e6),
        name="pick_rows",
    )(got, size_row, keep, to_core, to_y, to_both)

    beside, across, mine_y = swap(mine, 4), swap(mine, 8), swap(mine, 2)
    beside, mine_y = lax.optimization_barrier((beside, mine_y))

    beside_y = swap(beside, 2)
    far = [swap(mine, 1), swap(mine_y, 1), swap(beside, 1)]
    across, beside_y, *far = lax.optimization_barrier((across, beside_y, *far))

    corner, across_y = swap(across, 4), swap(across, 2)
    far += [swap(beside_y, 1), swap(across, 1)]
    corner, across_y, *far = lax.optimization_barrier((corner, across_y, *far))

    corner_y = swap(corner, 2)
    far += [swap(across_y, 1), swap(corner, 1)]
    near = [mine, mine_y, beside, beside_y, across, across_y, corner]
    count = len(near)
    half, late = pl.pallas_call(
        functools.partial(half_kernel, here),
        out_shape=(shape(2 * NOCC, room, dtype=F32), shape(2 * CAP, room)),
        grid=(1,),
        in_specs=[VMEM] * 2 + [ANY] * (2 * count),
        out_specs=(
            pl.BlockSpec((2 * NOCC, room), lambda i: (0, 0)),
            pl.BlockSpec((2 * CAP, room), lambda i: (0, 0)),
        ),
        scratch_shapes=[pltpu.VMEM((room, NOCC), BF16), pltpu.SemaphoreType.DMA((2 * count,))],
        compiler_params=params(24),
        cost_estimate=cost(4e9, 8e6),
        name="half_transform",
    )(got, size_row, *near, *far)
    corner_y, half, late = lax.optimization_barrier((corner_y, half, late))
    near.append(corner_y)
    far.append(swap(corner_y, 1))

    count = len(near)
    tile = width // 3
    out = pl.pallas_call(
        functools.partial(last_kernel, count),
        out_shape=shape(2, NOCC, nvir),
        grid_spec=pltpu.PrefetchScalarGridSpec(
            num_scalar_prefetch=1,
            grid=(nvir // tile,),
            in_specs=[
                pl.BlockSpec((2 * NOCC, room), lambda j, o: (0, 0)),
                pl.BlockSpec((2 * CAP, room), lambda j, o: (0, 0)),
            ]
            + [ANY] * (2 * count),
            out_specs=pl.BlockSpec((2, NOCC, tile), lambda j, o: (0, 0, (j + 3 * (o[0] % 2)) % 6)),
            scratch_shapes=[
                pltpu.VMEM((CORES, room, width), BF16),
                pltpu.VMEM((CAP, NOCC), BF16),
                pltpu.VMEM((2 * NOCC, room), BF16),
                pltpu.SemaphoreType.DMA((2 * count + 2,)),
            ],
        ),
        compiler_params=params(24),
        cost_estimate=cost(3e9, 1e7),
        name="last_product",
    )(me.reshape(1), half, late, *near, *far)
    return out, over[0], got


def per_device(*args):
    n = lax.axis_size("shell")
    here, nvir = args[5].shape
    sparse = LIVE_DEV * n * EDGE < n * here
    if not (sparse and n == Z * Y * CORES and here <= 256 and here % 16 == 0 and nvir % 768 == 0):
        return from_start(*args)
    out, over, got = short_way(*args)

    def again(carry):
        over, _ = carry
        over, got_now, *held = lax.optimization_barrier((over, got, *args[3:]))
        turned = got_now[:, : 2 * BLK_DEV].reshape(n, 2, BLK_DEV, EDGE * EDGE).swapaxes(1, 2)
        turned = turned.reshape(n * BLK_DEV, 2, EDGE * EDGE)
        ids = got_now[:, 2 * BLK_DEV :].reshape(n * BLK_DEV, 256).astype(jnp.int32)
        columns, rows = jnp.max(ids[:, :128], axis=1), jnp.max(ids[:, 128:], axis=1)
        pairs = jnp.maximum(jnp.stack([rows, columns], axis=1), 0)
        return over - 1, long_way(turned, pairs, columns >= 0, *held)

    return lax.while_loop(lambda carry: carry[0] > 0, again, (over, out))[1]


def solution(mesh):
    placed = (
        P(("groups", "shell"), None, None),
        P(("groups", "shell"), None),
        P(("groups", "shell")),
        P("groups"),
        P(("groups", "shell"), None),
        P(("groups", "shell"), None),
    )
    return jax.shard_map(
        per_device,
        mesh=mesh,
        in_specs=placed,
        out_specs=P(("groups", "shell"), None, None),
        check_vma=False,
    )
```

```python
import functools
import math

import jax
import jax.numpy as jnp
from jax import lax
from jax.experimental import pallas as pl
from jax.experimental.pallas import tpu as pltpu
from jax.sharding import PartitionSpec as P

EDGE = 16
NOCC = 256
BLK_DEV = 8
LIVE_DEV = 4
CAP = 128
Z, Y, CORES = 4, 2, 2
F32 = jnp.float32
BF16 = jnp.bfloat16


def padded_rows(matrix, starts, shell_size):
    offsets = jnp.arange(EDGE, dtype=jnp.int32)
    rows = jnp.minimum(starts[:, None] + offsets[None, :], matrix.shape[0] - 1)
    inside = offsets[None, :] < shell_size[:, None]
    return jnp.where(inside[:, :, None], matrix[rows], jnp.zeros((), matrix.dtype))


def half_transform(slot_rows, pairs, keep, occ_blocks):
    count = slot_rows.shape[0]
    vecs_here = slot_rows.shape[1]
    shells = occ_blocks.shape[0]
    group_size = math.gcd(512, count)
    turns = count // group_size
    shaped = slot_rows.reshape(count, vecs_here, EDGE, EDGE)

    def advance(total, turn):
        first = turn * group_size
        block = lax.dynamic_slice_in_dim(shaped, first, group_size, 0)
        okay = lax.dynamic_slice_in_dim(keep, first, group_size, 0)
        block = jnp.where(okay[:, None, None, None], block, jnp.zeros((), block.dtype))
        row_shell = lax.dynamic_slice_in_dim(pairs[:, 0], first, group_size, 0)
        col_shell = lax.dynamic_slice_in_dim(pairs[:, 1], first, group_size, 0)
        coefs = occ_blocks[row_shell]
        piece = jnp.einsum("kmi,kvmn->kvin", coefs, block, preferred_element_type=jnp.float32)
        return (total.at[col_shell].add(piece), None)

    start_total = jnp.zeros((shells, vecs_here, NOCC, EDGE), jnp.float32)
    half, _ = lax.scan(advance, start_total, jnp.arange(turns, dtype=jnp.int32))
    return half


def long_way(turned, pairs, live, shell_size, occ_coef, vir_coef):
    occ_full = lax.all_gather(occ_coef, "shell", axis=0, tiled=True)
    starts = jnp.cumsum(shell_size) - shell_size
    occ_blocks = padded_rows(occ_full, starts, shell_size)
    half = half_transform(turned, pairs, live, occ_blocks)
    hidden = half.astype(jnp.bfloat16)
    vir_full = lax.all_gather(vir_coef, "shell", axis=0, tiled=True)
    vir_blocks = padded_rows(vir_full, starts, shell_size)
    result = jnp.einsum("svin,sna->via", hidden, vir_blocks, preferred_element_type=jnp.float32)
    return result.astype(jnp.bfloat16)


def from_start(panels, block_pairs, block_count, *rest):
    pairs = lax.all_gather(block_pairs, "shell", axis=0, tiled=True)
    counts = lax.all_gather(block_count, "shell", axis=0, tiled=True)
    turned = lax.all_to_all(panels, "shell", split_axis=1, concat_axis=0, tiled=True)
    position = jnp.arange(turned.shape[0], dtype=jnp.int32)
    live = position % BLK_DEV < counts[position // BLK_DEV]
    return long_way(turned, pairs, live, *rest)


def iota(shape, dim):
    return lax.broadcasted_iota(jnp.int32, shape, dim)


def column_of(row, mask):
    return jnp.sum(jnp.where(mask, row, 0.0), axis=1, keepdims=True)


def row_of(column, mask):
    return jnp.sum(jnp.where(mask, column, 0.0), axis=0, keepdims=True)


def zero_one(mask):
    return jnp.where(mask, 1.0, 0.0)


def lane_value(row, index):
    return jnp.sum(jnp.where(iota(row.shape, 1) == index, row, 0.0), axis=1, keepdims=True)


def one_hots(ids, shells):
    lanes = iota(ids.shape, 1).astype(F32)
    return jnp.concatenate([zero_one(ids == lanes + 128.0 * k) for k in range(shells // 128)], axis=1)


def slot_hots(code, shells):
    code = code.reshape(-1, 128)
    kept = code >= 0
    columns = jnp.where(kept, code % shells, -1).astype(F32)
    return one_hots(columns, shells), one_hots(jnp.where(kept, code // shells, -1).astype(F32), shells)


class Shells:
    def __init__(self, size_row):
        shells = size_row.shape[1]
        sub, lane = iota((shells, shells), 0), iota((shells, shells), 1)
        self.before, self.same = lane < sub, lane == sub
        self.starts = column_of(size_row, self.before)
        self.size = column_of(size_row, self.same)
        self.odd = self.starts - 2.0 * jnp.floor(self.starts * 0.5)


class Used:
    def __init__(self, shells, hot, window):
        self.used = column_of(jnp.max(hot, axis=0, keepdims=True), shells.same)
        self.extra, self.ahead, self.edges = [], [], []
        edge = (iota((hot.shape[1], 128), 1) * window).astype(F32)
        reach = jnp.clip(edge - shells.starts, 0.0, shells.size)
        for parity in range(2):
            extra = 1.0 - shells.odd if parity == 0 else shells.odd
            count = self.used * jnp.floor((shells.size + extra) * 0.5)
            count_row = row_of(count, shells.same)
            self.extra.append(extra)
            self.ahead.append(column_of(count_row, shells.before))
            self.edges.append(jnp.sum(self.used * jnp.floor((reach + extra) * 0.5), axis=0, keepdims=True))


def pack_kernel(vir_ref, occ_ref, *outs):
    me = lax.axis_index("shell")
    core, y = lax.rem(me, 2), lax.rem(lax.div(me, 2), 2)
    here, nvir = vir_ref.shape
    width, thin = nvir // CORES, occ_ref.shape[1] // CORES
    for dy in range(2):
        parity = lax.rem(y + dy, 2)
        pick = zero_one(iota((here // 2, here), 1) == 2 * iota((here // 2, here), 0) + parity).astype(BF16)
        for dc in range(2):
            half = lax.rem(core + dc, 2)
            out = outs[2 * dy + dc]
            part = vir_ref[:, pl.ds(pl.multiple_of(half * width, 128), width)]
            out[:, :width] = jnp.dot(pick, part, preferred_element_type=F32).astype(BF16)
            part = occ_ref[:, pl.ds(pl.multiple_of(half * thin, 128), thin)]
            out[:, width:] = jnp.dot(pick, part, preferred_element_type=F32).astype(BF16)


def ids_kernel(shells, pairs_ref, count_ref, code_ref):
    code = pairs_ref[1:2, :] + shells * pairs_ref[0:1, :]
    code = jnp.where(iota((1, BLK_DEV), 1) < count_ref[...], code, -1).astype(F32)
    square = (BLK_DEV, BLK_DEV)
    code = column_of(code, iota(square, 0) == iota(square, 1)).astype(jnp.int32)
    code_ref[...] = jnp.broadcast_to(jnp.broadcast_to(code, (BLK_DEV, 128))[None], code_ref.shape)


def turn_kernel(panels_ref, send_ref):
    turned = jnp.swapaxes(panels_ref[...].astype(F32), 0, 1)
    send_ref[...] = turned.reshape(send_ref.shape).astype(BF16)


def pick_kernel(here, code_ref, size_ref, *refs):
    sources, (out_ref, over_ref) = refs[:4], refs[4:]
    me = lax.axis_index("shell")
    core, y, z = lax.rem(me, 2), lax.rem(lax.div(me, 2), 2), lax.div(me, 4)
    window = CORES * Y * here
    shell_count = size_ref.shape[1]
    shells = Shells(size_ref[...].astype(F32))
    lists = [Used(shells, hot, window) for hot in slot_hots(code_ref[...], shell_count)]
    most = jnp.zeros((1, 1), F32)
    lane = iota((1, 128), 1)
    for chosen in lists:
        for edges in chosen.edges:
            later = jnp.concatenate([edges[:, 1:], edges[:, :1]], axis=1)
            most = jnp.maximum(most, jnp.max(jnp.where(lane < Z, later - edges, 0.0), axis=1, keepdims=True))
    over_ref[0] = jnp.where(jnp.max(most) > CAP, 1, 0).astype(jnp.int32)

    width = out_ref.shape[1] - 128
    even = y == 0
    totals = [jnp.zeros((CAP, width), F32), jnp.zeros((CAP, 128), F32)]
    columns = [slice(0, width), slice(width, width + 128)]
    extra = jnp.where(even, lists[0].extra[0], lists[0].extra[1])
    for k, source in enumerate(sources):
        device = 4 * z + 2 * lax.rem(y + k // 2, 2) + lax.rem(core + k % 2, 2)
        row = (2 * iota((shell_count, 128), 1) + device * here + y).astype(F32)
        where = row - shells.starts
        inside = (where >= 0.0) & (where < shells.size)
        within = jnp.floor((where + extra) * 0.5)
        for chosen, total, column in zip(lists, range(2), columns):
            ahead = jnp.where(even, chosen.ahead[0], chosen.ahead[1])
            base = lane_value(jnp.where(even, chosen.edges[0], chosen.edges[1]), z)
            place = jnp.where(inside & (chosen.used > 0.0), ahead + within + 1.0, 0.0)
            place = jnp.sum(place, axis=0, keepdims=True)
            place = jnp.where(place > 0.0, place - 1.0 - base, -1.0)
            hot = zero_one(place == iota((CAP, 128), 0).astype(F32)).astype(BF16)
            totals[total] += jnp.dot(
                hot[:, : here // 2], source[:, column], preferred_element_type=F32
            )
    for total, column in zip(totals, columns):
        out_ref[:, column] = total.astype(BF16)


def slot_of(window, chip):
    rel = window ^ chip
    return jnp.where((rel == 3) | (rel == 4), rel ^ 7, rel)


def half_kernel(here, code_ref, got_ref, size_ref, *refs):
    count = (len(refs) - 4) // 2
    pieces, (half_ref, late_ref, occ_ref, sems) = refs[: 2 * count], refs[2 * count :]
    me = lax.axis_index("shell")
    core, chip = lax.rem(me, CORES), lax.div(me, CORES)
    width = pieces[0].shape[1] - 128
    copies = []
    for far in range(2):
        half = lax.rem(core + far, CORES)
        for k in range(count):
            at = far * count + k
            target = occ_ref.at[pl.ds(k * CAP, CAP), pl.ds(pl.multiple_of(half * 128, 128), 128)]
            copies.append(pltpu.make_async_copy(pieces[at].at[:, pl.ds(width, 128)], target, sems.at[at]))
    for copy in copies:
        copy.start()
    window = CORES * Y * here
    shell_count = size_ref.shape[1]
    got = got_ref[...].astype(F32)
    size_row = size_ref[...].astype(F32)
    shells = Shells(size_row)
    got = got_ref[...].astype(F32)
    hots = slot_hots(code_ref[...], shell_count)
    lists = [Used(shells, hot, window) for hot in hots]
    slots = hots[0].shape[0]
    kept = LIVE_DEV * (slots // BLK_DEV)
    alive = jnp.broadcast_to(jnp.sum(hots[0], axis=1, keepdims=True), (slots, slots))
    sub, lane = iota((slots, slots), 0), iota((slots, slots), 1)
    rank = row_of(alive, sub < lane)
    alive_row = row_of(alive, sub == lane)
    take = (rank == iota((kept, slots), 0).astype(F32)) & (alive_row > 0.0)
    take = zero_one(take).astype(BF16)

    def taken(array):
        return jnp.dot(take, array.astype(BF16), preferred_element_type=F32)

    def spread(hot, column):
        value = jnp.sum(hot * row_of(column, shells.same), axis=1, keepdims=True)
        wide = jnp.broadcast_to(value, (kept, 128)).reshape(kept, 1, 128)
        return jnp.broadcast_to(wide, (kept, EDGE, 128)).reshape(kept * EDGE, 128)

    at = iota((kept * EDGE, 128), 0) % EDGE
    step = at.astype(F32)

    def places(hot, chosen):
        hot = taken(hot)
        first, length = spread(hot, shells.starts), spread(hot, shells.size)
        row = first + step
        odd = (row - 2.0 * jnp.floor(row * 0.5)) > 0.0
        place = jnp.where(odd, spread(hot, chosen.ahead[1]), spread(hot, chosen.ahead[0]))
        place += jnp.floor(step * 0.5)
        offsets = [
            [slot_of(w * Y + k, chip).astype(F32) * CAP - lane_value(e, w) for w in range(Z)]
            for k, e in enumerate(chosen.edges)
        ]
        offset = jnp.where(odd, offsets[1][0], offsets[0][0])
        for w in range(1, Z):
            offset = jnp.where(row >= float(window * w), jnp.where(odd, offsets[1][w], offsets[0][w]), offset)
        return jnp.where(step < length, place + offset, -1.0)[:, :1]

    place_c, place_r = places(hots[0], lists[0]), places(hots[1], lists[1])
    span = 16 * EDGE
    width = half_ref.shape[1]
    s_in, l_in = iota((span, span), 0), iota((span, span), 1)
    keep_m = (l_in // EDGE) == (s_in % EDGE)
    fold = zero_one((s_in % EDGE) == (l_in % EDGE)).astype(BF16)
    same_slot = (s_in // EDGE) == (l_in // EDGE)
    blocks = [taken(got[:, p * BLK_DEV : (p + 1) * BLK_DEV, :].reshape(slots, span)) for p in range(2)]
    lanes = iota((span, width), 1).astype(F32)
    for copy in copies:
        copy.wait()
    occ = occ_ref[...]
    late = []
    for g in range(kept // 16):
        rows = slice(g * span, (g + 1) * span)
        r_hot = zero_one(place_r[rows] == lanes).astype(BF16)
        c_hot = zero_one(place_c[rows] == lanes).astype(BF16)
        part = jnp.dot(r_hot[:, : count * CAP], occ, preferred_element_type=F32).T.astype(BF16)
        for p in range(2):
            block = blocks[p][g * 16 : (g + 1) * 16].reshape(16, 1, span)
            block = jnp.broadcast_to(block, (16, EDGE, span)).reshape(span, span)
            block = jnp.where(keep_m, block, 0.0).astype(BF16)
            diag = jnp.dot(block, fold, preferred_element_type=F32)
            diag = jnp.where(same_slot, diag, 0.0).astype(BF16)
            placed = jnp.dot(diag, c_hot, preferred_element_type=F32).astype(BF16)
            piece = jnp.dot(part, placed, preferred_element_type=F32)
            rows_p = slice(p * NOCC, (p + 1) * NOCC)
            later = jnp.dot(r_hot[:, count * CAP :].T, placed, preferred_element_type=F32)
            if g == 0:
                half_ref[rows_p, :] = piece
                late.append(later)
            else:
                half_ref[rows_p, :] += piece
                late[p] += later
    for p in range(2):
        late_ref[p] = late[p].astype(BF16)


def last_kernel(count, early, me_ref, part_ref, late_ref, *refs):
    pieces, (out_ref, right_ref, occ_ref, half_ref, sems) = refs[: 2 * count], refs[2 * count :]
    tile = out_ref.shape[2]
    width = right_ref.shape[2]
    per = width // tile
    core = lax.rem(me_ref[0], CORES)
    j = pl.program_id(0)

    def occ_copies():
        for far in range(2):
            half = lax.rem(core + far, CORES)
            for k in range(early, count):
                at = far * count + k
                target = occ_ref.at[pl.ds((k - early) * CAP, CAP), pl.ds(pl.multiple_of(half * 128, 128), 128)]
                yield pltpu.make_async_copy(pieces[at].at[:, pl.ds(width, 128)], target, sems.at[2 * count + at])

    def copies(far):
        for k in range(count):
            at = far * count + k
            target = right_ref.at[far, pl.ds(k * CAP, CAP), :]
            yield pltpu.make_async_copy(pieces[at].at[:, pl.ds(0, width)], target, sems.at[at])

    @pl.when(j == 0)
    def _():
        for copy in (*occ_copies(), *copies(0), *copies(1)):
            copy.start()
        for copy in occ_copies():
            copy.wait()
        occ = occ_ref[...].T
        for p in range(2):
            rows = slice(p * NOCC, (p + 1) * NOCC)
            late = jnp.dot(occ, late_ref[p], preferred_element_type=F32)
            half_ref[rows, :] = (part_ref[rows, :] + late).astype(BF16)

    for far in range(2):

        @pl.when(j == far * per)
        def _():
            for copy in copies(far):
                copy.wait()

    right = right_ref[lax.div(j, per), :, pl.ds(pl.multiple_of(lax.rem(j, per) * tile, 128), tile)]
    total = jnp.dot(half_ref[...], right, preferred_element_type=F32).astype(BF16)
    out_ref[...] = total.reshape(out_ref.shape)


VMEM = pl.BlockSpec(memory_space=pltpu.VMEM)
SMEM = pl.BlockSpec(memory_space=pltpu.SMEM)
ANY = pl.BlockSpec(memory_space=pl.ANY)


def shape(*dims, dtype=BF16):
    return jax.ShapeDtypeStruct(dims, dtype)


def params(mib):
    return pltpu.CompilerParams(vmem_limit_bytes=mib << 20)


def cost(flops, nbytes):
    return pl.CostEstimate(flops=int(flops), bytes_accessed=int(nbytes), transcendentals=0)


def short_way(panels, block_pairs, block_count, shell_size, occ_coef, vir_coef):
    n = lax.axis_size("shell")
    here, nvir = vir_coef.shape
    width = nvir // CORES
    packed = width + NOCC // CORES
    room = Z * Y * CAP
    me = lax.axis_index("shell")
    size_row = shell_size.reshape(1, -1)

    def swap(array, bit):
        return lax.ppermute(array, "shell", [(i, i ^ bit) for i in range(n)])

    keep, to_core, to_y, to_both = pl.pallas_call(
        pack_kernel,
        out_shape=[shape(here // 2, packed)] * 4,
        in_specs=[VMEM] * 2,
        out_specs=[VMEM] * 4,
        compiler_params=params(12),
        cost_estimate=cost(3e8, 3e6),
        name="pack_rows",
    )(vir_coef, occ_coef)
    to_y, to_both, to_core = swap(to_y, 2), swap(to_both, 3), swap(to_core, 1)
    code = pl.pallas_call(
        functools.partial(ids_kernel, size_row.shape[1]),
        out_shape=shape(n, BLK_DEV, 128, dtype=jnp.int32),
        in_specs=[VMEM] * 2,
        out_specs=VMEM,
        compiler_params=params(12),
        cost_estimate=cost(1e4, 1e4),
        name="pack_ids",
    )(block_pairs.T, block_count.reshape(1, 1))
    code = lax.all_to_all(code, "shell", split_axis=0, concat_axis=0, tiled=True)

    mine, over = pl.pallas_call(
        functools.partial(pick_kernel, here),
        out_shape=(shape(CAP, packed), shape(1, dtype=jnp.int32)),
        in_specs=[VMEM] * 6,
        out_specs=(VMEM, SMEM),
        compiler_params=params(12),
        cost_estimate=cost(3e8, 2e6),
        name="pick_rows",
    )(code, size_row, keep, to_core, to_y, to_both)

    beside, across, mine_y = swap(mine, 4), swap(mine, 8), swap(mine, 2)
    panels, _ = lax.optimization_barrier((panels, mine))
    send = pl.pallas_call(
        turn_kernel,
        out_shape=shape(n, 2 * BLK_DEV, EDGE * EDGE),
        in_specs=[VMEM],
        out_specs=VMEM,
        compiler_params=params(12),
        cost_estimate=cost(1e6, 3e5),
        name="turn_panels",
    )(panels)
    got = lax.all_to_all(send, "shell", split_axis=0, concat_axis=0, tiled=True)
    beside, across, mine_y, got = lax.optimization_barrier((beside, across, mine_y, got))

    corner, beside_y, across_y = swap(across, 4), swap(beside, 2), swap(across, 2)
    near = [mine, mine_y, beside, across]
    far = [swap(piece, 1) for piece in near]
    early = len(near)
    half, late = pl.pallas_call(
        functools.partial(half_kernel, here),
        out_shape=(shape(2 * NOCC, room, dtype=F32), shape(2, room - early * CAP, room)),
        grid=(1,),
        in_specs=[VMEM] * 3 + [ANY] * (2 * early),
        out_specs=(
            pl.BlockSpec((2 * NOCC, room), lambda i: (0, 0)),
            pl.BlockSpec((2, room - early * CAP, room), lambda i: (0, 0, 0)),
        ),
        scratch_shapes=[pltpu.VMEM((early * CAP, NOCC), BF16), pltpu.SemaphoreType.DMA((2 * early,))],
        compiler_params=params(28),
        cost_estimate=cost(7e9, 1),
        name="half_transform",
    )(code, got, size_row, *near, *far)
    corner, beside_y, across_y, half, late = lax.optimization_barrier((corner, beside_y, across_y, half, late))

    corner_y = swap(corner, 2)
    near += [beside_y, across_y, corner]
    far += [swap(piece, 1) for piece in near[early:]]
    corner_y, *far = lax.optimization_barrier((corner_y, *far))
    near.append(corner_y)
    far.append(swap(corner_y, 1))

    count = len(near)
    tile = width // 3
    out = pl.pallas_call(
        functools.partial(last_kernel, count, early),
        out_shape=shape(2, NOCC, nvir),
        grid_spec=pltpu.PrefetchScalarGridSpec(
            num_scalar_prefetch=1,
            grid=(nvir // tile,),
            in_specs=[
                pl.BlockSpec((2 * NOCC, room), lambda j, o: (0, 0)),
                pl.BlockSpec((2, room - early * CAP, room), lambda j, o: (0, 0, 0)),
            ]
            + [ANY] * (2 * count),
            out_specs=pl.BlockSpec((2, NOCC, tile), lambda j, o: (0, 0, (j + 3 * (o[0] % 2)) % 6)),
            scratch_shapes=[
                pltpu.VMEM((CORES, room, width), BF16),
                pltpu.VMEM((room - early * CAP, NOCC), BF16),
                pltpu.VMEM((2 * NOCC, room), BF16),
                pltpu.SemaphoreType.DMA((4 * count,)),
            ],
        ),
        compiler_params=params(28),
        cost_estimate=cost(2e10, 1),
        name="last_product",
    )(me.reshape(1), half, late, *near, *far)
    return out, over[0], code, got


def per_device(*args):
    n = lax.axis_size("shell")
    here, nvir = args[5].shape
    shells = args[3].shape[0]
    sparse = LIVE_DEV * n * EDGE < n * here
    if not (sparse and n == Z * Y * CORES and here <= 256 and here % 16 == 0 and nvir % 768 == 0):
        return from_start(*args)
    out, over, code, got = short_way(*args)

    def again(carry):
        over, _ = carry
        over, code_now, turned, *held = lax.optimization_barrier((over, code, got, *args[3:]))
        turned = turned.reshape(n, 2, BLK_DEV, EDGE * EDGE).swapaxes(1, 2).reshape(n * BLK_DEV, 2, EDGE * EDGE)
        code_now = jnp.max(code_now, axis=2).reshape(n * BLK_DEV)
        ids = jnp.maximum(code_now, 0)
        pairs = jnp.stack([ids // shells, ids % shells], axis=1)
        return over - 1, long_way(turned, pairs, code_now >= 0, *held)

    return lax.while_loop(lambda carry: carry[0] > 0, again, (over, out))[1]


def solution(mesh):
    placed = (
        P(("groups", "shell"), None, None),
        P(("groups", "shell"), None),
        P(("groups", "shell")),
        P("groups"),
        P(("groups", "shell"), None),
        P(("groups", "shell"), None),
    )
    return jax.shard_map(
        per_device,
        mesh=mesh,
        in_specs=placed,
        out_specs=P(("groups", "shell"), None, None),
        check_vma=False,
    )
```

```python
import functools
import math

import jax
import jax.numpy as jnp
from jax import lax
from jax.experimental import pallas as pl
from jax.experimental.pallas import tpu as pltpu
from jax.sharding import PartitionSpec as P

EDGE = 16
NOCC = 256
BLK_DEV = 8
LIVE_DEV = 4
CAP = 128
Z, Y, CORES = 4, 2, 2
F32 = jnp.float32
BF16 = jnp.bfloat16


def padded_rows(matrix, starts, shell_size):
    offsets = jnp.arange(EDGE, dtype=jnp.int32)
    rows = jnp.minimum(starts[:, None] + offsets[None, :], matrix.shape[0] - 1)
    inside = offsets[None, :] < shell_size[:, None]
    return jnp.where(inside[:, :, None], matrix[rows], jnp.zeros((), matrix.dtype))


def half_transform(slot_rows, pairs, keep, occ_blocks):
    count = slot_rows.shape[0]
    vecs_here = slot_rows.shape[1]
    shells = occ_blocks.shape[0]
    group_size = math.gcd(512, count)
    turns = count // group_size
    shaped = slot_rows.reshape(count, vecs_here, EDGE, EDGE)

    def advance(total, turn):
        first = turn * group_size
        block = lax.dynamic_slice_in_dim(shaped, first, group_size, 0)
        okay = lax.dynamic_slice_in_dim(keep, first, group_size, 0)
        block = jnp.where(okay[:, None, None, None], block, jnp.zeros((), block.dtype))
        row_shell = lax.dynamic_slice_in_dim(pairs[:, 0], first, group_size, 0)
        col_shell = lax.dynamic_slice_in_dim(pairs[:, 1], first, group_size, 0)
        coefs = occ_blocks[row_shell]
        piece = jnp.einsum("kmi,kvmn->kvin", coefs, block, preferred_element_type=jnp.float32)
        return (total.at[col_shell].add(piece), None)

    start_total = jnp.zeros((shells, vecs_here, NOCC, EDGE), jnp.float32)
    half, _ = lax.scan(advance, start_total, jnp.arange(turns, dtype=jnp.int32))
    return half


def long_way(turned, pairs, live, shell_size, occ_coef, vir_coef):
    occ_full = lax.all_gather(occ_coef, "shell", axis=0, tiled=True)
    starts = jnp.cumsum(shell_size) - shell_size
    occ_blocks = padded_rows(occ_full, starts, shell_size)
    half = half_transform(turned, pairs, live, occ_blocks)
    hidden = half.astype(jnp.bfloat16)
    vir_full = lax.all_gather(vir_coef, "shell", axis=0, tiled=True)
    vir_blocks = padded_rows(vir_full, starts, shell_size)
    result = jnp.einsum("svin,sna->via", hidden, vir_blocks, preferred_element_type=jnp.float32)
    return result.astype(jnp.bfloat16)


def from_start(panels, block_pairs, block_count, *rest):
    pairs = lax.all_gather(block_pairs, "shell", axis=0, tiled=True)
    counts = lax.all_gather(block_count, "shell", axis=0, tiled=True)
    turned = lax.all_to_all(panels, "shell", split_axis=1, concat_axis=0, tiled=True)
    position = jnp.arange(turned.shape[0], dtype=jnp.int32)
    live = position % BLK_DEV < counts[position // BLK_DEV]
    return long_way(turned, pairs, live, *rest)


def iota(shape, dim):
    return lax.broadcasted_iota(jnp.int32, shape, dim)


def column_of(row, mask):
    return jnp.sum(jnp.where(mask, row, 0.0), axis=1, keepdims=True)


def row_of(column, mask):
    return jnp.sum(jnp.where(mask, column, 0.0), axis=0, keepdims=True)


def zero_one(mask):
    return jnp.where(mask, 1.0, 0.0)


def lane_value(row, index):
    return jnp.sum(jnp.where(iota(row.shape, 1) == index, row, 0.0), axis=1, keepdims=True)


def one_hots(ids, shells):
    lanes = iota(ids.shape, 1).astype(F32)
    return jnp.concatenate([zero_one(ids == lanes + 128.0 * k) for k in range(shells // 128)], axis=1)


def slot_hots(got, shells):
    ids = got[:, 2 * BLK_DEV :, :].reshape(-1, 256)
    return one_hots(ids[:, :128], shells), one_hots(ids[:, 128:], shells)


class Shells:
    def __init__(self, size_row):
        shells = size_row.shape[1]
        sub, lane = iota((shells, shells), 0), iota((shells, shells), 1)
        self.before, self.same = lane < sub, lane == sub
        self.starts = column_of(size_row, self.before)
        self.size = column_of(size_row, self.same)
        self.odd = self.starts - 2.0 * jnp.floor(self.starts * 0.5)


class Used:
    def __init__(self, shells, hot, window):
        self.used = column_of(jnp.max(hot, axis=0, keepdims=True), shells.same)
        self.extra, self.ahead, self.edges = [], [], []
        edge = (iota((hot.shape[1], 128), 1) * window).astype(F32)
        reach = jnp.clip(edge - shells.starts, 0.0, shells.size)
        for parity in range(2):
            extra = 1.0 - shells.odd if parity == 0 else shells.odd
            count = self.used * jnp.floor((shells.size + extra) * 0.5)
            count_row = row_of(count, shells.same)
            self.extra.append(extra)
            self.ahead.append(column_of(count_row, shells.before))
            self.edges.append(jnp.sum(self.used * jnp.floor((reach + extra) * 0.5), axis=0, keepdims=True))


def pack_kernel(vir_ref, occ_ref, out_ref):
    here, nvir = vir_ref.shape
    width, thin = nvir // CORES, occ_ref.shape[1] // CORES
    for y in range(Y):
        pick = zero_one(iota((here // 2, here), 1) == 2 * iota((here // 2, here), 0) + y).astype(BF16)
        for core in range(CORES):
            part = vir_ref[:, core * width : (core + 1) * width]
            out_ref[2 * y + core, :, :width] = jnp.dot(pick, part, preferred_element_type=F32).astype(BF16)
            part = occ_ref[:, core * thin : (core + 1) * thin]
            out_ref[2 * y + core, :, width:] = jnp.dot(pick, part, preferred_element_type=F32).astype(BF16)


def send_kernel(pairs_ref, count_ref, panels_ref, send_ref):
    n = send_ref.shape[0]
    turned = jnp.swapaxes(panels_ref[...].astype(F32), 0, 1)
    send_ref[:, : 2 * BLK_DEV, :] = turned.reshape(n, 2 * BLK_DEV, EDGE * EDGE).astype(BF16)
    kept = iota((1, BLK_DEV), 1) < count_ref[...]
    square = (BLK_DEV, BLK_DEV)
    same = iota(square, 0) == iota(square, 1)
    wide = (BLK_DEV, 128)
    columns, rows = (
        jnp.broadcast_to(column_of(jnp.where(kept, pairs_ref[k : k + 1, :], -1).astype(F32), same), wide)
        for k in (1, 0)
    )
    ids = jnp.concatenate([columns, rows], axis=1)
    send_ref[:, 2 * BLK_DEV :, :] = jnp.broadcast_to(ids[None], (n, BLK_DEV, 256)).astype(BF16)


def pick_kernel(here, got_ref, size_ref, blocks_ref, out_ref, over_ref, me_ref):
    me = lax.axis_index("shell")
    me_ref[0] = me
    y, z = lax.rem(lax.div(me, 2), 2), lax.div(me, 4)
    window = CORES * Y * here
    shell_count = size_ref.shape[1]
    shells = Shells(size_ref[...].astype(F32))
    lists = [Used(shells, hot, window) for hot in slot_hots(got_ref[...].astype(F32), shell_count)]
    most = jnp.zeros((1, 1), F32)
    lane = iota((1, 128), 1)
    for chosen in lists:
        for edges in chosen.edges:
            later = jnp.concatenate([edges[:, 1:], edges[:, :1]], axis=1)
            most = jnp.maximum(most, jnp.max(jnp.where(lane < Z, later - edges, 0.0), axis=1, keepdims=True))
    over_ref[0] = jnp.where(jnp.max(most) > CAP, 1, 0).astype(jnp.int32)

    width = out_ref.shape[1] - 128
    even = y == 0
    totals = [jnp.zeros((CAP, width), F32), jnp.zeros((CAP, 128), F32)]
    columns = [slice(0, width), slice(width, width + 128)]
    extra = jnp.where(even, lists[0].extra[0], lists[0].extra[1])
    for k in range(Y * CORES):
        device = 4 * z + k
        row = (2 * iota((shell_count, 128), 1) + device * here + y).astype(F32)
        where = row - shells.starts
        inside = (where >= 0.0) & (where < shells.size)
        within = jnp.floor((where + extra) * 0.5)
        for chosen, total, column in zip(lists, range(2), columns):
            ahead = jnp.where(even, chosen.ahead[0], chosen.ahead[1])
            base = lane_value(jnp.where(even, chosen.edges[0], chosen.edges[1]), z)
            place = jnp.where(inside & (chosen.used > 0.0), ahead + within + 1.0, 0.0)
            place = jnp.sum(place, axis=0, keepdims=True)
            place = jnp.where(place > 0.0, place - 1.0 - base, -1.0)
            hot = zero_one(place == iota((CAP, 128), 0).astype(F32)).astype(BF16)
            totals[total] += jnp.dot(
                hot[:, : here // 2], blocks_ref[k, :, column], preferred_element_type=F32
            )
    for total, column in zip(totals, columns):
        out_ref[:, column] = total.astype(BF16)


def slot_of(window, chip):
    rel = window ^ chip
    return jnp.where((rel == 3) | (rel == 4), rel ^ 7, rel)


def half_kernel(here, got_ref, size_ref, *refs):
    count = (len(refs) - 4) // 2
    pieces, (half_ref, late_ref, occ_ref, sems) = refs[: 2 * count], refs[2 * count :]
    me = lax.axis_index("shell")
    core, chip = lax.rem(me, CORES), lax.div(me, CORES)
    width = pieces[0].shape[1] - 128
    copies = []
    for far in range(2):
        half = lax.rem(core + far, CORES)
        for k in range(count):
            at = far * count + k
            target = occ_ref.at[pl.ds(k * CAP, CAP), pl.ds(pl.multiple_of(half * 128, 128), 128)]
            copies.append(pltpu.make_async_copy(pieces[at].at[:, pl.ds(width, 128)], target, sems.at[at]))
    for copy in copies:
        copy.start()
    window = CORES * Y * here
    shell_count = size_ref.shape[1]
    got = got_ref[...].astype(F32)
    size_row = size_ref[...].astype(F32)
    shells = Shells(size_row)
    got = got_ref[...].astype(F32)
    hots = slot_hots(got, shell_count)
    lists = [Used(shells, hot, window) for hot in hots]
    slots = hots[0].shape[0]
    kept = LIVE_DEV * (slots // BLK_DEV)
    alive = jnp.broadcast_to(jnp.sum(hots[0], axis=1, keepdims=True), (slots, slots))
    sub, lane = iota((slots, slots), 0), iota((slots, slots), 1)
    rank = row_of(alive, sub < lane)
    alive_row = row_of(alive, sub == lane)
    take = (rank == iota((kept, slots), 0).astype(F32)) & (alive_row > 0.0)
    take = zero_one(take).astype(BF16)

    def taken(array):
        return jnp.dot(take, array.astype(BF16), preferred_element_type=F32)

    def spread(hot, column):
        value = jnp.sum(hot * row_of(column, shells.same), axis=1, keepdims=True)
        wide = jnp.broadcast_to(value, (kept, 128)).reshape(kept, 1, 128)
        return jnp.broadcast_to(wide, (kept, EDGE, 128)).reshape(kept * EDGE, 128)

    at = iota((kept * EDGE, 128), 0) % EDGE
    step = at.astype(F32)

    def places(hot, chosen):
        hot = taken(hot)
        first, length = spread(hot, shells.starts), spread(hot, shells.size)
        row = first + step
        odd = (row - 2.0 * jnp.floor(row * 0.5)) > 0.0
        place = jnp.where(odd, spread(hot, chosen.ahead[1]), spread(hot, chosen.ahead[0]))
        place += jnp.floor(step * 0.5)
        offsets = [
            [slot_of(w * Y + k, chip).astype(F32) * CAP - lane_value(e, w) for w in range(Z)]
            for k, e in enumerate(chosen.edges)
        ]
        offset = jnp.where(odd, offsets[1][0], offsets[0][0])
        for w in range(1, Z):
            offset = jnp.where(row >= float(window * w), jnp.where(odd, offsets[1][w], offsets[0][w]), offset)
        return jnp.where(step < length, place + offset, -1.0)[:, :1]

    place_c, place_r = places(hots[0], lists[0]), places(hots[1], lists[1])
    span = 16 * EDGE
    width = half_ref.shape[1]
    s_in, l_in = iota((span, span), 0), iota((span, span), 1)
    keep_m = (l_in // EDGE) == (s_in % EDGE)
    fold = zero_one((s_in % EDGE) == (l_in % EDGE)).astype(BF16)
    same_slot = (s_in // EDGE) == (l_in // EDGE)
    blocks = [taken(got[:, p * BLK_DEV : (p + 1) * BLK_DEV, :].reshape(slots, span)) for p in range(2)]
    lanes = iota((span, width), 1).astype(F32)
    for copy in copies:
        copy.wait()
    occ = occ_ref[...]
    late = []
    for g in range(kept // 16):
        rows = slice(g * span, (g + 1) * span)
        r_hot = zero_one(place_r[rows] == lanes).astype(BF16)
        c_hot = zero_one(place_c[rows] == lanes).astype(BF16)
        part = jnp.dot(r_hot[:, : count * CAP], occ, preferred_element_type=F32).T.astype(BF16)
        for p in range(2):
            block = blocks[p][g * 16 : (g + 1) * 16].reshape(16, 1, span)
            block = jnp.broadcast_to(block, (16, EDGE, span)).reshape(span, span)
            block = jnp.where(keep_m, block, 0.0).astype(BF16)
            diag = jnp.dot(block, fold, preferred_element_type=F32)
            diag = jnp.where(same_slot, diag, 0.0).astype(BF16)
            placed = jnp.dot(diag, c_hot, preferred_element_type=F32).astype(BF16)
            piece = jnp.dot(part, placed, preferred_element_type=F32)
            rows_p = slice(p * NOCC, (p + 1) * NOCC)
            later = jnp.dot(r_hot[:, count * CAP :].T, placed, preferred_element_type=F32)
            if g == 0:
                half_ref[rows_p, :] = piece
                late.append(later)
            else:
                half_ref[rows_p, :] += piece
                late[p] += later
    for p in range(2):
        late_ref[p] = late[p].astype(BF16)


def last_kernel(count, early, me_ref, part_ref, late_ref, *refs):
    pieces, (out_ref, right_ref, occ_ref, half_ref, sems) = refs[: 2 * count], refs[2 * count :]
    tile = out_ref.shape[2]
    width = right_ref.shape[2]
    per = width // tile
    core = lax.rem(me_ref[0], CORES)
    j = pl.program_id(0)

    def occ_copies():
        for far in range(2):
            half = lax.rem(core + far, CORES)
            for k in range(early, count):
                at = far * count + k
                target = occ_ref.at[pl.ds((k - early) * CAP, CAP), pl.ds(pl.multiple_of(half * 128, 128), 128)]
                yield pltpu.make_async_copy(pieces[at].at[:, pl.ds(width, 128)], target, sems.at[2 * count + at])

    def copies(far):
        for k in range(count):
            at = far * count + k
            target = right_ref.at[far, pl.ds(k * CAP, CAP), :]
            yield pltpu.make_async_copy(pieces[at].at[:, pl.ds(0, width)], target, sems.at[at])

    @pl.when(j == 0)
    def _():
        for copy in (*occ_copies(), *copies(0), *copies(1)):
            copy.start()
        for copy in occ_copies():
            copy.wait()
        occ = occ_ref[...].T
        for p in range(2):
            rows = slice(p * NOCC, (p + 1) * NOCC)
            late = jnp.dot(occ, late_ref[p], preferred_element_type=F32)
            half_ref[rows, :] = (part_ref[rows, :] + late).astype(BF16)

    for far in range(2):

        @pl.when(j == far * per)
        def _():
            for copy in copies(far):
                copy.wait()

    right = right_ref[lax.div(j, per), :, pl.ds(pl.multiple_of(lax.rem(j, per) * tile, 128), tile)]
    total = jnp.dot(half_ref[...], right, preferred_element_type=F32).astype(BF16)
    out_ref[...] = total.reshape(out_ref.shape)


VMEM = pl.BlockSpec(memory_space=pltpu.VMEM)
SMEM = pl.BlockSpec(memory_space=pltpu.SMEM)
ANY = pl.BlockSpec(memory_space=pl.ANY)


def shape(*dims, dtype=BF16):
    return jax.ShapeDtypeStruct(dims, dtype)


def params(mib):
    return pltpu.CompilerParams(vmem_limit_bytes=mib << 20)


def cost(flops, nbytes):
    return pl.CostEstimate(flops=int(flops), bytes_accessed=int(nbytes), transcendentals=0)


def short_way(panels, block_pairs, block_count, shell_size, occ_coef, vir_coef):
    n = lax.axis_size("shell")
    here, nvir = vir_coef.shape
    width = nvir // CORES
    packed = width + NOCC // CORES
    room = Z * Y * CAP
    size_row = shell_size.reshape(1, -1)

    def swap(array, bit):
        return lax.ppermute(array, "shell", [(i, i ^ bit) for i in range(n)])

    blocks = pl.pallas_call(
        pack_kernel,
        out_shape=shape(Y * CORES, here // 2, packed),
        in_specs=[VMEM] * 2,
        out_specs=VMEM,
        compiler_params=params(12),
        cost_estimate=cost(3e8, 3e6),
        name="pack_rows",
    )(vir_coef, occ_coef)
    blocks, panels = lax.optimization_barrier((blocks, panels))
    planes = [[Y * CORES * z + k for k in range(Y * CORES)] for z in range(Z)]
    blocks = lax.all_to_all(blocks, "shell", split_axis=0, concat_axis=0, axis_index_groups=planes, tiled=True)
    send = pl.pallas_call(
        send_kernel,
        out_shape=shape(n, 3 * BLK_DEV, EDGE * EDGE),
        in_specs=[VMEM] * 3,
        out_specs=VMEM,
        compiler_params=params(12),
        cost_estimate=cost(1e6, 5e5),
        name="pack_panels",
    )(block_pairs.T, block_count.reshape(1, 1), panels)
    got = lax.all_to_all(send, "shell", split_axis=0, concat_axis=0, tiled=True)

    mine, over, me = pl.pallas_call(
        functools.partial(pick_kernel, here),
        out_shape=(shape(CAP, packed), shape(1, dtype=jnp.int32), shape(1, dtype=jnp.int32)),
        in_specs=[VMEM] * 3,
        out_specs=(VMEM, SMEM, SMEM),
        compiler_params=params(12),
        cost_estimate=cost(3e8, 2e6),
        name="pick_rows",
    )(got, size_row, blocks)

    beside, across, mine_y = swap(mine, 4), swap(mine, 8), swap(mine, 2)
    beside, across, mine_y = lax.optimization_barrier((beside, across, mine_y))

    corner, beside_y, across_y = swap(across, 4), swap(beside, 2), swap(across, 2)
    near = [mine, mine_y, beside, across]
    far = [swap(piece, 1) for piece in near]
    early = len(near)
    half, late = pl.pallas_call(
        functools.partial(half_kernel, here),
        out_shape=(shape(2 * NOCC, room, dtype=F32), shape(2, room - early * CAP, room)),
        grid=(1,),
        in_specs=[VMEM] * 2 + [ANY] * (2 * early),
        out_specs=(
            pl.BlockSpec((2 * NOCC, room), lambda i: (0, 0)),
            pl.BlockSpec((2, room - early * CAP, room), lambda i: (0, 0, 0)),
        ),
        scratch_shapes=[pltpu.VMEM((early * CAP, NOCC), BF16), pltpu.SemaphoreType.DMA((2 * early,))],
        compiler_params=params(28),
        cost_estimate=cost(7e9, 1),
        name="half_transform",
    )(got, size_row, *near, *far)
    corner, half, late = lax.optimization_barrier((corner, half, late))

    corner_y = swap(corner, 2)
    near += [beside_y, across_y, corner]
    far += [swap(piece, 1) for piece in near[early:]]
    corner_y, *far = lax.optimization_barrier((corner_y, *far))
    near.append(corner_y)
    far.append(swap(corner_y, 1))

    count = len(near)
    tile = width // 3
    out = pl.pallas_call(
        functools.partial(last_kernel, count, early),
        out_shape=shape(2, NOCC, nvir),
        grid_spec=pltpu.PrefetchScalarGridSpec(
            num_scalar_prefetch=1,
            grid=(nvir // tile,),
            in_specs=[
                pl.BlockSpec((2 * NOCC, room), lambda j, o: (0, 0)),
                pl.BlockSpec((2, room - early * CAP, room), lambda j, o: (0, 0, 0)),
            ]
            + [ANY] * (2 * count),
            out_specs=pl.BlockSpec((2, NOCC, tile), lambda j, o: (0, 0, (j + 3 * (o[0] % 2)) % 6)),
            scratch_shapes=[
                pltpu.VMEM((CORES, room, width), BF16),
                pltpu.VMEM((room - early * CAP, NOCC), BF16),
                pltpu.VMEM((2 * NOCC, room), BF16),
                pltpu.SemaphoreType.DMA((4 * count,)),
            ],
        ),
        compiler_params=params(28),
        cost_estimate=cost(2e10, 1),
        name="last_product",
    )(me, half, late, *near, *far)
    return out, over[0], got


def per_device(*args):
    n = lax.axis_size("shell")
    here, nvir = args[5].shape
    sparse = LIVE_DEV * n * EDGE < n * here
    if not (sparse and n == Z * Y * CORES and here <= 256 and here % 16 == 0 and nvir % 768 == 0):
        return from_start(*args)
    out, over, got = short_way(*args)

    def again(carry):
        over, _ = carry
        over, got_now, *held = lax.optimization_barrier((over, got, *args[3:]))
        turned = got_now[:, : 2 * BLK_DEV].reshape(n, 2, BLK_DEV, EDGE * EDGE).swapaxes(1, 2)
        turned = turned.reshape(n * BLK_DEV, 2, EDGE * EDGE)
        ids = got_now[:, 2 * BLK_DEV :].reshape(n * BLK_DEV, 256).astype(jnp.int32)
        columns, rows = jnp.max(ids[:, :128], axis=1), jnp.max(ids[:, 128:], axis=1)
        pairs = jnp.maximum(jnp.stack([rows, columns], axis=1), 0)
        return over - 1, long_way(turned, pairs, columns >= 0, *held)

    return lax.while_loop(lambda carry: carry[0] > 0, again, (over, out))[1]


def solution(mesh):
    placed = (
        P(("groups", "shell"), None, None),
        P(("groups", "shell"), None),
        P(("groups", "shell")),
        P("groups"),
        P(("groups", "shell"), None),
        P(("groups", "shell"), None),
    )
    return jax.shard_map(
        per_device,
        mesh=mesh,
        in_specs=placed,
        out_specs=P(("groups", "shell"), None, None),
        check_vma=False,
    )
```

```python
import functools
import math

import jax
import jax.numpy as jnp
from jax import lax
from jax.experimental import pallas as pl
from jax.experimental.pallas import tpu as pltpu
from jax.sharding import PartitionSpec as P

EDGE = 16
NOCC = 256
BLK_DEV = 8
LIVE_DEV = 4
CAP = 128
Z, Y, CORES = 4, 2, 2
F32 = jnp.float32
BF16 = jnp.bfloat16


def padded_rows(matrix, starts, shell_size):
    offsets = jnp.arange(EDGE, dtype=jnp.int32)
    rows = jnp.minimum(starts[:, None] + offsets[None, :], matrix.shape[0] - 1)
    inside = offsets[None, :] < shell_size[:, None]
    return jnp.where(inside[:, :, None], matrix[rows], jnp.zeros((), matrix.dtype))


def half_transform(slot_rows, pairs, keep, occ_blocks):
    count = slot_rows.shape[0]
    vecs_here = slot_rows.shape[1]
    shells = occ_blocks.shape[0]
    group_size = math.gcd(512, count)
    turns = count // group_size
    shaped = slot_rows.reshape(count, vecs_here, EDGE, EDGE)

    def advance(total, turn):
        first = turn * group_size
        block = lax.dynamic_slice_in_dim(shaped, first, group_size, 0)
        okay = lax.dynamic_slice_in_dim(keep, first, group_size, 0)
        block = jnp.where(okay[:, None, None, None], block, jnp.zeros((), block.dtype))
        row_shell = lax.dynamic_slice_in_dim(pairs[:, 0], first, group_size, 0)
        col_shell = lax.dynamic_slice_in_dim(pairs[:, 1], first, group_size, 0)
        coefs = occ_blocks[row_shell]
        piece = jnp.einsum("kmi,kvmn->kvin", coefs, block, preferred_element_type=jnp.float32)
        return (total.at[col_shell].add(piece), None)

    start_total = jnp.zeros((shells, vecs_here, NOCC, EDGE), jnp.float32)
    half, _ = lax.scan(advance, start_total, jnp.arange(turns, dtype=jnp.int32))
    return half


def long_way(turned, pairs, live, shell_size, occ_coef, vir_coef):
    occ_full = lax.all_gather(occ_coef, "shell", axis=0, tiled=True)
    starts = jnp.cumsum(shell_size) - shell_size
    occ_blocks = padded_rows(occ_full, starts, shell_size)
    half = half_transform(turned, pairs, live, occ_blocks)
    hidden = half.astype(jnp.bfloat16)
    vir_full = lax.all_gather(vir_coef, "shell", axis=0, tiled=True)
    vir_blocks = padded_rows(vir_full, starts, shell_size)
    result = jnp.einsum("svin,sna->via", hidden, vir_blocks, preferred_element_type=jnp.float32)
    return result.astype(jnp.bfloat16)


def from_start(panels, block_pairs, block_count, *rest):
    pairs = lax.all_gather(block_pairs, "shell", axis=0, tiled=True)
    counts = lax.all_gather(block_count, "shell", axis=0, tiled=True)
    turned = lax.all_to_all(panels, "shell", split_axis=1, concat_axis=0, tiled=True)
    position = jnp.arange(turned.shape[0], dtype=jnp.int32)
    live = position % BLK_DEV < counts[position // BLK_DEV]
    return long_way(turned, pairs, live, *rest)


def iota(shape, dim):
    return lax.broadcasted_iota(jnp.int32, shape, dim)


def column_of(row, mask):
    return jnp.sum(jnp.where(mask, row, 0.0), axis=1, keepdims=True)


def row_of(column, mask):
    return jnp.sum(jnp.where(mask, column, 0.0), axis=0, keepdims=True)


def zero_one(mask):
    return jnp.where(mask, 1.0, 0.0)


def lane_value(row, index):
    return jnp.sum(jnp.where(iota(row.shape, 1) == index, row, 0.0), axis=1, keepdims=True)


def one_hots(ids, shells):
    lanes = iota(ids.shape, 1).astype(F32)
    return jnp.concatenate([zero_one(ids == lanes + 128.0 * k) for k in range(shells // 128)], axis=1)


def slot_hots(code, shells):
    code = code.reshape(-1, 128)
    kept = code >= 0
    columns = jnp.where(kept, code % shells, -1).astype(F32)
    return one_hots(columns, shells), one_hots(jnp.where(kept, code // shells, -1).astype(F32), shells)


class Shells:
    def __init__(self, size_row):
        shells = size_row.shape[1]
        sub, lane = iota((shells, shells), 0), iota((shells, shells), 1)
        self.before, self.same = lane < sub, lane == sub
        self.starts = column_of(size_row, self.before)
        self.size = column_of(size_row, self.same)
        self.odd = self.starts - 2.0 * jnp.floor(self.starts * 0.5)


class Used:
    def __init__(self, shells, hot, window):
        self.used = column_of(jnp.max(hot, axis=0, keepdims=True), shells.same)
        self.extra, self.ahead, self.edges = [], [], []
        edge = (iota((hot.shape[1], 128), 1) * window).astype(F32)
        reach = jnp.clip(edge - shells.starts, 0.0, shells.size)
        for parity in range(2):
            extra = 1.0 - shells.odd if parity == 0 else shells.odd
            count = self.used * jnp.floor((shells.size + extra) * 0.5)
            count_row = row_of(count, shells.same)
            self.extra.append(extra)
            self.ahead.append(column_of(count_row, shells.before))
            self.edges.append(jnp.sum(self.used * jnp.floor((reach + extra) * 0.5), axis=0, keepdims=True))


def pack_kernel(vir_ref, occ_ref, *outs):
    me = lax.axis_index("shell")
    core, y = lax.rem(me, 2), lax.rem(lax.div(me, 2), 2)
    here, nvir = vir_ref.shape
    width, thin = nvir // CORES, occ_ref.shape[1] // CORES
    for dy in range(2):
        parity = lax.rem(y + dy, 2)
        pick = zero_one(iota((here // 2, here), 1) == 2 * iota((here // 2, here), 0) + parity).astype(BF16)
        for dc in range(2):
            half = lax.rem(core + dc, 2)
            out = outs[2 * dy + dc]
            part = vir_ref[:, pl.ds(pl.multiple_of(half * width, 128), width)]
            out[:, :width] = jnp.dot(pick, part, preferred_element_type=F32).astype(BF16)
            part = occ_ref[:, pl.ds(pl.multiple_of(half * thin, 128), thin)]
            out[:, width:] = jnp.dot(pick, part, preferred_element_type=F32).astype(BF16)


def ids_kernel(shells, pairs_ref, count_ref, code_ref):
    code = pairs_ref[1:2, :] + shells * pairs_ref[0:1, :]
    code = jnp.where(iota((1, BLK_DEV), 1) < count_ref[...], code, -1).astype(F32)
    square = (BLK_DEV, BLK_DEV)
    code = column_of(code, iota(square, 0) == iota(square, 1)).astype(jnp.int32)
    code_ref[...] = jnp.broadcast_to(jnp.broadcast_to(code, (BLK_DEV, 128))[None], code_ref.shape)


def turn_kernel(panels_ref, send_ref):
    turned = jnp.swapaxes(panels_ref[...].astype(F32), 0, 1)
    send_ref[...] = turned.reshape(send_ref.shape).astype(BF16)


def pick_kernel(here, code_ref, size_ref, *refs):
    sources, (out_ref, over_ref, me_ref) = refs[:4], refs[4:]
    me = lax.axis_index("shell")
    me_ref[0] = me
    core, y, z = lax.rem(me, 2), lax.rem(lax.div(me, 2), 2), lax.div(me, 4)
    window = CORES * Y * here
    shell_count = size_ref.shape[1]
    shells = Shells(size_ref[...].astype(F32))
    lists = [Used(shells, hot, window) for hot in slot_hots(code_ref[...], shell_count)]
    most = jnp.zeros((1, 1), F32)
    lane = iota((1, 128), 1)
    for chosen in lists:
        for edges in chosen.edges:
            later = jnp.concatenate([edges[:, 1:], edges[:, :1]], axis=1)
            most = jnp.maximum(most, jnp.max(jnp.where(lane < Z, later - edges, 0.0), axis=1, keepdims=True))
    over_ref[0] = jnp.where(jnp.max(most) > CAP, 1, 0).astype(jnp.int32)

    width = out_ref.shape[1] - 128
    even = y == 0
    totals = [jnp.zeros((CAP, width), F32), jnp.zeros((CAP, 128), F32)]
    columns = [slice(0, width), slice(width, width + 128)]
    extra = jnp.where(even, lists[0].extra[0], lists[0].extra[1])
    for k, source in enumerate(sources):
        device = 4 * z + 2 * lax.rem(y + k // 2, 2) + lax.rem(core + k % 2, 2)
        row = (2 * iota((shell_count, 128), 1) + device * here + y).astype(F32)
        where = row - shells.starts
        inside = (where >= 0.0) & (where < shells.size)
        within = jnp.floor((where + extra) * 0.5)
        for chosen, total, column in zip(lists, range(2), columns):
            ahead = jnp.where(even, chosen.ahead[0], chosen.ahead[1])
            base = lane_value(jnp.where(even, chosen.edges[0], chosen.edges[1]), z)
            place = jnp.where(inside & (chosen.used > 0.0), ahead + within + 1.0, 0.0)
            place = jnp.sum(place, axis=0, keepdims=True)
            place = jnp.where(place > 0.0, place - 1.0 - base, -1.0)
            hot = zero_one(place == iota((CAP, 128), 0).astype(F32)).astype(BF16)
            totals[total] += jnp.dot(
                hot[:, : here // 2], source[:, column], preferred_element_type=F32
            )
    for total, column in zip(totals, columns):
        out_ref[:, column] = total.astype(BF16)


def inner_chip(chip):
    z = lax.div(chip, Y)
    return (z == 1) | (z == 2)


def slot_of(window, chip):
    slot = window ^ chip
    return jnp.where(inner_chip(chip) & (slot >= 2 * Y), slot ^ Y, slot)


def choose_kernel(me_ref, inner_ref, outer_ref, out_ref, sem):
    inner = inner_chip(lax.div(me_ref[0], CORES))

    @pl.when(inner)
    def _():
        copy = pltpu.make_async_copy(inner_ref, out_ref, sem)
        copy.start()
        copy.wait()

    @pl.when(jnp.logical_not(inner))
    def _():
        copy = pltpu.make_async_copy(outer_ref, out_ref, sem)
        copy.start()
        copy.wait()


def half_kernel(here, code_ref, got_ref, size_ref, *refs):
    count = (len(refs) - 4) // 2
    pieces, (half_ref, late_ref, occ_ref, sems) = refs[: 2 * count], refs[2 * count :]
    me = lax.axis_index("shell")
    core, chip = lax.rem(me, CORES), lax.div(me, CORES)
    width = pieces[0].shape[1] - 128
    copies = []
    for far in range(2):
        half = lax.rem(core + far, CORES)
        for k in range(count):
            at = far * count + k
            target = occ_ref.at[pl.ds(k * CAP, CAP), pl.ds(pl.multiple_of(half * 128, 128), 128)]
            copies.append(pltpu.make_async_copy(pieces[at].at[:, pl.ds(width, 128)], target, sems.at[at]))
    for copy in copies:
        copy.start()
    window = CORES * Y * here
    shell_count = size_ref.shape[1]
    got = got_ref[...].astype(F32)
    size_row = size_ref[...].astype(F32)
    shells = Shells(size_row)
    got = got_ref[...].astype(F32)
    hots = slot_hots(code_ref[...], shell_count)
    lists = [Used(shells, hot, window) for hot in hots]
    slots = hots[0].shape[0]
    kept = LIVE_DEV * (slots // BLK_DEV)
    alive = jnp.broadcast_to(jnp.sum(hots[0], axis=1, keepdims=True), (slots, slots))
    sub, lane = iota((slots, slots), 0), iota((slots, slots), 1)
    rank = row_of(alive, sub < lane)
    alive_row = row_of(alive, sub == lane)
    take = (rank == iota((kept, slots), 0).astype(F32)) & (alive_row > 0.0)
    take = zero_one(take).astype(BF16)

    def taken(array):
        return jnp.dot(take, array.astype(BF16), preferred_element_type=F32)

    def spread(hot, column):
        value = jnp.sum(hot * row_of(column, shells.same), axis=1, keepdims=True)
        wide = jnp.broadcast_to(value, (kept, 128)).reshape(kept, 1, 128)
        return jnp.broadcast_to(wide, (kept, EDGE, 128)).reshape(kept * EDGE, 128)

    at = iota((kept * EDGE, 128), 0) % EDGE
    step = at.astype(F32)

    def places(hot, chosen):
        hot = taken(hot)
        first, length = spread(hot, shells.starts), spread(hot, shells.size)
        row = first + step
        odd = (row - 2.0 * jnp.floor(row * 0.5)) > 0.0
        place = jnp.where(odd, spread(hot, chosen.ahead[1]), spread(hot, chosen.ahead[0]))
        place += jnp.floor(step * 0.5)
        offsets = [
            [slot_of(w * Y + k, chip).astype(F32) * CAP - lane_value(e, w) for w in range(Z)]
            for k, e in enumerate(chosen.edges)
        ]
        offset = jnp.where(odd, offsets[1][0], offsets[0][0])
        for w in range(1, Z):
            offset = jnp.where(row >= float(window * w), jnp.where(odd, offsets[1][w], offsets[0][w]), offset)
        return jnp.where(step < length, place + offset, -1.0)[:, :1]

    place_c, place_r = places(hots[0], lists[0]), places(hots[1], lists[1])
    span = 16 * EDGE
    width = half_ref.shape[1]
    s_in, l_in = iota((span, span), 0), iota((span, span), 1)
    keep_m = (l_in // EDGE) == (s_in % EDGE)
    fold = zero_one((s_in % EDGE) == (l_in % EDGE)).astype(BF16)
    same_slot = (s_in // EDGE) == (l_in // EDGE)
    blocks = [taken(got[:, p * BLK_DEV : (p + 1) * BLK_DEV, :].reshape(slots, span)) for p in range(2)]
    lanes = iota((span, width), 1).astype(F32)
    for copy in copies:
        copy.wait()
    occ = occ_ref[...]
    late = []
    for g in range(kept // 16):
        rows = slice(g * span, (g + 1) * span)
        r_hot = zero_one(place_r[rows] == lanes).astype(BF16)
        c_hot = zero_one(place_c[rows] == lanes).astype(BF16)
        part = jnp.dot(r_hot[:, : count * CAP], occ, preferred_element_type=F32).T.astype(BF16)
        for p in range(2):
            block = blocks[p][g * 16 : (g + 1) * 16].reshape(16, 1, span)
            block = jnp.broadcast_to(block, (16, EDGE, span)).reshape(span, span)
            block = jnp.where(keep_m, block, 0.0).astype(BF16)
            diag = jnp.dot(block, fold, preferred_element_type=F32)
            diag = jnp.where(same_slot, diag, 0.0).astype(BF16)
            placed = jnp.dot(diag, c_hot, preferred_element_type=F32).astype(BF16)
            piece = jnp.dot(part, placed, preferred_element_type=F32)
            rows_p = slice(p * NOCC, (p + 1) * NOCC)
            later = jnp.dot(r_hot[:, count * CAP :].T, placed, preferred_element_type=F32)
            if g == 0:
                half_ref[rows_p, :] = piece
                late.append(later)
            else:
                half_ref[rows_p, :] += piece
                late[p] += later
    for p in range(2):
        late_ref[p] = late[p].astype(BF16)


def last_kernel(count, early, me_ref, part_ref, late_ref, *refs):
    pieces, (out_ref, right_ref, occ_ref, half_ref, sems) = refs[: 2 * count], refs[2 * count :]
    tile = out_ref.shape[2]
    width = right_ref.shape[2]
    per = width // tile
    core = lax.rem(me_ref[0], CORES)
    j = pl.program_id(0)

    def occ_copies():
        for far in range(2):
            half = lax.rem(core + far, CORES)
            for k in range(early, count):
                at = far * count + k
                target = occ_ref.at[pl.ds((k - early) * CAP, CAP), pl.ds(pl.multiple_of(half * 128, 128), 128)]
                yield pltpu.make_async_copy(pieces[at].at[:, pl.ds(width, 128)], target, sems.at[2 * count + at])

    def copies(far):
        for k in range(count):
            at = far * count + k
            target = right_ref.at[far, pl.ds(k * CAP, CAP), :]
            yield pltpu.make_async_copy(pieces[at].at[:, pl.ds(0, width)], target, sems.at[at])

    @pl.when(j == 0)
    def _():
        for copy in (*occ_copies(), *copies(0), *copies(1)):
            copy.start()
        for copy in occ_copies():
            copy.wait()
        occ = occ_ref[...].T
        for p in range(2):
            rows = slice(p * NOCC, (p + 1) * NOCC)
            late = jnp.dot(occ, late_ref[p], preferred_element_type=F32)
            half_ref[rows, :] = (part_ref[rows, :] + late).astype(BF16)

    for far in range(2):

        @pl.when(j == far * per)
        def _():
            for copy in copies(far):
                copy.wait()

    right = right_ref[lax.div(j, per), :, pl.ds(pl.multiple_of(lax.rem(j, per) * tile, 128), tile)]
    total = jnp.dot(half_ref[...], right, preferred_element_type=F32).astype(BF16)
    out_ref[...] = total.reshape(out_ref.shape)


VMEM = pl.BlockSpec(memory_space=pltpu.VMEM)
SMEM = pl.BlockSpec(memory_space=pltpu.SMEM)
ANY = pl.BlockSpec(memory_space=pl.ANY)


def shape(*dims, dtype=BF16):
    return jax.ShapeDtypeStruct(dims, dtype)


def params(mib):
    return pltpu.CompilerParams(vmem_limit_bytes=mib << 20)


def cost(flops, nbytes):
    return pl.CostEstimate(flops=int(flops), bytes_accessed=int(nbytes), transcendentals=0)


def short_way(panels, block_pairs, block_count, shell_size, occ_coef, vir_coef):
    n = lax.axis_size("shell")
    here, nvir = vir_coef.shape
    width = nvir // CORES
    packed = width + NOCC // CORES
    room = Z * Y * CAP
    size_row = shell_size.reshape(1, -1)

    def swap(array, bit):
        return lax.ppermute(array, "shell", [(i, i ^ bit) for i in range(n)])

    keep, to_core, to_y, to_both = pl.pallas_call(
        pack_kernel,
        out_shape=[shape(here // 2, packed)] * 4,
        in_specs=[VMEM] * 2,
        out_specs=[VMEM] * 4,
        compiler_params=params(12),
        cost_estimate=cost(3e8, 3e6),
        name="pack_rows",
    )(vir_coef, occ_coef)
    to_y, to_both, to_core = swap(to_y, 2), swap(to_both, 3), swap(to_core, 1)
    code = pl.pallas_call(
        functools.partial(ids_kernel, size_row.shape[1]),
        out_shape=shape(n, BLK_DEV, 128, dtype=jnp.int32),
        in_specs=[VMEM] * 2,
        out_specs=VMEM,
        compiler_params=params(12),
        cost_estimate=cost(1e4, 1e4),
        name="pack_ids",
    )(block_pairs.T, block_count.reshape(1, 1))
    code = lax.all_to_all(code, "shell", split_axis=0, concat_axis=0, tiled=True)

    mine, over, me = pl.pallas_call(
        functools.partial(pick_kernel, here),
        out_shape=(shape(CAP, packed), shape(1, dtype=jnp.int32), shape(1, dtype=jnp.int32)),
        in_specs=[VMEM] * 6,
        out_specs=(VMEM, SMEM, SMEM),
        compiler_params=params(12),
        cost_estimate=cost(3e8, 2e6),
        name="pick_rows",
    )(code, size_row, keep, to_core, to_y, to_both)

    ends, middle, outward = [(0, 1), (1, 0), (2, 3), (3, 2)], [(1, 2), (2, 1)], [(1, 0), (2, 3)]

    def hop(array, steps):
        return lax.ppermute(array, "shell", [(4 * a + k, 4 * b + k) for a, b in steps for k in range(4)])

    def choose(inner, outer):
        return pl.pallas_call(
            choose_kernel,
            out_shape=shape(*inner.shape),
            in_specs=[SMEM, ANY, ANY],
            out_specs=ANY,
            scratch_shapes=[pltpu.SemaphoreType.DMA],
            compiler_params=params(4),
            cost_estimate=cost(1, 1),
            name="choose_piece",
        )(me, inner, outer)

    mine_y, beside, across = swap(mine, 2), hop(mine, ends), hop(mine, middle)
    panels, _ = lax.optimization_barrier((panels, mine))
    send = pl.pallas_call(
        turn_kernel,
        out_shape=shape(n, 2 * BLK_DEV, EDGE * EDGE),
        in_specs=[VMEM],
        out_specs=VMEM,
        compiler_params=params(12),
        cost_estimate=cost(1e6, 3e5),
        name="turn_panels",
    )(panels)
    got = lax.all_to_all(send, "shell", split_axis=0, concat_axis=0, tiled=True)
    mine_y, beside, across, got = lax.optimization_barrier((mine_y, beside, across, got))

    beside_y, across_out, corner = swap(beside, 2), hop(across, outward), hop(beside, middle)
    far = [swap(piece, 1) for piece in (mine, mine_y, beside)]
    beside_y, across_out, corner, *far = lax.optimization_barrier((beside_y, across_out, corner, *far))

    across = choose(across, across_out)
    across_y, corner_out = swap(across, 2), hop(corner, outward)
    far += [swap(piece, 1) for piece in (beside_y, across)]
    across_y, corner_out, *far = lax.optimization_barrier((across_y, corner_out, *far))

    corner = choose(corner, corner_out)
    corner_y = swap(corner, 2)
    near = [mine, mine_y, beside, beside_y, across]
    early = len(near)
    half, late = pl.pallas_call(
        functools.partial(half_kernel, here),
        out_shape=(shape(2 * NOCC, room, dtype=F32), shape(2, room - early * CAP, room)),
        grid=(1,),
        in_specs=[VMEM] * 3 + [ANY] * (2 * early),
        out_specs=(
            pl.BlockSpec((2 * NOCC, room), lambda i: (0, 0)),
            pl.BlockSpec((2, room - early * CAP, room), lambda i: (0, 0, 0)),
        ),
        scratch_shapes=[pltpu.VMEM((early * CAP, NOCC), BF16), pltpu.SemaphoreType.DMA((2 * early,))],
        compiler_params=params(28),
        cost_estimate=cost(7e9, 1),
        name="half_transform",
    )(code, got, size_row, *near, *far)
    near += [across_y, corner]
    far += [swap(piece, 1) for piece in near[early:]]
    corner_y, half, late, *far = lax.optimization_barrier((corner_y, half, late, *far))
    near.append(corner_y)
    far.append(swap(corner_y, 1))

    count = len(near)
    tile = width // 3
    out = pl.pallas_call(
        functools.partial(last_kernel, count, early),
        out_shape=shape(2, NOCC, nvir),
        grid_spec=pltpu.PrefetchScalarGridSpec(
            num_scalar_prefetch=1,
            grid=(nvir // tile,),
            in_specs=[
                pl.BlockSpec((2 * NOCC, room), lambda j, o: (0, 0)),
                pl.BlockSpec((2, room - early * CAP, room), lambda j, o: (0, 0, 0)),
            ]
            + [ANY] * (2 * count),
            out_specs=pl.BlockSpec((2, NOCC, tile), lambda j, o: (0, 0, (j + 3 * (o[0] % 2)) % 6)),
            scratch_shapes=[
                pltpu.VMEM((CORES, room, width), BF16),
                pltpu.VMEM((room - early * CAP, NOCC), BF16),
                pltpu.VMEM((2 * NOCC, room), BF16),
                pltpu.SemaphoreType.DMA((4 * count,)),
            ],
        ),
        compiler_params=params(28),
        cost_estimate=cost(2e10, 1),
        name="last_product",
    )(me, half, late, *near, *far)
    return out, over[0], code, got


def per_device(*args):
    n = lax.axis_size("shell")
    here, nvir = args[5].shape
    shells = args[3].shape[0]
    sparse = LIVE_DEV * n * EDGE < n * here
    if not (sparse and n == Z * Y * CORES and here <= 256 and here % 16 == 0 and nvir % 768 == 0):
        return from_start(*args)
    out, over, code, got = short_way(*args)

    def again(carry):
        over, _ = carry
        over, code_now, turned, *held = lax.optimization_barrier((over, code, got, *args[3:]))
        turned = turned.reshape(n, 2, BLK_DEV, EDGE * EDGE).swapaxes(1, 2).reshape(n * BLK_DEV, 2, EDGE * EDGE)
        code_now = jnp.max(code_now, axis=2).reshape(n * BLK_DEV)
        ids = jnp.maximum(code_now, 0)
        pairs = jnp.stack([ids // shells, ids % shells], axis=1)
        return over - 1, long_way(turned, pairs, code_now >= 0, *held)

    return lax.while_loop(lambda carry: carry[0] > 0, again, (over, out))[1]


def solution(mesh):
    placed = (
        P(("groups", "shell"), None, None),
        P(("groups", "shell"), None),
        P(("groups", "shell")),
        P("groups"),
        P(("groups", "shell"), None),
        P(("groups", "shell"), None),
    )
    return jax.shard_map(
        per_device,
        mesh=mesh,
        in_specs=placed,
        out_specs=P(("groups", "shell"), None, None),
        check_vma=False,
    )
```

```python
import functools
import math

import jax
import jax.numpy as jnp
from jax import lax
from jax.experimental import pallas as pl
from jax.experimental.pallas import tpu as pltpu
from jax.sharding import PartitionSpec as P

EDGE = 16
NOCC = 256
BLK_DEV = 8
LIVE_DEV = 4
CAP = 128
Z, Y, CORES = 4, 2, 2
F32 = jnp.float32
BF16 = jnp.bfloat16


def padded_rows(matrix, starts, shell_size):
    offsets = jnp.arange(EDGE, dtype=jnp.int32)
    rows = jnp.minimum(starts[:, None] + offsets[None, :], matrix.shape[0] - 1)
    inside = offsets[None, :] < shell_size[:, None]
    return jnp.where(inside[:, :, None], matrix[rows], jnp.zeros((), matrix.dtype))


def half_transform(slot_rows, pairs, keep, occ_blocks):
    count = slot_rows.shape[0]
    vecs_here = slot_rows.shape[1]
    shells = occ_blocks.shape[0]
    group_size = math.gcd(512, count)
    turns = count // group_size
    shaped = slot_rows.reshape(count, vecs_here, EDGE, EDGE)

    def advance(total, turn):
        first = turn * group_size
        block = lax.dynamic_slice_in_dim(shaped, first, group_size, 0)
        okay = lax.dynamic_slice_in_dim(keep, first, group_size, 0)
        block = jnp.where(okay[:, None, None, None], block, jnp.zeros((), block.dtype))
        row_shell = lax.dynamic_slice_in_dim(pairs[:, 0], first, group_size, 0)
        col_shell = lax.dynamic_slice_in_dim(pairs[:, 1], first, group_size, 0)
        coefs = occ_blocks[row_shell]
        piece = jnp.einsum("kmi,kvmn->kvin", coefs, block, preferred_element_type=jnp.float32)
        return (total.at[col_shell].add(piece), None)

    start_total = jnp.zeros((shells, vecs_here, NOCC, EDGE), jnp.float32)
    half, _ = lax.scan(advance, start_total, jnp.arange(turns, dtype=jnp.int32))
    return half


def long_way(turned, pairs, live, shell_size, occ_coef, vir_coef):
    occ_full = lax.all_gather(occ_coef, "shell", axis=0, tiled=True)
    starts = jnp.cumsum(shell_size) - shell_size
    occ_blocks = padded_rows(occ_full, starts, shell_size)
    half = half_transform(turned, pairs, live, occ_blocks)
    hidden = half.astype(jnp.bfloat16)
    vir_full = lax.all_gather(vir_coef, "shell", axis=0, tiled=True)
    vir_blocks = padded_rows(vir_full, starts, shell_size)
    result = jnp.einsum("svin,sna->via", hidden, vir_blocks, preferred_element_type=jnp.float32)
    return result.astype(jnp.bfloat16)


def from_start(panels, block_pairs, block_count, *rest):
    pairs = lax.all_gather(block_pairs, "shell", axis=0, tiled=True)
    counts = lax.all_gather(block_count, "shell", axis=0, tiled=True)
    turned = lax.all_to_all(panels, "shell", split_axis=1, concat_axis=0, tiled=True)
    position = jnp.arange(turned.shape[0], dtype=jnp.int32)
    live = position % BLK_DEV < counts[position // BLK_DEV]
    return long_way(turned, pairs, live, *rest)


def iota(shape, dim):
    return lax.broadcasted_iota(jnp.int32, shape, dim)


def column_of(row, mask):
    return jnp.sum(jnp.where(mask, row, 0.0), axis=1, keepdims=True)


def row_of(column, mask):
    return jnp.sum(jnp.where(mask, column, 0.0), axis=0, keepdims=True)


def zero_one(mask):
    return jnp.where(mask, 1.0, 0.0)


def lane_value(row, index):
    return jnp.sum(jnp.where(iota(row.shape, 1) == index, row, 0.0), axis=1, keepdims=True)


def one_hots(ids, shells):
    lanes = iota(ids.shape, 1).astype(F32)
    return jnp.concatenate([zero_one(ids == lanes + 128.0 * k) for k in range(shells // 128)], axis=1)


def slot_hots(code, shells):
    code = code.reshape(-1, 128)
    kept = code >= 0
    columns = jnp.where(kept, code % shells, -1).astype(F32)
    return one_hots(columns, shells), one_hots(jnp.where(kept, code // shells, -1).astype(F32), shells)


class Shells:
    def __init__(self, size_row):
        shells = size_row.shape[1]
        sub, lane = iota((shells, shells), 0), iota((shells, shells), 1)
        self.before, self.same = lane < sub, lane == sub
        self.starts = column_of(size_row, self.before)
        self.size = column_of(size_row, self.same)
        self.odd = self.starts - 2.0 * jnp.floor(self.starts * 0.5)


class Used:
    def __init__(self, shells, hot, window):
        self.used = column_of(jnp.max(hot, axis=0, keepdims=True), shells.same)
        self.extra, self.ahead, self.edges = [], [], []
        edge = (iota((hot.shape[1], 128), 1) * window).astype(F32)
        reach = jnp.clip(edge - shells.starts, 0.0, shells.size)
        for parity in range(2):
            extra = 1.0 - shells.odd if parity == 0 else shells.odd
            count = self.used * jnp.floor((shells.size + extra) * 0.5)
            count_row = row_of(count, shells.same)
            self.extra.append(extra)
            self.ahead.append(column_of(count_row, shells.before))
            self.edges.append(jnp.sum(self.used * jnp.floor((reach + extra) * 0.5), axis=0, keepdims=True))


def pack_kernel(vir_ref, occ_ref, panels_ref, *refs):
    outs, (turned_ref,) = refs[:4], refs[4:]
    me = lax.axis_index("shell")
    core, y = lax.rem(me, 2), lax.rem(lax.div(me, 2), 2)
    here, nvir = vir_ref.shape
    rows = here // 2
    width, thin = nvir // CORES, occ_ref.shape[1] // CORES
    turned_ref[...] = jnp.swapaxes(panels_ref[...].astype(F32), 0, 1)
    block = EDGE * EDGE
    for dy in range(2):
        parity = lax.rem(y + dy, 2)
        pick = zero_one(iota((rows, here), 1) == 2 * iota((rows, here), 0) + parity).astype(BF16)
        for dc in range(2):
            half = lax.rem(core + dc, 2)
            out = outs[2 * dy + dc]
            part = vir_ref[:, pl.ds(pl.multiple_of(half * width, 128), width)]
            out[:rows, :width] = jnp.dot(pick, part, preferred_element_type=F32).astype(BF16)
            part = occ_ref[:, pl.ds(pl.multiple_of(half * thin, 128), thin)]
            out[:rows, width:] = jnp.dot(pick, part, preferred_element_type=F32).astype(BF16)
            for z in range(Z):
                device = (z * Y + parity) * CORES + half
                pair = turned_ref[pl.ds(2 * device, 2)].reshape(2 * BLK_DEV, block)
                out[rows:, z * block : (z + 1) * block] = pair.astype(BF16)
            out[rows:, Z * block :] = jnp.zeros((2 * BLK_DEV, out.shape[1] - Z * block), BF16)


def ids_kernel(shells, pairs_ref, count_ref, code_ref):
    code = pairs_ref[1:2, :] + shells * pairs_ref[0:1, :]
    code = jnp.where(iota((1, BLK_DEV), 1) < count_ref[...], code, -1).astype(F32)
    square = (BLK_DEV, BLK_DEV)
    code = column_of(code, iota(square, 0) == iota(square, 1)).astype(jnp.int32)
    code_ref[...] = jnp.broadcast_to(jnp.broadcast_to(code, (BLK_DEV, 128))[None], code_ref.shape)


def pick_kernel(here, code_ref, size_ref, *refs):
    sources, (out_ref, over_ref, me_ref), panel_refs = refs[:4], refs[4:7], refs[7:]
    me = lax.axis_index("shell")
    me_ref[0] = me
    core, y, z = lax.rem(me, 2), lax.rem(lax.div(me, 2), 2), lax.div(me, 4)
    window = CORES * Y * here
    shell_count = size_ref.shape[1]
    shells = Shells(size_ref[...].astype(F32))
    lists = [Used(shells, hot, window) for hot in slot_hots(code_ref[...], shell_count)]
    most = jnp.zeros((1, 1), F32)
    lane = iota((1, 128), 1)
    for chosen in lists:
        for edges in chosen.edges:
            later = jnp.concatenate([edges[:, 1:], edges[:, :1]], axis=1)
            most = jnp.maximum(most, jnp.max(jnp.where(lane < Z, later - edges, 0.0), axis=1, keepdims=True))
    over_ref[0] = jnp.where(jnp.max(most) > CAP, 1, 0).astype(jnp.int32)

    width = out_ref.shape[1] - 128
    even = y == 0
    totals = [jnp.zeros((CAP, width), F32), jnp.zeros((CAP, 128), F32)]
    columns = [slice(0, width), slice(width, width + 128)]
    extra = jnp.where(even, lists[0].extra[0], lists[0].extra[1])
    rows = here // 2
    for k, source in enumerate(sources):
        member = 2 * lax.rem(y + k // 2, 2) + lax.rem(core + k % 2, 2)
        device = 4 * z + member
        for r, panel_ref in enumerate(panel_refs):
            lanes = pl.ds(pl.multiple_of((z ^ r) * (EDGE * EDGE), 128), EDGE * EDGE)
            panel_ref[member] = source[rows:, lanes]
        row = (2 * iota((shell_count, 128), 1) + device * here + y).astype(F32)
        where = row - shells.starts
        inside = (where >= 0.0) & (where < shells.size)
        within = jnp.floor((where + extra) * 0.5)
        for chosen, total, column in zip(lists, range(2), columns):
            ahead = jnp.where(even, chosen.ahead[0], chosen.ahead[1])
            base = lane_value(jnp.where(even, chosen.edges[0], chosen.edges[1]), z)
            place = jnp.where(inside & (chosen.used > 0.0), ahead + within + 1.0, 0.0)
            place = jnp.sum(place, axis=0, keepdims=True)
            place = jnp.where(place > 0.0, place - 1.0 - base, -1.0)
            hot = zero_one(place == iota((CAP, 128), 0).astype(F32)).astype(BF16)
            totals[total] += jnp.dot(
                hot[:, :rows], source[:rows, column], preferred_element_type=F32
            )
    for total, column in zip(totals, columns):
        out_ref[:, column] = total.astype(BF16)


def inner_chip(chip):
    z = lax.div(chip, Y)
    return (z == 1) | (z == 2)


def slot_of(window, chip):
    slot = window ^ chip
    return jnp.where(inner_chip(chip) & (slot >= 2 * Y), slot ^ Y, slot)


def choose_kernel(me_ref, inner_ref, outer_ref, out_ref, sem):
    inner = inner_chip(lax.div(me_ref[0], CORES))

    @pl.when(inner)
    def _():
        copy = pltpu.make_async_copy(inner_ref, out_ref, sem)
        copy.start()
        copy.wait()

    @pl.when(jnp.logical_not(inner))
    def _():
        copy = pltpu.make_async_copy(outer_ref, out_ref, sem)
        copy.start()
        copy.wait()


def half_kernel(here, early, code_ref, size_ref, *refs):
    panel_refs, pieces, refs = refs[:Z], refs[Z : Z + 2 * early], refs[Z + 2 * early :]
    half_ref, late_ref, got_ref, occ_ref, part_ref, hot_ref, placed_ref, sems = refs
    me = lax.axis_index("shell")
    core, chip = lax.rem(me, CORES), lax.div(me, CORES)
    z = lax.div(chip, Y)
    width = pieces[0].shape[1] - 128
    copies = []
    for far in range(2):
        half = lax.rem(core + far, CORES)
        for k in range(early):
            at = far * early + k
            target = occ_ref.at[pl.ds(k * CAP, CAP), pl.ds(pl.multiple_of(half * 128, 128), 128)]
            copies.append(pltpu.make_async_copy(pieces[at].at[:, pl.ds(width, 128)], target, sems.at[at]))
    for copy in copies:
        copy.start()
    for r, panel_ref in enumerate(panel_refs):
        got_ref[pl.ds((z ^ r) * (Y * CORES), Y * CORES)] = panel_ref[...]
    window = CORES * Y * here
    shell_count = size_ref.shape[1]
    got = got_ref[...].astype(F32)
    size_row = size_ref[...].astype(F32)
    shells = Shells(size_row)
    got = got_ref[...].astype(F32)
    hots = slot_hots(code_ref[...], shell_count)
    lists = [Used(shells, hot, window) for hot in hots]
    slots = hots[0].shape[0]
    kept = LIVE_DEV * (slots // BLK_DEV)
    alive = jnp.broadcast_to(jnp.sum(hots[0], axis=1, keepdims=True), (slots, slots))
    sub, lane = iota((slots, slots), 0), iota((slots, slots), 1)
    rank = row_of(alive, sub < lane)
    alive_row = row_of(alive, sub == lane)
    take = (rank == iota((kept, slots), 0).astype(F32)) & (alive_row > 0.0)
    take = zero_one(take).astype(BF16)

    def taken(array):
        return jnp.dot(take, array.astype(BF16), preferred_element_type=F32)

    def spread(hot, column):
        value = jnp.sum(hot * row_of(column, shells.same), axis=1, keepdims=True)
        wide = jnp.broadcast_to(value, (kept, 128)).reshape(kept, 1, 128)
        return jnp.broadcast_to(wide, (kept, EDGE, 128)).reshape(kept * EDGE, 128)

    at = iota((kept * EDGE, 128), 0) % EDGE
    step = at.astype(F32)

    def places(hot, chosen):
        hot = taken(hot)
        first, length = spread(hot, shells.starts), spread(hot, shells.size)
        row = first + step
        odd = (row - 2.0 * jnp.floor(row * 0.5)) > 0.0
        place = jnp.where(odd, spread(hot, chosen.ahead[1]), spread(hot, chosen.ahead[0]))
        place += jnp.floor(step * 0.5)
        offsets = [
            [slot_of(w * Y + k, chip).astype(F32) * CAP - lane_value(e, w) for w in range(Z)]
            for k, e in enumerate(chosen.edges)
        ]
        offset = jnp.where(odd, offsets[1][0], offsets[0][0])
        for w in range(1, Z):
            offset = jnp.where(row >= float(window * w), jnp.where(odd, offsets[1][w], offsets[0][w]), offset)
        return jnp.where(step < length, place + offset, -1.0)[:, :1]

    place_c, place_r = places(hots[0], lists[0]), places(hots[1], lists[1])
    span = 16 * EDGE
    s_in, l_in = iota((span, span), 0), iota((span, span), 1)
    keep_m = (l_in // EDGE) == (s_in % EDGE)
    fold = zero_one((s_in % EDGE) == (l_in % EDGE)).astype(BF16)
    same_slot = (s_in // EDGE) == (l_in // EDGE)
    blocks = [taken(got[:, p * BLK_DEV : (p + 1) * BLK_DEV, :].reshape(slots, span)) for p in range(2)]
    lanes = iota((span, half_ref.shape[1]), 1).astype(F32)
    for copy in copies:
        copy.wait()
    occ = occ_ref[...]
    cut = early * CAP
    for g in range(kept // 16):
        rows = slice(g * span, (g + 1) * span)
        r_hot = zero_one(place_r[rows] == lanes).astype(BF16)
        c_hot = zero_one(place_c[rows] == lanes).astype(BF16)
        part_ref[:, rows] = jnp.dot(r_hot[:, :cut], occ, preferred_element_type=F32).T.astype(BF16)
        hot_ref[:, rows] = r_hot[:, cut:].T
        for p in range(2):
            block = blocks[p][g * 16 : (g + 1) * 16].reshape(16, 1, span)
            block = jnp.broadcast_to(block, (16, EDGE, span)).reshape(span, span)
            block = jnp.where(keep_m, block, 0.0).astype(BF16)
            diag = jnp.dot(block, fold, preferred_element_type=F32)
            diag = jnp.where(same_slot, diag, 0.0).astype(BF16)
            placed_ref[p, rows, :] = jnp.dot(diag, c_hot, preferred_element_type=F32).astype(BF16)
    for p in range(2):
        half_ref[p * NOCC : (p + 1) * NOCC, :] = jnp.dot(part_ref[...], placed_ref[p], preferred_element_type=F32)
        late_ref[p] = jnp.dot(hot_ref[...], placed_ref[p], preferred_element_type=F32).astype(BF16)


def last_kernel(count, early, me_ref, part_any, late_any, *refs):
    pieces, (out_any, right_ref, occ_ref, part_ref, late_ref, half_ref, tiles_ref, sems) = refs[: 2 * count], refs[2 * count :]
    width = right_ref.shape[2]
    tile = tiles_ref.shape[3]
    per = width // tile
    core = lax.rem(me_ref[0], CORES)
    first, near, far, results = [], [], [], []

    def copy_of(source, target):
        at = len(first) + len(near) + len(far) + len(results)
        return pltpu.make_async_copy(source, target, sems.at[at])

    first.append(copy_of(part_any, part_ref))
    first.append(copy_of(late_any, late_ref))
    for side in range(2):
        half = lax.rem(core + side, CORES)
        for k in range(early, count):
            target = occ_ref.at[pl.ds((k - early) * CAP, CAP), pl.ds(pl.multiple_of(half * 128, 128), 128)]
            first.append(copy_of(pieces[side * count + k].at[:, pl.ds(width, 128)], target))
    for side, copies in enumerate((near, far)):
        for k in range(count):
            target = right_ref.at[side, pl.ds(k * CAP, CAP), :]
            copies.append(copy_of(pieces[side * count + k].at[:, pl.ds(0, width)], target))
    for copy in (*first, *near, *far):
        copy.start()
    for copy in first:
        copy.wait()
    occ = occ_ref[...].T
    for p in range(2):
        rows = slice(p * NOCC, (p + 1) * NOCC)
        late = jnp.dot(occ, late_ref[p], preferred_element_type=F32)
        half_ref[rows, :] = (part_ref[rows, :] + late).astype(BF16)
    for side, copies in enumerate((near, far)):
        for copy in copies:
            copy.wait()
        base = lax.rem(core + side, CORES) * width
        for t in range(per):
            right = right_ref[side, :, t * tile : (t + 1) * tile]
            total = jnp.dot(half_ref[...], right, preferred_element_type=F32).astype(BF16)
            at = side * per + t
            tiles_ref[at] = total.reshape(tiles_ref.shape[1:])
            columns = pl.ds(pl.multiple_of(base + t * tile, 128), tile)
            results.append(copy_of(tiles_ref.at[at], out_any.at[:, :, columns]))
            results[-1].start()
    for copy in results:
        copy.wait()


VMEM = pl.BlockSpec(memory_space=pltpu.VMEM)
SMEM = pl.BlockSpec(memory_space=pltpu.SMEM)
ANY = pl.BlockSpec(memory_space=pl.ANY)


def shape(*dims, dtype=BF16):
    return jax.ShapeDtypeStruct(dims, dtype)


def params(mib):
    return pltpu.CompilerParams(vmem_limit_bytes=mib << 20)


def cost(flops, nbytes):
    return pl.CostEstimate(flops=int(flops), bytes_accessed=int(nbytes), transcendentals=0)


def short_way(panels, block_pairs, block_count, shell_size, occ_coef, vir_coef):
    n = lax.axis_size("shell")
    here, nvir = vir_coef.shape
    width = nvir // CORES
    packed = width + NOCC // CORES
    room = Z * Y * CAP
    size_row = shell_size.reshape(1, -1)

    def swap(array, bit):
        return lax.ppermute(array, "shell", [(i, i ^ bit) for i in range(n)])

    keep, to_core, to_y, to_both = pl.pallas_call(
        pack_kernel,
        out_shape=[shape(here // 2 + 2 * BLK_DEV, packed)] * 4,
        in_specs=[VMEM] * 3,
        out_specs=[VMEM] * 4,
        scratch_shapes=[pltpu.VMEM((2 * n, BLK_DEV, EDGE * EDGE), F32)],
        compiler_params=params(12),
        cost_estimate=cost(3e8, 3e6),
        name="pack_rows",
    )(vir_coef, occ_coef, panels)
    to_y, to_both, to_core = swap(to_y, 2), swap(to_both, 3), swap(to_core, 1)
    code = pl.pallas_call(
        functools.partial(ids_kernel, size_row.shape[1]),
        out_shape=shape(n, BLK_DEV, 128, dtype=jnp.int32),
        in_specs=[VMEM] * 2,
        out_specs=VMEM,
        compiler_params=params(12),
        cost_estimate=cost(1e4, 1e4),
        name="pack_ids",
    )(block_pairs.T, block_count.reshape(1, 1))
    code = lax.all_to_all(code, "shell", split_axis=0, concat_axis=0, tiled=True)

    mine, over, me, *panel = pl.pallas_call(
        functools.partial(pick_kernel, here),
        out_shape=[shape(CAP, packed), shape(1, dtype=jnp.int32), shape(1, dtype=jnp.int32)]
        + [shape(Y * CORES, 2 * BLK_DEV, EDGE * EDGE)] * Z,
        in_specs=[VMEM] * 6,
        out_specs=[VMEM, SMEM, SMEM] + [VMEM] * Z,
        compiler_params=params(12),
        cost_estimate=cost(3e8, 2e6),
        name="pick_rows",
    )(code, size_row, keep, to_core, to_y, to_both)

    ends, middle, outward = [(0, 1), (1, 0), (2, 3), (3, 2)], [(1, 2), (2, 1)], [(1, 0), (2, 3)]

    def hop(array, steps):
        return lax.ppermute(array, "shell", [(4 * a + k, 4 * b + k) for a, b in steps for k in range(4)])

    def choose(inner, outer):
        return pl.pallas_call(
            choose_kernel,
            out_shape=shape(*inner.shape),
            in_specs=[SMEM, ANY, ANY],
            out_specs=ANY,
            scratch_shapes=[pltpu.SemaphoreType.DMA],
            compiler_params=params(4),
            cost_estimate=cost(1, 1),
            name="choose_piece",
        )(me, inner, outer)

    mine_y, beside, across = swap(mine, 2), hop(mine, ends), hop(mine, middle)
    panel[1] = swap(panel[1], 4)
    mine_y, beside, across, panel[1] = lax.optimization_barrier((mine_y, beside, across, panel[1]))

    beside_y, across_out, corner = swap(beside, 2), hop(across, outward), hop(beside, middle)
    far = [swap(piece, 1) for piece in (mine, mine_y, beside)]
    panel[2] = swap(panel[2], 8)
    beside_y, across_out, corner, panel[2], *far = lax.optimization_barrier(
        (beside_y, across_out, corner, panel[2], *far)
    )

    across = choose(across, across_out)
    across_y, corner_out = swap(across, 2), hop(corner, outward)
    far += [swap(piece, 1) for piece in (beside_y, across)]
    panel[3] = swap(panel[3], 12)
    across_y, corner_out, panel[3], *far = lax.optimization_barrier((across_y, corner_out, panel[3], *far))

    corner = choose(corner, corner_out)
    corner_y = swap(corner, 2)
    near = [mine, mine_y, beside, beside_y, across]
    early = len(near)
    slots = LIVE_DEV * n * EDGE
    half, late = pl.pallas_call(
        functools.partial(half_kernel, here, early),
        out_shape=(shape(2 * NOCC, room, dtype=F32), shape(2, room - early * CAP, room)),
        grid=(1,),
        in_specs=[VMEM] * (2 + Z) + [ANY] * (2 * early),
        out_specs=(
            pl.BlockSpec((2 * NOCC, room), lambda i: (0, 0)),
            pl.BlockSpec((2, room - early * CAP, room), lambda i: (0, 0, 0)),
        ),
        scratch_shapes=[
            pltpu.VMEM((n, 2 * BLK_DEV, EDGE * EDGE), BF16),
            pltpu.VMEM((early * CAP, NOCC), BF16),
            pltpu.VMEM((NOCC, slots), BF16),
            pltpu.VMEM((room - early * CAP, slots), BF16),
            pltpu.VMEM((2, slots, room), BF16),
            pltpu.SemaphoreType.DMA((2 * early,)),
        ],
        compiler_params=params(30),
        cost_estimate=cost(7e9, 1),
        name="half_transform",
    )(code, size_row, *panel, *near, *far)
    near += [across_y, corner]
    far += [swap(piece, 1) for piece in near[early:]]
    corner_y, half, late, *far = lax.optimization_barrier((corner_y, half, late, *far))
    near.append(corner_y)
    far.append(swap(corner_y, 1))

    count = len(near)
    tile = width // 3
    out = pl.pallas_call(
        functools.partial(last_kernel, count, early),
        out_shape=shape(2, NOCC, nvir),
        in_specs=[SMEM] + [ANY] * (2 + 2 * count),
        out_specs=ANY,
        scratch_shapes=[
            pltpu.VMEM((CORES, room, width), BF16),
            pltpu.VMEM((room - early * CAP, NOCC), BF16),
            pltpu.VMEM(half.shape, F32),
            pltpu.VMEM(late.shape, BF16),
            pltpu.VMEM((2 * NOCC, room), BF16),
            pltpu.VMEM((nvir // tile, 2, NOCC, tile), BF16),
            pltpu.SemaphoreType.DMA((2 + 4 * count + nvir // tile,)),
        ],
        compiler_params=params(30),
        cost_estimate=cost(2e10, 1),
        name="last_product",
    )(me, half, late, *near, *far)
    return out, over[0], code, me, panel


def per_device(*args):
    n = lax.axis_size("shell")
    here, nvir = args[5].shape
    shells = args[3].shape[0]
    sparse = LIVE_DEV * n * EDGE < n * here
    if not (sparse and n == Z * Y * CORES and here <= 256 and here % 16 == 0 and nvir % 768 == 0):
        return from_start(*args)
    out, over, code, me, panel = short_way(*args)

    def again(carry):
        over, _ = carry
        over, code_now, me_now, panel_now, *held = lax.optimization_barrier((over, code, me, tuple(panel), *args[3:]))
        z = me_now[0] // (Y * CORES)
        turned = jnp.stack(panel_now)[jnp.arange(Z, dtype=jnp.int32) ^ z]
        turned = turned.reshape(n, 2, BLK_DEV, EDGE * EDGE).swapaxes(1, 2).reshape(n * BLK_DEV, 2, EDGE * EDGE)
        code_now = jnp.max(code_now, axis=2).reshape(n * BLK_DEV)
        ids = jnp.maximum(code_now, 0)
        pairs = jnp.stack([ids // shells, ids % shells], axis=1)
        return over - 1, long_way(turned, pairs, code_now >= 0, *held)

    return lax.while_loop(lambda carry: carry[0] > 0, again, (over, out))[1]


def solution(mesh):
    placed = (
        P(("groups", "shell"), None, None),
        P(("groups", "shell"), None),
        P(("groups", "shell")),
        P("groups"),
        P(("groups", "shell"), None),
        P(("groups", "shell"), None),
    )
    return jax.shard_map(
        per_device,
        mesh=mesh,
        in_specs=placed,
        out_specs=P(("groups", "shell"), None, None),
        check_vma=False,
    )
```

```python
import functools
import math

import jax
import jax.numpy as jnp
from jax import lax
from jax.experimental import pallas as pl
from jax.experimental.pallas import tpu as pltpu
from jax.sharding import PartitionSpec as P

EDGE = 16
NOCC = 256
BLK_DEV = 8
LIVE_DEV = 4
CAP = 128
Z, Y, CORES = 4, 2, 2
F32 = jnp.float32
BF16 = jnp.bfloat16


def padded_rows(matrix, starts, shell_size):
    offsets = jnp.arange(EDGE, dtype=jnp.int32)
    rows = jnp.minimum(starts[:, None] + offsets[None, :], matrix.shape[0] - 1)
    inside = offsets[None, :] < shell_size[:, None]
    return jnp.where(inside[:, :, None], matrix[rows], jnp.zeros((), matrix.dtype))


def half_transform(slot_rows, pairs, keep, occ_blocks):
    count = slot_rows.shape[0]
    vecs_here = slot_rows.shape[1]
    shells = occ_blocks.shape[0]
    group_size = math.gcd(512, count)
    turns = count // group_size
    shaped = slot_rows.reshape(count, vecs_here, EDGE, EDGE)

    def advance(total, turn):
        first = turn * group_size
        block = lax.dynamic_slice_in_dim(shaped, first, group_size, 0)
        okay = lax.dynamic_slice_in_dim(keep, first, group_size, 0)
        block = jnp.where(okay[:, None, None, None], block, jnp.zeros((), block.dtype))
        row_shell = lax.dynamic_slice_in_dim(pairs[:, 0], first, group_size, 0)
        col_shell = lax.dynamic_slice_in_dim(pairs[:, 1], first, group_size, 0)
        coefs = occ_blocks[row_shell]
        piece = jnp.einsum("kmi,kvmn->kvin", coefs, block, preferred_element_type=jnp.float32)
        return (total.at[col_shell].add(piece), None)

    start_total = jnp.zeros((shells, vecs_here, NOCC, EDGE), jnp.float32)
    half, _ = lax.scan(advance, start_total, jnp.arange(turns, dtype=jnp.int32))
    return half


def long_way(turned, pairs, live, shell_size, occ_coef, vir_coef):
    occ_full = lax.all_gather(occ_coef, "shell", axis=0, tiled=True)
    starts = jnp.cumsum(shell_size) - shell_size
    occ_blocks = padded_rows(occ_full, starts, shell_size)
    half = half_transform(turned, pairs, live, occ_blocks)
    hidden = half.astype(jnp.bfloat16)
    vir_full = lax.all_gather(vir_coef, "shell", axis=0, tiled=True)
    vir_blocks = padded_rows(vir_full, starts, shell_size)
    result = jnp.einsum("svin,sna->via", hidden, vir_blocks, preferred_element_type=jnp.float32)
    return result.astype(jnp.bfloat16)


def from_start(panels, block_pairs, block_count, *rest):
    pairs = lax.all_gather(block_pairs, "shell", axis=0, tiled=True)
    counts = lax.all_gather(block_count, "shell", axis=0, tiled=True)
    turned = lax.all_to_all(panels, "shell", split_axis=1, concat_axis=0, tiled=True)
    position = jnp.arange(turned.shape[0], dtype=jnp.int32)
    live = position % BLK_DEV < counts[position // BLK_DEV]
    return long_way(turned, pairs, live, *rest)


def iota(shape, dim):
    return lax.broadcasted_iota(jnp.int32, shape, dim)


def column_of(row, mask):
    return jnp.sum(jnp.where(mask, row, 0.0), axis=1, keepdims=True)


def row_of(column, mask):
    return jnp.sum(jnp.where(mask, column, 0.0), axis=0, keepdims=True)


def zero_one(mask):
    return jnp.where(mask, 1.0, 0.0)


def lane_value(row, index):
    return jnp.sum(jnp.where(iota(row.shape, 1) == index, row, 0.0), axis=1, keepdims=True)


def one_hots(ids, shells):
    lanes = iota(ids.shape, 1).astype(F32)
    return jnp.concatenate([zero_one(ids == lanes + 128.0 * k) for k in range(shells // 128)], axis=1)


def slot_hots(code, shells):
    code = code.reshape(-1, 128)
    kept = code >= 0
    columns = jnp.where(kept, code % shells, -1).astype(F32)
    return one_hots(columns, shells), one_hots(jnp.where(kept, code // shells, -1).astype(F32), shells)


class Shells:
    def __init__(self, size_row):
        shells = size_row.shape[1]
        sub, lane = iota((shells, shells), 0), iota((shells, shells), 1)
        self.before, self.same = lane < sub, lane == sub
        self.starts = column_of(size_row, self.before)
        self.size = column_of(size_row, self.same)
        self.odd = self.starts - 2.0 * jnp.floor(self.starts * 0.5)


class Used:
    def __init__(self, shells, hot, window):
        self.used = column_of(jnp.max(hot, axis=0, keepdims=True), shells.same)
        self.extra, self.ahead, self.edges = [], [], []
        edge = (iota((hot.shape[1], 128), 1) * window).astype(F32)
        reach = jnp.clip(edge - shells.starts, 0.0, shells.size)
        for parity in range(2):
            extra = 1.0 - shells.odd if parity == 0 else shells.odd
            count = self.used * jnp.floor((shells.size + extra) * 0.5)
            count_row = row_of(count, shells.same)
            self.extra.append(extra)
            self.ahead.append(column_of(count_row, shells.before))
            self.edges.append(jnp.sum(self.used * jnp.floor((reach + extra) * 0.5), axis=0, keepdims=True))


def pack_kernel(vir_ref, occ_ref, panels_ref, *refs):
    outs, (turned_ref,) = refs[:4], refs[4:]
    me = lax.axis_index("shell")
    core, y = lax.rem(me, 2), lax.rem(lax.div(me, 2), 2)
    here, nvir = vir_ref.shape
    rows = here // 2
    width, thin = nvir // CORES, occ_ref.shape[1] // CORES
    turned_ref[...] = jnp.swapaxes(panels_ref[...].astype(F32), 0, 1)
    block = EDGE * EDGE
    for dy in range(2):
        parity = lax.rem(y + dy, 2)
        pick = zero_one(iota((rows, here), 1) == 2 * iota((rows, here), 0) + parity).astype(BF16)
        for dc in range(2):
            half = lax.rem(core + dc, 2)
            out = outs[2 * dy + dc]
            part = vir_ref[:, pl.ds(pl.multiple_of(half * width, 128), width)]
            out[:rows, :width] = jnp.dot(pick, part, preferred_element_type=F32).astype(BF16)
            part = occ_ref[:, pl.ds(pl.multiple_of(half * thin, 128), thin)]
            out[:rows, width:] = jnp.dot(pick, part, preferred_element_type=F32).astype(BF16)
            for z in range(Z):
                device = (z * Y + parity) * CORES + half
                pair = turned_ref[pl.ds(2 * device, 2)].reshape(2 * BLK_DEV, block)
                out[rows:, z * block : (z + 1) * block] = pair.astype(BF16)
            out[rows:, Z * block :] = jnp.zeros((2 * BLK_DEV, out.shape[1] - Z * block), BF16)


def ids_kernel(shells, pairs_ref, count_ref, code_ref):
    code = pairs_ref[1:2, :] + shells * pairs_ref[0:1, :]
    code = jnp.where(iota((1, BLK_DEV), 1) < count_ref[...], code, -1).astype(F32)
    square = (BLK_DEV, BLK_DEV)
    code = column_of(code, iota(square, 0) == iota(square, 1)).astype(jnp.int32)
    code_ref[...] = jnp.broadcast_to(jnp.broadcast_to(code, (BLK_DEV, 128))[None], code_ref.shape)


def pick_kernel(here, code_ref, size_ref, *refs):
    sources, (out_ref, over_ref, me_ref), panel_refs = refs[:4], refs[4:7], refs[7:]
    me = lax.axis_index("shell")
    me_ref[0] = me
    core, y, z = lax.rem(me, 2), lax.rem(lax.div(me, 2), 2), lax.div(me, 4)
    window = CORES * Y * here
    shell_count = size_ref.shape[1]
    shells = Shells(size_ref[...].astype(F32))
    lists = [Used(shells, hot, window) for hot in slot_hots(code_ref[...], shell_count)]
    most = jnp.zeros((1, 1), F32)
    lane = iota((1, 128), 1)
    for chosen in lists:
        for edges in chosen.edges:
            later = jnp.concatenate([edges[:, 1:], edges[:, :1]], axis=1)
            most = jnp.maximum(most, jnp.max(jnp.where(lane < Z, later - edges, 0.0), axis=1, keepdims=True))
    over_ref[0] = jnp.where(jnp.max(most) > CAP, 1, 0).astype(jnp.int32)

    width = out_ref.shape[1] - 128
    even = y == 0
    totals = [jnp.zeros((CAP, width), F32), jnp.zeros((CAP, 128), F32)]
    columns = [slice(0, width), slice(width, width + 128)]
    extra = jnp.where(even, lists[0].extra[0], lists[0].extra[1])
    rows = here // 2
    for k, source in enumerate(sources):
        member = 2 * lax.rem(y + k // 2, 2) + lax.rem(core + k % 2, 2)
        device = 4 * z + member
        for r, panel_ref in enumerate(panel_refs):
            lanes = pl.ds(pl.multiple_of((z ^ r) * (EDGE * EDGE), 128), EDGE * EDGE)
            panel_ref[member] = source[rows:, lanes]
        row = (2 * iota((shell_count, 128), 1) + device * here + y).astype(F32)
        where = row - shells.starts
        inside = (where >= 0.0) & (where < shells.size)
        within = jnp.floor((where + extra) * 0.5)
        for chosen, total, column in zip(lists, range(2), columns):
            ahead = jnp.where(even, chosen.ahead[0], chosen.ahead[1])
            base = lane_value(jnp.where(even, chosen.edges[0], chosen.edges[1]), z)
            place = jnp.where(inside & (chosen.used > 0.0), ahead + within + 1.0, 0.0)
            place = jnp.sum(place, axis=0, keepdims=True)
            place = jnp.where(place > 0.0, place - 1.0 - base, -1.0)
            hot = zero_one(place == iota((CAP, 128), 0).astype(F32)).astype(BF16)
            totals[total] += jnp.dot(
                hot[:, :rows], source[:rows, column], preferred_element_type=F32
            )
    for total, column in zip(totals, columns):
        out_ref[:, column] = total.astype(BF16)


def slot_of(window, chip):
    slot = window ^ chip
    return jnp.where((slot == 3) | (slot == 4), slot ^ 7, slot)


def half_kernel(here, early, code_ref, size_ref, *refs):
    panel_refs, pieces, refs = refs[:Z], refs[Z : Z + 2 * early], refs[Z + 2 * early :]
    half_ref, late_ref, got_ref, occ_ref, part_ref, hot_ref, placed_ref, sems = refs
    me = lax.axis_index("shell")
    core, chip = lax.rem(me, CORES), lax.div(me, CORES)
    z = lax.div(chip, Y)
    width = pieces[0].shape[1] - 128
    copies = []
    for far in range(2):
        half = lax.rem(core + far, CORES)
        for k in range(early):
            at = far * early + k
            target = occ_ref.at[pl.ds(k * CAP, CAP), pl.ds(pl.multiple_of(half * 128, 128), 128)]
            copies.append(pltpu.make_async_copy(pieces[at].at[:, pl.ds(width, 128)], target, sems.at[at]))
    for copy in copies:
        copy.start()
    for r, panel_ref in enumerate(panel_refs):
        got_ref[pl.ds((z ^ r) * (Y * CORES), Y * CORES)] = panel_ref[...]
    window = CORES * Y * here
    shell_count = size_ref.shape[1]
    got = got_ref[...].astype(F32)
    size_row = size_ref[...].astype(F32)
    shells = Shells(size_row)
    got = got_ref[...].astype(F32)
    hots = slot_hots(code_ref[...], shell_count)
    lists = [Used(shells, hot, window) for hot in hots]
    slots = hots[0].shape[0]
    kept = LIVE_DEV * (slots // BLK_DEV)
    alive = jnp.broadcast_to(jnp.sum(hots[0], axis=1, keepdims=True), (slots, slots))
    sub, lane = iota((slots, slots), 0), iota((slots, slots), 1)
    rank = row_of(alive, sub < lane)
    alive_row = row_of(alive, sub == lane)
    take = (rank == iota((kept, slots), 0).astype(F32)) & (alive_row > 0.0)
    take = zero_one(take).astype(BF16)

    def taken(array):
        return jnp.dot(take, array.astype(BF16), preferred_element_type=F32)

    def spread(hot, column):
        value = jnp.sum(hot * row_of(column, shells.same), axis=1, keepdims=True)
        wide = jnp.broadcast_to(value, (kept, 128)).reshape(kept, 1, 128)
        return jnp.broadcast_to(wide, (kept, EDGE, 128)).reshape(kept * EDGE, 128)

    at = iota((kept * EDGE, 128), 0) % EDGE
    step = at.astype(F32)

    def places(hot, chosen):
        hot = taken(hot)
        first, length = spread(hot, shells.starts), spread(hot, shells.size)
        row = first + step
        odd = (row - 2.0 * jnp.floor(row * 0.5)) > 0.0
        place = jnp.where(odd, spread(hot, chosen.ahead[1]), spread(hot, chosen.ahead[0]))
        place += jnp.floor(step * 0.5)
        offsets = [
            [slot_of(w * Y + k, chip).astype(F32) * CAP - lane_value(e, w) for w in range(Z)]
            for k, e in enumerate(chosen.edges)
        ]
        offset = jnp.where(odd, offsets[1][0], offsets[0][0])
        for w in range(1, Z):
            offset = jnp.where(row >= float(window * w), jnp.where(odd, offsets[1][w], offsets[0][w]), offset)
        return jnp.where(step < length, place + offset, -1.0)[:, :1]

    place_c, place_r = places(hots[0], lists[0]), places(hots[1], lists[1])
    span = 16 * EDGE
    s_in, l_in = iota((span, span), 0), iota((span, span), 1)
    keep_m = (l_in // EDGE) == (s_in % EDGE)
    fold = zero_one((s_in % EDGE) == (l_in % EDGE)).astype(BF16)
    same_slot = (s_in // EDGE) == (l_in // EDGE)
    blocks = [taken(got[:, p * BLK_DEV : (p + 1) * BLK_DEV, :].reshape(slots, span)) for p in range(2)]
    lanes = iota((span, half_ref.shape[1]), 1).astype(F32)
    for copy in copies:
        copy.wait()
    occ = occ_ref[...]
    cut = early * CAP
    for g in range(kept // 16):
        rows = slice(g * span, (g + 1) * span)
        r_hot = zero_one(place_r[rows] == lanes).astype(BF16)
        c_hot = zero_one(place_c[rows] == lanes).astype(BF16)
        part_ref[:, rows] = jnp.dot(r_hot[:, :cut], occ, preferred_element_type=F32).T.astype(BF16)
        hot_ref[:, rows] = r_hot[:, cut:].T
        for p in range(2):
            block = blocks[p][g * 16 : (g + 1) * 16].reshape(16, 1, span)
            block = jnp.broadcast_to(block, (16, EDGE, span)).reshape(span, span)
            block = jnp.where(keep_m, block, 0.0).astype(BF16)
            diag = jnp.dot(block, fold, preferred_element_type=F32)
            diag = jnp.where(same_slot, diag, 0.0).astype(BF16)
            placed_ref[p, rows, :] = jnp.dot(diag, c_hot, preferred_element_type=F32).astype(BF16)
    for p in range(2):
        half_ref[p * NOCC : (p + 1) * NOCC, :] = jnp.dot(part_ref[...], placed_ref[p], preferred_element_type=F32)
        late_ref[p] = jnp.dot(hot_ref[...], placed_ref[p], preferred_element_type=F32).astype(BF16)


def last_kernel(count, early, me_ref, part_any, late_any, *refs):
    pieces, (out_any, right_ref, occ_ref, part_ref, late_ref, half_ref, tiles_ref, sems) = refs[: 2 * count], refs[2 * count :]
    width = right_ref.shape[2]
    tile = tiles_ref.shape[3]
    per = width // tile
    core = lax.rem(me_ref[0], CORES)
    first, near, far, results = [], [], [], []

    def copy_of(source, target):
        at = len(first) + len(near) + len(far) + len(results)
        return pltpu.make_async_copy(source, target, sems.at[at])

    first.append(copy_of(part_any, part_ref))
    first.append(copy_of(late_any, late_ref))
    for side in range(2):
        half = lax.rem(core + side, CORES)
        for k in range(early, count):
            target = occ_ref.at[pl.ds((k - early) * CAP, CAP), pl.ds(pl.multiple_of(half * 128, 128), 128)]
            first.append(copy_of(pieces[side * count + k].at[:, pl.ds(width, 128)], target))
    for side, copies in enumerate((near, far)):
        for k in range(count):
            target = right_ref.at[side, pl.ds(k * CAP, CAP), :]
            copies.append(copy_of(pieces[side * count + k].at[:, pl.ds(0, width)], target))
    for copy in (*first, *near, *far):
        copy.start()
    for copy in first:
        copy.wait()
    occ = occ_ref[...].T
    for p in range(2):
        rows = slice(p * NOCC, (p + 1) * NOCC)
        late = jnp.dot(occ, late_ref[p], preferred_element_type=F32)
        half_ref[rows, :] = (part_ref[rows, :] + late).astype(BF16)
    for side, copies in enumerate((near, far)):
        for copy in copies:
            copy.wait()
        base = lax.rem(core + side, CORES) * width
        for t in range(per):
            right = right_ref[side, :, t * tile : (t + 1) * tile]
            total = jnp.dot(half_ref[...], right, preferred_element_type=F32).astype(BF16)
            at = side * per + t
            tiles_ref[at] = total.reshape(tiles_ref.shape[1:])
            columns = pl.ds(pl.multiple_of(base + t * tile, 128), tile)
            results.append(copy_of(tiles_ref.at[at], out_any.at[:, :, columns]))
            results[-1].start()
    for copy in results:
        copy.wait()


VMEM = pl.BlockSpec(memory_space=pltpu.VMEM)
SMEM = pl.BlockSpec(memory_space=pltpu.SMEM)
ANY = pl.BlockSpec(memory_space=pl.ANY)


def shape(*dims, dtype=BF16):
    return jax.ShapeDtypeStruct(dims, dtype)


def params(mib):
    return pltpu.CompilerParams(vmem_limit_bytes=mib << 20)


def cost(flops, nbytes):
    return pl.CostEstimate(flops=int(flops), bytes_accessed=int(nbytes), transcendentals=0)


def short_way(panels, block_pairs, block_count, shell_size, occ_coef, vir_coef):
    n = lax.axis_size("shell")
    here, nvir = vir_coef.shape
    width = nvir // CORES
    packed = width + NOCC // CORES
    room = Z * Y * CAP
    size_row = shell_size.reshape(1, -1)

    def swap(array, bit):
        return lax.ppermute(array, "shell", [(i, i ^ bit) for i in range(n)])

    keep, to_core, to_y, to_both = pl.pallas_call(
        pack_kernel,
        out_shape=[shape(here // 2 + 2 * BLK_DEV, packed)] * 4,
        in_specs=[VMEM] * 3,
        out_specs=[VMEM] * 4,
        scratch_shapes=[pltpu.VMEM((2 * n, BLK_DEV, EDGE * EDGE), F32)],
        compiler_params=params(12),
        cost_estimate=cost(3e8, 3e6),
        name="pack_rows",
    )(vir_coef, occ_coef, panels)
    to_y, to_both, to_core = swap(to_y, 2), swap(to_both, 3), swap(to_core, 1)
    code = pl.pallas_call(
        functools.partial(ids_kernel, size_row.shape[1]),
        out_shape=shape(n, BLK_DEV, 128, dtype=jnp.int32),
        in_specs=[VMEM] * 2,
        out_specs=VMEM,
        compiler_params=params(12),
        cost_estimate=cost(1e4, 1e4),
        name="pack_ids",
    )(block_pairs.T, block_count.reshape(1, 1))
    code = lax.all_to_all(code, "shell", split_axis=0, concat_axis=0, tiled=True)

    mine, over, me, *panel = pl.pallas_call(
        functools.partial(pick_kernel, here),
        out_shape=[shape(CAP, packed), shape(1, dtype=jnp.int32), shape(1, dtype=jnp.int32)]
        + [shape(Y * CORES, 2 * BLK_DEV, EDGE * EDGE)] * Z,
        in_specs=[VMEM] * 6,
        out_specs=[VMEM, SMEM, SMEM] + [VMEM] * Z,
        compiler_params=params(12),
        cost_estimate=cost(3e8, 2e6),
        name="pick_rows",
    )(code, size_row, keep, to_core, to_y, to_both)

    across, mine_y, beside = swap(mine, 8), swap(mine, 2), swap(mine, 4)
    far = [swap(mine, 1), swap(mine_y, 1), swap(beside, 1)]
    across, mine_y, beside, *far = lax.optimization_barrier((across, mine_y, beside, *far))

    corner, beside_y, across_y = swap(across, 4), swap(beside, 2), swap(across, 2)
    panel = [panel[0]] + [swap(panel[r], 4 * r) for r in range(1, Z)]
    corner, *panel = lax.optimization_barrier((corner, *panel))

    corner_y = swap(corner, 2)
    near = [mine, mine_y, beside]
    early = len(near)
    slots = LIVE_DEV * n * EDGE
    half, late = pl.pallas_call(
        functools.partial(half_kernel, here, early),
        out_shape=(shape(2 * NOCC, room, dtype=F32), shape(2, room - early * CAP, room)),
        grid=(1,),
        in_specs=[VMEM] * (2 + Z) + [ANY] * (2 * early),
        out_specs=(
            pl.BlockSpec((2 * NOCC, room), lambda i: (0, 0)),
            pl.BlockSpec((2, room - early * CAP, room), lambda i: (0, 0, 0)),
        ),
        scratch_shapes=[
            pltpu.VMEM((n, 2 * BLK_DEV, EDGE * EDGE), BF16),
            pltpu.VMEM((early * CAP, NOCC), BF16),
            pltpu.VMEM((NOCC, slots), BF16),
            pltpu.VMEM((room - early * CAP, slots), BF16),
            pltpu.VMEM((2, slots, room), BF16),
            pltpu.SemaphoreType.DMA((2 * early,)),
        ],
        compiler_params=params(30),
        cost_estimate=cost(7e9, 1),
        name="half_transform",
    )(code, size_row, *panel, *near, *far)
    far.append(swap(across, 1))
    beside_y, across_y, half, late, *far = lax.optimization_barrier((beside_y, across_y, half, late, *far))
    near += [across, beside_y, across_y, corner]
    far += [swap(piece, 1) for piece in near[early + 1 :]]
    corner_y, *far = lax.optimization_barrier((corner_y, *far))
    near.append(corner_y)
    far.append(swap(corner_y, 1))

    count = len(near)
    tile = width // 3
    out = pl.pallas_call(
        functools.partial(last_kernel, count, early),
        out_shape=shape(2, NOCC, nvir),
        in_specs=[SMEM] + [ANY] * (2 + 2 * count),
        out_specs=ANY,
        scratch_shapes=[
            pltpu.VMEM((CORES, room, width), BF16),
            pltpu.VMEM((room - early * CAP, NOCC), BF16),
            pltpu.VMEM(half.shape, F32),
            pltpu.VMEM(late.shape, BF16),
            pltpu.VMEM((2 * NOCC, room), BF16),
            pltpu.VMEM((nvir // tile, 2, NOCC, tile), BF16),
            pltpu.SemaphoreType.DMA((2 + 4 * count + nvir // tile,)),
        ],
        compiler_params=params(30),
        cost_estimate=cost(2e10, 1),
        name="last_product",
    )(me, half, late, *near, *far)
    return out, over[0], code, me, panel


def per_device(*args):
    n = lax.axis_size("shell")
    here, nvir = args[5].shape
    shells = args[3].shape[0]
    sparse = LIVE_DEV * n * EDGE < n * here
    if not (sparse and n == Z * Y * CORES and here <= 256 and here % 16 == 0 and nvir % 768 == 0):
        return from_start(*args)
    out, over, code, me, panel = short_way(*args)

    def again(carry):
        over, _ = carry
        over, code_now, me_now, panel_now, *held = lax.optimization_barrier((over, code, me, tuple(panel), *args[3:]))
        z = me_now[0] // (Y * CORES)
        turned = jnp.stack(panel_now)[jnp.arange(Z, dtype=jnp.int32) ^ z]
        turned = turned.reshape(n, 2, BLK_DEV, EDGE * EDGE).swapaxes(1, 2).reshape(n * BLK_DEV, 2, EDGE * EDGE)
        code_now = jnp.max(code_now, axis=2).reshape(n * BLK_DEV)
        ids = jnp.maximum(code_now, 0)
        pairs = jnp.stack([ids // shells, ids % shells], axis=1)
        return over - 1, long_way(turned, pairs, code_now >= 0, *held)

    return lax.while_loop(lambda carry: carry[0] > 0, again, (over, out))[1]


def solution(mesh):
    placed = (
        P(("groups", "shell"), None, None),
        P(("groups", "shell"), None),
        P(("groups", "shell")),
        P("groups"),
        P(("groups", "shell"), None),
        P(("groups", "shell"), None),
    )
    return jax.shard_map(
        per_device,
        mesh=mesh,
        in_specs=placed,
        out_specs=P(("groups", "shell"), None, None),
        check_vma=False,
    )
```

```python
import functools
import math

import jax
import jax.numpy as jnp
from jax import lax
from jax.experimental import pallas as pl
from jax.experimental.pallas import tpu as pltpu
from jax.sharding import PartitionSpec as P

EDGE = 16
NOCC = 256
BLK_DEV = 8
LIVE_DEV = 4
CAP = 128
Z, Y, CORES = 4, 2, 2
F32 = jnp.float32
BF16 = jnp.bfloat16


def padded_rows(matrix, starts, shell_size):
    offsets = jnp.arange(EDGE, dtype=jnp.int32)
    rows = jnp.minimum(starts[:, None] + offsets[None, :], matrix.shape[0] - 1)
    inside = offsets[None, :] < shell_size[:, None]
    return jnp.where(inside[:, :, None], matrix[rows], jnp.zeros((), matrix.dtype))


def half_transform(slot_rows, pairs, keep, occ_blocks):
    count = slot_rows.shape[0]
    vecs_here = slot_rows.shape[1]
    shells = occ_blocks.shape[0]
    group_size = math.gcd(512, count)
    turns = count // group_size
    shaped = slot_rows.reshape(count, vecs_here, EDGE, EDGE)

    def advance(total, turn):
        first = turn * group_size
        block = lax.dynamic_slice_in_dim(shaped, first, group_size, 0)
        okay = lax.dynamic_slice_in_dim(keep, first, group_size, 0)
        block = jnp.where(okay[:, None, None, None], block, jnp.zeros((), block.dtype))
        row_shell = lax.dynamic_slice_in_dim(pairs[:, 0], first, group_size, 0)
        col_shell = lax.dynamic_slice_in_dim(pairs[:, 1], first, group_size, 0)
        coefs = occ_blocks[row_shell]
        piece = jnp.einsum("kmi,kvmn->kvin", coefs, block, preferred_element_type=jnp.float32)
        return (total.at[col_shell].add(piece), None)

    start_total = jnp.zeros((shells, vecs_here, NOCC, EDGE), jnp.float32)
    half, _ = lax.scan(advance, start_total, jnp.arange(turns, dtype=jnp.int32))
    return half


def long_way(turned, pairs, live, shell_size, occ_coef, vir_coef):
    occ_full = lax.all_gather(occ_coef, "shell", axis=0, tiled=True)
    starts = jnp.cumsum(shell_size) - shell_size
    occ_blocks = padded_rows(occ_full, starts, shell_size)
    half = half_transform(turned, pairs, live, occ_blocks)
    hidden = half.astype(jnp.bfloat16)
    vir_full = lax.all_gather(vir_coef, "shell", axis=0, tiled=True)
    vir_blocks = padded_rows(vir_full, starts, shell_size)
    result = jnp.einsum("svin,sna->via", hidden, vir_blocks, preferred_element_type=jnp.float32)
    return result.astype(jnp.bfloat16)


def from_start(panels, block_pairs, block_count, *rest):
    pairs = lax.all_gather(block_pairs, "shell", axis=0, tiled=True)
    counts = lax.all_gather(block_count, "shell", axis=0, tiled=True)
    turned = lax.all_to_all(panels, "shell", split_axis=1, concat_axis=0, tiled=True)
    position = jnp.arange(turned.shape[0], dtype=jnp.int32)
    live = position % BLK_DEV < counts[position // BLK_DEV]
    return long_way(turned, pairs, live, *rest)


def iota(shape, dim):
    return lax.broadcasted_iota(jnp.int32, shape, dim)


def column_of(row, mask):
    return jnp.sum(jnp.where(mask, row, 0.0), axis=1, keepdims=True)


def row_of(column, mask):
    return jnp.sum(jnp.where(mask, column, 0.0), axis=0, keepdims=True)


def zero_one(mask):
    return jnp.where(mask, 1.0, 0.0)


def lane_value(row, index):
    return jnp.sum(jnp.where(iota(row.shape, 1) == index, row, 0.0), axis=1, keepdims=True)


def one_hots(ids, shells):
    lanes = iota(ids.shape, 1).astype(F32)
    return jnp.concatenate([zero_one(ids == lanes + 128.0 * k) for k in range(shells // 128)], axis=1)


def slot_hots(code, shells):
    code = code.reshape(-1, 128)
    kept = code >= 0
    columns = jnp.where(kept, code % shells, -1).astype(F32)
    return one_hots(columns, shells), one_hots(jnp.where(kept, code // shells, -1).astype(F32), shells)


class Shells:
    def __init__(self, size_row):
        shells = size_row.shape[1]
        sub, lane = iota((shells, shells), 0), iota((shells, shells), 1)
        self.before, self.same = lane < sub, lane == sub
        self.starts = column_of(size_row, self.before)
        self.size = column_of(size_row, self.same)
        self.odd = self.starts - 2.0 * jnp.floor(self.starts * 0.5)


class Used:
    def __init__(self, shells, hot, window):
        self.used = column_of(jnp.max(hot, axis=0, keepdims=True), shells.same)
        self.extra, self.ahead, self.edges = [], [], []
        edge = (iota((hot.shape[1], 128), 1) * window).astype(F32)
        reach = jnp.clip(edge - shells.starts, 0.0, shells.size)
        for parity in range(2):
            extra = 1.0 - shells.odd if parity == 0 else shells.odd
            count = self.used * jnp.floor((shells.size + extra) * 0.5)
            count_row = row_of(count, shells.same)
            self.extra.append(extra)
            self.ahead.append(column_of(count_row, shells.before))
            self.edges.append(jnp.sum(self.used * jnp.floor((reach + extra) * 0.5), axis=0, keepdims=True))


def pack_kernel(vir_ref, occ_ref, panels_ref, *refs):
    outs, (turned_ref,) = refs[:4], refs[4:]
    me = lax.axis_index("shell")
    core, y = lax.rem(me, 2), lax.rem(lax.div(me, 2), 2)
    here, nvir = vir_ref.shape
    rows = here // 2
    width, thin = nvir // CORES, occ_ref.shape[1] // CORES
    turned_ref[...] = jnp.swapaxes(panels_ref[...].astype(F32), 0, 1)
    block = EDGE * EDGE
    for dy in range(2):
        parity = lax.rem(y + dy, 2)
        pick = zero_one(iota((rows, here), 1) == 2 * iota((rows, here), 0) + parity).astype(BF16)
        for dc in range(2):
            half = lax.rem(core + dc, 2)
            out = outs[2 * dy + dc]
            part = vir_ref[:, pl.ds(pl.multiple_of(half * width, 128), width)]
            out[:rows, :width] = jnp.dot(pick, part, preferred_element_type=F32).astype(BF16)
            part = occ_ref[:, pl.ds(pl.multiple_of(half * thin, 128), thin)]
            out[:rows, width:] = jnp.dot(pick, part, preferred_element_type=F32).astype(BF16)
            for z in range(Z):
                device = (z * Y + parity) * CORES + half
                pair = turned_ref[pl.ds(2 * device, 2)].reshape(2 * BLK_DEV, block)
                out[rows:, z * block : (z + 1) * block] = pair.astype(BF16)
            out[rows:, Z * block :] = jnp.zeros((2 * BLK_DEV, out.shape[1] - Z * block), BF16)


def ids_kernel(shells, pairs_ref, count_ref, code_ref):
    code = pairs_ref[1:2, :] + shells * pairs_ref[0:1, :]
    code = jnp.where(iota((1, BLK_DEV), 1) < count_ref[...], code, -1).astype(F32)
    square = (BLK_DEV, BLK_DEV)
    code = column_of(code, iota(square, 0) == iota(square, 1)).astype(jnp.int32)
    code_ref[...] = jnp.broadcast_to(jnp.broadcast_to(code, (BLK_DEV, 128))[None], code_ref.shape)


def pick_kernel(here, code_ref, size_ref, *refs):
    sources, (out_ref, over_ref, me_ref), panel_refs = refs[:4], refs[4:7], refs[7:]
    me = lax.axis_index("shell")
    me_ref[0] = me
    core, y, z = lax.rem(me, 2), lax.rem(lax.div(me, 2), 2), lax.div(me, 4)
    window = CORES * Y * here
    shell_count = size_ref.shape[1]
    shells = Shells(size_ref[...].astype(F32))
    lists = [Used(shells, hot, window) for hot in slot_hots(code_ref[...], shell_count)]
    most = jnp.zeros((1, 1), F32)
    lane = iota((1, 128), 1)
    for chosen in lists:
        for edges in chosen.edges:
            later = jnp.concatenate([edges[:, 1:], edges[:, :1]], axis=1)
            most = jnp.maximum(most, jnp.max(jnp.where(lane < Z, later - edges, 0.0), axis=1, keepdims=True))
    over_ref[0] = jnp.where(jnp.max(most) > CAP, 1, 0).astype(jnp.int32)

    width = out_ref.shape[1] - 128
    even = y == 0
    totals = [jnp.zeros((CAP, width), F32), jnp.zeros((CAP, 128), F32)]
    columns = [slice(0, width), slice(width, width + 128)]
    extra = jnp.where(even, lists[0].extra[0], lists[0].extra[1])
    rows = here // 2
    for k, source in enumerate(sources):
        member = 2 * lax.rem(y + k // 2, 2) + lax.rem(core + k % 2, 2)
        device = 4 * z + member
        for r, panel_ref in enumerate(panel_refs):
            lanes = pl.ds(pl.multiple_of((z ^ r) * (EDGE * EDGE), 128), EDGE * EDGE)
            panel_ref[member] = source[rows:, lanes]
        row = (2 * iota((shell_count, 128), 1) + device * here + y).astype(F32)
        where = row - shells.starts
        inside = (where >= 0.0) & (where < shells.size)
        within = jnp.floor((where + extra) * 0.5)
        for chosen, total, column in zip(lists, range(2), columns):
            ahead = jnp.where(even, chosen.ahead[0], chosen.ahead[1])
            base = lane_value(jnp.where(even, chosen.edges[0], chosen.edges[1]), z)
            place = jnp.where(inside & (chosen.used > 0.0), ahead + within + 1.0, 0.0)
            place = jnp.sum(place, axis=0, keepdims=True)
            place = jnp.where(place > 0.0, place - 1.0 - base, -1.0)
            hot = zero_one(place == iota((CAP, 128), 0).astype(F32)).astype(BF16)
            totals[total] += jnp.dot(
                hot[:, :rows], source[:rows, column], preferred_element_type=F32
            )
    for total, column in zip(totals, columns):
        out_ref[:, column] = total.astype(BF16)


def slot_of(window, chip):
    slot = window ^ chip
    return jnp.where((slot == 3) | (slot == 4), slot ^ 7, slot)


def half_kernel(here, early, code_ref, size_ref, *refs):
    panel_refs, pieces, refs = refs[:Z], refs[Z : Z + 2 * early], refs[Z + 2 * early :]
    half_ref, late_ref, got_ref, occ_ref, part_ref, hot_ref, placed_ref, sems = refs
    me = lax.axis_index("shell")
    core, chip = lax.rem(me, CORES), lax.div(me, CORES)
    z = lax.div(chip, Y)
    width = pieces[0].shape[1] - 128
    copies = []
    for far in range(2):
        half = lax.rem(core + far, CORES)
        for k in range(early):
            at = far * early + k
            target = occ_ref.at[pl.ds(k * CAP, CAP), pl.ds(pl.multiple_of(half * 128, 128), 128)]
            copies.append(pltpu.make_async_copy(pieces[at].at[:, pl.ds(width, 128)], target, sems.at[at]))
    for copy in copies:
        copy.start()
    for r, panel_ref in enumerate(panel_refs):
        got_ref[pl.ds((z ^ r) * (Y * CORES), Y * CORES)] = panel_ref[...]
    window = CORES * Y * here
    shell_count = size_ref.shape[1]
    got = got_ref[...].astype(F32)
    size_row = size_ref[...].astype(F32)
    shells = Shells(size_row)
    got = got_ref[...].astype(F32)
    hots = slot_hots(code_ref[...], shell_count)
    lists = [Used(shells, hot, window) for hot in hots]
    slots = hots[0].shape[0]
    kept = LIVE_DEV * (slots // BLK_DEV)
    alive = jnp.broadcast_to(jnp.sum(hots[0], axis=1, keepdims=True), (slots, slots))
    sub, lane = iota((slots, slots), 0), iota((slots, slots), 1)
    rank = row_of(alive, sub < lane)
    alive_row = row_of(alive, sub == lane)
    take = (rank == iota((kept, slots), 0).astype(F32)) & (alive_row > 0.0)
    take = zero_one(take).astype(BF16)

    def taken(array):
        return jnp.dot(take, array.astype(BF16), preferred_element_type=F32)

    def spread(hot, column):
        value = jnp.sum(hot * row_of(column, shells.same), axis=1, keepdims=True)
        wide = jnp.broadcast_to(value, (kept, 128)).reshape(kept, 1, 128)
        return jnp.broadcast_to(wide, (kept, EDGE, 128)).reshape(kept * EDGE, 128)

    at = iota((kept * EDGE, 128), 0) % EDGE
    step = at.astype(F32)

    def places(hot, chosen):
        hot = taken(hot)
        first, length = spread(hot, shells.starts), spread(hot, shells.size)
        row = first + step
        odd = (row - 2.0 * jnp.floor(row * 0.5)) > 0.0
        place = jnp.where(odd, spread(hot, chosen.ahead[1]), spread(hot, chosen.ahead[0]))
        place += jnp.floor(step * 0.5)
        offsets = [
            [slot_of(w * Y + k, chip).astype(F32) * CAP - lane_value(e, w) for w in range(Z)]
            for k, e in enumerate(chosen.edges)
        ]
        offset = jnp.where(odd, offsets[1][0], offsets[0][0])
        for w in range(1, Z):
            offset = jnp.where(row >= float(window * w), jnp.where(odd, offsets[1][w], offsets[0][w]), offset)
        return jnp.where(step < length, place + offset, -1.0)[:, :1]

    place_c, place_r = places(hots[0], lists[0]), places(hots[1], lists[1])
    span = 16 * EDGE
    s_in, l_in = iota((span, span), 0), iota((span, span), 1)
    keep_m = (l_in // EDGE) == (s_in % EDGE)
    fold = zero_one((s_in % EDGE) == (l_in % EDGE)).astype(BF16)
    same_slot = (s_in // EDGE) == (l_in // EDGE)
    blocks = [taken(got[:, p * BLK_DEV : (p + 1) * BLK_DEV, :].reshape(slots, span)) for p in range(2)]
    lanes = iota((span, half_ref.shape[1]), 1).astype(F32)
    for copy in copies:
        copy.wait()
    occ = occ_ref[...]
    cut = early * CAP
    for g in range(kept // 16):
        rows = slice(g * span, (g + 1) * span)
        r_hot = zero_one(place_r[rows] == lanes).astype(BF16)
        c_hot = zero_one(place_c[rows] == lanes).astype(BF16)
        part_ref[:, rows] = jnp.dot(r_hot[:, :cut], occ, preferred_element_type=F32).T.astype(BF16)
        hot_ref[:, rows] = r_hot[:, cut:].T
        for p in range(2):
            block = blocks[p][g * 16 : (g + 1) * 16].reshape(16, 1, span)
            block = jnp.broadcast_to(block, (16, EDGE, span)).reshape(span, span)
            block = jnp.where(keep_m, block, 0.0).astype(BF16)
            diag = jnp.dot(block, fold, preferred_element_type=F32)
            diag = jnp.where(same_slot, diag, 0.0).astype(BF16)
            placed_ref[p, rows, :] = jnp.dot(diag, c_hot, preferred_element_type=F32).astype(BF16)
    for p in range(2):
        half_ref[p * NOCC : (p + 1) * NOCC, :] = jnp.dot(part_ref[...], placed_ref[p], preferred_element_type=F32)
        late_ref[p] = jnp.dot(hot_ref[...], placed_ref[p], preferred_element_type=F32).astype(BF16)


def last_kernel(count, early, me_ref, part_any, late_any, *refs):
    pieces, (out_any, right_ref, occ_ref, part_ref, late_ref, half_ref, tiles_ref, sems) = refs[: 2 * count], refs[2 * count :]
    width = right_ref.shape[2]
    tile = tiles_ref.shape[3]
    per = width // tile
    core = lax.rem(me_ref[0], CORES)
    first, near, far, results = [], [], [], []

    def copy_of(source, target):
        at = len(first) + len(near) + len(far) + len(results)
        return pltpu.make_async_copy(source, target, sems.at[at])

    first.append(copy_of(part_any, part_ref))
    first.append(copy_of(late_any, late_ref))
    for side in range(2):
        half = lax.rem(core + side, CORES)
        for k in range(early, count):
            target = occ_ref.at[pl.ds((k - early) * CAP, CAP), pl.ds(pl.multiple_of(half * 128, 128), 128)]
            first.append(copy_of(pieces[side * count + k].at[:, pl.ds(width, 128)], target))
    for side, copies in enumerate((near, far)):
        for k in range(count):
            target = right_ref.at[side, pl.ds(k * CAP, CAP), :]
            copies.append(copy_of(pieces[side * count + k].at[:, pl.ds(0, width)], target))
    for copy in (*first, *near, *far):
        copy.start()
    for copy in first:
        copy.wait()
    occ = occ_ref[...].T
    for p in range(2):
        rows = slice(p * NOCC, (p + 1) * NOCC)
        late = jnp.dot(occ, late_ref[p], preferred_element_type=F32)
        half_ref[rows, :] = (part_ref[rows, :] + late).astype(BF16)
    for side, copies in enumerate((near, far)):
        for copy in copies:
            copy.wait()
        base = lax.rem(core + side, CORES) * width
        for t in range(per):
            right = right_ref[side, :, t * tile : (t + 1) * tile]
            total = jnp.dot(half_ref[...], right, preferred_element_type=F32).astype(BF16)
            at = side * per + t
            tiles_ref[at] = total.reshape(tiles_ref.shape[1:])
            columns = pl.ds(pl.multiple_of(base + t * tile, 128), tile)
            results.append(copy_of(tiles_ref.at[at], out_any.at[:, :, columns]))
            results[-1].start()
    for copy in results:
        copy.wait()


VMEM = pl.BlockSpec(memory_space=pltpu.VMEM)
SMEM = pl.BlockSpec(memory_space=pltpu.SMEM)
ANY = pl.BlockSpec(memory_space=pl.ANY)


def shape(*dims, dtype=BF16):
    return jax.ShapeDtypeStruct(dims, dtype)


def params(mib):
    return pltpu.CompilerParams(vmem_limit_bytes=mib << 20)


def cost(flops, nbytes):
    return pl.CostEstimate(flops=int(flops), bytes_accessed=int(nbytes), transcendentals=0)


def short_way(panels, block_pairs, block_count, shell_size, occ_coef, vir_coef):
    n = lax.axis_size("shell")
    here, nvir = vir_coef.shape
    width = nvir // CORES
    packed = width + NOCC // CORES
    room = Z * Y * CAP
    size_row = shell_size.reshape(1, -1)

    def swap(array, bit):
        return lax.ppermute(array, "shell", [(i, i ^ bit) for i in range(n)])

    keep, to_core, to_y, to_both = pl.pallas_call(
        pack_kernel,
        out_shape=[shape(here // 2 + 2 * BLK_DEV, packed)] * 4,
        in_specs=[VMEM] * 3,
        out_specs=[VMEM] * 4,
        scratch_shapes=[pltpu.VMEM((2 * n, BLK_DEV, EDGE * EDGE), F32)],
        compiler_params=params(12),
        cost_estimate=cost(3e8, 3e6),
        name="pack_rows",
    )(vir_coef, occ_coef, panels)
    to_y, to_both, to_core = swap(to_y, 2), swap(to_both, 3), swap(to_core, 1)
    code = pl.pallas_call(
        functools.partial(ids_kernel, size_row.shape[1]),
        out_shape=shape(n, BLK_DEV, 128, dtype=jnp.int32),
        in_specs=[VMEM] * 2,
        out_specs=VMEM,
        compiler_params=params(12),
        cost_estimate=cost(1e4, 1e4),
        name="pack_ids",
    )(block_pairs.T, block_count.reshape(1, 1))
    code = lax.all_to_all(code, "shell", split_axis=0, concat_axis=0, tiled=True)

    mine, over, me, *panel = pl.pallas_call(
        functools.partial(pick_kernel, here),
        out_shape=[shape(CAP, packed), shape(1, dtype=jnp.int32), shape(1, dtype=jnp.int32)]
        + [shape(Y * CORES, 2 * BLK_DEV, EDGE * EDGE)] * Z,
        in_specs=[VMEM] * 6,
        out_specs=[VMEM, SMEM, SMEM] + [VMEM] * Z,
        compiler_params=params(12),
        cost_estimate=cost(3e8, 2e6),
        name="pick_rows",
    )(code, size_row, keep, to_core, to_y, to_both)

    across, mine_y, beside = swap(mine, 8), swap(mine, 2), swap(mine, 4)
    panel = [panel[0]] + [swap(panel[r], 4 * r) for r in range(1, Z)]
    mine_y, panel[1], panel[2] = lax.optimization_barrier((mine_y, panel[1], panel[2]))
    far = [swap(mine, 1), swap(mine_y, 1), swap(beside, 1)]
    across, beside, panel[3], *far = lax.optimization_barrier((across, beside, panel[3], *far))

    corner, beside_y, across_y = swap(across, 4), swap(beside, 2), swap(across, 2)
    near = [mine, mine_y, beside]
    early = len(near)
    slots = LIVE_DEV * n * EDGE
    half, late = pl.pallas_call(
        functools.partial(half_kernel, here, early),
        out_shape=(shape(2 * NOCC, room, dtype=F32), shape(2, room - early * CAP, room)),
        grid=(1,),
        in_specs=[VMEM] * (2 + Z) + [ANY] * (2 * early),
        out_specs=(
            pl.BlockSpec((2 * NOCC, room), lambda i: (0, 0)),
            pl.BlockSpec((2, room - early * CAP, room), lambda i: (0, 0, 0)),
        ),
        scratch_shapes=[
            pltpu.VMEM((n, 2 * BLK_DEV, EDGE * EDGE), BF16),
            pltpu.VMEM((early * CAP, NOCC), BF16),
            pltpu.VMEM((NOCC, slots), BF16),
            pltpu.VMEM((room - early * CAP, slots), BF16),
            pltpu.VMEM((2, slots, room), BF16),
            pltpu.SemaphoreType.DMA((2 * early,)),
        ],
        compiler_params=params(30),
        cost_estimate=cost(7e9, 1),
        name="half_transform",
    )(code, size_row, *panel, *near, *far)
    corner, half, late = lax.optimization_barrier((corner, half, late))
    corner_y = swap(corner, 2)
    near += [across, beside_y, across_y, corner]
    far += [swap(piece, 1) for piece in near[early:]]
    corner_y, *far = lax.optimization_barrier((corner_y, *far))
    near.append(corner_y)
    far.append(swap(corner_y, 1))

    count = len(near)
    tile = width // 3
    out = pl.pallas_call(
        functools.partial(last_kernel, count, early),
        out_shape=shape(2, NOCC, nvir),
        in_specs=[SMEM] + [ANY] * (2 + 2 * count),
        out_specs=ANY,
        scratch_shapes=[
            pltpu.VMEM((CORES, room, width), BF16),
            pltpu.VMEM((room - early * CAP, NOCC), BF16),
            pltpu.VMEM(half.shape, F32),
            pltpu.VMEM(late.shape, BF16),
            pltpu.VMEM((2 * NOCC, room), BF16),
            pltpu.VMEM((nvir // tile, 2, NOCC, tile), BF16),
            pltpu.SemaphoreType.DMA((2 + 4 * count + nvir // tile,)),
        ],
        compiler_params=params(30),
        cost_estimate=cost(2e10, 1),
        name="last_product",
    )(me, half, late, *near, *far)
    return out, over[0], code, me, panel


def per_device(*args):
    n = lax.axis_size("shell")
    here, nvir = args[5].shape
    shells = args[3].shape[0]
    sparse = LIVE_DEV * n * EDGE < n * here
    if not (sparse and n == Z * Y * CORES and here <= 256 and here % 16 == 0 and nvir % 768 == 0):
        return from_start(*args)
    out, over, code, me, panel = short_way(*args)

    def again(carry):
        over, _ = carry
        over, code_now, me_now, panel_now, *held = lax.optimization_barrier((over, code, me, tuple(panel), *args[3:]))
        z = me_now[0] // (Y * CORES)
        turned = jnp.stack(panel_now)[jnp.arange(Z, dtype=jnp.int32) ^ z]
        turned = turned.reshape(n, 2, BLK_DEV, EDGE * EDGE).swapaxes(1, 2).reshape(n * BLK_DEV, 2, EDGE * EDGE)
        code_now = jnp.max(code_now, axis=2).reshape(n * BLK_DEV)
        ids = jnp.maximum(code_now, 0)
        pairs = jnp.stack([ids // shells, ids % shells], axis=1)
        return over - 1, long_way(turned, pairs, code_now >= 0, *held)

    return lax.while_loop(lambda carry: carry[0] > 0, again, (over, out))[1]


def solution(mesh):
    placed = (
        P(("groups", "shell"), None, None),
        P(("groups", "shell"), None),
        P(("groups", "shell")),
        P("groups"),
        P(("groups", "shell"), None),
        P(("groups", "shell"), None),
    )
    return jax.shard_map(
        per_device,
        mesh=mesh,
        in_specs=placed,
        out_specs=P(("groups", "shell"), None, None),
        check_vma=False,
    )
```

```python
import functools
import math

import jax
import jax.numpy as jnp
from jax import lax
from jax.experimental import pallas as pl
from jax.experimental.pallas import tpu as pltpu
from jax.sharding import PartitionSpec as P

EDGE = 16
NOCC = 256
BLK_DEV = 8
LIVE_DEV = 4
CAP = 128
Z, Y, CORES = 4, 2, 2
F32 = jnp.float32
BF16 = jnp.bfloat16


def padded_rows(matrix, starts, shell_size):
    offsets = jnp.arange(EDGE, dtype=jnp.int32)
    rows = jnp.minimum(starts[:, None] + offsets[None, :], matrix.shape[0] - 1)
    inside = offsets[None, :] < shell_size[:, None]
    return jnp.where(inside[:, :, None], matrix[rows], jnp.zeros((), matrix.dtype))


def half_transform(slot_rows, pairs, keep, occ_blocks):
    count = slot_rows.shape[0]
    vecs_here = slot_rows.shape[1]
    shells = occ_blocks.shape[0]
    group_size = math.gcd(512, count)
    turns = count // group_size
    shaped = slot_rows.reshape(count, vecs_here, EDGE, EDGE)

    def advance(total, turn):
        first = turn * group_size
        block = lax.dynamic_slice_in_dim(shaped, first, group_size, 0)
        okay = lax.dynamic_slice_in_dim(keep, first, group_size, 0)
        block = jnp.where(okay[:, None, None, None], block, jnp.zeros((), block.dtype))
        row_shell = lax.dynamic_slice_in_dim(pairs[:, 0], first, group_size, 0)
        col_shell = lax.dynamic_slice_in_dim(pairs[:, 1], first, group_size, 0)
        coefs = occ_blocks[row_shell]
        piece = jnp.einsum("kmi,kvmn->kvin", coefs, block, preferred_element_type=jnp.float32)
        return (total.at[col_shell].add(piece), None)

    start_total = jnp.zeros((shells, vecs_here, NOCC, EDGE), jnp.float32)
    half, _ = lax.scan(advance, start_total, jnp.arange(turns, dtype=jnp.int32))
    return half


def long_way(turned, pairs, live, shell_size, occ_coef, vir_coef):
    occ_full = lax.all_gather(occ_coef, "shell", axis=0, tiled=True)
    starts = jnp.cumsum(shell_size) - shell_size
    occ_blocks = padded_rows(occ_full, starts, shell_size)
    half = half_transform(turned, pairs, live, occ_blocks)
    hidden = half.astype(jnp.bfloat16)
    vir_full = lax.all_gather(vir_coef, "shell", axis=0, tiled=True)
    vir_blocks = padded_rows(vir_full, starts, shell_size)
    result = jnp.einsum("svin,sna->via", hidden, vir_blocks, preferred_element_type=jnp.float32)
    return result.astype(jnp.bfloat16)


def from_start(panels, block_pairs, block_count, *rest):
    pairs = lax.all_gather(block_pairs, "shell", axis=0, tiled=True)
    counts = lax.all_gather(block_count, "shell", axis=0, tiled=True)
    turned = lax.all_to_all(panels, "shell", split_axis=1, concat_axis=0, tiled=True)
    position = jnp.arange(turned.shape[0], dtype=jnp.int32)
    live = position % BLK_DEV < counts[position // BLK_DEV]
    return long_way(turned, pairs, live, *rest)


def iota(shape, dim):
    return lax.broadcasted_iota(jnp.int32, shape, dim)


def column_of(row, mask):
    return jnp.sum(jnp.where(mask, row, 0.0), axis=1, keepdims=True)


def row_of(column, mask):
    return jnp.sum(jnp.where(mask, column, 0.0), axis=0, keepdims=True)


def zero_one(mask):
    return jnp.where(mask, 1.0, 0.0)


def lane_value(row, index):
    return jnp.sum(jnp.where(iota(row.shape, 1) == index, row, 0.0), axis=1, keepdims=True)


def one_hots(ids, shells):
    lanes = iota(ids.shape, 1).astype(F32)
    return jnp.concatenate([zero_one(ids == lanes + 128.0 * k) for k in range(shells // 128)], axis=1)


def slot_hots(got, shells):
    sources, slots = got.shape[0], got.shape[0] * BLK_DEV
    rows = got[:, 2 * BLK_DEV :, :].reshape(sources, got.shape[2]).astype(BF16)
    owner = zero_one(iota((slots, sources), 0) // BLK_DEV == iota((slots, sources), 1)).astype(BF16)
    ids = jnp.dot(owner, rows, preferred_element_type=F32)
    slot, lane = iota(ids.shape, 0) % BLK_DEV, iota(ids.shape, 1)
    columns, rows = (
        jnp.broadcast_to(column_of(ids, lane == slot + first), (slots, 128)) for first in (0, BLK_DEV)
    )
    return one_hots(columns, shells), one_hots(rows, shells)


class Shells:
    def __init__(self, size_row):
        shells = size_row.shape[1]
        sub, lane = iota((shells, shells), 0), iota((shells, shells), 1)
        self.before, self.same = lane < sub, lane == sub
        self.starts = column_of(size_row, self.before)
        self.size = column_of(size_row, self.same)
        self.odd = self.starts - 2.0 * jnp.floor(self.starts * 0.5)


class Used:
    def __init__(self, shells, hot, window):
        self.used = column_of(jnp.max(hot, axis=0, keepdims=True), shells.same)
        self.extra, self.ahead, self.edges = [], [], []
        edge = (iota((hot.shape[1], 128), 1) * window).astype(F32)
        reach = jnp.clip(edge - shells.starts, 0.0, shells.size)
        for parity in range(2):
            extra = 1.0 - shells.odd if parity == 0 else shells.odd
            count = self.used * jnp.floor((shells.size + extra) * 0.5)
            count_row = row_of(count, shells.same)
            self.extra.append(extra)
            self.ahead.append(column_of(count_row, shells.before))
            self.edges.append(jnp.sum(self.used * jnp.floor((reach + extra) * 0.5), axis=0, keepdims=True))


def pack_kernel(vir_ref, occ_ref, *outs):
    me = lax.axis_index("shell")
    core, y = lax.rem(me, 2), lax.rem(lax.div(me, 2), 2)
    here, nvir = vir_ref.shape
    width, thin = nvir // CORES, occ_ref.shape[1] // CORES
    for dy in range(2):
        parity = lax.rem(y + dy, 2)
        pick = zero_one(iota((here // 2, here), 1) == 2 * iota((here // 2, here), 0) + parity).astype(BF16)
        for dc in range(2):
            half = lax.rem(core + dc, 2)
            out = outs[2 * dy + dc]
            part = vir_ref[:, pl.ds(pl.multiple_of(half * width, 128), width)]
            out[:, :width] = jnp.dot(pick, part, preferred_element_type=F32).astype(BF16)
            part = occ_ref[:, pl.ds(pl.multiple_of(half * thin, 128), thin)]
            out[:, width:] = jnp.dot(pick, part, preferred_element_type=F32).astype(BF16)


def send_kernel(pairs_ref, count_ref, panels_ref, send_ref):
    n = send_ref.shape[0]
    turned = jnp.swapaxes(panels_ref[...].astype(F32), 0, 1)
    send_ref[:, : 2 * BLK_DEV, :] = turned.reshape(n, 2 * BLK_DEV, EDGE * EDGE).astype(BF16)
    kept = iota((1, BLK_DEV), 1) < count_ref[...]
    square, wide = (BLK_DEV, BLK_DEV), (BLK_DEV, EDGE * EDGE)
    same = iota(square, 0) == iota(square, 1)
    row = jnp.zeros((1, EDGE * EDGE), F32)
    for first, k in ((0, 1), (BLK_DEV, 0)):
        ids = column_of(jnp.where(kept, pairs_ref[k : k + 1, :], -1).astype(F32), same)
        row += row_of(ids, iota(wide, 1) == iota(wide, 0) + first)
    send_ref[:, 2 * BLK_DEV :, :] = jnp.broadcast_to(row[None], (n, 1, EDGE * EDGE)).astype(BF16)


def pick_kernel(here, got_ref, size_ref, *refs):
    sources, (out_ref, over_ref, me_ref) = refs[:4], refs[4:]
    me = lax.axis_index("shell")
    me_ref[0] = me
    core, y, z = lax.rem(me, 2), lax.rem(lax.div(me, 2), 2), lax.div(me, 4)
    window = CORES * Y * here
    shell_count = size_ref.shape[1]
    shells = Shells(size_ref[...].astype(F32))
    lists = [Used(shells, hot, window) for hot in slot_hots(got_ref[...].astype(F32), shell_count)]
    most = jnp.zeros((1, 1), F32)
    lane = iota((1, 128), 1)
    for chosen in lists:
        for edges in chosen.edges:
            later = jnp.concatenate([edges[:, 1:], edges[:, :1]], axis=1)
            most = jnp.maximum(most, jnp.max(jnp.where(lane < Z, later - edges, 0.0), axis=1, keepdims=True))
    over_ref[0] = jnp.where(jnp.max(most) > CAP, 1, 0).astype(jnp.int32)

    width = out_ref.shape[1] - 128
    even = y == 0
    totals = [jnp.zeros((CAP, width), F32), jnp.zeros((CAP, 128), F32)]
    columns = [slice(0, width), slice(width, width + 128)]
    extra = jnp.where(even, lists[0].extra[0], lists[0].extra[1])
    rows = here // 2
    for k, source in enumerate(sources):
        device = 4 * z + 2 * lax.rem(y + k // 2, 2) + lax.rem(core + k % 2, 2)
        row = (2 * iota((shell_count, 128), 1) + device * here + y).astype(F32)
        where = row - shells.starts
        inside = (where >= 0.0) & (where < shells.size)
        within = jnp.floor((where + extra) * 0.5)
        for chosen, total, column in zip(lists, range(2), columns):
            ahead = jnp.where(even, chosen.ahead[0], chosen.ahead[1])
            base = lane_value(jnp.where(even, chosen.edges[0], chosen.edges[1]), z)
            place = jnp.where(inside & (chosen.used > 0.0), ahead + within + 1.0, 0.0)
            place = jnp.sum(place, axis=0, keepdims=True)
            place = jnp.where(place > 0.0, place - 1.0 - base, -1.0)
            hot = zero_one(place == iota((CAP, 128), 0).astype(F32)).astype(BF16)
            totals[total] += jnp.dot(
                hot[:, :rows], source[:, column], preferred_element_type=F32
            )
    for total, column in zip(totals, columns):
        out_ref[:, column] = total.astype(BF16)


def slot_of(window, chip):
    slot = window ^ chip
    return jnp.where((slot == 3) | (slot == 4), slot ^ 7, slot)


def half_kernel(here, early, got_ref, size_ref, *refs):
    pieces, refs = refs[: 2 * early], refs[2 * early :]
    half_ref, late_ref, panels_ref, ids_ref, occ_ref, part_ref, hot_ref, placed_ref, sems = refs
    me = lax.axis_index("shell")
    core, chip = lax.rem(me, CORES), lax.div(me, CORES)
    width = pieces[0].shape[1] - 128
    copies = []
    for far in range(2):
        half = lax.rem(core + far, CORES)
        for k in range(early):
            at = far * early + k
            target = occ_ref.at[pl.ds(k * CAP, CAP), pl.ds(pl.multiple_of(half * 128, 128), 128)]
            copies.append(pltpu.make_async_copy(pieces[at].at[:, pl.ds(width, 128)], target, sems.at[at]))
    for copy in copies:
        copy.start()
    window = CORES * Y * here
    shell_count = size_ref.shape[1]
    got = got_ref[...].astype(F32)
    size_row = size_ref[...].astype(F32)
    shells = Shells(size_row)
    got = got_ref[...].astype(F32)
    panels_ref[...] = got[:, : 2 * BLK_DEV, :].astype(BF16)
    ids_ref[...] = got[:, 2 * BLK_DEV :, :].reshape(ids_ref.shape)
    hots = slot_hots(got, shell_count)
    lists = [Used(shells, hot, window) for hot in hots]
    slots = hots[0].shape[0]
    kept = LIVE_DEV * (slots // BLK_DEV)
    alive = jnp.broadcast_to(jnp.sum(hots[0], axis=1, keepdims=True), (slots, slots))
    sub, lane = iota((slots, slots), 0), iota((slots, slots), 1)
    rank = row_of(alive, sub < lane)
    alive_row = row_of(alive, sub == lane)
    take = (rank == iota((kept, slots), 0).astype(F32)) & (alive_row > 0.0)
    take = zero_one(take).astype(BF16)

    def taken(array):
        return jnp.dot(take, array.astype(BF16), preferred_element_type=F32)

    def spread(hot, column):
        value = jnp.sum(hot * row_of(column, shells.same), axis=1, keepdims=True)
        wide = jnp.broadcast_to(value, (kept, 128)).reshape(kept, 1, 128)
        return jnp.broadcast_to(wide, (kept, EDGE, 128)).reshape(kept * EDGE, 128)

    at = iota((kept * EDGE, 128), 0) % EDGE
    step = at.astype(F32)

    def places(hot, chosen):
        hot = taken(hot)
        first, length = spread(hot, shells.starts), spread(hot, shells.size)
        row = first + step
        odd = (row - 2.0 * jnp.floor(row * 0.5)) > 0.0
        place = jnp.where(odd, spread(hot, chosen.ahead[1]), spread(hot, chosen.ahead[0]))
        place += jnp.floor(step * 0.5)
        offsets = [
            [slot_of(w * Y + k, chip).astype(F32) * CAP - lane_value(e, w) for w in range(Z)]
            for k, e in enumerate(chosen.edges)
        ]
        offset = jnp.where(odd, offsets[1][0], offsets[0][0])
        for w in range(1, Z):
            offset = jnp.where(row >= float(window * w), jnp.where(odd, offsets[1][w], offsets[0][w]), offset)
        return jnp.where(step < length, place + offset, -1.0)[:, :1]

    place_c, place_r = places(hots[0], lists[0]), places(hots[1], lists[1])
    span = 16 * EDGE
    s_in, l_in = iota((span, span), 0), iota((span, span), 1)
    keep_m = (l_in // EDGE) == (s_in % EDGE)
    fold = zero_one((s_in % EDGE) == (l_in % EDGE)).astype(BF16)
    same_slot = (s_in // EDGE) == (l_in // EDGE)
    blocks = [taken(got[:, p * BLK_DEV : (p + 1) * BLK_DEV, :].reshape(slots, span)) for p in range(2)]
    lanes = iota((span, half_ref.shape[1]), 1).astype(F32)
    for copy in copies:
        copy.wait()
    occ = occ_ref[...]
    cut = early * CAP
    for g in range(kept // 16):
        rows = slice(g * span, (g + 1) * span)
        r_hot = zero_one(place_r[rows] == lanes).astype(BF16)
        c_hot = zero_one(place_c[rows] == lanes).astype(BF16)
        part_ref[:, rows] = jnp.dot(r_hot[:, :cut], occ, preferred_element_type=F32).T.astype(BF16)
        hot_ref[:, rows] = r_hot[:, cut:].T
        for p in range(2):
            block = blocks[p][g * 16 : (g + 1) * 16].reshape(16, 1, span)
            block = jnp.broadcast_to(block, (16, EDGE, span)).reshape(span, span)
            block = jnp.where(keep_m, block, 0.0).astype(BF16)
            diag = jnp.dot(block, fold, preferred_element_type=F32)
            diag = jnp.where(same_slot, diag, 0.0).astype(BF16)
            placed_ref[p, rows, :] = jnp.dot(diag, c_hot, preferred_element_type=F32).astype(BF16)
    for p in range(2):
        half_ref[p * NOCC : (p + 1) * NOCC, :] = jnp.dot(part_ref[...], placed_ref[p], preferred_element_type=F32)
        late_ref[p] = jnp.dot(hot_ref[...], placed_ref[p], preferred_element_type=F32).astype(BF16)


def last_kernel(count, early, me_ref, part_any, late_any, *refs):
    pieces, (out_any, right_ref, occ_ref, part_ref, late_ref, half_ref, tiles_ref, sems) = refs[: 2 * count], refs[2 * count :]
    width = right_ref.shape[2]
    tile = tiles_ref.shape[3]
    per = width // tile
    core = lax.rem(me_ref[0], CORES)
    first, near, far, results = [], [], [], []

    def copy_of(source, target):
        at = len(first) + len(near) + len(far) + len(results)
        return pltpu.make_async_copy(source, target, sems.at[at])

    first.append(copy_of(part_any, part_ref))
    first.append(copy_of(late_any, late_ref))
    for side in range(2):
        half = lax.rem(core + side, CORES)
        for k in range(early, count):
            target = occ_ref.at[pl.ds((k - early) * CAP, CAP), pl.ds(pl.multiple_of(half * 128, 128), 128)]
            first.append(copy_of(pieces[side * count + k].at[:, pl.ds(width, 128)], target))
    for side, copies in enumerate((near, far)):
        for k in range(count):
            target = right_ref.at[side, pl.ds(k * CAP, CAP), :]
            copies.append(copy_of(pieces[side * count + k].at[:, pl.ds(0, width)], target))
    for copy in (*first, *near, *far):
        copy.start()
    for copy in first:
        copy.wait()
    occ = occ_ref[...].T
    for p in range(2):
        rows = slice(p * NOCC, (p + 1) * NOCC)
        late = jnp.dot(occ, late_ref[p], preferred_element_type=F32)
        half_ref[rows, :] = (part_ref[rows, :] + late).astype(BF16)
    for side, copies in enumerate((near, far)):
        for copy in copies:
            copy.wait()
        base = lax.rem(core + side, CORES) * width
        for t in range(per):
            right = right_ref[side, :, t * tile : (t + 1) * tile]
            total = jnp.dot(half_ref[...], right, preferred_element_type=F32).astype(BF16)
            at = side * per + t
            tiles_ref[at] = total.reshape(tiles_ref.shape[1:])
            columns = pl.ds(pl.multiple_of(base + t * tile, 128), tile)
            results.append(copy_of(tiles_ref.at[at], out_any.at[:, :, columns]))
            results[-1].start()
    for copy in results:
        copy.wait()


VMEM = pl.BlockSpec(memory_space=pltpu.VMEM)
SMEM = pl.BlockSpec(memory_space=pltpu.SMEM)
ANY = pl.BlockSpec(memory_space=pl.ANY)


def shape(*dims, dtype=BF16):
    return jax.ShapeDtypeStruct(dims, dtype)


def params(mib):
    return pltpu.CompilerParams(vmem_limit_bytes=mib << 20)


def cost(flops, nbytes):
    return pl.CostEstimate(flops=int(flops), bytes_accessed=int(nbytes), transcendentals=0)


def short_way(panels, block_pairs, block_count, shell_size, occ_coef, vir_coef):
    n = lax.axis_size("shell")
    here, nvir = vir_coef.shape
    width = nvir // CORES
    packed = width + NOCC // CORES
    room = Z * Y * CAP
    size_row = shell_size.reshape(1, -1)

    def swap(array, bit):
        return lax.ppermute(array, "shell", [(i, i ^ bit) for i in range(n)])

    keep, to_core, to_y, to_both = pl.pallas_call(
        pack_kernel,
        out_shape=[shape(here // 2, packed)] * 4,
        in_specs=[VMEM] * 2,
        out_specs=[VMEM] * 4,
        compiler_params=params(12),
        cost_estimate=cost(3e8, 3e6),
        name="pack_rows",
    )(vir_coef, occ_coef)
    to_y, to_both, to_core = swap(to_y, 2), swap(to_both, 3), swap(to_core, 1)
    send = pl.pallas_call(
        send_kernel,
        out_shape=shape(n, 2 * BLK_DEV + 1, EDGE * EDGE),
        in_specs=[VMEM] * 3,
        out_specs=VMEM,
        compiler_params=params(12),
        cost_estimate=cost(1e6, 5e5),
        name="pack_panels",
    )(block_pairs.T, block_count.reshape(1, 1), panels)
    got = lax.all_to_all(send, "shell", split_axis=0, concat_axis=0, tiled=True)

    mine, over, me = pl.pallas_call(
        functools.partial(pick_kernel, here),
        out_shape=(shape(CAP, packed), shape(1, dtype=jnp.int32), shape(1, dtype=jnp.int32)),
        in_specs=[VMEM] * 6,
        out_specs=(VMEM, SMEM, SMEM),
        compiler_params=params(12),
        cost_estimate=cost(3e8, 2e6),
        name="pick_rows",
    )(got, size_row, keep, to_core, to_y, to_both)

    across, mine_y, beside = swap(mine, 8), swap(mine, 2), swap(mine, 4)
    far = [swap(mine, 1), swap(mine_y, 1), swap(beside, 1)]
    across, mine_y, beside, *far = lax.optimization_barrier((across, mine_y, beside, *far))

    corner, beside_y, across_y = swap(across, 4), swap(beside, 2), swap(across, 2)
    near = [mine, mine_y, beside]
    early = len(near)
    slots = LIVE_DEV * n * EDGE
    half, late, got_panels, got_ids = pl.pallas_call(
        functools.partial(half_kernel, here, early),
        out_shape=(
            shape(2 * NOCC, room, dtype=F32),
            shape(2, room - early * CAP, room),
            shape(n, 2 * BLK_DEV, EDGE * EDGE),
            shape(n, EDGE * EDGE, dtype=F32),
        ),
        grid=(1,),
        in_specs=[VMEM] * 2 + [ANY] * (2 * early),
        out_specs=(
            pl.BlockSpec((2 * NOCC, room), lambda i: (0, 0)),
            pl.BlockSpec((2, room - early * CAP, room), lambda i: (0, 0, 0)),
            pl.BlockSpec((n, 2 * BLK_DEV, EDGE * EDGE), lambda i: (0, 0, 0)),
            pl.BlockSpec((n, EDGE * EDGE), lambda i: (0, 0)),
        ),
        scratch_shapes=[
            pltpu.VMEM((early * CAP, NOCC), BF16),
            pltpu.VMEM((NOCC, slots), BF16),
            pltpu.VMEM((room - early * CAP, slots), BF16),
            pltpu.VMEM((2, slots, room), BF16),
            pltpu.SemaphoreType.DMA((2 * early,)),
        ],
        compiler_params=params(30),
        cost_estimate=cost(7e9, 1),
        name="half_transform",
    )(got, size_row, *near, *far)
    corner, half, late = lax.optimization_barrier((corner, half, late))
    corner_y = swap(corner, 2)
    near += [across, beside_y, across_y, corner]
    far += [swap(piece, 1) for piece in near[early:]]
    corner_y, *far = lax.optimization_barrier((corner_y, *far))
    near.append(corner_y)
    far.append(swap(corner_y, 1))

    count = len(near)
    tile = width // 3
    out = pl.pallas_call(
        functools.partial(last_kernel, count, early),
        out_shape=shape(2, NOCC, nvir),
        in_specs=[SMEM] + [ANY] * (2 + 2 * count),
        out_specs=ANY,
        scratch_shapes=[
            pltpu.VMEM((CORES, room, width), BF16),
            pltpu.VMEM((room - early * CAP, NOCC), BF16),
            pltpu.VMEM(half.shape, F32),
            pltpu.VMEM(late.shape, BF16),
            pltpu.VMEM((2 * NOCC, room), BF16),
            pltpu.VMEM((nvir // tile, 2, NOCC, tile), BF16),
            pltpu.SemaphoreType.DMA((2 + 4 * count + nvir // tile,)),
        ],
        compiler_params=params(30),
        cost_estimate=cost(2e10, 1),
        name="last_product",
    )(me, half, late, *near, *far)
    return out, over[0], got_panels, got_ids


def per_device(*args):
    n = lax.axis_size("shell")
    here, nvir = args[5].shape
    sparse = LIVE_DEV * n * EDGE < n * here
    if not (sparse and n == Z * Y * CORES and here <= 256 and here % 16 == 0 and nvir % 768 == 0):
        return from_start(*args)
    out, over, got_panels, got_ids = short_way(*args)

    def again(carry):
        over, _ = carry
        over, turned, ids, *held = lax.optimization_barrier((over, got_panels, got_ids, *args[3:]))
        turned = turned.reshape(n, 2, BLK_DEV, EDGE * EDGE).swapaxes(1, 2).reshape(n * BLK_DEV, 2, EDGE * EDGE)
        ids = ids[:, : 2 * BLK_DEV].astype(jnp.int32)
        columns, rows = ids[:, :BLK_DEV].reshape(n * BLK_DEV), ids[:, BLK_DEV:].reshape(n * BLK_DEV)
        pairs = jnp.maximum(jnp.stack([rows, columns], axis=1), 0)
        return over - 1, long_way(turned, pairs, columns >= 0, *held)

    return lax.while_loop(lambda carry: carry[0] > 0, again, (over, out))[1]


def solution(mesh):
    placed = (
        P(("groups", "shell"), None, None),
        P(("groups", "shell"), None),
        P(("groups", "shell")),
        P("groups"),
        P(("groups", "shell"), None),
        P(("groups", "shell"), None),
    )
    return jax.shard_map(
        per_device,
        mesh=mesh,
        in_specs=placed,
        out_specs=P(("groups", "shell"), None, None),
        check_vma=False,
    )
```

```python
import functools
import math

import jax
import jax.numpy as jnp
from jax import lax
from jax.experimental import pallas as pl
from jax.experimental.pallas import tpu as pltpu
from jax.sharding import PartitionSpec as P

EDGE = 16
NOCC = 256
BLK_DEV = 8
LIVE_DEV = 4
CAP = 128
Z, Y, CORES = 4, 2, 2
F32 = jnp.float32
BF16 = jnp.bfloat16


def padded_rows(matrix, starts, shell_size):
    offsets = jnp.arange(EDGE, dtype=jnp.int32)
    rows = jnp.minimum(starts[:, None] + offsets[None, :], matrix.shape[0] - 1)
    inside = offsets[None, :] < shell_size[:, None]
    return jnp.where(inside[:, :, None], matrix[rows], jnp.zeros((), matrix.dtype))


def half_transform(slot_rows, pairs, keep, occ_blocks):
    count = slot_rows.shape[0]
    vecs_here = slot_rows.shape[1]
    shells = occ_blocks.shape[0]
    group_size = math.gcd(512, count)
    turns = count // group_size
    shaped = slot_rows.reshape(count, vecs_here, EDGE, EDGE)

    def advance(total, turn):
        first = turn * group_size
        block = lax.dynamic_slice_in_dim(shaped, first, group_size, 0)
        okay = lax.dynamic_slice_in_dim(keep, first, group_size, 0)
        block = jnp.where(okay[:, None, None, None], block, jnp.zeros((), block.dtype))
        row_shell = lax.dynamic_slice_in_dim(pairs[:, 0], first, group_size, 0)
        col_shell = lax.dynamic_slice_in_dim(pairs[:, 1], first, group_size, 0)
        coefs = occ_blocks[row_shell]
        piece = jnp.einsum("kmi,kvmn->kvin", coefs, block, preferred_element_type=jnp.float32)
        return (total.at[col_shell].add(piece), None)

    start_total = jnp.zeros((shells, vecs_here, NOCC, EDGE), jnp.float32)
    half, _ = lax.scan(advance, start_total, jnp.arange(turns, dtype=jnp.int32))
    return half


def long_way(turned, pairs, live, shell_size, occ_coef, vir_coef):
    occ_full = lax.all_gather(occ_coef, "shell", axis=0, tiled=True)
    starts = jnp.cumsum(shell_size) - shell_size
    occ_blocks = padded_rows(occ_full, starts, shell_size)
    half = half_transform(turned, pairs, live, occ_blocks)
    hidden = half.astype(jnp.bfloat16)
    vir_full = lax.all_gather(vir_coef, "shell", axis=0, tiled=True)
    vir_blocks = padded_rows(vir_full, starts, shell_size)
    result = jnp.einsum("svin,sna->via", hidden, vir_blocks, preferred_element_type=jnp.float32)
    return result.astype(jnp.bfloat16)


def from_start(panels, block_pairs, block_count, *rest):
    pairs = lax.all_gather(block_pairs, "shell", axis=0, tiled=True)
    counts = lax.all_gather(block_count, "shell", axis=0, tiled=True)
    turned = lax.all_to_all(panels, "shell", split_axis=1, concat_axis=0, tiled=True)
    position = jnp.arange(turned.shape[0], dtype=jnp.int32)
    live = position % BLK_DEV < counts[position // BLK_DEV]
    return long_way(turned, pairs, live, *rest)


def iota(shape, dim):
    return lax.broadcasted_iota(jnp.int32, shape, dim)


def column_of(row, mask):
    return jnp.sum(jnp.where(mask, row, 0.0), axis=1, keepdims=True)


def row_of(column, mask):
    return jnp.sum(jnp.where(mask, column, 0.0), axis=0, keepdims=True)


def zero_one(mask):
    return jnp.where(mask, 1.0, 0.0)


def lane_value(row, index):
    return jnp.sum(jnp.where(iota(row.shape, 1) == index, row, 0.0), axis=1, keepdims=True)


def one_hots(ids, shells):
    lanes = iota(ids.shape, 1).astype(F32)
    return jnp.concatenate([zero_one(ids == lanes + 128.0 * k) for k in range(shells // 128)], axis=1)


def slot_hots(code, shells):
    code = code.reshape(-1, 128)
    kept = code >= 0
    columns = jnp.where(kept, code % shells, -1).astype(F32)
    return one_hots(columns, shells), one_hots(jnp.where(kept, code // shells, -1).astype(F32), shells)


class Shells:
    def __init__(self, size_row):
        shells = size_row.shape[1]
        sub, lane = iota((shells, shells), 0), iota((shells, shells), 1)
        self.before, self.same = lane < sub, lane == sub
        self.starts = column_of(size_row, self.before)
        self.size = column_of(size_row, self.same)
        self.odd = self.starts - 2.0 * jnp.floor(self.starts * 0.5)


class Used:
    def __init__(self, shells, hot, window):
        self.used = column_of(jnp.max(hot, axis=0, keepdims=True), shells.same)
        self.extra, self.ahead, self.edges = [], [], []
        edge = (iota((hot.shape[1], 128), 1) * window).astype(F32)
        reach = jnp.clip(edge - shells.starts, 0.0, shells.size)
        for parity in range(2):
            extra = 1.0 - shells.odd if parity == 0 else shells.odd
            count = self.used * jnp.floor((shells.size + extra) * 0.5)
            count_row = row_of(count, shells.same)
            self.extra.append(extra)
            self.ahead.append(column_of(count_row, shells.before))
            self.edges.append(jnp.sum(self.used * jnp.floor((reach + extra) * 0.5), axis=0, keepdims=True))


def pack_kernel(vir_ref, occ_ref, panels_ref, *refs):
    outs, (turned_ref,) = refs[:4], refs[4:]
    me = lax.axis_index("shell")
    core, y = lax.rem(me, 2), lax.rem(lax.div(me, 2), 2)
    here, nvir = vir_ref.shape
    rows = here // 2
    width, thin = nvir // CORES, occ_ref.shape[1] // CORES
    turned_ref[...] = jnp.swapaxes(panels_ref[...].astype(F32), 0, 1)
    block = EDGE * EDGE
    for dy in range(2):
        parity = lax.rem(y + dy, 2)
        pick = zero_one(iota((rows, here), 1) == 2 * iota((rows, here), 0) + parity).astype(BF16)
        for dc in range(2):
            half = lax.rem(core + dc, 2)
            out = outs[2 * dy + dc]
            part = vir_ref[:, pl.ds(pl.multiple_of(half * width, 128), width)]
            out[:rows, :width] = jnp.dot(pick, part, preferred_element_type=F32).astype(BF16)
            part = occ_ref[:, pl.ds(pl.multiple_of(half * thin, 128), thin)]
            out[:rows, width:] = jnp.dot(pick, part, preferred_element_type=F32).astype(BF16)
            for z in range(Z):
                device = (z * Y + parity) * CORES + half
                pair = turned_ref[pl.ds(2 * device, 2)].reshape(2 * BLK_DEV, block)
                out[rows:, z * block : (z + 1) * block] = pair.astype(BF16)
            out[rows:, Z * block :] = jnp.zeros((2 * BLK_DEV, out.shape[1] - Z * block), BF16)


def ids_kernel(shells, pairs_ref, count_ref, code_ref):
    code = pairs_ref[1:2, :] + shells * pairs_ref[0:1, :]
    code = jnp.where(iota((1, BLK_DEV), 1) < count_ref[...], code, -1).astype(F32)
    square = (BLK_DEV, BLK_DEV)
    code = column_of(code, iota(square, 0) == iota(square, 1)).astype(jnp.int32)
    code_ref[...] = jnp.broadcast_to(jnp.broadcast_to(code, (BLK_DEV, 128))[None], code_ref.shape)


def pick_kernel(here, code_ref, size_ref, *refs):
    sources, (out_ref, over_ref, me_ref), panel_refs = refs[:4], refs[4:7], refs[7:]
    me = lax.axis_index("shell")
    me_ref[0] = me
    core, y, z = lax.rem(me, 2), lax.rem(lax.div(me, 2), 2), lax.div(me, 4)
    window = CORES * Y * here
    shell_count = size_ref.shape[1]
    shells = Shells(size_ref[...].astype(F32))
    lists = [Used(shells, hot, window) for hot in slot_hots(code_ref[...], shell_count)]
    most = jnp.zeros((1, 1), F32)
    lane = iota((1, 128), 1)
    for chosen in lists:
        for edges in chosen.edges:
            later = jnp.concatenate([edges[:, 1:], edges[:, :1]], axis=1)
            most = jnp.maximum(most, jnp.max(jnp.where(lane < Z, later - edges, 0.0), axis=1, keepdims=True))
    over_ref[0] = jnp.where(jnp.max(most) > CAP, 1, 0).astype(jnp.int32)

    width = out_ref.shape[1] - 128
    even = y == 0
    totals = [jnp.zeros((CAP, width), F32), jnp.zeros((CAP, 128), F32)]
    columns = [slice(0, width), slice(width, width + 128)]
    extra = jnp.where(even, lists[0].extra[0], lists[0].extra[1])
    rows = here // 2
    for k, source in enumerate(sources):
        member = 2 * lax.rem(y + k // 2, 2) + lax.rem(core + k % 2, 2)
        device = 4 * z + member
        for r, panel_ref in enumerate(panel_refs):
            lanes = pl.ds(pl.multiple_of((z ^ r) * (EDGE * EDGE), 128), EDGE * EDGE)
            panel_ref[member] = source[rows:, lanes]
        row = (2 * iota((shell_count, 128), 1) + device * here + y).astype(F32)
        where = row - shells.starts
        inside = (where >= 0.0) & (where < shells.size)
        within = jnp.floor((where + extra) * 0.5)
        for chosen, total, column in zip(lists, range(2), columns):
            ahead = jnp.where(even, chosen.ahead[0], chosen.ahead[1])
            base = lane_value(jnp.where(even, chosen.edges[0], chosen.edges[1]), z)
            place = jnp.where(inside & (chosen.used > 0.0), ahead + within + 1.0, 0.0)
            place = jnp.sum(place, axis=0, keepdims=True)
            place = jnp.where(place > 0.0, place - 1.0 - base, -1.0)
            hot = zero_one(place == iota((CAP, 128), 0).astype(F32)).astype(BF16)
            totals[total] += jnp.dot(
                hot[:, :rows], source[:rows, column], preferred_element_type=F32
            )
    for total, column in zip(totals, columns):
        out_ref[:, column] = total.astype(BF16)


def slot_of(window, chip):
    slot = window ^ chip
    return jnp.where((slot == 3) | (slot == 4), slot ^ 7, slot)


def half_kernel(here, early, code_ref, size_ref, *refs):
    panel_refs, pieces, refs = refs[:Z], refs[Z : Z + 2 * early], refs[Z + 2 * early :]
    half_ref, late_ref, got_ref, occ_ref, part_ref, hot_ref, placed_ref, sems = refs
    me = lax.axis_index("shell")
    core, chip = lax.rem(me, CORES), lax.div(me, CORES)
    z = lax.div(chip, Y)
    width = pieces[0].shape[1] - 128
    copies = []
    for far in range(2):
        half = lax.rem(core + far, CORES)
        for k in range(early):
            at = far * early + k
            target = occ_ref.at[pl.ds(k * CAP, CAP), pl.ds(pl.multiple_of(half * 128, 128), 128)]
            copies.append(pltpu.make_async_copy(pieces[at].at[:, pl.ds(width, 128)], target, sems.at[at]))
    for copy in copies:
        copy.start()
    for r, panel_ref in enumerate(panel_refs):
        got_ref[pl.ds((z ^ r) * (Y * CORES), Y * CORES)] = panel_ref[...]
    window = CORES * Y * here
    shell_count = size_ref.shape[1]
    got = got_ref[...].astype(F32)
    size_row = size_ref[...].astype(F32)
    shells = Shells(size_row)
    got = got_ref[...].astype(F32)
    hots = slot_hots(code_ref[...], shell_count)
    lists = [Used(shells, hot, window) for hot in hots]
    slots = hots[0].shape[0]
    kept = LIVE_DEV * (slots // BLK_DEV)
    alive = jnp.broadcast_to(jnp.sum(hots[0], axis=1, keepdims=True), (slots, slots))
    sub, lane = iota((slots, slots), 0), iota((slots, slots), 1)
    rank = row_of(alive, sub < lane)
    alive_row = row_of(alive, sub == lane)
    take = (rank == iota((kept, slots), 0).astype(F32)) & (alive_row > 0.0)
    take = zero_one(take).astype(BF16)

    def taken(array):
        return jnp.dot(take, array.astype(BF16), preferred_element_type=F32)

    def spread(hot, column):
        value = jnp.sum(hot * row_of(column, shells.same), axis=1, keepdims=True)
        wide = jnp.broadcast_to(value, (kept, 128)).reshape(kept, 1, 128)
        return jnp.broadcast_to(wide, (kept, EDGE, 128)).reshape(kept * EDGE, 128)

    at = iota((kept * EDGE, 128), 0) % EDGE
    step = at.astype(F32)

    def places(hot, chosen):
        hot = taken(hot)
        first, length = spread(hot, shells.starts), spread(hot, shells.size)
        row = first + step
        odd = (row - 2.0 * jnp.floor(row * 0.5)) > 0.0
        place = jnp.where(odd, spread(hot, chosen.ahead[1]), spread(hot, chosen.ahead[0]))
        place += jnp.floor(step * 0.5)
        offsets = [
            [slot_of(w * Y + k, chip).astype(F32) * CAP - lane_value(e, w) for w in range(Z)]
            for k, e in enumerate(chosen.edges)
        ]
        offset = jnp.where(odd, offsets[1][0], offsets[0][0])
        for w in range(1, Z):
            offset = jnp.where(row >= float(window * w), jnp.where(odd, offsets[1][w], offsets[0][w]), offset)
        return jnp.where(step < length, place + offset, -1.0)[:, :1]

    place_c, place_r = places(hots[0], lists[0]), places(hots[1], lists[1])
    span = 16 * EDGE
    s_in, l_in = iota((span, span), 0), iota((span, span), 1)
    keep_m = (l_in // EDGE) == (s_in % EDGE)
    fold = zero_one((s_in % EDGE) == (l_in % EDGE)).astype(BF16)
    same_slot = (s_in // EDGE) == (l_in // EDGE)
    blocks = [taken(got[:, p * BLK_DEV : (p + 1) * BLK_DEV, :].reshape(slots, span)) for p in range(2)]
    lanes = iota((span, half_ref.shape[1]), 1).astype(F32)
    for copy in copies:
        copy.wait()
    occ = occ_ref[...]
    cut = early * CAP
    for g in range(kept // 16):
        rows = slice(g * span, (g + 1) * span)
        r_hot = zero_one(place_r[rows] == lanes).astype(BF16)
        c_hot = zero_one(place_c[rows] == lanes).astype(BF16)
        part_ref[:, rows] = jnp.dot(r_hot[:, :cut], occ, preferred_element_type=F32).T.astype(BF16)
        hot_ref[:, rows] = r_hot[:, cut:].T
        for p in range(2):
            block = blocks[p][g * 16 : (g + 1) * 16].reshape(16, 1, span)
            block = jnp.broadcast_to(block, (16, EDGE, span)).reshape(span, span)
            block = jnp.where(keep_m, block, 0.0).astype(BF16)
            diag = jnp.dot(block, fold, preferred_element_type=F32)
            diag = jnp.where(same_slot, diag, 0.0).astype(BF16)
            placed_ref[p, rows, :] = jnp.dot(diag, c_hot, preferred_element_type=F32).astype(BF16)
    for p in range(2):
        half_ref[p * NOCC : (p + 1) * NOCC, :] = jnp.dot(part_ref[...], placed_ref[p], preferred_element_type=F32)
        late_ref[p] = jnp.dot(hot_ref[...], placed_ref[p], preferred_element_type=F32).astype(BF16)


def last_kernel(count, early, me_ref, part_any, late_any, *refs):
    pieces, (out_any, right_ref, occ_ref, part_ref, late_ref, half_ref, tiles_ref, sems) = refs[: 2 * count], refs[2 * count :]
    width = right_ref.shape[2]
    tile = tiles_ref.shape[3]
    per = width // tile
    core = lax.rem(me_ref[0], CORES)
    first, near, far, results = [], [], [], []

    def copy_of(source, target):
        at = len(first) + len(near) + len(far) + len(results)
        return pltpu.make_async_copy(source, target, sems.at[at])

    first.append(copy_of(part_any, part_ref))
    first.append(copy_of(late_any, late_ref))
    for side in range(2):
        half = lax.rem(core + side, CORES)
        for k in range(early, count):
            target = occ_ref.at[pl.ds((k - early) * CAP, CAP), pl.ds(pl.multiple_of(half * 128, 128), 128)]
            first.append(copy_of(pieces[side * count + k].at[:, pl.ds(width, 128)], target))
    for side, copies in enumerate((near, far)):
        for k in range(count):
            target = right_ref.at[side, pl.ds(k * CAP, CAP), :]
            copies.append(copy_of(pieces[side * count + k].at[:, pl.ds(0, width)], target))
    for copy in (*first, *near, *far):
        copy.start()
    for copy in first:
        copy.wait()
    occ = occ_ref[...].T
    for p in range(2):
        rows = slice(p * NOCC, (p + 1) * NOCC)
        late = jnp.dot(occ, late_ref[p], preferred_element_type=F32)
        half_ref[rows, :] = (part_ref[rows, :] + late).astype(BF16)
    for side, copies in enumerate((near, far)):
        for copy in copies:
            copy.wait()
        base = lax.rem(core + side, CORES) * width
        for t in range(per):
            right = right_ref[side, :, t * tile : (t + 1) * tile]
            total = jnp.dot(half_ref[...], right, preferred_element_type=F32).astype(BF16)
            at = side * per + t
            tiles_ref[at] = total.reshape(tiles_ref.shape[1:])
            columns = pl.ds(pl.multiple_of(base + t * tile, 128), tile)
            results.append(copy_of(tiles_ref.at[at], out_any.at[:, :, columns]))
            results[-1].start()
    for copy in results:
        copy.wait()


VMEM = pl.BlockSpec(memory_space=pltpu.VMEM)
SMEM = pl.BlockSpec(memory_space=pltpu.SMEM)
ANY = pl.BlockSpec(memory_space=pl.ANY)


def shape(*dims, dtype=BF16):
    return jax.ShapeDtypeStruct(dims, dtype)


def params(mib):
    return pltpu.CompilerParams(vmem_limit_bytes=mib << 20)


def cost(flops, nbytes):
    return pl.CostEstimate(flops=int(flops), bytes_accessed=int(nbytes), transcendentals=0)


def short_way(panels, block_pairs, block_count, shell_size, occ_coef, vir_coef):
    n = lax.axis_size("shell")
    here, nvir = vir_coef.shape
    width = nvir // CORES
    packed = width + NOCC // CORES
    room = Z * Y * CAP
    size_row = shell_size.reshape(1, -1)

    def swap(array, bit):
        return lax.ppermute(array, "shell", [(i, i ^ bit) for i in range(n)])

    keep, to_core, to_y, to_both = pl.pallas_call(
        pack_kernel,
        out_shape=[shape(here // 2 + 2 * BLK_DEV, packed)] * 4,
        in_specs=[VMEM] * 3,
        out_specs=[VMEM] * 4,
        scratch_shapes=[pltpu.VMEM((2 * n, BLK_DEV, EDGE * EDGE), F32)],
        compiler_params=params(12),
        cost_estimate=cost(3e8, 3e6),
        name="pack_rows",
    )(vir_coef, occ_coef, panels)
    to_y, to_both, to_core = swap(to_y, 2), swap(to_both, 3), swap(to_core, 1)
    code = pl.pallas_call(
        functools.partial(ids_kernel, size_row.shape[1]),
        out_shape=shape(n, BLK_DEV, 128, dtype=jnp.int32),
        in_specs=[VMEM] * 2,
        out_specs=VMEM,
        compiler_params=params(12),
        cost_estimate=cost(1e4, 1e4),
        name="pack_ids",
    )(block_pairs.T, block_count.reshape(1, 1))
    code = lax.all_to_all(code, "shell", split_axis=0, concat_axis=0, tiled=True)

    mine, over, me, *panel = pl.pallas_call(
        functools.partial(pick_kernel, here),
        out_shape=[shape(CAP, packed), shape(1, dtype=jnp.int32), shape(1, dtype=jnp.int32)]
        + [shape(Y * CORES, 2 * BLK_DEV, EDGE * EDGE)] * Z,
        in_specs=[VMEM] * 6,
        out_specs=[VMEM, SMEM, SMEM] + [VMEM] * Z,
        compiler_params=params(12),
        cost_estimate=cost(3e8, 2e6),
        name="pick_rows",
    )(code, size_row, keep, to_core, to_y, to_both)

    beside, mine_y, far = swap(mine, 4), swap(mine, 2), [swap(mine, 1)]
    mine, far[0] = lax.optimization_barrier((mine, far[0]))
    across = swap(mine, 8)
    beside, mine_y = lax.optimization_barrier((beside, mine_y))

    beside_y = swap(beside, 2)
    far += [swap(mine_y, 1), swap(beside, 1)]
    *panel, far[1], far[2] = lax.optimization_barrier((*panel, far[1], far[2]))
    panel = [panel[0]] + [swap(panel[r], 4 * r) for r in range(1, Z)]
    across, beside_y, *panel = lax.optimization_barrier((across, beside_y, *panel))

    corner, across_y = swap(across, 4), swap(across, 2)
    near = [mine, mine_y, beside]
    early = len(near)
    slots = LIVE_DEV * n * EDGE
    half, late = pl.pallas_call(
        functools.partial(half_kernel, here, early),
        out_shape=(shape(2 * NOCC, room, dtype=F32), shape(2, room - early * CAP, room)),
        grid=(1,),
        in_specs=[VMEM] * (2 + Z) + [ANY] * (2 * early),
        out_specs=(
            pl.BlockSpec((2 * NOCC, room), lambda i: (0, 0)),
            pl.BlockSpec((2, room - early * CAP, room), lambda i: (0, 0, 0)),
        ),
        scratch_shapes=[
            pltpu.VMEM((n, 2 * BLK_DEV, EDGE * EDGE), BF16),
            pltpu.VMEM((early * CAP, NOCC), BF16),
            pltpu.VMEM((NOCC, slots), BF16),
            pltpu.VMEM((room - early * CAP, slots), BF16),
            pltpu.VMEM((2, slots, room), BF16),
            pltpu.SemaphoreType.DMA((2 * early,)),
        ],
        compiler_params=params(30),
        cost_estimate=cost(7e9, 1),
        name="half_transform",
    )(code, size_row, *panel, *near, *far)
    corner, half, late = lax.optimization_barrier((corner, half, late))
    corner_y = swap(corner, 2)
    near += [across, beside_y, across_y, corner]
    far += [swap(piece, 1) for piece in near[early:]]
    corner_y, *far = lax.optimization_barrier((corner_y, *far))
    near.append(corner_y)
    far.append(swap(corner_y, 1))

    count = len(near)
    tile = width // 3
    out = pl.pallas_call(
        functools.partial(last_kernel, count, early),
        out_shape=shape(2, NOCC, nvir),
        in_specs=[SMEM] + [ANY] * (2 + 2 * count),
        out_specs=ANY,
        scratch_shapes=[
            pltpu.VMEM((CORES, room, width), BF16),
            pltpu.VMEM((room - early * CAP, NOCC), BF16),
            pltpu.VMEM(half.shape, F32),
            pltpu.VMEM(late.shape, BF16),
            pltpu.VMEM((2 * NOCC, room), BF16),
            pltpu.VMEM((nvir // tile, 2, NOCC, tile), BF16),
            pltpu.SemaphoreType.DMA((2 + 4 * count + nvir // tile,)),
        ],
        compiler_params=params(30),
        cost_estimate=cost(2e10, 1),
        name="last_product",
    )(me, half, late, *near, *far)
    return out, over[0], code, me, panel


def per_device(*args):
    n = lax.axis_size("shell")
    here, nvir = args[5].shape
    shells = args[3].shape[0]
    sparse = LIVE_DEV * n * EDGE < n * here
    if not (sparse and n == Z * Y * CORES and here <= 256 and here % 16 == 0 and nvir % 768 == 0):
        return from_start(*args)
    out, over, code, me, panel = short_way(*args)

    def again(carry):
        over, _ = carry
        over, code_now, me_now, panel_now, *held = lax.optimization_barrier((over, code, me, tuple(panel), *args[3:]))
        z = me_now[0] // (Y * CORES)
        turned = jnp.stack(panel_now)[jnp.arange(Z, dtype=jnp.int32) ^ z]
        turned = turned.reshape(n, 2, BLK_DEV, EDGE * EDGE).swapaxes(1, 2).reshape(n * BLK_DEV, 2, EDGE * EDGE)
        code_now = jnp.max(code_now, axis=2).reshape(n * BLK_DEV)
        ids = jnp.maximum(code_now, 0)
        pairs = jnp.stack([ids // shells, ids % shells], axis=1)
        return over - 1, long_way(turned, pairs, code_now >= 0, *held)

    return lax.while_loop(lambda carry: carry[0] > 0, again, (over, out))[1]


def solution(mesh):
    placed = (
        P(("groups", "shell"), None, None),
        P(("groups", "shell"), None),
        P(("groups", "shell")),
        P("groups"),
        P(("groups", "shell"), None),
        P(("groups", "shell"), None),
    )
    return jax.shard_map(
        per_device,
        mesh=mesh,
        in_specs=placed,
        out_specs=P(("groups", "shell"), None, None),
        check_vma=False,
    )
```

```python
import functools
import math

import jax
import jax.numpy as jnp
from jax import lax
from jax.experimental import pallas as pl
from jax.experimental.pallas import tpu as pltpu
from jax.sharding import PartitionSpec as P

EDGE = 16
NOCC = 256
BLK_DEV = 8
LIVE_DEV = 4
CAP = 96
Z, Y, CORES = 4, 2, 2
CHIPS = Z * Y
F32 = jnp.float32
BF16 = jnp.bfloat16


def padded_rows(matrix, starts, shell_size):
    offsets = jnp.arange(EDGE, dtype=jnp.int32)
    rows = jnp.minimum(starts[:, None] + offsets[None, :], matrix.shape[0] - 1)
    inside = offsets[None, :] < shell_size[:, None]
    return jnp.where(inside[:, :, None], matrix[rows], jnp.zeros((), matrix.dtype))


def half_transform(slot_rows, pairs, keep, occ_blocks):
    count = slot_rows.shape[0]
    vecs_here = slot_rows.shape[1]
    shells = occ_blocks.shape[0]
    group_size = math.gcd(512, count)
    turns = count // group_size
    shaped = slot_rows.reshape(count, vecs_here, EDGE, EDGE)

    def advance(total, turn):
        first = turn * group_size
        block = lax.dynamic_slice_in_dim(shaped, first, group_size, 0)
        okay = lax.dynamic_slice_in_dim(keep, first, group_size, 0)
        block = jnp.where(okay[:, None, None, None], block, jnp.zeros((), block.dtype))
        row_shell = lax.dynamic_slice_in_dim(pairs[:, 0], first, group_size, 0)
        col_shell = lax.dynamic_slice_in_dim(pairs[:, 1], first, group_size, 0)
        coefs = occ_blocks[row_shell]
        piece = jnp.einsum("kmi,kvmn->kvin", coefs, block, preferred_element_type=jnp.float32)
        return (total.at[col_shell].add(piece), None)

    start_total = jnp.zeros((shells, vecs_here, NOCC, EDGE), jnp.float32)
    half, _ = lax.scan(advance, start_total, jnp.arange(turns, dtype=jnp.int32))
    return half


def long_way(turned, pairs, live, shell_size, occ_coef, vir_coef):
    occ_full = lax.all_gather(occ_coef, "shell", axis=0, tiled=True)
    starts = jnp.cumsum(shell_size) - shell_size
    occ_blocks = padded_rows(occ_full, starts, shell_size)
    half = half_transform(turned, pairs, live, occ_blocks)
    hidden = half.astype(jnp.bfloat16)
    vir_full = lax.all_gather(vir_coef, "shell", axis=0, tiled=True)
    vir_blocks = padded_rows(vir_full, starts, shell_size)
    result = jnp.einsum("svin,sna->via", hidden, vir_blocks, preferred_element_type=jnp.float32)
    return result.astype(jnp.bfloat16)


def from_start(panels, block_pairs, block_count, *rest):
    pairs = lax.all_gather(block_pairs, "shell", axis=0, tiled=True)
    counts = lax.all_gather(block_count, "shell", axis=0, tiled=True)
    turned = lax.all_to_all(panels, "shell", split_axis=1, concat_axis=0, tiled=True)
    position = jnp.arange(turned.shape[0], dtype=jnp.int32)
    live = position % BLK_DEV < counts[position // BLK_DEV]
    return long_way(turned, pairs, live, *rest)


def iota(shape, dim):
    return lax.broadcasted_iota(jnp.int32, shape, dim)


def column_of(row, mask):
    return jnp.sum(jnp.where(mask, row, 0.0), axis=1, keepdims=True)


def row_of(column, mask):
    return jnp.sum(jnp.where(mask, column, 0.0), axis=0, keepdims=True)


def zero_one(mask):
    return jnp.where(mask, 1.0, 0.0)


def lane_value(row, index):
    return jnp.sum(jnp.where(iota(row.shape, 1) == index, row, 0.0), axis=1, keepdims=True)


def one_hots(ids, shells):
    lanes = iota(ids.shape, 1).astype(F32)
    return jnp.concatenate([zero_one(ids == lanes + 128.0 * k) for k in range(shells // 128)], axis=1)


def slot_hots(rows, shells):
    sources, slots = rows.shape[0], rows.shape[0] * BLK_DEV
    owner = zero_one(iota((slots, sources), 0) // BLK_DEV == iota((slots, sources), 1)).astype(BF16)
    ids = jnp.dot(owner, rows.astype(BF16), preferred_element_type=F32)
    slot, lane = iota(ids.shape, 0) % BLK_DEV, iota(ids.shape, 1)
    columns, rows = (
        jnp.broadcast_to(column_of(ids, lane == slot + first), (slots, 128)) for first in (0, BLK_DEV)
    )
    return one_hots(columns, shells), one_hots(rows, shells)


def chunk(tail, i):
    row, lane = 4 + i // 5, (i % 5) * 256
    return tail[:, row : row + 1, lane : lane + 256]


class Shells:
    def __init__(self, size_row):
        shells = size_row.shape[1]
        sub, lane = iota((shells, shells), 0), iota((shells, shells), 1)
        self.before, self.same = lane < sub, lane == sub
        self.starts = column_of(size_row, self.before)
        self.size = column_of(size_row, self.same)

    def members(self, chip):
        ahead = chip - self.starts
        ahead = ahead - CHIPS * jnp.floor(ahead / CHIPS)
        return jnp.floor((self.size + (CHIPS - 1.0) - ahead) / CHIPS)


def used_shells(shells, hot):
    return column_of(jnp.max(hot, axis=0, keepdims=True), shells.same)


def pack_kernel(pairs_ref, count_ref, panels_ref, vir_ref, occ_ref, out_ref):
    n, rows, packed = out_ref.shape
    here, nvir = vir_ref.shape
    width, thin = nvir // CORES, occ_ref.shape[1] // CORES
    row, column = iota((CHIPS * rows, here), 0), iota((CHIPS * rows, here), 1)
    deal = zero_one((row % rows < here // CHIPS) & (column == CHIPS * (row % rows) + row // rows)).astype(BF16)
    for core in range(CORES):
        part = jnp.dot(deal, vir_ref[:, core * width : (core + 1) * width], preferred_element_type=F32)
        thin_part = jnp.dot(deal, occ_ref[:, core * thin : (core + 1) * thin], preferred_element_type=F32)
        for chip in range(CHIPS):
            at = slice(chip * rows, (chip + 1) * rows)
            out_ref[CORES * chip + core, :, :width] = part[at].astype(BF16)
            out_ref[CORES * chip + core, :, width:] = thin_part[at].astype(BF16)
    turned = jnp.swapaxes(panels_ref[...].astype(F32), 0, 1).reshape(n, 2 * BLK_DEV, EDGE * EDGE)
    kept = iota((1, BLK_DEV), 1) < count_ref[...]
    square, wide = (BLK_DEV, BLK_DEV), (BLK_DEV, EDGE * EDGE)
    same = iota(square, 0) == iota(square, 1)
    ids_row = jnp.zeros((1, EDGE * EDGE), F32)
    for first, k in ((0, 1), (BLK_DEV, 0)):
        ids = column_of(jnp.where(kept, pairs_ref[k : k + 1, :], -1).astype(F32), same)
        ids_row += row_of(ids, iota(wide, 1) == iota(wide, 0) + first)
    chunks = [turned[:, i : i + 1, :] for i in range(2 * BLK_DEV)]
    chunks.append(jnp.broadcast_to(ids_row[None], (n, 1, EDGE * EDGE)))
    chunks += [jnp.zeros((n, 1, EDGE * EDGE), F32)] * 3
    tail = [jnp.concatenate(chunks[5 * k : 5 * k + 5], axis=2) for k in range(4)]
    out_ref[:, rows - 4 :, :] = jnp.concatenate(tail, axis=1).astype(BF16)


def pick_kernel(here, got_ref, size_ref, out_ref, over_ref, me_ref):
    me = lax.axis_index("shell")
    me_ref[0] = me
    chip = lax.div(me, CORES).astype(F32)
    shell_count = size_ref.shape[1]
    n, rows, packed = got_ref.shape
    tail = got_ref[:, rows - 8 :, :].astype(F32)
    hots = slot_hots(chunk(tail, 2 * BLK_DEV).reshape(n, EDGE * EDGE), shell_count)
    shells = Shells(size_ref[...].astype(F32))
    lists = [used_shells(shells, hot) for hot in hots]
    most = jnp.zeros((1, 1), F32)
    for other in range(CHIPS):
        members = shells.members(float(other))
        for used in lists:
            most = jnp.maximum(most, jnp.sum(used * members, axis=0, keepdims=True))
    over_ref[0] = jnp.where(jnp.max(most) > CAP, 1, 0).astype(jnp.int32)

    lane = iota((shell_count, n * rows), 1)
    row = (lane // rows * here + CHIPS * (lane % rows)).astype(F32) + chip
    where = row - shells.starts
    inside = (where >= 0.0) & (where < shells.size) & (lane % rows < here // CHIPS)
    within = jnp.floor(where / CHIPS) + 1.0
    members = shells.members(chip)
    width = packed - 128
    blocks = got_ref[...].reshape(n * rows, packed)
    for used, column in zip(lists, (slice(0, width), slice(width, packed))):
        ahead = column_of(row_of(used * members, shells.same), shells.before)
        place = jnp.where(inside & (used > 0.0), ahead + within, 0.0)
        place = jnp.sum(place, axis=0, keepdims=True) - 1.0
        hot = zero_one(place == iota((CAP, n * rows), 0).astype(F32)).astype(BF16)
        out_ref[:, column] = jnp.dot(hot, blocks[:, column], preferred_element_type=F32).astype(BF16)


def slot_of(window, chip):
    slot = window ^ chip
    return jnp.where((slot == 3) | (slot == 4), slot ^ 7, slot)


def half_kernel(here, early, got_ref, size_ref, *refs):
    pieces, refs = refs[: 2 * early], refs[2 * early :]
    half_ref, late_ref, panels_ref, ids_ref, occ_ref, part_ref, hot_ref, placed_ref, sems = refs
    me = lax.axis_index("shell")
    core, chip = lax.rem(me, CORES), lax.div(me, CORES)
    width = pieces[0].shape[1] - 128
    copies = []
    for far in range(2):
        half = lax.rem(core + far, CORES)
        for k in range(early):
            at = far * early + k
            target = occ_ref.at[pl.ds(k * CAP, CAP), pl.ds(pl.multiple_of(half * 128, 128), 128)]
            copies.append(pltpu.make_async_copy(pieces[at].at[:, pl.ds(width, 128)], target, sems.at[at]))
    for copy in copies:
        copy.start()
    shell_count = size_ref.shape[1]
    n, rows, _ = got_ref.shape
    tail = got_ref[:, rows - 8 :, :].astype(F32)
    blocks = [jnp.concatenate([chunk(tail, p * BLK_DEV + k) for k in range(BLK_DEV)], axis=1) for p in range(2)]
    panels_ref[...] = jnp.concatenate(blocks, axis=1).astype(BF16)
    ids_ref[...] = chunk(tail, 2 * BLK_DEV).reshape(ids_ref.shape)
    shells = Shells(size_ref[...].astype(F32))
    hots = slot_hots(chunk(tail, 2 * BLK_DEV).reshape(n, EDGE * EDGE), shell_count)
    sub, lane = iota((shell_count, 128), 0), iota((shell_count, 128), 1)
    members = shells.members(lane.astype(F32))
    earlier = zero_one(shells.before).astype(BF16)
    lists = [
        jnp.dot(earlier, (used_shells(shells, hot) * members).astype(BF16), preferred_element_type=F32) for hot in hots
    ]
    first_place = jnp.zeros((1, 128), F32)
    for other in range(CHIPS):
        first_place += jnp.where(iota((1, 128), 1) == other, (slot_of(other, chip) * CAP).astype(F32), 0.0)
    slots = hots[0].shape[0]
    kept = LIVE_DEV * (slots // BLK_DEV)
    alive = jnp.broadcast_to(jnp.sum(hots[0], axis=1, keepdims=True), (slots, slots))
    sub, lane = iota((slots, slots), 0), iota((slots, slots), 1)
    rank = row_of(alive, sub < lane)
    alive_row = row_of(alive, sub == lane)
    take = (rank == iota((kept, slots), 0).astype(F32)) & (alive_row > 0.0)
    take = zero_one(take).astype(BF16)

    def taken(array):
        return jnp.dot(take, array.astype(BF16), preferred_element_type=F32)

    def spread(wide):
        wide = wide.reshape(kept, 1, 128)
        return jnp.broadcast_to(wide, (kept, EDGE, 128)).reshape(kept * EDGE, 128)

    def of_slot(hot, column):
        value = jnp.sum(hot * row_of(column, shells.same), axis=1, keepdims=True)
        return spread(jnp.broadcast_to(value, (kept, 128)))

    step = (iota((kept * EDGE, 128), 0) % EDGE).astype(F32)
    lane = iota((kept * EDGE, 128), 1).astype(F32)

    def places(hot, ahead):
        hot = taken(hot)
        row = of_slot(hot, shells.starts) + step
        table = jnp.dot(hot.astype(BF16), ahead.astype(BF16), preferred_element_type=F32) + first_place
        mine = lane == row - CHIPS * jnp.floor(row / CHIPS)
        place = jnp.sum(jnp.where(mine, spread(table), 0.0), axis=1, keepdims=True) + jnp.floor(step / CHIPS)[:, :1]
        return jnp.where((step < of_slot(hot, shells.size))[:, :1], place, -1.0)

    place_c, place_r = places(hots[0], lists[0]), places(hots[1], lists[1])
    span = 16 * EDGE
    s_in, l_in = iota((span, span), 0), iota((span, span), 1)
    keep_m = (l_in // EDGE) == (s_in % EDGE)
    fold = zero_one((s_in % EDGE) == (l_in % EDGE)).astype(BF16)
    same_slot = (s_in // EDGE) == (l_in // EDGE)
    blocks = [taken(block.reshape(slots, span)) for block in blocks]
    lanes = iota((span, half_ref.shape[1]), 1).astype(F32)
    for copy in copies:
        copy.wait()
    occ = occ_ref[...]
    cut = early * CAP
    for g in range(kept // 16):
        rows = slice(g * span, (g + 1) * span)
        r_hot = zero_one(place_r[rows] == lanes).astype(BF16)
        c_hot = zero_one(place_c[rows] == lanes).astype(BF16)
        part_ref[:, rows] = jnp.dot(r_hot[:, :cut], occ, preferred_element_type=F32).T.astype(BF16)
        hot_ref[:, rows] = r_hot[:, cut:].T
        for p in range(2):
            block = blocks[p][g * 16 : (g + 1) * 16].reshape(16, 1, span)
            block = jnp.broadcast_to(block, (16, EDGE, span)).reshape(span, span)
            block = jnp.where(keep_m, block, 0.0).astype(BF16)
            diag = jnp.dot(block, fold, preferred_element_type=F32)
            diag = jnp.where(same_slot, diag, 0.0).astype(BF16)
            placed_ref[p, rows, :] = jnp.dot(diag, c_hot, preferred_element_type=F32).astype(BF16)
    for p in range(2):
        half_ref[p * NOCC : (p + 1) * NOCC, :] = jnp.dot(part_ref[...], placed_ref[p], preferred_element_type=F32)
        late_ref[p] = jnp.dot(hot_ref[...], placed_ref[p], preferred_element_type=F32).astype(BF16)


def last_kernel(count, early, me_ref, part_any, late_any, *refs):
    pieces, (out_any, right_ref, occ_ref, part_ref, late_ref, half_ref, tiles_ref, sems) = refs[: 2 * count], refs[2 * count :]
    width = right_ref.shape[2]
    tile = tiles_ref.shape[3]
    per = width // tile
    core = lax.rem(me_ref[0], CORES)
    first, near, far, results = [], [], [], []

    def copy_of(source, target):
        at = len(first) + len(near) + len(far) + len(results)
        return pltpu.make_async_copy(source, target, sems.at[at])

    first.append(copy_of(part_any, part_ref))
    first.append(copy_of(late_any, late_ref))
    for side in range(2):
        half = lax.rem(core + side, CORES)
        for k in range(early, count):
            target = occ_ref.at[pl.ds((k - early) * CAP, CAP), pl.ds(pl.multiple_of(half * 128, 128), 128)]
            first.append(copy_of(pieces[side * count + k].at[:, pl.ds(width, 128)], target))
    for side, copies in enumerate((near, far)):
        for k in range(count):
            target = right_ref.at[side, pl.ds(k * CAP, CAP), :]
            copies.append(copy_of(pieces[side * count + k].at[:, pl.ds(0, width)], target))
    for copy in (*first, *near, *far):
        copy.start()
    for copy in first:
        copy.wait()
    occ = occ_ref[...].T
    for p in range(2):
        rows = slice(p * NOCC, (p + 1) * NOCC)
        late = jnp.dot(occ, late_ref[p], preferred_element_type=F32)
        half_ref[rows, :] = (part_ref[rows, :] + late).astype(BF16)
    for side, copies in enumerate((near, far)):
        for copy in copies:
            copy.wait()
        base = lax.rem(core + side, CORES) * width
        for t in range(per):
            right = right_ref[side, :, t * tile : (t + 1) * tile]
            total = jnp.dot(half_ref[...], right, preferred_element_type=F32).astype(BF16)
            at = side * per + t
            tiles_ref[at] = total.reshape(tiles_ref.shape[1:])
            columns = pl.ds(pl.multiple_of(base + t * tile, 128), tile)
            results.append(copy_of(tiles_ref.at[at], out_any.at[:, :, columns]))
            results[-1].start()
    for copy in results:
        copy.wait()


VMEM = pl.BlockSpec(memory_space=pltpu.VMEM)
SMEM = pl.BlockSpec(memory_space=pltpu.SMEM)
ANY = pl.BlockSpec(memory_space=pl.ANY)


def shape(*dims, dtype=BF16):
    return jax.ShapeDtypeStruct(dims, dtype)


def params(mib):
    return pltpu.CompilerParams(vmem_limit_bytes=mib << 20)


def cost(flops, nbytes):
    return pl.CostEstimate(flops=int(flops), bytes_accessed=int(nbytes), transcendentals=0)


def short_way(panels, block_pairs, block_count, shell_size, occ_coef, vir_coef):
    n = lax.axis_size("shell")
    here, nvir = vir_coef.shape
    width = nvir // CORES
    packed = width + NOCC // CORES
    room = CHIPS * CAP
    size_row = shell_size.reshape(1, -1)

    def swap(array, bit):
        return lax.ppermute(array, "shell", [(i, i ^ bit) for i in range(n)])

    rows = here // CHIPS + 4
    blocks = pl.pallas_call(
        pack_kernel,
        out_shape=shape(n, rows, packed),
        in_specs=[VMEM] * 5,
        out_specs=VMEM,
        compiler_params=params(16),
        cost_estimate=cost(3e9, 1),
        name="pack_rows",
    )(block_pairs.T, block_count.reshape(1, 1), panels, vir_coef, occ_coef)
    got = lax.all_to_all(blocks, "shell", split_axis=0, concat_axis=0, tiled=True)

    mine, over, me = pl.pallas_call(
        functools.partial(pick_kernel, here),
        out_shape=(shape(CAP, packed), shape(1, dtype=jnp.int32), shape(1, dtype=jnp.int32)),
        in_specs=[VMEM] * 2,
        out_specs=(VMEM, SMEM, SMEM),
        compiler_params=params(16),
        cost_estimate=cost(3e8, 2e6),
        name="pick_rows",
    )(got, size_row)

    across, mine_y, beside = swap(mine, 8), swap(mine, 2), swap(mine, 4)
    far = [swap(mine, 1), swap(mine_y, 1), swap(beside, 1)]
    across, mine_y, beside, *far = lax.optimization_barrier((across, mine_y, beside, *far))

    corner, beside_y, across_y = swap(across, 4), swap(beside, 2), swap(across, 2)
    near = [mine, mine_y, beside, across]
    far.append(swap(across, 1))
    early = len(near)
    slots = LIVE_DEV * n * EDGE
    half, late, got_panels, got_ids = pl.pallas_call(
        functools.partial(half_kernel, here, early),
        out_shape=(
            shape(2 * NOCC, room, dtype=F32),
            shape(2, room - early * CAP, room),
            shape(n, 2 * BLK_DEV, EDGE * EDGE),
            shape(n, EDGE * EDGE, dtype=F32),
        ),
        grid=(1,),
        in_specs=[VMEM] * 2 + [ANY] * (2 * early),
        out_specs=(
            pl.BlockSpec((2 * NOCC, room), lambda i: (0, 0)),
            pl.BlockSpec((2, room - early * CAP, room), lambda i: (0, 0, 0)),
            pl.BlockSpec((n, 2 * BLK_DEV, EDGE * EDGE), lambda i: (0, 0, 0)),
            pl.BlockSpec((n, EDGE * EDGE), lambda i: (0, 0)),
        ),
        scratch_shapes=[
            pltpu.VMEM((early * CAP, NOCC), BF16),
            pltpu.VMEM((NOCC, slots), BF16),
            pltpu.VMEM((room - early * CAP, slots), BF16),
            pltpu.VMEM((2, slots, room), BF16),
            pltpu.SemaphoreType.DMA((2 * early,)),
        ],
        compiler_params=params(30),
        cost_estimate=cost(7e9, 1),
        name="half_transform",
    )(got, size_row, *near, *far)
    corner, half, late = lax.optimization_barrier((corner, half, late))
    corner_y = swap(corner, 2)
    near += [beside_y, across_y, corner]
    far += [swap(piece, 1) for piece in near[early:]]
    corner_y, *far = lax.optimization_barrier((corner_y, *far))
    near.append(corner_y)
    far.append(swap(corner_y, 1))

    count = len(near)
    tile = width // 3
    out = pl.pallas_call(
        functools.partial(last_kernel, count, early),
        out_shape=shape(2, NOCC, nvir),
        in_specs=[SMEM] + [ANY] * (2 + 2 * count),
        out_specs=ANY,
        scratch_shapes=[
            pltpu.VMEM((CORES, room, width), BF16),
            pltpu.VMEM((room - early * CAP, NOCC), BF16),
            pltpu.VMEM(half.shape, F32),
            pltpu.VMEM(late.shape, BF16),
            pltpu.VMEM((2 * NOCC, room), BF16),
            pltpu.VMEM((nvir // tile, 2, NOCC, tile), BF16),
            pltpu.SemaphoreType.DMA((2 + 4 * count + nvir // tile,)),
        ],
        compiler_params=params(30),
        cost_estimate=cost(2e10, 1),
        name="last_product",
    )(me, half, late, *near, *far)
    return out, over[0], got_panels, got_ids


def per_device(*args):
    n = lax.axis_size("shell")
    here, nvir = args[5].shape
    sparse = LIVE_DEV * n * EDGE < n * here
    if not (sparse and n == Z * Y * CORES and here % (2 * CHIPS) == 0 and nvir % 768 == 0):
        return from_start(*args)
    out, over, got_panels, got_ids = short_way(*args)

    def again(carry):
        over, _ = carry
        over, turned, ids, *held = lax.optimization_barrier((over, got_panels, got_ids, *args[3:]))
        turned = turned.reshape(n, 2, BLK_DEV, EDGE * EDGE).swapaxes(1, 2).reshape(n * BLK_DEV, 2, EDGE * EDGE)
        ids = ids[:, : 2 * BLK_DEV].astype(jnp.int32)
        columns, rows = ids[:, :BLK_DEV].reshape(n * BLK_DEV), ids[:, BLK_DEV:].reshape(n * BLK_DEV)
        pairs = jnp.maximum(jnp.stack([rows, columns], axis=1), 0)
        return over - 1, long_way(turned, pairs, columns >= 0, *held)

    return lax.while_loop(lambda carry: carry[0] > 0, again, (over, out))[1]


def solution(mesh):
    placed = (
        P(("groups", "shell"), None, None),
        P(("groups", "shell"), None),
        P(("groups", "shell")),
        P("groups"),
        P(("groups", "shell"), None),
        P(("groups", "shell"), None),
    )
    return jax.shard_map(
        per_device,
        mesh=mesh,
        in_specs=placed,
        out_specs=P(("groups", "shell"), None, None),
        check_vma=False,
    )
```

```python
import functools
import math

import jax
import jax.numpy as jnp
from jax import lax
from jax.experimental import pallas as pl
from jax.experimental.pallas import tpu as pltpu
from jax.sharding import PartitionSpec as P

EDGE = 16
NOCC = 256
BLK_DEV = 8
LIVE_DEV = 4
CAP = 128
Z, Y, CORES = 4, 2, 2
F32 = jnp.float32
BF16 = jnp.bfloat16


def padded_rows(matrix, starts, shell_size):
    offsets = jnp.arange(EDGE, dtype=jnp.int32)
    rows = jnp.minimum(starts[:, None] + offsets[None, :], matrix.shape[0] - 1)
    inside = offsets[None, :] < shell_size[:, None]
    return jnp.where(inside[:, :, None], matrix[rows], jnp.zeros((), matrix.dtype))


def half_transform(slot_rows, pairs, keep, occ_blocks):
    count = slot_rows.shape[0]
    vecs_here = slot_rows.shape[1]
    shells = occ_blocks.shape[0]
    group_size = math.gcd(512, count)
    turns = count // group_size
    shaped = slot_rows.reshape(count, vecs_here, EDGE, EDGE)

    def advance(total, turn):
        first = turn * group_size
        block = lax.dynamic_slice_in_dim(shaped, first, group_size, 0)
        okay = lax.dynamic_slice_in_dim(keep, first, group_size, 0)
        block = jnp.where(okay[:, None, None, None], block, jnp.zeros((), block.dtype))
        row_shell = lax.dynamic_slice_in_dim(pairs[:, 0], first, group_size, 0)
        col_shell = lax.dynamic_slice_in_dim(pairs[:, 1], first, group_size, 0)
        coefs = occ_blocks[row_shell]
        piece = jnp.einsum("kmi,kvmn->kvin", coefs, block, preferred_element_type=jnp.float32)
        return (total.at[col_shell].add(piece), None)

    start_total = jnp.zeros((shells, vecs_here, NOCC, EDGE), jnp.float32)
    half, _ = lax.scan(advance, start_total, jnp.arange(turns, dtype=jnp.int32))
    return half


def long_way(turned, pairs, live, shell_size, occ_coef, vir_coef):
    occ_full = lax.all_gather(occ_coef, "shell", axis=0, tiled=True)
    starts = jnp.cumsum(shell_size) - shell_size
    occ_blocks = padded_rows(occ_full, starts, shell_size)
    half = half_transform(turned, pairs, live, occ_blocks)
    hidden = half.astype(jnp.bfloat16)
    vir_full = lax.all_gather(vir_coef, "shell", axis=0, tiled=True)
    vir_blocks = padded_rows(vir_full, starts, shell_size)
    result = jnp.einsum("svin,sna->via", hidden, vir_blocks, preferred_element_type=jnp.float32)
    return result.astype(jnp.bfloat16)


def from_start(panels, block_pairs, block_count, *rest):
    pairs = lax.all_gather(block_pairs, "shell", axis=0, tiled=True)
    counts = lax.all_gather(block_count, "shell", axis=0, tiled=True)
    turned = lax.all_to_all(panels, "shell", split_axis=1, concat_axis=0, tiled=True)
    position = jnp.arange(turned.shape[0], dtype=jnp.int32)
    live = position % BLK_DEV < counts[position // BLK_DEV]
    return long_way(turned, pairs, live, *rest)


def iota(shape, dim):
    return lax.broadcasted_iota(jnp.int32, shape, dim)


def column_of(row, mask):
    return jnp.sum(jnp.where(mask, row, 0.0), axis=1, keepdims=True)


def row_of(column, mask):
    return jnp.sum(jnp.where(mask, column, 0.0), axis=0, keepdims=True)


def zero_one(mask):
    return jnp.where(mask, 1.0, 0.0)


def lane_value(row, index):
    return jnp.sum(jnp.where(iota(row.shape, 1) == index, row, 0.0), axis=1, keepdims=True)


def one_hots(ids, shells):
    lanes = iota(ids.shape, 1).astype(F32)
    return jnp.concatenate([zero_one(ids == lanes + 128.0 * k) for k in range(shells // 128)], axis=1)


def slot_hots(code, shells):
    code = code.reshape(-1, 128)
    kept = code >= 0
    columns = jnp.where(kept, code % shells, -1).astype(F32)
    return one_hots(columns, shells), one_hots(jnp.where(kept, code // shells, -1).astype(F32), shells)


class Shells:
    def __init__(self, size_row):
        shells = size_row.shape[1]
        sub, lane = iota((shells, shells), 0), iota((shells, shells), 1)
        self.before, self.same = lane < sub, lane == sub
        self.starts = column_of(size_row, self.before)
        self.size = column_of(size_row, self.same)
        self.odd = self.starts - 2.0 * jnp.floor(self.starts * 0.5)


class Used:
    def __init__(self, shells, hot, window):
        self.used = column_of(jnp.max(hot, axis=0, keepdims=True), shells.same)
        self.extra, self.ahead, self.edges = [], [], []
        edge = (iota((hot.shape[1], 128), 1) * window).astype(F32)
        reach = jnp.clip(edge - shells.starts, 0.0, shells.size)
        for parity in range(2):
            extra = 1.0 - shells.odd if parity == 0 else shells.odd
            count = self.used * jnp.floor((shells.size + extra) * 0.5)
            count_row = row_of(count, shells.same)
            self.extra.append(extra)
            self.ahead.append(column_of(count_row, shells.before))
            self.edges.append(jnp.sum(self.used * jnp.floor((reach + extra) * 0.5), axis=0, keepdims=True))


def pack_kernel(shells, pairs_ref, count_ref, vir_ref, occ_ref, panels_ref, code_ref, *refs):
    outs, (turned_ref,) = refs[:4], refs[4:]
    me = lax.axis_index("shell")
    core, y = lax.rem(me, 2), lax.rem(lax.div(me, 2), 2)
    here, nvir = vir_ref.shape
    rows = here // 2
    width, thin = nvir // CORES, occ_ref.shape[1] // CORES
    turned_ref[...] = jnp.swapaxes(panels_ref[...].astype(F32), 0, 1)
    block = EDGE * EDGE
    for dy in range(2):
        parity = lax.rem(y + dy, 2)
        pick = zero_one(iota((rows, here), 1) == 2 * iota((rows, here), 0) + parity).astype(BF16)
        for dc in range(2):
            half = lax.rem(core + dc, 2)
            out = outs[2 * dy + dc]
            part = vir_ref[:, pl.ds(pl.multiple_of(half * width, 128), width)]
            out[:rows, :width] = jnp.dot(pick, part, preferred_element_type=F32).astype(BF16)
            part = occ_ref[:, pl.ds(pl.multiple_of(half * thin, 128), thin)]
            out[:rows, width:] = jnp.dot(pick, part, preferred_element_type=F32).astype(BF16)
            for z in range(Z):
                device = (z * Y + parity) * CORES + half
                pair = turned_ref[pl.ds(2 * device, 2)].reshape(2 * BLK_DEV, block)
                out[rows:, z * block : (z + 1) * block] = pair.astype(BF16)
            out[rows:, Z * block :] = jnp.zeros((2 * BLK_DEV, out.shape[1] - Z * block), BF16)
    code = pairs_ref[1:2, :] + shells * pairs_ref[0:1, :]
    code = jnp.where(iota((1, BLK_DEV), 1) < count_ref[...], code, -1).astype(F32)
    square = (BLK_DEV, BLK_DEV)
    code = column_of(code, iota(square, 0) == iota(square, 1)).astype(jnp.int32)
    code_ref[...] = jnp.broadcast_to(jnp.broadcast_to(code, (BLK_DEV, 128))[None], code_ref.shape)


def pick_kernel(here, code_ref, size_ref, *refs):
    sources, (out_ref, over_ref, me_ref), panel_refs = refs[:4], refs[4:7], refs[7:]
    me = lax.axis_index("shell")
    me_ref[0] = me
    core, y, z = lax.rem(me, 2), lax.rem(lax.div(me, 2), 2), lax.div(me, 4)
    window = CORES * Y * here
    shell_count = size_ref.shape[1]
    shells = Shells(size_ref[...].astype(F32))
    lists = [Used(shells, hot, window) for hot in slot_hots(code_ref[...], shell_count)]
    most = jnp.zeros((1, 1), F32)
    lane = iota((1, 128), 1)
    for chosen in lists:
        for edges in chosen.edges:
            later = jnp.concatenate([edges[:, 1:], edges[:, :1]], axis=1)
            most = jnp.maximum(most, jnp.max(jnp.where(lane < Z, later - edges, 0.0), axis=1, keepdims=True))
    over_ref[0] = jnp.where(jnp.max(most) > CAP, 1, 0).astype(jnp.int32)

    width = out_ref.shape[1] - 128
    even = y == 0
    totals = [jnp.zeros((CAP, width), F32), jnp.zeros((CAP, 128), F32)]
    columns = [slice(0, width), slice(width, width + 128)]
    extra = jnp.where(even, lists[0].extra[0], lists[0].extra[1])
    rows = here // 2
    for k, source in enumerate(sources):
        member = 2 * lax.rem(y + k // 2, 2) + lax.rem(core + k % 2, 2)
        device = 4 * z + member
        for r, panel_ref in enumerate(panel_refs):
            lanes = pl.ds(pl.multiple_of((z ^ r) * (EDGE * EDGE), 128), EDGE * EDGE)
            panel_ref[member] = source[rows:, lanes]
        row = (2 * iota((shell_count, 128), 1) + device * here + y).astype(F32)
        where = row - shells.starts
        inside = (where >= 0.0) & (where < shells.size)
        within = jnp.floor((where + extra) * 0.5)
        for chosen, total, column in zip(lists, range(2), columns):
            ahead = jnp.where(even, chosen.ahead[0], chosen.ahead[1])
            base = lane_value(jnp.where(even, chosen.edges[0], chosen.edges[1]), z)
            place = jnp.where(inside & (chosen.used > 0.0), ahead + within + 1.0, 0.0)
            place = jnp.sum(place, axis=0, keepdims=True)
            place = jnp.where(place > 0.0, place - 1.0 - base, -1.0)
            hot = zero_one(place == iota((CAP, 128), 0).astype(F32)).astype(BF16)
            totals[total] += jnp.dot(
                hot[:, :rows], source[:rows, column], preferred_element_type=F32
            )
    for total, column in zip(totals, columns):
        out_ref[:, column] = total.astype(BF16)


def slot_of(window, chip):
    slot = window ^ chip
    return jnp.where((slot == 3) | (slot == 4), slot ^ 7, slot)


def half_kernel(here, early, code_ref, size_ref, *refs):
    panel_refs, pieces, refs = refs[:Z], refs[Z : Z + 2 * early], refs[Z + 2 * early :]
    half_ref, late_ref, got_ref, occ_ref, part_ref, hot_ref, placed_ref, sems = refs
    me = lax.axis_index("shell")
    core, chip = lax.rem(me, CORES), lax.div(me, CORES)
    z = lax.div(chip, Y)
    width = pieces[0].shape[1] - 128
    copies = []
    for far in range(2):
        half = lax.rem(core + far, CORES)
        for k in range(early):
            at = far * early + k
            target = occ_ref.at[pl.ds(k * CAP, CAP), pl.ds(pl.multiple_of(half * 128, 128), 128)]
            copies.append(pltpu.make_async_copy(pieces[at].at[:, pl.ds(width, 128)], target, sems.at[at]))
    for copy in copies:
        copy.start()
    for r, panel_ref in enumerate(panel_refs):
        got_ref[pl.ds((z ^ r) * (Y * CORES), Y * CORES)] = panel_ref[...]
    window = CORES * Y * here
    shell_count = size_ref.shape[1]
    got = got_ref[...].astype(F32)
    size_row = size_ref[...].astype(F32)
    shells = Shells(size_row)
    got = got_ref[...].astype(F32)
    hots = slot_hots(code_ref[...], shell_count)
    lists = [Used(shells, hot, window) for hot in hots]
    slots = hots[0].shape[0]
    kept = LIVE_DEV * (slots // BLK_DEV)
    alive = jnp.broadcast_to(jnp.sum(hots[0], axis=1, keepdims=True), (slots, slots))
    sub, lane = iota((slots, slots), 0), iota((slots, slots), 1)
    rank = row_of(alive, sub < lane)
    alive_row = row_of(alive, sub == lane)
    take = (rank == iota((kept, slots), 0).astype(F32)) & (alive_row > 0.0)
    take = zero_one(take).astype(BF16)

    def taken(array):
        return jnp.dot(take, array.astype(BF16), preferred_element_type=F32)

    def spread(hot, column):
        value = jnp.sum(hot * row_of(column, shells.same), axis=1, keepdims=True)
        wide = jnp.broadcast_to(value, (kept, 128)).reshape(kept, 1, 128)
        return jnp.broadcast_to(wide, (kept, EDGE, 128)).reshape(kept * EDGE, 128)

    at = iota((kept * EDGE, 128), 0) % EDGE
    step = at.astype(F32)

    def places(hot, chosen):
        hot = taken(hot)
        first, length = spread(hot, shells.starts), spread(hot, shells.size)
        row = first + step
        odd = (row - 2.0 * jnp.floor(row * 0.5)) > 0.0
        place = jnp.where(odd, spread(hot, chosen.ahead[1]), spread(hot, chosen.ahead[0]))
        place += jnp.floor(step * 0.5)
        offsets = [
            [slot_of(w * Y + k, chip).astype(F32) * CAP - lane_value(e, w) for w in range(Z)]
            for k, e in enumerate(chosen.edges)
        ]
        offset = jnp.where(odd, offsets[1][0], offsets[0][0])
        for w in range(1, Z):
            offset = jnp.where(row >= float(window * w), jnp.where(odd, offsets[1][w], offsets[0][w]), offset)
        return jnp.where(step < length, place + offset, -1.0)[:, :1]

    place_c, place_r = places(hots[0], lists[0]), places(hots[1], lists[1])
    span = 16 * EDGE
    s_in, l_in = iota((span, span), 0), iota((span, span), 1)
    keep_m = (l_in // EDGE) == (s_in % EDGE)
    fold = zero_one((s_in % EDGE) == (l_in % EDGE)).astype(BF16)
    same_slot = (s_in // EDGE) == (l_in // EDGE)
    blocks = [taken(got[:, p * BLK_DEV : (p + 1) * BLK_DEV, :].reshape(slots, span)) for p in range(2)]
    lanes = iota((span, half_ref.shape[1]), 1).astype(F32)
    for copy in copies:
        copy.wait()
    occ = occ_ref[...]
    cut = early * CAP
    for g in range(kept // 16):
        rows = slice(g * span, (g + 1) * span)
        r_hot = zero_one(place_r[rows] == lanes).astype(BF16)
        c_hot = zero_one(place_c[rows] == lanes).astype(BF16)
        part_ref[:, rows] = jnp.dot(r_hot[:, :cut], occ, preferred_element_type=F32).T.astype(BF16)
        hot_ref[:, rows] = r_hot[:, cut:].T
        for p in range(2):
            block = blocks[p][g * 16 : (g + 1) * 16].reshape(16, 1, span)
            block = jnp.broadcast_to(block, (16, EDGE, span)).reshape(span, span)
            block = jnp.where(keep_m, block, 0.0).astype(BF16)
            diag = jnp.dot(block, fold, preferred_element_type=F32)
            diag = jnp.where(same_slot, diag, 0.0).astype(BF16)
            placed_ref[p, rows, :] = jnp.dot(diag, c_hot, preferred_element_type=F32).astype(BF16)
    for p in range(2):
        half_ref[p * NOCC : (p + 1) * NOCC, :] = jnp.dot(part_ref[...], placed_ref[p], preferred_element_type=F32)
        late_ref[p] = jnp.dot(hot_ref[...], placed_ref[p], preferred_element_type=F32).astype(BF16)


def last_kernel(count, early, me_ref, part_any, late_any, *refs):
    pieces, (out_any, right_ref, occ_ref, part_ref, late_ref, half_ref, tiles_ref, sems) = refs[: 2 * count], refs[2 * count :]
    width = right_ref.shape[2]
    tile = tiles_ref.shape[3]
    per = width // tile
    core = lax.rem(me_ref[0], CORES)
    first, near, far, results = [], [], [], []

    def copy_of(source, target):
        at = len(first) + len(near) + len(far) + len(results)
        return pltpu.make_async_copy(source, target, sems.at[at])

    first.append(copy_of(part_any, part_ref))
    first.append(copy_of(late_any, late_ref))
    for side in range(2):
        half = lax.rem(core + side, CORES)
        for k in range(early, count):
            target = occ_ref.at[pl.ds((k - early) * CAP, CAP), pl.ds(pl.multiple_of(half * 128, 128), 128)]
            first.append(copy_of(pieces[side * count + k].at[:, pl.ds(width, 128)], target))
    for side, copies in enumerate((near, far)):
        for k in range(count):
            target = right_ref.at[side, pl.ds(k * CAP, CAP), :]
            copies.append(copy_of(pieces[side * count + k].at[:, pl.ds(0, width)], target))
    for copy in (*first, *near, *far):
        copy.start()
    for copy in first:
        copy.wait()
    occ = occ_ref[...].T
    for p in range(2):
        rows = slice(p * NOCC, (p + 1) * NOCC)
        late = jnp.dot(occ, late_ref[p], preferred_element_type=F32)
        half_ref[rows, :] = (part_ref[rows, :] + late).astype(BF16)
    for side, copies in enumerate((near, far)):
        for copy in copies:
            copy.wait()
        base = lax.rem(core + side, CORES) * width
        for t in range(per):
            right = right_ref[side, :, t * tile : (t + 1) * tile]
            total = jnp.dot(half_ref[...], right, preferred_element_type=F32).astype(BF16)
            at = side * per + t
            tiles_ref[at] = total.reshape(tiles_ref.shape[1:])
            columns = pl.ds(pl.multiple_of(base + t * tile, 128), tile)
            results.append(copy_of(tiles_ref.at[at], out_any.at[:, :, columns]))
            results[-1].start()
    for copy in results:
        copy.wait()


VMEM = pl.BlockSpec(memory_space=pltpu.VMEM)
SMEM = pl.BlockSpec(memory_space=pltpu.SMEM)
ANY = pl.BlockSpec(memory_space=pl.ANY)


def shape(*dims, dtype=BF16):
    return jax.ShapeDtypeStruct(dims, dtype)


def params(mib):
    return pltpu.CompilerParams(vmem_limit_bytes=mib << 20)


def cost(flops, nbytes):
    return pl.CostEstimate(flops=int(flops), bytes_accessed=int(nbytes), transcendentals=0)


def short_way(panels, block_pairs, block_count, shell_size, occ_coef, vir_coef):
    n = lax.axis_size("shell")
    here, nvir = vir_coef.shape
    width = nvir // CORES
    packed = width + NOCC // CORES
    room = Z * Y * CAP
    size_row = shell_size.reshape(1, -1)

    def swap(array, bit):
        return lax.ppermute(array, "shell", [(i, i ^ bit) for i in range(n)])

    code, keep, to_core, to_y, to_both = pl.pallas_call(
        functools.partial(pack_kernel, size_row.shape[1]),
        out_shape=[shape(n, BLK_DEV, 128, dtype=jnp.int32)] + [shape(here // 2 + 2 * BLK_DEV, packed)] * 4,
        in_specs=[VMEM] * 5,
        out_specs=[VMEM] * 5,
        scratch_shapes=[pltpu.VMEM((2 * n, BLK_DEV, EDGE * EDGE), F32)],
        compiler_params=params(12),
        cost_estimate=cost(3e9, 1),
        name="pack_rows",
    )(block_pairs.T, block_count.reshape(1, 1), vir_coef, occ_coef, panels)
    to_y, to_both, to_core = swap(to_y, 2), swap(to_both, 3), swap(to_core, 1)
    code = lax.all_to_all(code, "shell", split_axis=0, concat_axis=0, tiled=True)

    mine, over, me, *panel = pl.pallas_call(
        functools.partial(pick_kernel, here),
        out_shape=[shape(CAP, packed), shape(1, dtype=jnp.int32), shape(1, dtype=jnp.int32)]
        + [shape(Y * CORES, 2 * BLK_DEV, EDGE * EDGE)] * Z,
        in_specs=[VMEM] * 6,
        out_specs=[VMEM, SMEM, SMEM] + [VMEM] * Z,
        compiler_params=params(12),
        cost_estimate=cost(3e8, 2e6),
        name="pick_rows",
    )(code, size_row, keep, to_core, to_y, to_both)

    across, mine_y, beside = swap(mine, 8), swap(mine, 2), swap(mine, 4)
    far = [swap(mine, 1), swap(mine_y, 1), swap(beside, 1)]
    across, mine_y, beside, *far = lax.optimization_barrier((across, mine_y, beside, *far))

    corner, beside_y, across_y = swap(across, 4), swap(beside, 2), swap(across, 2)
    panel = [panel[0]] + [swap(panel[r], 4 * r) for r in range(1, Z)]
    corner, *panel = lax.optimization_barrier((corner, *panel))

    corner_y = swap(corner, 2)
    near = [mine, mine_y, beside, across]
    far.append(swap(across, 1))
    early = len(near)
    slots = LIVE_DEV * n * EDGE
    half, late = pl.pallas_call(
        functools.partial(half_kernel, here, early),
        out_shape=(shape(2 * NOCC, room, dtype=F32), shape(2, room - early * CAP, room)),
        grid=(1,),
        in_specs=[VMEM] * (2 + Z) + [ANY] * (2 * early),
        out_specs=(
            pl.BlockSpec((2 * NOCC, room), lambda i: (0, 0)),
            pl.BlockSpec((2, room - early * CAP, room), lambda i: (0, 0, 0)),
        ),
        scratch_shapes=[
            pltpu.VMEM((n, 2 * BLK_DEV, EDGE * EDGE), BF16),
            pltpu.VMEM((early * CAP, NOCC), BF16),
            pltpu.VMEM((NOCC, slots), BF16),
            pltpu.VMEM((room - early * CAP, slots), BF16),
            pltpu.VMEM((2, slots, room), BF16),
            pltpu.SemaphoreType.DMA((2 * early,)),
        ],
        compiler_params=params(30),
        cost_estimate=cost(7e9, 1),
        name="half_transform",
    )(code, size_row, *panel, *near, *far)
    near += [beside_y, across_y, corner]
    far += [swap(piece, 1) for piece in near[early:]]
    corner_y, half, late, *far = lax.optimization_barrier((corner_y, half, late, *far))
    near.append(corner_y)
    far.append(swap(corner_y, 1))

    count = len(near)
    tile = width // 3
    out = pl.pallas_call(
        functools.partial(last_kernel, count, early),
        out_shape=shape(2, NOCC, nvir),
        in_specs=[SMEM] + [ANY] * (2 + 2 * count),
        out_specs=ANY,
        scratch_shapes=[
            pltpu.VMEM((CORES, room, width), BF16),
            pltpu.VMEM((room - early * CAP, NOCC), BF16),
            pltpu.VMEM(half.shape, F32),
            pltpu.VMEM(late.shape, BF16),
            pltpu.VMEM((2 * NOCC, room), BF16),
            pltpu.VMEM((nvir // tile, 2, NOCC, tile), BF16),
            pltpu.SemaphoreType.DMA((2 + 4 * count + nvir // tile,)),
        ],
        compiler_params=params(30),
        cost_estimate=cost(2e10, 1),
        name="last_product",
    )(me, half, late, *near, *far)
    return out, over[0], code, me, panel


def per_device(*args):
    n = lax.axis_size("shell")
    here, nvir = args[5].shape
    shells = args[3].shape[0]
    sparse = LIVE_DEV * n * EDGE < n * here
    if not (sparse and n == Z * Y * CORES and here <= 256 and here % 16 == 0 and nvir % 768 == 0):
        return from_start(*args)
    out, over, code, me, panel = short_way(*args)

    def again(carry):
        over, _ = carry
        over, code_now, me_now, panel_now, *held = lax.optimization_barrier((over, code, me, tuple(panel), *args[3:]))
        z = me_now[0] // (Y * CORES)
        turned = jnp.stack(panel_now)[jnp.arange(Z, dtype=jnp.int32) ^ z]
        turned = turned.reshape(n, 2, BLK_DEV, EDGE * EDGE).swapaxes(1, 2).reshape(n * BLK_DEV, 2, EDGE * EDGE)
        code_now = jnp.max(code_now, axis=2).reshape(n * BLK_DEV)
        ids = jnp.maximum(code_now, 0)
        pairs = jnp.stack([ids // shells, ids % shells], axis=1)
        return over - 1, long_way(turned, pairs, code_now >= 0, *held)

    return lax.while_loop(lambda carry: carry[0] > 0, again, (over, out))[1]


def solution(mesh):
    placed = (
        P(("groups", "shell"), None, None),
        P(("groups", "shell"), None),
        P(("groups", "shell")),
        P("groups"),
        P(("groups", "shell"), None),
        P(("groups", "shell"), None),
    )
    return jax.shard_map(
        per_device,
        mesh=mesh,
        in_specs=placed,
        out_specs=P(("groups", "shell"), None, None),
        check_vma=False,
    )
```

```python
import functools
import math

import jax
import jax.numpy as jnp
from jax import lax
from jax.experimental import pallas as pl
from jax.experimental.pallas import tpu as pltpu
from jax.sharding import PartitionSpec as P

EDGE = 16
NOCC = 256
BLK_DEV = 8
LIVE_DEV = 4
CAP = 128
Z, Y, CORES = 4, 2, 2
F32 = jnp.float32
BF16 = jnp.bfloat16


def padded_rows(matrix, starts, shell_size):
    offsets = jnp.arange(EDGE, dtype=jnp.int32)
    rows = jnp.minimum(starts[:, None] + offsets[None, :], matrix.shape[0] - 1)
    inside = offsets[None, :] < shell_size[:, None]
    return jnp.where(inside[:, :, None], matrix[rows], jnp.zeros((), matrix.dtype))


def half_transform(slot_rows, pairs, keep, occ_blocks):
    count = slot_rows.shape[0]
    vecs_here = slot_rows.shape[1]
    shells = occ_blocks.shape[0]
    group_size = math.gcd(512, count)
    turns = count // group_size
    shaped = slot_rows.reshape(count, vecs_here, EDGE, EDGE)

    def advance(total, turn):
        first = turn * group_size
        block = lax.dynamic_slice_in_dim(shaped, first, group_size, 0)
        okay = lax.dynamic_slice_in_dim(keep, first, group_size, 0)
        block = jnp.where(okay[:, None, None, None], block, jnp.zeros((), block.dtype))
        row_shell = lax.dynamic_slice_in_dim(pairs[:, 0], first, group_size, 0)
        col_shell = lax.dynamic_slice_in_dim(pairs[:, 1], first, group_size, 0)
        coefs = occ_blocks[row_shell]
        piece = jnp.einsum("kmi,kvmn->kvin", coefs, block, preferred_element_type=jnp.float32)
        return (total.at[col_shell].add(piece), None)

    start_total = jnp.zeros((shells, vecs_here, NOCC, EDGE), jnp.float32)
    half, _ = lax.scan(advance, start_total, jnp.arange(turns, dtype=jnp.int32))
    return half


def long_way(turned, pairs, live, shell_size, occ_coef, vir_coef):
    occ_full = lax.all_gather(occ_coef, "shell", axis=0, tiled=True)
    starts = jnp.cumsum(shell_size) - shell_size
    occ_blocks = padded_rows(occ_full, starts, shell_size)
    half = half_transform(turned, pairs, live, occ_blocks)
    hidden = half.astype(jnp.bfloat16)
    vir_full = lax.all_gather(vir_coef, "shell", axis=0, tiled=True)
    vir_blocks = padded_rows(vir_full, starts, shell_size)
    result = jnp.einsum("svin,sna->via", hidden, vir_blocks, preferred_element_type=jnp.float32)
    return result.astype(jnp.bfloat16)


def from_start(panels, block_pairs, block_count, *rest):
    pairs = lax.all_gather(block_pairs, "shell", axis=0, tiled=True)
    counts = lax.all_gather(block_count, "shell", axis=0, tiled=True)
    turned = lax.all_to_all(panels, "shell", split_axis=1, concat_axis=0, tiled=True)
    position = jnp.arange(turned.shape[0], dtype=jnp.int32)
    live = position % BLK_DEV < counts[position // BLK_DEV]
    return long_way(turned, pairs, live, *rest)


def iota(shape, dim):
    return lax.broadcasted_iota(jnp.int32, shape, dim)


def column_of(row, mask):
    return jnp.sum(jnp.where(mask, row, 0.0), axis=1, keepdims=True)


def row_of(column, mask):
    return jnp.sum(jnp.where(mask, column, 0.0), axis=0, keepdims=True)


def zero_one(mask):
    return jnp.where(mask, 1.0, 0.0)


def lane_value(row, index):
    return jnp.sum(jnp.where(iota(row.shape, 1) == index, row, 0.0), axis=1, keepdims=True)


def one_hots(ids, shells):
    lanes = iota(ids.shape, 1).astype(F32)
    return jnp.concatenate([zero_one(ids == lanes + 128.0 * k) for k in range(shells // 128)], axis=1)


def slot_hots(code, shells):
    code = code.reshape(-1, 128)
    kept = code >= 0
    columns = jnp.where(kept, code % shells, -1).astype(F32)
    return one_hots(columns, shells), one_hots(jnp.where(kept, code // shells, -1).astype(F32), shells)


class Shells:
    def __init__(self, size_row):
        shells = size_row.shape[1]
        sub, lane = iota((shells, shells), 0), iota((shells, shells), 1)
        self.before, self.same = lane < sub, lane == sub
        self.starts = column_of(size_row, self.before)
        self.size = column_of(size_row, self.same)
        self.odd = self.starts - 2.0 * jnp.floor(self.starts * 0.5)


class Used:
    def __init__(self, shells, hot, window):
        self.used = column_of(jnp.max(hot, axis=0, keepdims=True), shells.same)
        self.extra, self.ahead, self.edges = [], [], []
        edge = (iota((hot.shape[1], 128), 1) * window).astype(F32)
        reach = jnp.clip(edge - shells.starts, 0.0, shells.size)
        for parity in range(2):
            extra = 1.0 - shells.odd if parity == 0 else shells.odd
            count = self.used * jnp.floor((shells.size + extra) * 0.5)
            count_row = row_of(count, shells.same)
            self.extra.append(extra)
            self.ahead.append(column_of(count_row, shells.before))
            self.edges.append(jnp.sum(self.used * jnp.floor((reach + extra) * 0.5), axis=0, keepdims=True))


def pack_kernel(vir_ref, occ_ref, panels_ref, *refs):
    outs, (turned_ref,) = refs[:4], refs[4:]
    me = lax.axis_index("shell")
    core, y = lax.rem(me, 2), lax.rem(lax.div(me, 2), 2)
    here, nvir = vir_ref.shape
    rows = here // 2
    width, thin = nvir // CORES, occ_ref.shape[1] // CORES
    turned_ref[...] = jnp.swapaxes(panels_ref[...].astype(F32), 0, 1)
    block = EDGE * EDGE
    for dy in range(2):
        parity = lax.rem(y + dy, 2)
        pick = zero_one(iota((rows, here), 1) == 2 * iota((rows, here), 0) + parity).astype(BF16)
        for dc in range(2):
            half = lax.rem(core + dc, 2)
            out = outs[2 * dy + dc]
            part = vir_ref[:, pl.ds(pl.multiple_of(half * width, 128), width)]
            out[:rows, :width] = jnp.dot(pick, part, preferred_element_type=F32).astype(BF16)
            part = occ_ref[:, pl.ds(pl.multiple_of(half * thin, 128), thin)]
            out[:rows, width:] = jnp.dot(pick, part, preferred_element_type=F32).astype(BF16)
            for z in range(Z):
                device = (z * Y + parity) * CORES + half
                pair = turned_ref[pl.ds(2 * device, 2)].reshape(2 * BLK_DEV, block)
                out[rows:, z * block : (z + 1) * block] = pair.astype(BF16)
            out[rows:, Z * block :] = jnp.zeros((2 * BLK_DEV, out.shape[1] - Z * block), BF16)


def ids_kernel(shells, pairs_ref, count_ref, code_ref):
    code = pairs_ref[1:2, :] + shells * pairs_ref[0:1, :]
    code = jnp.where(iota((1, BLK_DEV), 1) < count_ref[...], code, -1).astype(F32)
    square = (BLK_DEV, BLK_DEV)
    code = column_of(code, iota(square, 0) == iota(square, 1)).astype(jnp.int32)
    code_ref[...] = jnp.broadcast_to(jnp.broadcast_to(code, (BLK_DEV, 128))[None], code_ref.shape)


def pick_kernel(here, code_ref, size_ref, *refs):
    sources, (out_ref, over_ref, me_ref, panel_ref) = refs[:4], refs[4:]
    me = lax.axis_index("shell")
    me_ref[0] = me
    core, y, z = lax.rem(me, 2), lax.rem(lax.div(me, 2), 2), lax.div(me, 4)
    window = CORES * Y * here
    shell_count = size_ref.shape[1]
    shells = Shells(size_ref[...].astype(F32))
    lists = [Used(shells, hot, window) for hot in slot_hots(code_ref[...], shell_count)]
    most = jnp.zeros((1, 1), F32)
    lane = iota((1, 128), 1)
    for chosen in lists:
        for edges in chosen.edges:
            later = jnp.concatenate([edges[:, 1:], edges[:, :1]], axis=1)
            most = jnp.maximum(most, jnp.max(jnp.where(lane < Z, later - edges, 0.0), axis=1, keepdims=True))
    over_ref[0] = jnp.where(jnp.max(most) > CAP, 1, 0).astype(jnp.int32)

    width = out_ref.shape[1] - 128
    even = y == 0
    totals = [jnp.zeros((CAP, width), F32), jnp.zeros((CAP, 128), F32)]
    columns = [slice(0, width), slice(width, width + 128)]
    extra = jnp.where(even, lists[0].extra[0], lists[0].extra[1])
    rows = here // 2
    for k, source in enumerate(sources):
        member = 2 * lax.rem(y + k // 2, 2) + lax.rem(core + k % 2, 2)
        device = 4 * z + member
        for to_z in range(Z):
            panel_ref[to_z, member] = source[rows:, to_z * EDGE * EDGE : (to_z + 1) * EDGE * EDGE]
        row = (2 * iota((shell_count, 128), 1) + device * here + y).astype(F32)
        where = row - shells.starts
        inside = (where >= 0.0) & (where < shells.size)
        within = jnp.floor((where + extra) * 0.5)
        for chosen, total, column in zip(lists, range(2), columns):
            ahead = jnp.where(even, chosen.ahead[0], chosen.ahead[1])
            base = lane_value(jnp.where(even, chosen.edges[0], chosen.edges[1]), z)
            place = jnp.where(inside & (chosen.used > 0.0), ahead + within + 1.0, 0.0)
            place = jnp.sum(place, axis=0, keepdims=True)
            place = jnp.where(place > 0.0, place - 1.0 - base, -1.0)
            hot = zero_one(place == iota((CAP, 128), 0).astype(F32)).astype(BF16)
            totals[total] += jnp.dot(
                hot[:, :rows], source[:rows, column], preferred_element_type=F32
            )
    for total, column in zip(totals, columns):
        out_ref[:, column] = total.astype(BF16)


def slot_of(window, chip):
    slot = window ^ chip
    return jnp.where((slot == 3) | (slot == 4), slot ^ 7, slot)


def half_kernel(here, early, code_ref, got_ref, size_ref, *refs):
    pieces, refs = refs[: 2 * early], refs[2 * early :]
    half_ref, late_ref, occ_ref, part_ref, hot_ref, placed_ref, sems = refs
    me = lax.axis_index("shell")
    core, chip = lax.rem(me, CORES), lax.div(me, CORES)
    width = pieces[0].shape[1] - 128
    copies = []
    for far in range(2):
        half = lax.rem(core + far, CORES)
        for k in range(early):
            at = far * early + k
            target = occ_ref.at[pl.ds(k * CAP, CAP), pl.ds(pl.multiple_of(half * 128, 128), 128)]
            copies.append(pltpu.make_async_copy(pieces[at].at[:, pl.ds(width, 128)], target, sems.at[at]))
    for copy in copies:
        copy.start()
    window = CORES * Y * here
    shell_count = size_ref.shape[1]
    got = got_ref[...].astype(F32)
    size_row = size_ref[...].astype(F32)
    shells = Shells(size_row)
    got = got_ref[...].astype(F32)
    hots = slot_hots(code_ref[...], shell_count)
    lists = [Used(shells, hot, window) for hot in hots]
    slots = hots[0].shape[0]
    kept = LIVE_DEV * (slots // BLK_DEV)
    alive = jnp.broadcast_to(jnp.sum(hots[0], axis=1, keepdims=True), (slots, slots))
    sub, lane = iota((slots, slots), 0), iota((slots, slots), 1)
    rank = row_of(alive, sub < lane)
    alive_row = row_of(alive, sub == lane)
    take = (rank == iota((kept, slots), 0).astype(F32)) & (alive_row > 0.0)
    take = zero_one(take).astype(BF16)

    def taken(array):
        return jnp.dot(take, array.astype(BF16), preferred_element_type=F32)

    def spread(hot, column):
        value = jnp.sum(hot * row_of(column, shells.same), axis=1, keepdims=True)
        wide = jnp.broadcast_to(value, (kept, 128)).reshape(kept, 1, 128)
        return jnp.broadcast_to(wide, (kept, EDGE, 128)).reshape(kept * EDGE, 128)

    at = iota((kept * EDGE, 128), 0) % EDGE
    step = at.astype(F32)

    def places(hot, chosen):
        hot = taken(hot)
        first, length = spread(hot, shells.starts), spread(hot, shells.size)
        row = first + step
        odd = (row - 2.0 * jnp.floor(row * 0.5)) > 0.0
        place = jnp.where(odd, spread(hot, chosen.ahead[1]), spread(hot, chosen.ahead[0]))
        place += jnp.floor(step * 0.5)
        offsets = [
            [slot_of(w * Y + k, chip).astype(F32) * CAP - lane_value(e, w) for w in range(Z)]
            for k, e in enumerate(chosen.edges)
        ]
        offset = jnp.where(odd, offsets[1][0], offsets[0][0])
        for w in range(1, Z):
            offset = jnp.where(row >= float(window * w), jnp.where(odd, offsets[1][w], offsets[0][w]), offset)
        return jnp.where(step < length, place + offset, -1.0)[:, :1]

    place_c, place_r = places(hots[0], lists[0]), places(hots[1], lists[1])
    span = 16 * EDGE
    s_in, l_in = iota((span, span), 0), iota((span, span), 1)
    keep_m = (l_in // EDGE) == (s_in % EDGE)
    fold = zero_one((s_in % EDGE) == (l_in % EDGE)).astype(BF16)
    same_slot = (s_in // EDGE) == (l_in // EDGE)
    blocks = [taken(got[:, p * BLK_DEV : (p + 1) * BLK_DEV, :].reshape(slots, span)) for p in range(2)]
    lanes = iota((span, half_ref.shape[1]), 1).astype(F32)
    for copy in copies:
        copy.wait()
    occ = occ_ref[...]
    cut = early * CAP
    for g in range(kept // 16):
        rows = slice(g * span, (g + 1) * span)
        r_hot = zero_one(place_r[rows] == lanes).astype(BF16)
        c_hot = zero_one(place_c[rows] == lanes).astype(BF16)
        part_ref[:, rows] = jnp.dot(r_hot[:, :cut], occ, preferred_element_type=F32).T.astype(BF16)
        hot_ref[:, rows] = r_hot[:, cut:].T
        for p in range(2):
            block = blocks[p][g * 16 : (g + 1) * 16].reshape(16, 1, span)
            block = jnp.broadcast_to(block, (16, EDGE, span)).reshape(span, span)
            block = jnp.where(keep_m, block, 0.0).astype(BF16)
            diag = jnp.dot(block, fold, preferred_element_type=F32)
            diag = jnp.where(same_slot, diag, 0.0).astype(BF16)
            placed_ref[p, rows, :] = jnp.dot(diag, c_hot, preferred_element_type=F32).astype(BF16)
    for p in range(2):
        half_ref[p * NOCC : (p + 1) * NOCC, :] = jnp.dot(part_ref[...], placed_ref[p], preferred_element_type=F32)
        late_ref[p] = jnp.dot(hot_ref[...], placed_ref[p], preferred_element_type=F32).astype(BF16)


def last_kernel(count, early, me_ref, part_any, late_any, *refs):
    pieces, (out_any, right_ref, occ_ref, part_ref, late_ref, half_ref, tiles_ref, sems) = refs[: 2 * count], refs[2 * count :]
    width = right_ref.shape[2]
    tile = tiles_ref.shape[3]
    per = width // tile
    core = lax.rem(me_ref[0], CORES)
    first, near, far, results = [], [], [], []

    def copy_of(source, target):
        at = len(first) + len(near) + len(far) + len(results)
        return pltpu.make_async_copy(source, target, sems.at[at])

    first.append(copy_of(part_any, part_ref))
    first.append(copy_of(late_any, late_ref))
    for side in range(2):
        half = lax.rem(core + side, CORES)
        for k in range(early, count):
            target = occ_ref.at[pl.ds((k - early) * CAP, CAP), pl.ds(pl.multiple_of(half * 128, 128), 128)]
            first.append(copy_of(pieces[side * count + k].at[:, pl.ds(width, 128)], target))
    for side, copies in enumerate((near, far)):
        for k in range(count):
            target = right_ref.at[side, pl.ds(k * CAP, CAP), :]
            copies.append(copy_of(pieces[side * count + k].at[:, pl.ds(0, width)], target))
    for copy in (*first, *near, *far):
        copy.start()
    for copy in first:
        copy.wait()
    occ = occ_ref[...].T
    for p in range(2):
        rows = slice(p * NOCC, (p + 1) * NOCC)
        late = jnp.dot(occ, late_ref[p], preferred_element_type=F32)
        half_ref[rows, :] = (part_ref[rows, :] + late).astype(BF16)
    for side, copies in enumerate((near, far)):
        for copy in copies:
            copy.wait()
        base = lax.rem(core + side, CORES) * width
        for t in range(per):
            right = right_ref[side, :, t * tile : (t + 1) * tile]
            total = jnp.dot(half_ref[...], right, preferred_element_type=F32).astype(BF16)
            at = side * per + t
            tiles_ref[at] = total.reshape(tiles_ref.shape[1:])
            columns = pl.ds(pl.multiple_of(base + t * tile, 128), tile)
            results.append(copy_of(tiles_ref.at[at], out_any.at[:, :, columns]))
            results[-1].start()
    for copy in results:
        copy.wait()


VMEM = pl.BlockSpec(memory_space=pltpu.VMEM)
SMEM = pl.BlockSpec(memory_space=pltpu.SMEM)
ANY = pl.BlockSpec(memory_space=pl.ANY)


def shape(*dims, dtype=BF16):
    return jax.ShapeDtypeStruct(dims, dtype)


def params(mib):
    return pltpu.CompilerParams(vmem_limit_bytes=mib << 20)


def cost(flops, nbytes):
    return pl.CostEstimate(flops=int(flops), bytes_accessed=int(nbytes), transcendentals=0)


def short_way(panels, block_pairs, block_count, shell_size, occ_coef, vir_coef):
    n = lax.axis_size("shell")
    here, nvir = vir_coef.shape
    width = nvir // CORES
    packed = width + NOCC // CORES
    room = Z * Y * CAP
    size_row = shell_size.reshape(1, -1)

    def swap(array, bit):
        return lax.ppermute(array, "shell", [(i, i ^ bit) for i in range(n)])

    keep, to_core, to_y, to_both = pl.pallas_call(
        pack_kernel,
        out_shape=[shape(here // 2 + 2 * BLK_DEV, packed)] * 4,
        in_specs=[VMEM] * 3,
        out_specs=[VMEM] * 4,
        scratch_shapes=[pltpu.VMEM((2 * n, BLK_DEV, EDGE * EDGE), F32)],
        compiler_params=params(12),
        cost_estimate=cost(3e8, 3e6),
        name="pack_rows",
    )(vir_coef, occ_coef, panels)
    to_y, to_both, to_core = swap(to_y, 2), swap(to_both, 3), swap(to_core, 1)
    code = pl.pallas_call(
        functools.partial(ids_kernel, size_row.shape[1]),
        out_shape=shape(n, BLK_DEV, 128, dtype=jnp.int32),
        in_specs=[VMEM] * 2,
        out_specs=VMEM,
        compiler_params=params(12),
        cost_estimate=cost(1e4, 1e4),
        name="pack_ids",
    )(block_pairs.T, block_count.reshape(1, 1))
    code = lax.all_to_all(code, "shell", split_axis=0, concat_axis=0, tiled=True)

    mine, over, me, panel = pl.pallas_call(
        functools.partial(pick_kernel, here),
        out_shape=[shape(CAP, packed), shape(1, dtype=jnp.int32), shape(1, dtype=jnp.int32)]
        + [shape(Z, Y * CORES, 2 * BLK_DEV, EDGE * EDGE)],
        in_specs=[VMEM] * 6,
        out_specs=[VMEM, SMEM, SMEM, VMEM],
        compiler_params=params(12),
        cost_estimate=cost(3e8, 2e6),
        name="pick_rows",
    )(code, size_row, keep, to_core, to_y, to_both)

    across, mine_y, beside = swap(mine, 8), swap(mine, 2), swap(mine, 4)
    lines = [[Y * CORES * z + k for z in range(Z)] for k in range(Y * CORES)]
    got = lax.all_to_all(panel, "shell", split_axis=0, concat_axis=0, axis_index_groups=lines, tiled=True)
    got = got.reshape(n, 2 * BLK_DEV, EDGE * EDGE)
    far = [swap(mine, 1)]
    across, mine_y, beside, got, *far = lax.optimization_barrier((across, mine_y, beside, got, *far))

    corner, beside_y, across_y = swap(across, 4), swap(beside, 2), swap(across, 2)
    near = [mine, mine_y, beside, across]
    far += [swap(piece, 1) for piece in near[1:]]
    early = len(near)
    slots = LIVE_DEV * n * EDGE
    half, late = pl.pallas_call(
        functools.partial(half_kernel, here, early),
        out_shape=(shape(2 * NOCC, room, dtype=F32), shape(2, room - early * CAP, room)),
        grid=(1,),
        in_specs=[VMEM] * 3 + [ANY] * (2 * early),
        out_specs=(
            pl.BlockSpec((2 * NOCC, room), lambda i: (0, 0)),
            pl.BlockSpec((2, room - early * CAP, room), lambda i: (0, 0, 0)),
        ),
        scratch_shapes=[
            pltpu.VMEM((early * CAP, NOCC), BF16),
            pltpu.VMEM((NOCC, slots), BF16),
            pltpu.VMEM((room - early * CAP, slots), BF16),
            pltpu.VMEM((2, slots, room), BF16),
            pltpu.SemaphoreType.DMA((2 * early,)),
        ],
        compiler_params=params(30),
        cost_estimate=cost(7e9, 1),
        name="half_transform",
    )(code, got, size_row, *near, *far)
    corner, half, late = lax.optimization_barrier((corner, half, late))
    corner_y = swap(corner, 2)
    near += [beside_y, across_y, corner]
    far += [swap(piece, 1) for piece in near[early:]]
    corner_y, *far = lax.optimization_barrier((corner_y, *far))
    near.append(corner_y)
    far.append(swap(corner_y, 1))

    count = len(near)
    tile = width // 3
    out = pl.pallas_call(
        functools.partial(last_kernel, count, early),
        out_shape=shape(2, NOCC, nvir),
        in_specs=[SMEM] + [ANY] * (2 + 2 * count),
        out_specs=ANY,
        scratch_shapes=[
            pltpu.VMEM((CORES, room, width), BF16),
            pltpu.VMEM((room - early * CAP, NOCC), BF16),
            pltpu.VMEM(half.shape, F32),
            pltpu.VMEM(late.shape, BF16),
            pltpu.VMEM((2 * NOCC, room), BF16),
            pltpu.VMEM((nvir // tile, 2, NOCC, tile), BF16),
            pltpu.SemaphoreType.DMA((2 + 4 * count + nvir // tile,)),
        ],
        compiler_params=params(30),
        cost_estimate=cost(2e10, 1),
        name="last_product",
    )(me, half, late, *near, *far)
    return out, over[0], code, got


def per_device(*args):
    n = lax.axis_size("shell")
    here, nvir = args[5].shape
    shells = args[3].shape[0]
    sparse = LIVE_DEV * n * EDGE < n * here
    if not (sparse and n == Z * Y * CORES and here <= 256 and here % 16 == 0 and nvir % 768 == 0):
        return from_start(*args)
    out, over, code, got = short_way(*args)

    def again(carry):
        over, _ = carry
        over, code_now, turned, *held = lax.optimization_barrier((over, code, got, *args[3:]))
        turned = turned.reshape(n, 2, BLK_DEV, EDGE * EDGE).swapaxes(1, 2).reshape(n * BLK_DEV, 2, EDGE * EDGE)
        code_now = jnp.max(code_now, axis=2).reshape(n * BLK_DEV)
        ids = jnp.maximum(code_now, 0)
        pairs = jnp.stack([ids // shells, ids % shells], axis=1)
        return over - 1, long_way(turned, pairs, code_now >= 0, *held)

    return lax.while_loop(lambda carry: carry[0] > 0, again, (over, out))[1]


def solution(mesh):
    placed = (
        P(("groups", "shell"), None, None),
        P(("groups", "shell"), None),
        P(("groups", "shell")),
        P("groups"),
        P(("groups", "shell"), None),
        P(("groups", "shell"), None),
    )
    return jax.shard_map(
        per_device,
        mesh=mesh,
        in_specs=placed,
        out_specs=P(("groups", "shell"), None, None),
        check_vma=False,
    )
```

```python
import functools
import math

import jax
import jax.numpy as jnp
from jax import lax
from jax.experimental import pallas as pl
from jax.experimental.pallas import tpu as pltpu
from jax.sharding import PartitionSpec as P

EDGE = 16
NOCC = 256
BLK_DEV = 8
LIVE_DEV = 4
CAP = 128
Z, Y, CORES = 4, 2, 2
F32 = jnp.float32
BF16 = jnp.bfloat16


def padded_rows(matrix, starts, shell_size):
    offsets = jnp.arange(EDGE, dtype=jnp.int32)
    rows = jnp.minimum(starts[:, None] + offsets[None, :], matrix.shape[0] - 1)
    inside = offsets[None, :] < shell_size[:, None]
    return jnp.where(inside[:, :, None], matrix[rows], jnp.zeros((), matrix.dtype))


def half_transform(slot_rows, pairs, keep, occ_blocks):
    count = slot_rows.shape[0]
    vecs_here = slot_rows.shape[1]
    shells = occ_blocks.shape[0]
    group_size = math.gcd(512, count)
    turns = count // group_size
    shaped = slot_rows.reshape(count, vecs_here, EDGE, EDGE)

    def advance(total, turn):
        first = turn * group_size
        block = lax.dynamic_slice_in_dim(shaped, first, group_size, 0)
        okay = lax.dynamic_slice_in_dim(keep, first, group_size, 0)
        block = jnp.where(okay[:, None, None, None], block, jnp.zeros((), block.dtype))
        row_shell = lax.dynamic_slice_in_dim(pairs[:, 0], first, group_size, 0)
        col_shell = lax.dynamic_slice_in_dim(pairs[:, 1], first, group_size, 0)
        coefs = occ_blocks[row_shell]
        piece = jnp.einsum("kmi,kvmn->kvin", coefs, block, preferred_element_type=jnp.float32)
        return (total.at[col_shell].add(piece), None)

    start_total = jnp.zeros((shells, vecs_here, NOCC, EDGE), jnp.float32)
    half, _ = lax.scan(advance, start_total, jnp.arange(turns, dtype=jnp.int32))
    return half


def long_way(turned, pairs, live, shell_size, occ_coef, vir_coef):
    occ_full = lax.all_gather(occ_coef, "shell", axis=0, tiled=True)
    starts = jnp.cumsum(shell_size) - shell_size
    occ_blocks = padded_rows(occ_full, starts, shell_size)
    half = half_transform(turned, pairs, live, occ_blocks)
    hidden = half.astype(jnp.bfloat16)
    vir_full = lax.all_gather(vir_coef, "shell", axis=0, tiled=True)
    vir_blocks = padded_rows(vir_full, starts, shell_size)
    result = jnp.einsum("svin,sna->via", hidden, vir_blocks, preferred_element_type=jnp.float32)
    return result.astype(jnp.bfloat16)


def from_start(panels, block_pairs, block_count, *rest):
    pairs = lax.all_gather(block_pairs, "shell", axis=0, tiled=True)
    counts = lax.all_gather(block_count, "shell", axis=0, tiled=True)
    turned = lax.all_to_all(panels, "shell", split_axis=1, concat_axis=0, tiled=True)
    position = jnp.arange(turned.shape[0], dtype=jnp.int32)
    live = position % BLK_DEV < counts[position // BLK_DEV]
    return long_way(turned, pairs, live, *rest)


def iota(shape, dim):
    return lax.broadcasted_iota(jnp.int32, shape, dim)


def column_of(row, mask):
    return jnp.sum(jnp.where(mask, row, 0.0), axis=1, keepdims=True)


def row_of(column, mask):
    return jnp.sum(jnp.where(mask, column, 0.0), axis=0, keepdims=True)


def zero_one(mask):
    return jnp.where(mask, 1.0, 0.0)


def lane_value(row, index):
    return jnp.sum(jnp.where(iota(row.shape, 1) == index, row, 0.0), axis=1, keepdims=True)


def one_hots(ids, shells):
    lanes = iota(ids.shape, 1).astype(F32)
    return jnp.concatenate([zero_one(ids == lanes + 128.0 * k) for k in range(shells // 128)], axis=1)


def slot_hots(code, shells):
    code = code.reshape(-1, 128)
    kept = code >= 0
    columns = jnp.where(kept, code % shells, -1).astype(F32)
    return one_hots(columns, shells), one_hots(jnp.where(kept, code // shells, -1).astype(F32), shells)


class Shells:
    def __init__(self, size_row):
        shells = size_row.shape[1]
        sub, lane = iota((shells, shells), 0), iota((shells, shells), 1)
        self.before, self.same = lane < sub, lane == sub
        self.starts = column_of(size_row, self.before)
        self.size = column_of(size_row, self.same)
        self.odd = self.starts - 2.0 * jnp.floor(self.starts * 0.5)


class Used:
    def __init__(self, shells, hot, window):
        self.used = column_of(jnp.max(hot, axis=0, keepdims=True), shells.same)
        self.extra, self.ahead, self.edges = [], [], []
        edge = (iota((hot.shape[1], 128), 1) * window).astype(F32)
        reach = jnp.clip(edge - shells.starts, 0.0, shells.size)
        for parity in range(2):
            extra = 1.0 - shells.odd if parity == 0 else shells.odd
            count = self.used * jnp.floor((shells.size + extra) * 0.5)
            count_row = row_of(count, shells.same)
            self.extra.append(extra)
            self.ahead.append(column_of(count_row, shells.before))
            self.edges.append(jnp.sum(self.used * jnp.floor((reach + extra) * 0.5), axis=0, keepdims=True))


def pack_kernel(vir_ref, occ_ref, panels_ref, *refs):
    outs, (turned_ref,) = refs[:4], refs[4:]
    me = lax.axis_index("shell")
    core, y = lax.rem(me, 2), lax.rem(lax.div(me, 2), 2)
    here, nvir = vir_ref.shape
    rows = here // 2
    width, thin = nvir // CORES, occ_ref.shape[1] // CORES
    turned_ref[...] = jnp.swapaxes(panels_ref[...].astype(F32), 0, 1)
    block = EDGE * EDGE
    for dy in range(2):
        parity = lax.rem(y + dy, 2)
        pick = zero_one(iota((rows, here), 1) == 2 * iota((rows, here), 0) + parity).astype(BF16)
        for dc in range(2):
            half = lax.rem(core + dc, 2)
            out = outs[2 * dy + dc]
            part = vir_ref[:, pl.ds(pl.multiple_of(half * width, 128), width)]
            out[:rows, :width] = jnp.dot(pick, part, preferred_element_type=F32).astype(BF16)
            part = occ_ref[:, pl.ds(pl.multiple_of(half * thin, 128), thin)]
            out[:rows, width:] = jnp.dot(pick, part, preferred_element_type=F32).astype(BF16)
            for z in range(Z):
                device = (z * Y + parity) * CORES + half
                pair = turned_ref[pl.ds(2 * device, 2)].reshape(2 * BLK_DEV, block)
                out[rows:, z * block : (z + 1) * block] = pair.astype(BF16)
            out[rows:, Z * block :] = jnp.zeros((2 * BLK_DEV, out.shape[1] - Z * block), BF16)


def ids_kernel(shells, pairs_ref, count_ref, code_ref):
    code = pairs_ref[1:2, :] + shells * pairs_ref[0:1, :]
    code = jnp.where(iota((1, BLK_DEV), 1) < count_ref[...], code, -1).astype(F32)
    square = (BLK_DEV, BLK_DEV)
    code = column_of(code, iota(square, 0) == iota(square, 1)).astype(jnp.int32)
    code_ref[...] = jnp.broadcast_to(jnp.broadcast_to(code, (BLK_DEV, 128))[None], code_ref.shape)


def pick_kernel(here, code_ref, size_ref, *refs):
    sources, (out_ref, over_ref, me_ref), panel_refs = refs[:4], refs[4:7], refs[7:]
    me = lax.axis_index("shell")
    me_ref[0] = me
    core, y, z = lax.rem(me, 2), lax.rem(lax.div(me, 2), 2), lax.div(me, 4)
    window = CORES * Y * here
    shell_count = size_ref.shape[1]
    shells = Shells(size_ref[...].astype(F32))
    lists = [Used(shells, hot, window) for hot in slot_hots(code_ref[...], shell_count)]
    most = jnp.zeros((1, 1), F32)
    lane = iota((1, 128), 1)
    for chosen in lists:
        for edges in chosen.edges:
            later = jnp.concatenate([edges[:, 1:], edges[:, :1]], axis=1)
            most = jnp.maximum(most, jnp.max(jnp.where(lane < Z, later - edges, 0.0), axis=1, keepdims=True))
    over_ref[0] = jnp.where(jnp.max(most) > CAP, 1, 0).astype(jnp.int32)

    width = out_ref.shape[1] - 128
    even = y == 0
    totals = [jnp.zeros((CAP, width), F32), jnp.zeros((CAP, 128), F32)]
    columns = [slice(0, width), slice(width, width + 128)]
    extra = jnp.where(even, lists[0].extra[0], lists[0].extra[1])
    rows = here // 2
    for k, source in enumerate(sources):
        member = 2 * lax.rem(y + k // 2, 2) + lax.rem(core + k % 2, 2)
        device = 4 * z + member
        for r, panel_ref in enumerate(panel_refs):
            lanes = pl.ds(pl.multiple_of((z ^ r) * (EDGE * EDGE), 128), EDGE * EDGE)
            panel_ref[member] = source[rows:, lanes]
        row = (2 * iota((shell_count, 128), 1) + device * here + y).astype(F32)
        where = row - shells.starts
        inside = (where >= 0.0) & (where < shells.size)
        within = jnp.floor((where + extra) * 0.5)
        for chosen, total, column in zip(lists, range(2), columns):
            ahead = jnp.where(even, chosen.ahead[0], chosen.ahead[1])
            base = lane_value(jnp.where(even, chosen.edges[0], chosen.edges[1]), z)
            place = jnp.where(inside & (chosen.used > 0.0), ahead + within + 1.0, 0.0)
            place = jnp.sum(place, axis=0, keepdims=True)
            place = jnp.where(place > 0.0, place - 1.0 - base, -1.0)
            hot = zero_one(place == iota((CAP, 128), 0).astype(F32)).astype(BF16)
            totals[total] += jnp.dot(
                hot[:, :rows], source[:rows, column], preferred_element_type=F32
            )
    for total, column in zip(totals, columns):
        out_ref[:, column] = total.astype(BF16)


def slot_of(window, chip):
    slot = window ^ chip
    return jnp.where((slot == 3) | (slot == 4), slot ^ 7, slot)


def half_kernel(here, early, code_ref, size_ref, *refs):
    panel_refs, pieces, refs = refs[:Z], refs[Z : Z + 2 * early], refs[Z + 2 * early :]
    half_ref, late_ref, got_ref, occ_ref, part_ref, hot_ref, placed_ref, sems = refs
    me = lax.axis_index("shell")
    core, chip = lax.rem(me, CORES), lax.div(me, CORES)
    z = lax.div(chip, Y)
    width = pieces[0].shape[1] - 128
    copies = []
    for far in range(2):
        half = lax.rem(core + far, CORES)
        for k in range(early):
            at = far * early + k
            target = occ_ref.at[pl.ds(k * CAP, CAP), pl.ds(pl.multiple_of(half * 128, 128), 128)]
            copies.append(pltpu.make_async_copy(pieces[at].at[:, pl.ds(width, 128)], target, sems.at[at]))
    for copy in copies:
        copy.start()
    for r, panel_ref in enumerate(panel_refs):
        got_ref[pl.ds((z ^ r) * (Y * CORES), Y * CORES)] = panel_ref[...]
    window = CORES * Y * here
    shell_count = size_ref.shape[1]
    got = got_ref[...].astype(F32)
    size_row = size_ref[...].astype(F32)
    shells = Shells(size_row)
    got = got_ref[...].astype(F32)
    hots = slot_hots(code_ref[...], shell_count)
    lists = [Used(shells, hot, window) for hot in hots]
    slots = hots[0].shape[0]
    kept = LIVE_DEV * (slots // BLK_DEV)
    alive = jnp.broadcast_to(jnp.sum(hots[0], axis=1, keepdims=True), (slots, slots))
    sub, lane = iota((slots, slots), 0), iota((slots, slots), 1)
    rank = row_of(alive, sub < lane)
    alive_row = row_of(alive, sub == lane)
    take = (rank == iota((kept, slots), 0).astype(F32)) & (alive_row > 0.0)
    take = zero_one(take).astype(BF16)

    def taken(array):
        return jnp.dot(take, array.astype(BF16), preferred_element_type=F32)

    def spread(hot, column):
        value = jnp.sum(hot * row_of(column, shells.same), axis=1, keepdims=True)
        wide = jnp.broadcast_to(value, (kept, 128)).reshape(kept, 1, 128)
        return jnp.broadcast_to(wide, (kept, EDGE, 128)).reshape(kept * EDGE, 128)

    at = iota((kept * EDGE, 128), 0) % EDGE
    step = at.astype(F32)

    def places(hot, chosen):
        hot = taken(hot)
        first, length = spread(hot, shells.starts), spread(hot, shells.size)
        row = first + step
        odd = (row - 2.0 * jnp.floor(row * 0.5)) > 0.0
        place = jnp.where(odd, spread(hot, chosen.ahead[1]), spread(hot, chosen.ahead[0]))
        place += jnp.floor(step * 0.5)
        offsets = [
            [slot_of(w * Y + k, chip).astype(F32) * CAP - lane_value(e, w) for w in range(Z)]
            for k, e in enumerate(chosen.edges)
        ]
        offset = jnp.where(odd, offsets[1][0], offsets[0][0])
        for w in range(1, Z):
            offset = jnp.where(row >= float(window * w), jnp.where(odd, offsets[1][w], offsets[0][w]), offset)
        return jnp.where(step < length, place + offset, -1.0)[:, :1]

    place_c, place_r = places(hots[0], lists[0]), places(hots[1], lists[1])
    span = 16 * EDGE
    s_in, l_in = iota((span, span), 0), iota((span, span), 1)
    keep_m = (l_in // EDGE) == (s_in % EDGE)
    fold = zero_one((s_in % EDGE) == (l_in % EDGE)).astype(BF16)
    same_slot = (s_in // EDGE) == (l_in // EDGE)
    blocks = [taken(got[:, p * BLK_DEV : (p + 1) * BLK_DEV, :].reshape(slots, span)) for p in range(2)]
    lanes = iota((span, half_ref.shape[1]), 1).astype(F32)
    for copy in copies:
        copy.wait()
    occ = occ_ref[...]
    cut = early * CAP
    for g in range(kept // 16):
        rows = slice(g * span, (g + 1) * span)
        r_hot = zero_one(place_r[rows] == lanes).astype(BF16)
        c_hot = zero_one(place_c[rows] == lanes).astype(BF16)
        part_ref[:, rows] = jnp.dot(r_hot[:, :cut], occ, preferred_element_type=F32).T.astype(BF16)
        hot_ref[:, rows] = r_hot[:, cut:].T
        for p in range(2):
            block = blocks[p][g * 16 : (g + 1) * 16].reshape(16, 1, span)
            block = jnp.broadcast_to(block, (16, EDGE, span)).reshape(span, span)
            block = jnp.where(keep_m, block, 0.0).astype(BF16)
            diag = jnp.dot(block, fold, preferred_element_type=F32)
            diag = jnp.where(same_slot, diag, 0.0).astype(BF16)
            placed_ref[p, rows, :] = jnp.dot(diag, c_hot, preferred_element_type=F32).astype(BF16)
    for p in range(2):
        half_ref[p * NOCC : (p + 1) * NOCC, :] = jnp.dot(part_ref[...], placed_ref[p], preferred_element_type=F32)
        late_ref[p] = jnp.dot(hot_ref[...], placed_ref[p], preferred_element_type=F32).astype(BF16)


def last_kernel(count, early, me_ref, part_any, late_any, *refs):
    pieces, (out_any, right_ref, occ_ref, part_ref, late_ref, half_ref, tiles_ref, sems) = refs[: 2 * count], refs[2 * count :]
    width = right_ref.shape[2]
    tile = tiles_ref.shape[3]
    per = width // tile
    core = lax.rem(me_ref[0], CORES)
    first, near, far, results = [], [], [], []

    def copy_of(source, target):
        at = len(first) + len(near) + len(far) + len(results)
        return pltpu.make_async_copy(source, target, sems.at[at])

    first.append(copy_of(part_any, part_ref))
    first.append(copy_of(late_any, late_ref))
    for side in range(2):
        half = lax.rem(core + side, CORES)
        for k in range(early, count):
            target = occ_ref.at[pl.ds((k - early) * CAP, CAP), pl.ds(pl.multiple_of(half * 128, 128), 128)]
            first.append(copy_of(pieces[side * count + k].at[:, pl.ds(width, 128)], target))
    for side, copies in enumerate((near, far)):
        for k in range(count):
            target = right_ref.at[side, pl.ds(k * CAP, CAP), :]
            copies.append(copy_of(pieces[side * count + k].at[:, pl.ds(0, width)], target))
    for copy in (*first, *near, *far):
        copy.start()
    for copy in first:
        copy.wait()
    occ = occ_ref[...].T
    for p in range(2):
        rows = slice(p * NOCC, (p + 1) * NOCC)
        late = jnp.dot(occ, late_ref[p], preferred_element_type=F32)
        half_ref[rows, :] = (part_ref[rows, :] + late).astype(BF16)
    for side, copies in enumerate((near, far)):
        for copy in copies:
            copy.wait()
        base = lax.rem(core + side, CORES) * width
        for t in range(per):
            right = right_ref[side, :, t * tile : (t + 1) * tile]
            total = jnp.dot(half_ref[...], right, preferred_element_type=F32).astype(BF16)
            at = side * per + t
            tiles_ref[at] = total.reshape(tiles_ref.shape[1:])
            columns = pl.ds(pl.multiple_of(base + t * tile, 128), tile)
            results.append(copy_of(tiles_ref.at[at], out_any.at[:, :, columns]))
            results[-1].start()
    for copy in results:
        copy.wait()


VMEM = pl.BlockSpec(memory_space=pltpu.VMEM)
SMEM = pl.BlockSpec(memory_space=pltpu.SMEM)
ANY = pl.BlockSpec(memory_space=pl.ANY)


def shape(*dims, dtype=BF16):
    return jax.ShapeDtypeStruct(dims, dtype)


def params(mib):
    return pltpu.CompilerParams(vmem_limit_bytes=mib << 20)


def cost(flops, nbytes):
    return pl.CostEstimate(flops=int(flops), bytes_accessed=int(nbytes), transcendentals=0)


def short_way(panels, block_pairs, block_count, shell_size, occ_coef, vir_coef):
    n = lax.axis_size("shell")
    here, nvir = vir_coef.shape
    width = nvir // CORES
    packed = width + NOCC // CORES
    room = Z * Y * CAP
    size_row = shell_size.reshape(1, -1)

    def swap(array, bit):
        return lax.ppermute(array, "shell", [(i, i ^ bit) for i in range(n)])

    keep, to_core, to_y, to_both = pl.pallas_call(
        pack_kernel,
        out_shape=[shape(here // 2 + 2 * BLK_DEV, packed)] * 4,
        in_specs=[VMEM] * 3,
        out_specs=[VMEM] * 4,
        scratch_shapes=[pltpu.VMEM((2 * n, BLK_DEV, EDGE * EDGE), F32)],
        compiler_params=params(12),
        cost_estimate=cost(3e8, 3e6),
        name="pack_rows",
    )(vir_coef, occ_coef, panels)
    to_y, to_both, to_core = swap(to_y, 2), swap(to_both, 3), swap(to_core, 1)
    code = pl.pallas_call(
        functools.partial(ids_kernel, size_row.shape[1]),
        out_shape=shape(n, BLK_DEV, 128, dtype=jnp.int32),
        in_specs=[VMEM] * 2,
        out_specs=VMEM,
        compiler_params=params(12),
        cost_estimate=cost(1e4, 1e4),
        name="pack_ids",
    )(block_pairs.T, block_count.reshape(1, 1))
    code = lax.all_to_all(code, "shell", split_axis=0, concat_axis=0, tiled=True)

    mine, over, me, *panel = pl.pallas_call(
        functools.partial(pick_kernel, here),
        out_shape=[shape(CAP, packed), shape(1, dtype=jnp.int32), shape(1, dtype=jnp.int32)]
        + [shape(Y * CORES, 2 * BLK_DEV, EDGE * EDGE)] * Z,
        in_specs=[VMEM] * 6,
        out_specs=[VMEM, SMEM, SMEM] + [VMEM] * Z,
        compiler_params=params(12),
        cost_estimate=cost(3e8, 2e6),
        name="pick_rows",
    )(code, size_row, keep, to_core, to_y, to_both)

    beside, mine_y, across = swap(mine, 4), swap(mine, 2), swap(mine, 8)
    far = [swap(mine, 1)]
    beside, mine_y, *panel = lax.optimization_barrier((beside, mine_y, *panel))

    beside_y = swap(beside, 2)
    panel = [panel[0]] + [swap(panel[r], 4 * r) for r in range(1, Z)]
    far += [swap(mine_y, 1), swap(beside, 1)]
    across, beside_y, *rest = lax.optimization_barrier((across, beside_y, *panel, *far))
    panel, far = rest[:Z], rest[Z:]

    corner, across_y = swap(across, 4), swap(across, 2)
    near = [mine, mine_y, beside]
    early = len(near)
    slots = LIVE_DEV * n * EDGE
    half, late = pl.pallas_call(
        functools.partial(half_kernel, here, early),
        out_shape=(shape(2 * NOCC, room, dtype=F32), shape(2, room - early * CAP, room)),
        grid=(1,),
        in_specs=[VMEM] * (2 + Z) + [ANY] * (2 * early),
        out_specs=(
            pl.BlockSpec((2 * NOCC, room), lambda i: (0, 0)),
            pl.BlockSpec((2, room - early * CAP, room), lambda i: (0, 0, 0)),
        ),
        scratch_shapes=[
            pltpu.VMEM((n, 2 * BLK_DEV, EDGE * EDGE), BF16),
            pltpu.VMEM((early * CAP, NOCC), BF16),
            pltpu.VMEM((NOCC, slots), BF16),
            pltpu.VMEM((room - early * CAP, slots), BF16),
            pltpu.VMEM((2, slots, room), BF16),
            pltpu.SemaphoreType.DMA((2 * early,)),
        ],
        compiler_params=params(30),
        cost_estimate=cost(7e9, 1),
        name="half_transform",
    )(code, size_row, *panel, *near, *far)
    corner, half, late = lax.optimization_barrier((corner, half, late))
    corner_y = swap(corner, 2)
    near += [across, beside_y, across_y, corner]
    far += [swap(piece, 1) for piece in near[early:]]
    corner_y, *far = lax.optimization_barrier((corner_y, *far))
    near.append(corner_y)
    far.append(swap(corner_y, 1))

    count = len(near)
    tile = width // 3
    out = pl.pallas_call(
        functools.partial(last_kernel, count, early),
        out_shape=shape(2, NOCC, nvir),
        in_specs=[SMEM] + [ANY] * (2 + 2 * count),
        out_specs=ANY,
        scratch_shapes=[
            pltpu.VMEM((CORES, room, width), BF16),
            pltpu.VMEM((room - early * CAP, NOCC), BF16),
            pltpu.VMEM(half.shape, F32),
            pltpu.VMEM(late.shape, BF16),
            pltpu.VMEM((2 * NOCC, room), BF16),
            pltpu.VMEM((nvir // tile, 2, NOCC, tile), BF16),
            pltpu.SemaphoreType.DMA((2 + 4 * count + nvir // tile,)),
        ],
        compiler_params=params(30),
        cost_estimate=cost(2e10, 1),
        name="last_product",
    )(me, half, late, *near, *far)
    return out, over[0], code, me, panel


def per_device(*args):
    n = lax.axis_size("shell")
    here, nvir = args[5].shape
    shells = args[3].shape[0]
    sparse = LIVE_DEV * n * EDGE < n * here
    if not (sparse and n == Z * Y * CORES and here <= 256 and here % 16 == 0 and nvir % 768 == 0):
        return from_start(*args)
    out, over, code, me, panel = short_way(*args)

    def again(carry):
        over, _ = carry
        over, code_now, me_now, panel_now, *held = lax.optimization_barrier((over, code, me, tuple(panel), *args[3:]))
        z = me_now[0] // (Y * CORES)
        turned = jnp.stack(panel_now)[jnp.arange(Z, dtype=jnp.int32) ^ z]
        turned = turned.reshape(n, 2, BLK_DEV, EDGE * EDGE).swapaxes(1, 2).reshape(n * BLK_DEV, 2, EDGE * EDGE)
        code_now = jnp.max(code_now, axis=2).reshape(n * BLK_DEV)
        ids = jnp.maximum(code_now, 0)
        pairs = jnp.stack([ids // shells, ids % shells], axis=1)
        return over - 1, long_way(turned, pairs, code_now >= 0, *held)

    return lax.while_loop(lambda carry: carry[0] > 0, again, (over, out))[1]


def solution(mesh):
    placed = (
        P(("groups", "shell"), None, None),
        P(("groups", "shell"), None),
        P(("groups", "shell")),
        P("groups"),
        P(("groups", "shell"), None),
        P(("groups", "shell"), None),
    )
    return jax.shard_map(
        per_device,
        mesh=mesh,
        in_specs=placed,
        out_specs=P(("groups", "shell"), None, None),
        check_vma=False,
    )
```

```python
import functools
import math

import jax
import jax.numpy as jnp
from jax import lax
from jax.experimental import pallas as pl
from jax.experimental.pallas import tpu as pltpu
from jax.sharding import PartitionSpec as P

EDGE = 16
NOCC = 256
BLK_DEV = 8
LIVE_DEV = 4
CAP = 128
Z, Y, CORES = 4, 2, 2
F32 = jnp.float32
BF16 = jnp.bfloat16


def padded_rows(matrix, starts, shell_size):
    offsets = jnp.arange(EDGE, dtype=jnp.int32)
    rows = jnp.minimum(starts[:, None] + offsets[None, :], matrix.shape[0] - 1)
    inside = offsets[None, :] < shell_size[:, None]
    return jnp.where(inside[:, :, None], matrix[rows], jnp.zeros((), matrix.dtype))


def half_transform(slot_rows, pairs, keep, occ_blocks):
    count = slot_rows.shape[0]
    vecs_here = slot_rows.shape[1]
    shells = occ_blocks.shape[0]
    group_size = math.gcd(512, count)
    turns = count // group_size
    shaped = slot_rows.reshape(count, vecs_here, EDGE, EDGE)

    def advance(total, turn):
        first = turn * group_size
        block = lax.dynamic_slice_in_dim(shaped, first, group_size, 0)
        okay = lax.dynamic_slice_in_dim(keep, first, group_size, 0)
        block = jnp.where(okay[:, None, None, None], block, jnp.zeros((), block.dtype))
        row_shell = lax.dynamic_slice_in_dim(pairs[:, 0], first, group_size, 0)
        col_shell = lax.dynamic_slice_in_dim(pairs[:, 1], first, group_size, 0)
        coefs = occ_blocks[row_shell]
        piece = jnp.einsum("kmi,kvmn->kvin", coefs, block, preferred_element_type=jnp.float32)
        return (total.at[col_shell].add(piece), None)

    start_total = jnp.zeros((shells, vecs_here, NOCC, EDGE), jnp.float32)
    half, _ = lax.scan(advance, start_total, jnp.arange(turns, dtype=jnp.int32))
    return half


def long_way(turned, pairs, live, shell_size, occ_coef, vir_coef):
    occ_full = lax.all_gather(occ_coef, "shell", axis=0, tiled=True)
    starts = jnp.cumsum(shell_size) - shell_size
    occ_blocks = padded_rows(occ_full, starts, shell_size)
    half = half_transform(turned, pairs, live, occ_blocks)
    hidden = half.astype(jnp.bfloat16)
    vir_full = lax.all_gather(vir_coef, "shell", axis=0, tiled=True)
    vir_blocks = padded_rows(vir_full, starts, shell_size)
    result = jnp.einsum("svin,sna->via", hidden, vir_blocks, preferred_element_type=jnp.float32)
    return result.astype(jnp.bfloat16)


def from_start(panels, block_pairs, block_count, *rest):
    pairs = lax.all_gather(block_pairs, "shell", axis=0, tiled=True)
    counts = lax.all_gather(block_count, "shell", axis=0, tiled=True)
    turned = lax.all_to_all(panels, "shell", split_axis=1, concat_axis=0, tiled=True)
    position = jnp.arange(turned.shape[0], dtype=jnp.int32)
    live = position % BLK_DEV < counts[position // BLK_DEV]
    return long_way(turned, pairs, live, *rest)


def iota(shape, dim):
    return lax.broadcasted_iota(jnp.int32, shape, dim)


def column_of(row, mask):
    return jnp.sum(jnp.where(mask, row, 0.0), axis=1, keepdims=True)


def row_of(column, mask):
    return jnp.sum(jnp.where(mask, column, 0.0), axis=0, keepdims=True)


def zero_one(mask):
    return jnp.where(mask, 1.0, 0.0)


def lane_value(row, index):
    return jnp.sum(jnp.where(iota(row.shape, 1) == index, row, 0.0), axis=1, keepdims=True)


def one_hots(ids, shells):
    lanes = iota(ids.shape, 1).astype(F32)
    return jnp.concatenate([zero_one(ids == lanes + 128.0 * k) for k in range(shells // 128)], axis=1)


def slot_hots(code, shells):
    code = code.reshape(-1, 128)
    kept = code >= 0
    columns = jnp.where(kept, code % shells, -1).astype(F32)
    return one_hots(columns, shells), one_hots(jnp.where(kept, code // shells, -1).astype(F32), shells)


class Shells:
    def __init__(self, size_row):
        shells = size_row.shape[1]
        sub, lane = iota((shells, shells), 0), iota((shells, shells), 1)
        self.before, self.same = lane < sub, lane == sub
        self.starts = column_of(size_row, self.before)
        self.size = column_of(size_row, self.same)
        self.odd = self.starts - 2.0 * jnp.floor(self.starts * 0.5)


class Used:
    def __init__(self, shells, hot, window):
        self.used = column_of(jnp.max(hot, axis=0, keepdims=True), shells.same)
        self.extra, self.ahead, self.edges = [], [], []
        edge = (iota((hot.shape[1], 128), 1) * window).astype(F32)
        reach = jnp.clip(edge - shells.starts, 0.0, shells.size)
        for parity in range(2):
            extra = 1.0 - shells.odd if parity == 0 else shells.odd
            count = self.used * jnp.floor((shells.size + extra) * 0.5)
            count_row = row_of(count, shells.same)
            self.extra.append(extra)
            self.ahead.append(column_of(count_row, shells.before))
            self.edges.append(jnp.sum(self.used * jnp.floor((reach + extra) * 0.5), axis=0, keepdims=True))


def pack_kernel(vir_ref, occ_ref, panels_ref, *refs):
    outs, (turned_ref,) = refs[:4], refs[4:]
    me = lax.axis_index("shell")
    core, y = lax.rem(me, 2), lax.rem(lax.div(me, 2), 2)
    here, nvir = vir_ref.shape
    rows = here // 2
    width, thin = nvir // CORES, occ_ref.shape[1] // CORES
    turned_ref[...] = jnp.swapaxes(panels_ref[...].astype(F32), 0, 1)
    block = EDGE * EDGE
    for dy in range(2):
        parity = lax.rem(y + dy, 2)
        pick = zero_one(iota((rows, here), 1) == 2 * iota((rows, here), 0) + parity).astype(BF16)
        for dc in range(2):
            half = lax.rem(core + dc, 2)
            out = outs[2 * dy + dc]
            part = vir_ref[:, pl.ds(pl.multiple_of(half * width, 128), width)]
            out[:rows, :width] = jnp.dot(pick, part, preferred_element_type=F32).astype(BF16)
            part = occ_ref[:, pl.ds(pl.multiple_of(half * thin, 128), thin)]
            out[:rows, width:] = jnp.dot(pick, part, preferred_element_type=F32).astype(BF16)
            for z in range(Z):
                device = (z * Y + parity) * CORES + half
                pair = turned_ref[pl.ds(2 * device, 2)].reshape(2 * BLK_DEV, block)
                out[rows:, z * block : (z + 1) * block] = pair.astype(BF16)
            out[rows:, Z * block :] = jnp.zeros((2 * BLK_DEV, out.shape[1] - Z * block), BF16)


def ids_kernel(shells, pairs_ref, count_ref, code_ref):
    code = pairs_ref[1:2, :] + shells * pairs_ref[0:1, :]
    code = jnp.where(iota((1, BLK_DEV), 1) < count_ref[...], code, -1).astype(F32)
    square = (BLK_DEV, BLK_DEV)
    code = column_of(code, iota(square, 0) == iota(square, 1)).astype(jnp.int32)
    code_ref[...] = jnp.broadcast_to(jnp.broadcast_to(code, (BLK_DEV, 128))[None], code_ref.shape)


def pick_kernel(here, code_ref, size_ref, *refs):
    sources, (out_ref, over_ref, me_ref, panel_ref) = refs[:4], refs[4:]
    me = lax.axis_index("shell")
    me_ref[0] = me
    core, y, z = lax.rem(me, 2), lax.rem(lax.div(me, 2), 2), lax.div(me, 4)
    window = CORES * Y * here
    shell_count = size_ref.shape[1]
    shells = Shells(size_ref[...].astype(F32))
    lists = [Used(shells, hot, window) for hot in slot_hots(code_ref[...], shell_count)]
    most = jnp.zeros((1, 1), F32)
    lane = iota((1, 128), 1)
    for chosen in lists:
        for edges in chosen.edges:
            later = jnp.concatenate([edges[:, 1:], edges[:, :1]], axis=1)
            most = jnp.maximum(most, jnp.max(jnp.where(lane < Z, later - edges, 0.0), axis=1, keepdims=True))
    over_ref[0] = jnp.where(jnp.max(most) > CAP, 1, 0).astype(jnp.int32)

    width = out_ref.shape[1] - 128
    even = y == 0
    totals = [jnp.zeros((CAP, width), F32), jnp.zeros((CAP, 128), F32)]
    columns = [slice(0, width), slice(width, width + 128)]
    extra = jnp.where(even, lists[0].extra[0], lists[0].extra[1])
    rows = here // 2
    for k, source in enumerate(sources):
        member = 2 * lax.rem(y + k // 2, 2) + lax.rem(core + k % 2, 2)
        device = 4 * z + member
        for to_z in range(Z):
            panel_ref[to_z, member] = source[rows:, to_z * EDGE * EDGE : (to_z + 1) * EDGE * EDGE]
        row = (2 * iota((shell_count, 128), 1) + device * here + y).astype(F32)
        where = row - shells.starts
        inside = (where >= 0.0) & (where < shells.size)
        within = jnp.floor((where + extra) * 0.5)
        for chosen, total, column in zip(lists, range(2), columns):
            ahead = jnp.where(even, chosen.ahead[0], chosen.ahead[1])
            base = lane_value(jnp.where(even, chosen.edges[0], chosen.edges[1]), z)
            place = jnp.where(inside & (chosen.used > 0.0), ahead + within + 1.0, 0.0)
            place = jnp.sum(place, axis=0, keepdims=True)
            place = jnp.where(place > 0.0, place - 1.0 - base, -1.0)
            hot = zero_one(place == iota((CAP, 128), 0).astype(F32)).astype(BF16)
            totals[total] += jnp.dot(
                hot[:, :rows], source[:rows, column], preferred_element_type=F32
            )
    for total, column in zip(totals, columns):
        out_ref[:, column] = total.astype(BF16)


def slot_of(window, chip):
    rel = window ^ chip
    early = jnp.where((rel == 3) | (rel == 4), rel ^ 7, rel)
    return jnp.where((rel == 5) | (rel == 6), rel ^ 3, early)


def half_kernel(here, early, code_ref, got_ref, size_ref, *refs):
    pieces, refs = refs[: 2 * early], refs[2 * early :]
    half_ref, late_ref, occ_ref, part_ref, hot_ref, placed_ref, sems = refs
    me = lax.axis_index("shell")
    core, chip = lax.rem(me, CORES), lax.div(me, CORES)
    width = pieces[0].shape[1] - 128
    copies = []
    for far in range(2):
        half = lax.rem(core + far, CORES)
        for k in range(early):
            at = far * early + k
            target = occ_ref.at[pl.ds(k * CAP, CAP), pl.ds(pl.multiple_of(half * 128, 128), 128)]
            copies.append(pltpu.make_async_copy(pieces[at].at[:, pl.ds(width, 128)], target, sems.at[at]))
    for copy in copies:
        copy.start()
    window = CORES * Y * here
    shell_count = size_ref.shape[1]
    got = got_ref[...].astype(F32)
    size_row = size_ref[...].astype(F32)
    shells = Shells(size_row)
    got = got_ref[...].astype(F32)
    hots = slot_hots(code_ref[...], shell_count)
    lists = [Used(shells, hot, window) for hot in hots]
    slots = hots[0].shape[0]
    kept = LIVE_DEV * (slots // BLK_DEV)
    alive = jnp.broadcast_to(jnp.sum(hots[0], axis=1, keepdims=True), (slots, slots))
    sub, lane = iota((slots, slots), 0), iota((slots, slots), 1)
    rank = row_of(alive, sub < lane)
    alive_row = row_of(alive, sub == lane)
    take = (rank == iota((kept, slots), 0).astype(F32)) & (alive_row > 0.0)
    take = zero_one(take).astype(BF16)

    def taken(array):
        return jnp.dot(take, array.astype(BF16), preferred_element_type=F32)

    def spread(hot, column):
        value = jnp.sum(hot * row_of(column, shells.same), axis=1, keepdims=True)
        wide = jnp.broadcast_to(value, (kept, 128)).reshape(kept, 1, 128)
        return jnp.broadcast_to(wide, (kept, EDGE, 128)).reshape(kept * EDGE, 128)

    at = iota((kept * EDGE, 128), 0) % EDGE
    step = at.astype(F32)

    def places(hot, chosen):
        hot = taken(hot)
        first, length = spread(hot, shells.starts), spread(hot, shells.size)
        row = first + step
        odd = (row - 2.0 * jnp.floor(row * 0.5)) > 0.0
        place = jnp.where(odd, spread(hot, chosen.ahead[1]), spread(hot, chosen.ahead[0]))
        place += jnp.floor(step * 0.5)
        offsets = [
            [slot_of(w * Y + k, chip).astype(F32) * CAP - lane_value(e, w) for w in range(Z)]
            for k, e in enumerate(chosen.edges)
        ]
        offset = jnp.where(odd, offsets[1][0], offsets[0][0])
        for w in range(1, Z):
            offset = jnp.where(row >= float(window * w), jnp.where(odd, offsets[1][w], offsets[0][w]), offset)
        return jnp.where(step < length, place + offset, -1.0)[:, :1]

    place_c, place_r = places(hots[0], lists[0]), places(hots[1], lists[1])
    span = 16 * EDGE
    s_in, l_in = iota((span, span), 0), iota((span, span), 1)
    keep_m = (l_in // EDGE) == (s_in % EDGE)
    fold = zero_one((s_in % EDGE) == (l_in % EDGE)).astype(BF16)
    same_slot = (s_in // EDGE) == (l_in // EDGE)
    blocks = [taken(got[:, p * BLK_DEV : (p + 1) * BLK_DEV, :].reshape(slots, span)) for p in range(2)]
    lanes = iota((span, half_ref.shape[1]), 1).astype(F32)
    for copy in copies:
        copy.wait()
    occ = occ_ref[...]
    cut = early * CAP
    for g in range(kept // 16):
        rows = slice(g * span, (g + 1) * span)
        r_hot = zero_one(place_r[rows] == lanes).astype(BF16)
        c_hot = zero_one(place_c[rows] == lanes).astype(BF16)
        part_ref[:, rows] = jnp.dot(r_hot[:, :cut], occ, preferred_element_type=F32).T.astype(BF16)
        hot_ref[:, rows] = r_hot[:, cut:].T
        for p in range(2):
            block = blocks[p][g * 16 : (g + 1) * 16].reshape(16, 1, span)
            block = jnp.broadcast_to(block, (16, EDGE, span)).reshape(span, span)
            block = jnp.where(keep_m, block, 0.0).astype(BF16)
            diag = jnp.dot(block, fold, preferred_element_type=F32)
            diag = jnp.where(same_slot, diag, 0.0).astype(BF16)
            placed_ref[p, rows, :] = jnp.dot(diag, c_hot, preferred_element_type=F32).astype(BF16)
    for p in range(2):
        half_ref[p * NOCC : (p + 1) * NOCC, :] = jnp.dot(part_ref[...], placed_ref[p], preferred_element_type=F32)
        late_ref[p] = jnp.dot(hot_ref[...], placed_ref[p], preferred_element_type=F32).astype(BF16)


def gather_kernel(early, me_ref, part_ref, late_ref, *refs):
    count = (len(refs) - 4) // 2
    pieces, (right_ref, half_ref, occ_ref, sems) = refs[: 2 * count], refs[2 * count :]
    width = right_ref.shape[2]
    core = lax.rem(me_ref[0], CORES)
    first, copies = [], []
    for side in range(2):
        half = lax.rem(core + side, CORES)
        for k in range(count):
            at = side * count + k
            if k >= early:
                target = occ_ref.at[pl.ds((k - early) * CAP, CAP), pl.ds(pl.multiple_of(half * 128, 128), 128)]
                source = pieces[at].at[:, pl.ds(width, 128)]
                first.append(pltpu.make_async_copy(source, target, sems.at[2 * count + at]))
            target = right_ref.at[side, pl.ds(k * CAP, CAP), :]
            copies.append(pltpu.make_async_copy(pieces[at].at[:, pl.ds(0, width)], target, sems.at[at]))
    for copy in (*first, *copies):
        copy.start()
    for copy in first:
        copy.wait()
    occ = occ_ref[...].T
    for p in range(2):
        rows = slice(p * NOCC, (p + 1) * NOCC)
        late = jnp.dot(occ, late_ref[p, : occ_ref.shape[0], :], preferred_element_type=F32)
        half_ref[rows, :] = part_ref[rows, :] + late
    for copy in copies:
        copy.wait()


def last_kernel(me_ref, part_ref, right_ref, late_any, *refs):
    pieces, (out_any, late_ref, half_ref, tiles_ref, sems) = (refs[:2], refs[2:4]), refs[4:]
    width = right_ref.shape[2]
    cut = right_ref.shape[1]
    tile = tiles_ref.shape[3]
    per = width // tile
    core = lax.rem(me_ref[0], CORES)
    rows = late_any.shape[1] - 2 * CAP
    copy = pltpu.make_async_copy(late_any.at[:, pl.ds(rows, 2 * CAP), :], late_ref, sems.at[0])
    copy.start()
    copy.wait()
    sides = [jnp.concatenate([ref[:, width:] for ref in side], axis=0).T for side in pieces]
    for p in range(2):
        for side, occ in enumerate(sides):
            half = lax.rem(core + side, CORES)
            rows = pl.ds(pl.multiple_of(p * NOCC + half * 128, 128), 128)
            late = jnp.dot(occ, late_ref[p], preferred_element_type=F32)
            half_ref[rows, :] = (part_ref[rows, :] + late).astype(BF16)
    results = []
    for side, tail in enumerate(pieces):
        base = lax.rem(core + side, CORES) * width
        for t in range(per):
            columns = slice(t * tile, (t + 1) * tile)
            total = jnp.dot(half_ref[:, :cut], right_ref[side, :, columns], preferred_element_type=F32)
            below = jnp.concatenate([ref[:, columns] for ref in tail], axis=0)
            total += jnp.dot(half_ref[:, cut:], below, preferred_element_type=F32)
            at = side * per + t
            tiles_ref[at] = total.astype(BF16).reshape(tiles_ref.shape[1:])
            target = out_any.at[:, :, pl.ds(pl.multiple_of(base + t * tile, 128), tile)]
            results.append(pltpu.make_async_copy(tiles_ref.at[at], target, sems.at[1 + at]))
            results[-1].start()
    for copy in results:
        copy.wait()


VMEM = pl.BlockSpec(memory_space=pltpu.VMEM)
SMEM = pl.BlockSpec(memory_space=pltpu.SMEM)
ANY = pl.BlockSpec(memory_space=pl.ANY)


def shape(*dims, dtype=BF16):
    return jax.ShapeDtypeStruct(dims, dtype)


def params(mib):
    return pltpu.CompilerParams(vmem_limit_bytes=mib << 20)


def cost(flops, nbytes):
    return pl.CostEstimate(flops=int(flops), bytes_accessed=int(nbytes), transcendentals=0)


def short_way(panels, block_pairs, block_count, shell_size, occ_coef, vir_coef):
    n = lax.axis_size("shell")
    here, nvir = vir_coef.shape
    width = nvir // CORES
    packed = width + NOCC // CORES
    room = Z * Y * CAP
    size_row = shell_size.reshape(1, -1)

    def swap(array, bit):
        return lax.ppermute(array, "shell", [(i, i ^ bit) for i in range(n)])

    keep, to_core, to_y, to_both = pl.pallas_call(
        pack_kernel,
        out_shape=[shape(here // 2 + 2 * BLK_DEV, packed)] * 4,
        in_specs=[VMEM] * 3,
        out_specs=[VMEM] * 4,
        scratch_shapes=[pltpu.VMEM((2 * n, BLK_DEV, EDGE * EDGE), F32)],
        compiler_params=params(12),
        cost_estimate=cost(3e8, 3e6),
        name="pack_rows",
    )(vir_coef, occ_coef, panels)
    to_y, to_both, to_core = swap(to_y, 2), swap(to_both, 3), swap(to_core, 1)
    code = pl.pallas_call(
        functools.partial(ids_kernel, size_row.shape[1]),
        out_shape=shape(n, BLK_DEV, 128, dtype=jnp.int32),
        in_specs=[VMEM] * 2,
        out_specs=VMEM,
        compiler_params=params(12),
        cost_estimate=cost(1e4, 1e4),
        name="pack_ids",
    )(block_pairs.T, block_count.reshape(1, 1))
    code = lax.all_to_all(code, "shell", split_axis=0, concat_axis=0, tiled=True)

    mine, over, me, panel = pl.pallas_call(
        functools.partial(pick_kernel, here),
        out_shape=[shape(CAP, packed), shape(1, dtype=jnp.int32), shape(1, dtype=jnp.int32)]
        + [shape(Z, Y * CORES, 2 * BLK_DEV, EDGE * EDGE)],
        in_specs=[VMEM] * 6,
        out_specs=[VMEM, SMEM, SMEM, VMEM],
        compiler_params=params(12),
        cost_estimate=cost(3e8, 2e6),
        name="pick_rows",
    )(code, size_row, keep, to_core, to_y, to_both)

    across, mine_y, beside = swap(mine, 8), swap(mine, 2), swap(mine, 4)
    lines = [[Y * CORES * z + k for z in range(Z)] for k in range(Y * CORES)]
    got = lax.all_to_all(panel, "shell", split_axis=0, concat_axis=0, axis_index_groups=lines, tiled=True)
    got = got.reshape(n, 2 * BLK_DEV, EDGE * EDGE)
    far = [swap(mine, 1)]
    across, mine_y, beside, got, *far = lax.optimization_barrier((across, mine_y, beside, got, *far))

    corner, beside_y, across_y = swap(across, 4), swap(beside, 2), swap(across, 2)
    near = [mine, mine_y, beside, across]
    far += [swap(piece, 1) for piece in near[1:]]
    early = len(near)
    slots = LIVE_DEV * n * EDGE
    half, late = pl.pallas_call(
        functools.partial(half_kernel, here, early),
        out_shape=(shape(2 * NOCC, room, dtype=F32), shape(2, room - early * CAP, room)),
        grid=(1,),
        in_specs=[VMEM] * 3 + [ANY] * (2 * early),
        out_specs=(
            pl.BlockSpec((2 * NOCC, room), lambda i: (0, 0)),
            pl.BlockSpec((2, room - early * CAP, room), lambda i: (0, 0, 0)),
        ),
        scratch_shapes=[
            pltpu.VMEM((early * CAP, NOCC), BF16),
            pltpu.VMEM((NOCC, slots), BF16),
            pltpu.VMEM((room - early * CAP, slots), BF16),
            pltpu.VMEM((2, slots, room), BF16),
            pltpu.SemaphoreType.DMA((2 * early,)),
        ],
        compiler_params=params(30),
        cost_estimate=cost(7e9, 1),
        name="half_transform",
    )(code, got, size_row, *near, *far)
    corner, beside_y, half, late = lax.optimization_barrier((corner, beside_y, half, late))
    corner_y = swap(corner, 2)
    near += [beside_y, corner]
    far += [swap(piece, 1) for piece in near[early:]]
    count = len(near)
    right, half = pl.pallas_call(
        functools.partial(gather_kernel, early),
        out_shape=(shape(CORES, count * CAP, width), shape(2 * NOCC, room, dtype=F32)),
        in_specs=[SMEM] + [VMEM] * 2 + [ANY] * (2 * count),
        out_specs=(VMEM, VMEM),
        scratch_shapes=[pltpu.VMEM(((count - early) * CAP, NOCC), BF16), pltpu.SemaphoreType.DMA((4 * count,))],
        compiler_params=params(20),
        cost_estimate=cost(1, 1),
        name="gather_pieces",
    )(me, half, late, *near, *far)
    corner_y, right, half = lax.optimization_barrier((corner_y, right, half))
    tails = [across_y, corner_y, swap(across_y, 1), swap(corner_y, 1)]

    tile = width // 3
    out = pl.pallas_call(
        last_kernel,
        out_shape=shape(2, NOCC, nvir),
        in_specs=[SMEM] + [VMEM] * 2 + [ANY] + [VMEM] * 4,
        out_specs=ANY,
        scratch_shapes=[
            pltpu.VMEM((2, 2 * CAP, room), BF16),
            pltpu.VMEM((2 * NOCC, room), BF16),
            pltpu.VMEM((nvir // tile, 2, NOCC, tile), BF16),
            pltpu.SemaphoreType.DMA((1 + nvir // tile,)),
        ],
        compiler_params=params(24),
        cost_estimate=cost(2e10, 1),
        name="last_product",
    )(me, half, right, late, *tails)
    return out, over[0], code, got


def per_device(*args):
    n = lax.axis_size("shell")
    here, nvir = args[5].shape
    shells = args[3].shape[0]
    sparse = LIVE_DEV * n * EDGE < n * here
    if not (sparse and n == Z * Y * CORES and here <= 256 and here % 16 == 0 and nvir % 768 == 0):
        return from_start(*args)
    out, over, code, got = short_way(*args)

    def again(carry):
        over, _ = carry
        over, code_now, turned, *held = lax.optimization_barrier((over, code, got, *args[3:]))
        turned = turned.reshape(n, 2, BLK_DEV, EDGE * EDGE).swapaxes(1, 2).reshape(n * BLK_DEV, 2, EDGE * EDGE)
        code_now = jnp.max(code_now, axis=2).reshape(n * BLK_DEV)
        ids = jnp.maximum(code_now, 0)
        pairs = jnp.stack([ids // shells, ids % shells], axis=1)
        return over - 1, long_way(turned, pairs, code_now >= 0, *held)

    return lax.while_loop(lambda carry: carry[0] > 0, again, (over, out))[1]


def solution(mesh):
    placed = (
        P(("groups", "shell"), None, None),
        P(("groups", "shell"), None),
        P(("groups", "shell")),
        P("groups"),
        P(("groups", "shell"), None),
        P(("groups", "shell"), None),
    )
    return jax.shard_map(
        per_device,
        mesh=mesh,
        in_specs=placed,
        out_specs=P(("groups", "shell"), None, None),
        check_vma=False,
    )
```

```python
import functools
import math

import jax
import jax.numpy as jnp
from jax import lax
from jax.experimental import pallas as pl
from jax.experimental.pallas import tpu as pltpu
from jax.sharding import PartitionSpec as P

EDGE = 16
NOCC = 256
BLK_DEV = 8
LIVE_DEV = 4
CAP = 128
Z, Y, CORES = 4, 2, 2
F32 = jnp.float32
BF16 = jnp.bfloat16


def padded_rows(matrix, starts, shell_size):
    offsets = jnp.arange(EDGE, dtype=jnp.int32)
    rows = jnp.minimum(starts[:, None] + offsets[None, :], matrix.shape[0] - 1)
    inside = offsets[None, :] < shell_size[:, None]
    return jnp.where(inside[:, :, None], matrix[rows], jnp.zeros((), matrix.dtype))


def half_transform(slot_rows, pairs, keep, occ_blocks):
    count = slot_rows.shape[0]
    vecs_here = slot_rows.shape[1]
    shells = occ_blocks.shape[0]
    group_size = math.gcd(512, count)
    turns = count // group_size
    shaped = slot_rows.reshape(count, vecs_here, EDGE, EDGE)

    def advance(total, turn):
        first = turn * group_size
        block = lax.dynamic_slice_in_dim(shaped, first, group_size, 0)
        okay = lax.dynamic_slice_in_dim(keep, first, group_size, 0)
        block = jnp.where(okay[:, None, None, None], block, jnp.zeros((), block.dtype))
        row_shell = lax.dynamic_slice_in_dim(pairs[:, 0], first, group_size, 0)
        col_shell = lax.dynamic_slice_in_dim(pairs[:, 1], first, group_size, 0)
        coefs = occ_blocks[row_shell]
        piece = jnp.einsum("kmi,kvmn->kvin", coefs, block, preferred_element_type=jnp.float32)
        return (total.at[col_shell].add(piece), None)

    start_total = jnp.zeros((shells, vecs_here, NOCC, EDGE), jnp.float32)
    half, _ = lax.scan(advance, start_total, jnp.arange(turns, dtype=jnp.int32))
    return half


def long_way(turned, pairs, live, shell_size, occ_coef, vir_coef):
    occ_full = lax.all_gather(occ_coef, "shell", axis=0, tiled=True)
    starts = jnp.cumsum(shell_size) - shell_size
    occ_blocks = padded_rows(occ_full, starts, shell_size)
    half = half_transform(turned, pairs, live, occ_blocks)
    hidden = half.astype(jnp.bfloat16)
    vir_full = lax.all_gather(vir_coef, "shell", axis=0, tiled=True)
    vir_blocks = padded_rows(vir_full, starts, shell_size)
    result = jnp.einsum("svin,sna->via", hidden, vir_blocks, preferred_element_type=jnp.float32)
    return result.astype(jnp.bfloat16)


def from_start(panels, block_pairs, block_count, *rest):
    pairs = lax.all_gather(block_pairs, "shell", axis=0, tiled=True)
    counts = lax.all_gather(block_count, "shell", axis=0, tiled=True)
    turned = lax.all_to_all(panels, "shell", split_axis=1, concat_axis=0, tiled=True)
    position = jnp.arange(turned.shape[0], dtype=jnp.int32)
    live = position % BLK_DEV < counts[position // BLK_DEV]
    return long_way(turned, pairs, live, *rest)


def iota(shape, dim):
    return lax.broadcasted_iota(jnp.int32, shape, dim)


def column_of(row, mask):
    return jnp.sum(jnp.where(mask, row, 0.0), axis=1, keepdims=True)


def row_of(column, mask):
    return jnp.sum(jnp.where(mask, column, 0.0), axis=0, keepdims=True)


def zero_one(mask):
    return jnp.where(mask, 1.0, 0.0)


def lane_value(row, index):
    return jnp.sum(jnp.where(iota(row.shape, 1) == index, row, 0.0), axis=1, keepdims=True)


def one_hots(ids, shells):
    lanes = iota(ids.shape, 1).astype(F32)
    return jnp.concatenate([zero_one(ids == lanes + 128.0 * k) for k in range(shells // 128)], axis=1)


def slot_hots(code, shells):
    code = code.reshape(-1, 128)
    kept = code >= 0
    columns = jnp.where(kept, code % shells, -1).astype(F32)
    return one_hots(columns, shells), one_hots(jnp.where(kept, code // shells, -1).astype(F32), shells)


class Shells:
    def __init__(self, size_row):
        shells = size_row.shape[1]
        sub, lane = iota((shells, shells), 0), iota((shells, shells), 1)
        self.before, self.same = lane < sub, lane == sub
        self.starts = column_of(size_row, self.before)
        self.size = column_of(size_row, self.same)
        self.odd = self.starts - 2.0 * jnp.floor(self.starts * 0.5)


class Used:
    def __init__(self, shells, hot, window):
        self.used = column_of(jnp.max(hot, axis=0, keepdims=True), shells.same)
        self.extra, self.ahead, self.edges = [], [], []
        edge = (iota((hot.shape[1], 128), 1) * window).astype(F32)
        reach = jnp.clip(edge - shells.starts, 0.0, shells.size)
        for parity in range(2):
            extra = 1.0 - shells.odd if parity == 0 else shells.odd
            count = self.used * jnp.floor((shells.size + extra) * 0.5)
            count_row = row_of(count, shells.same)
            self.extra.append(extra)
            self.ahead.append(column_of(count_row, shells.before))
            self.edges.append(jnp.sum(self.used * jnp.floor((reach + extra) * 0.5), axis=0, keepdims=True))


def pack_kernel(vir_ref, occ_ref, panels_ref, *refs):
    outs, (turned_ref,) = refs[:4], refs[4:]
    me = lax.axis_index("shell")
    core, y = lax.rem(me, 2), lax.rem(lax.div(me, 2), 2)
    here, nvir = vir_ref.shape
    rows = here // 2
    width, thin = nvir // CORES, occ_ref.shape[1] // CORES
    turned_ref[...] = jnp.swapaxes(panels_ref[...].astype(F32), 0, 1)
    block = EDGE * EDGE
    for dy in range(2):
        parity = lax.rem(y + dy, 2)
        pick = zero_one(iota((rows, here), 1) == 2 * iota((rows, here), 0) + parity).astype(BF16)
        for dc in range(2):
            half = lax.rem(core + dc, 2)
            out = outs[2 * dy + dc]
            part = vir_ref[:, pl.ds(pl.multiple_of(half * width, 128), width)]
            out[:rows, :width] = jnp.dot(pick, part, preferred_element_type=F32).astype(BF16)
            part = occ_ref[:, pl.ds(pl.multiple_of(half * thin, 128), thin)]
            out[:rows, width:] = jnp.dot(pick, part, preferred_element_type=F32).astype(BF16)
            for z in range(Z):
                device = (z * Y + parity) * CORES + half
                pair = turned_ref[pl.ds(2 * device, 2)].reshape(2 * BLK_DEV, block)
                out[rows:, z * block : (z + 1) * block] = pair.astype(BF16)
            out[rows:, Z * block :] = jnp.zeros((2 * BLK_DEV, out.shape[1] - Z * block), BF16)


def ids_kernel(shells, pairs_ref, count_ref, size_ref, code_ref, size_out_ref):
    size_out_ref[...] = size_ref[...]
    code = pairs_ref[1:2, :] + shells * pairs_ref[0:1, :]
    code = jnp.where(iota((1, BLK_DEV), 1) < count_ref[...], code, -1).astype(F32)
    square = (BLK_DEV, BLK_DEV)
    code = column_of(code, iota(square, 0) == iota(square, 1)).astype(jnp.int32)
    code_ref[...] = jnp.broadcast_to(jnp.broadcast_to(code, (BLK_DEV, 128))[None], code_ref.shape)


def pick_kernel(here, code_ref, size_ref, *refs):
    sources, (out_ref, over_ref, me_ref, panel_ref) = refs[:4], refs[4:]
    me = lax.axis_index("shell")
    me_ref[0] = me
    core, y, z = lax.rem(me, 2), lax.rem(lax.div(me, 2), 2), lax.div(me, 4)
    window = CORES * Y * here
    shell_count = size_ref.shape[1]
    shells = Shells(size_ref[...].astype(F32))
    lists = [Used(shells, hot, window) for hot in slot_hots(code_ref[...], shell_count)]
    most = jnp.zeros((1, 1), F32)
    lane = iota((1, 128), 1)
    for chosen in lists:
        for edges in chosen.edges:
            later = jnp.concatenate([edges[:, 1:], edges[:, :1]], axis=1)
            most = jnp.maximum(most, jnp.max(jnp.where(lane < Z, later - edges, 0.0), axis=1, keepdims=True))
    over_ref[0] = jnp.where(jnp.max(most) > CAP, 1, 0).astype(jnp.int32)

    width = out_ref.shape[1] - 128
    even = y == 0
    totals = [jnp.zeros((CAP, width), F32), jnp.zeros((CAP, 128), F32)]
    columns = [slice(0, width), slice(width, width + 128)]
    extra = jnp.where(even, lists[0].extra[0], lists[0].extra[1])
    rows = here // 2
    for k, source in enumerate(sources):
        member = 2 * lax.rem(y + k // 2, 2) + lax.rem(core + k % 2, 2)
        device = 4 * z + member
        for to_z in range(Z):
            panel_ref[to_z, member] = source[rows:, to_z * EDGE * EDGE : (to_z + 1) * EDGE * EDGE]
        row = (2 * iota((shell_count, 128), 1) + device * here + y).astype(F32)
        where = row - shells.starts
        inside = (where >= 0.0) & (where < shells.size)
        within = jnp.floor((where + extra) * 0.5)
        for chosen, total, column in zip(lists, range(2), columns):
            ahead = jnp.where(even, chosen.ahead[0], chosen.ahead[1])
            base = lane_value(jnp.where(even, chosen.edges[0], chosen.edges[1]), z)
            place = jnp.where(inside & (chosen.used > 0.0), ahead + within + 1.0, 0.0)
            place = jnp.sum(place, axis=0, keepdims=True)
            place = jnp.where(place > 0.0, place - 1.0 - base, -1.0)
            hot = zero_one(place == iota((CAP, 128), 0).astype(F32)).astype(BF16)
            totals[total] += jnp.dot(
                hot[:, :rows], source[:rows, column], preferred_element_type=F32
            )
    for total, column in zip(totals, columns):
        out_ref[:, column] = total.astype(BF16)


def slot_of(window, chip):
    rel = window ^ chip
    early = jnp.where((rel == 3) | (rel == 4), rel ^ 7, rel)
    return jnp.where((rel == 5) | (rel == 6), rel ^ 3, early)


def half_kernel(here, early, code_ref, got_ref, size_ref, *refs):
    pieces, refs = refs[: 2 * early], refs[2 * early :]
    half_ref, late_ref, occ_ref, part_ref, hot_ref, placed_ref, sems = refs
    me = lax.axis_index("shell")
    core, chip = lax.rem(me, CORES), lax.div(me, CORES)
    width = pieces[0].shape[1] - 128
    copies = []
    for far in range(2):
        half = lax.rem(core + far, CORES)
        for k in range(early):
            at = far * early + k
            target = occ_ref.at[pl.ds(k * CAP, CAP), pl.ds(pl.multiple_of(half * 128, 128), 128)]
            copies.append(pltpu.make_async_copy(pieces[at].at[:, pl.ds(width, 128)], target, sems.at[at]))
    for copy in copies:
        copy.start()
    window = CORES * Y * here
    shell_count = size_ref.shape[1]
    got = got_ref[...].astype(F32)
    size_row = size_ref[...].astype(F32)
    shells = Shells(size_row)
    got = got_ref[...].astype(F32)
    hots = slot_hots(code_ref[...], shell_count)
    lists = [Used(shells, hot, window) for hot in hots]
    slots = hots[0].shape[0]
    kept = LIVE_DEV * (slots // BLK_DEV)
    alive = jnp.broadcast_to(jnp.sum(hots[0], axis=1, keepdims=True), (slots, slots))
    sub, lane = iota((slots, slots), 0), iota((slots, slots), 1)
    rank = row_of(alive, sub < lane)
    alive_row = row_of(alive, sub == lane)
    take = (rank == iota((kept, slots), 0).astype(F32)) & (alive_row > 0.0)
    take = zero_one(take).astype(BF16)

    def taken(array):
        return jnp.dot(take, array.astype(BF16), preferred_element_type=F32)

    def spread(hot, column):
        value = jnp.sum(hot * row_of(column, shells.same), axis=1, keepdims=True)
        wide = jnp.broadcast_to(value, (kept, 128)).reshape(kept, 1, 128)
        return jnp.broadcast_to(wide, (kept, EDGE, 128)).reshape(kept * EDGE, 128)

    at = iota((kept * EDGE, 128), 0) % EDGE
    step = at.astype(F32)

    def places(hot, chosen):
        hot = taken(hot)
        first, length = spread(hot, shells.starts), spread(hot, shells.size)
        row = first + step
        odd = (row - 2.0 * jnp.floor(row * 0.5)) > 0.0
        place = jnp.where(odd, spread(hot, chosen.ahead[1]), spread(hot, chosen.ahead[0]))
        place += jnp.floor(step * 0.5)
        offsets = [
            [slot_of(w * Y + k, chip).astype(F32) * CAP - lane_value(e, w) for w in range(Z)]
            for k, e in enumerate(chosen.edges)
        ]
        offset = jnp.where(odd, offsets[1][0], offsets[0][0])
        for w in range(1, Z):
            offset = jnp.where(row >= float(window * w), jnp.where(odd, offsets[1][w], offsets[0][w]), offset)
        return jnp.where(step < length, place + offset, -1.0)[:, :1]

    place_c, place_r = places(hots[0], lists[0]), places(hots[1], lists[1])
    span = 16 * EDGE
    s_in, l_in = iota((span, span), 0), iota((span, span), 1)
    keep_m = (l_in // EDGE) == (s_in % EDGE)
    fold = zero_one((s_in % EDGE) == (l_in % EDGE)).astype(BF16)
    same_slot = (s_in // EDGE) == (l_in // EDGE)
    blocks = [taken(got[:, p * BLK_DEV : (p + 1) * BLK_DEV, :].reshape(slots, span)) for p in range(2)]
    lanes = iota((span, half_ref.shape[1]), 1).astype(F32)
    for copy in copies:
        copy.wait()
    occ = occ_ref[...]
    cut = early * CAP
    for g in range(kept // 16):
        rows = slice(g * span, (g + 1) * span)
        r_hot = zero_one(place_r[rows] == lanes).astype(BF16)
        c_hot = zero_one(place_c[rows] == lanes).astype(BF16)
        part_ref[:, rows] = jnp.dot(r_hot[:, :cut], occ, preferred_element_type=F32).T.astype(BF16)
        hot_ref[:, rows] = r_hot[:, cut:].T
        for p in range(2):
            block = blocks[p][g * 16 : (g + 1) * 16].reshape(16, 1, span)
            block = jnp.broadcast_to(block, (16, EDGE, span)).reshape(span, span)
            block = jnp.where(keep_m, block, 0.0).astype(BF16)
            diag = jnp.dot(block, fold, preferred_element_type=F32)
            diag = jnp.where(same_slot, diag, 0.0).astype(BF16)
            placed_ref[p, rows, :] = jnp.dot(diag, c_hot, preferred_element_type=F32).astype(BF16)
    for p in range(2):
        half_ref[p * NOCC : (p + 1) * NOCC, :] = jnp.dot(part_ref[...], placed_ref[p], preferred_element_type=F32)
        late_ref[p] = jnp.dot(hot_ref[...], placed_ref[p], preferred_element_type=F32).astype(BF16)


def gather_kernel(early, me_ref, part_ref, late_ref, *refs):
    count = (len(refs) - 4) // 2
    pieces, (right_ref, half_ref, occ_ref, sems) = refs[: 2 * count], refs[2 * count :]
    width = right_ref.shape[2]
    core = lax.rem(me_ref[0], CORES)
    first, copies = [], []
    for side in range(2):
        half = lax.rem(core + side, CORES)
        for k in range(count):
            at = side * count + k
            if k >= early:
                target = occ_ref.at[pl.ds((k - early) * CAP, CAP), pl.ds(pl.multiple_of(half * 128, 128), 128)]
                source = pieces[at].at[:, pl.ds(width, 128)]
                first.append(pltpu.make_async_copy(source, target, sems.at[2 * count + at]))
            target = right_ref.at[side, pl.ds(k * CAP, CAP), :]
            copies.append(pltpu.make_async_copy(pieces[at].at[:, pl.ds(0, width)], target, sems.at[at]))
    for copy in (*first, *copies):
        copy.start()
    for copy in first:
        copy.wait()
    occ = occ_ref[...].T
    for p in range(2):
        rows = slice(p * NOCC, (p + 1) * NOCC)
        late = jnp.dot(occ, late_ref[p, : occ_ref.shape[0], :], preferred_element_type=F32)
        half_ref[rows, :] = part_ref[rows, :] + late
    for copy in copies:
        copy.wait()


def last_kernel(me_ref, part_ref, right_ref, late_any, *refs):
    pieces, (out_any, late_ref, half_ref, tiles_ref, sems) = (refs[:2], refs[2:4]), refs[4:]
    width = right_ref.shape[2]
    cut = right_ref.shape[1]
    tile = tiles_ref.shape[3]
    per = width // tile
    core = lax.rem(me_ref[0], CORES)
    rows = late_any.shape[1] - 2 * CAP
    copy = pltpu.make_async_copy(late_any.at[:, pl.ds(rows, 2 * CAP), :], late_ref, sems.at[0])
    copy.start()
    copy.wait()
    sides = [jnp.concatenate([ref[:, width:] for ref in side], axis=0).T for side in pieces]
    for p in range(2):
        for side, occ in enumerate(sides):
            half = lax.rem(core + side, CORES)
            rows = pl.ds(pl.multiple_of(p * NOCC + half * 128, 128), 128)
            late = jnp.dot(occ, late_ref[p], preferred_element_type=F32)
            half_ref[rows, :] = (part_ref[rows, :] + late).astype(BF16)
    results = []
    for side, tail in enumerate(pieces):
        base = lax.rem(core + side, CORES) * width
        for t in range(per):
            columns = slice(t * tile, (t + 1) * tile)
            total = jnp.dot(half_ref[:, :cut], right_ref[side, :, columns], preferred_element_type=F32)
            below = jnp.concatenate([ref[:, columns] for ref in tail], axis=0)
            total += jnp.dot(half_ref[:, cut:], below, preferred_element_type=F32)
            at = side * per + t
            tiles_ref[at] = total.astype(BF16).reshape(tiles_ref.shape[1:])
            target = out_any.at[:, :, pl.ds(pl.multiple_of(base + t * tile, 128), tile)]
            results.append(pltpu.make_async_copy(tiles_ref.at[at], target, sems.at[1 + at]))
            results[-1].start()
    for copy in results:
        copy.wait()


VMEM = pl.BlockSpec(memory_space=pltpu.VMEM)
SMEM = pl.BlockSpec(memory_space=pltpu.SMEM)
ANY = pl.BlockSpec(memory_space=pl.ANY)


def shape(*dims, dtype=BF16):
    return jax.ShapeDtypeStruct(dims, dtype)


def params(mib):
    return pltpu.CompilerParams(vmem_limit_bytes=mib << 20)


def cost(flops, nbytes):
    return pl.CostEstimate(flops=int(flops), bytes_accessed=int(nbytes), transcendentals=0)


def short_way(panels, block_pairs, block_count, shell_size, occ_coef, vir_coef):
    n = lax.axis_size("shell")
    here, nvir = vir_coef.shape
    width = nvir // CORES
    packed = width + NOCC // CORES
    room = Z * Y * CAP
    size_row = shell_size.reshape(1, -1)

    def swap(array, bit):
        return lax.ppermute(array, "shell", [(i, i ^ bit) for i in range(n)])

    code, size_row = pl.pallas_call(
        functools.partial(ids_kernel, size_row.shape[1]),
        out_shape=(shape(n, BLK_DEV, 128, dtype=jnp.int32), shape(*size_row.shape, dtype=jnp.int32)),
        in_specs=[VMEM] * 3,
        out_specs=(VMEM, VMEM),
        compiler_params=params(12),
        cost_estimate=cost(1e4, 1e4),
        name="pack_ids",
    )(block_pairs.T, block_count.reshape(1, 1), size_row)
    code, panels = lax.optimization_barrier((code, panels))
    keep, to_core, to_y, to_both = pl.pallas_call(
        pack_kernel,
        out_shape=[shape(here // 2 + 2 * BLK_DEV, packed)] * 4,
        in_specs=[VMEM] * 3,
        out_specs=[VMEM] * 4,
        scratch_shapes=[pltpu.VMEM((2 * n, BLK_DEV, EDGE * EDGE), F32)],
        compiler_params=params(12),
        cost_estimate=cost(3e8, 3e6),
        name="pack_rows",
    )(vir_coef, occ_coef, panels)
    to_y, to_both, to_core = swap(to_y, 2), swap(to_both, 3), swap(to_core, 1)
    code = lax.all_to_all(code, "shell", split_axis=0, concat_axis=0, tiled=True)

    mine, over, me, panel = pl.pallas_call(
        functools.partial(pick_kernel, here),
        out_shape=[shape(CAP, packed), shape(1, dtype=jnp.int32), shape(1, dtype=jnp.int32)]
        + [shape(Z, Y * CORES, 2 * BLK_DEV, EDGE * EDGE)],
        in_specs=[VMEM] * 6,
        out_specs=[VMEM, SMEM, SMEM, VMEM],
        compiler_params=params(12),
        cost_estimate=cost(3e8, 2e6),
        name="pick_rows",
    )(code, size_row, keep, to_core, to_y, to_both)

    across, mine_y, beside = swap(mine, 8), swap(mine, 2), swap(mine, 4)
    lines = [[Y * CORES * z + k for z in range(Z)] for k in range(Y * CORES)]
    got = lax.all_to_all(panel, "shell", split_axis=0, concat_axis=0, axis_index_groups=lines, tiled=True)
    got = got.reshape(n, 2 * BLK_DEV, EDGE * EDGE)
    far = [swap(mine, 1)]
    across, mine_y, beside, got, *far = lax.optimization_barrier((across, mine_y, beside, got, *far))

    corner, beside_y, across_y = swap(across, 4), swap(beside, 2), swap(across, 2)
    near = [mine, mine_y, beside, across]
    far += [swap(piece, 1) for piece in near[1:]]
    early = len(near)
    slots = LIVE_DEV * n * EDGE
    half, late = pl.pallas_call(
        functools.partial(half_kernel, here, early),
        out_shape=(shape(2 * NOCC, room, dtype=F32), shape(2, room - early * CAP, room)),
        grid=(1,),
        in_specs=[VMEM] * 3 + [ANY] * (2 * early),
        out_specs=(
            pl.BlockSpec((2 * NOCC, room), lambda i: (0, 0)),
            pl.BlockSpec((2, room - early * CAP, room), lambda i: (0, 0, 0)),
        ),
        scratch_shapes=[
            pltpu.VMEM((early * CAP, NOCC), BF16),
            pltpu.VMEM((NOCC, slots), BF16),
            pltpu.VMEM((room - early * CAP, slots), BF16),
            pltpu.VMEM((2, slots, room), BF16),
            pltpu.SemaphoreType.DMA((2 * early,)),
        ],
        compiler_params=params(30),
        cost_estimate=cost(7e9, 1),
        name="half_transform",
    )(code, got, size_row, *near, *far)
    corner, beside_y, half, late = lax.optimization_barrier((corner, beside_y, half, late))
    corner_y = swap(corner, 2)
    near += [beside_y, corner]
    far += [swap(piece, 1) for piece in near[early:]]
    count = len(near)
    right, half = pl.pallas_call(
        functools.partial(gather_kernel, early),
        out_shape=(shape(CORES, count * CAP, width), shape(2 * NOCC, room, dtype=F32)),
        in_specs=[SMEM] + [VMEM] * 2 + [ANY] * (2 * count),
        out_specs=(VMEM, VMEM),
        scratch_shapes=[pltpu.VMEM(((count - early) * CAP, NOCC), BF16), pltpu.SemaphoreType.DMA((4 * count,))],
        compiler_params=params(20),
        cost_estimate=cost(1, 1),
        name="gather_pieces",
    )(me, half, late, *near, *far)
    corner_y, right, half = lax.optimization_barrier((corner_y, right, half))
    tails = [across_y, corner_y, swap(across_y, 1), swap(corner_y, 1)]

    tile = width // 3
    out = pl.pallas_call(
        last_kernel,
        out_shape=shape(2, NOCC, nvir),
        in_specs=[SMEM] + [VMEM] * 2 + [ANY] + [VMEM] * 4,
        out_specs=ANY,
        scratch_shapes=[
            pltpu.VMEM((2, 2 * CAP, room), BF16),
            pltpu.VMEM((2 * NOCC, room), BF16),
            pltpu.VMEM((nvir // tile, 2, NOCC, tile), BF16),
            pltpu.SemaphoreType.DMA((1 + nvir // tile,)),
        ],
        compiler_params=params(24),
        cost_estimate=cost(2e10, 1),
        name="last_product",
    )(me, half, right, late, *tails)
    return out, over[0], code, got


def per_device(*args):
    n = lax.axis_size("shell")
    here, nvir = args[5].shape
    shells = args[3].shape[0]
    sparse = LIVE_DEV * n * EDGE < n * here
    if not (sparse and n == Z * Y * CORES and here <= 256 and here % 16 == 0 and nvir % 768 == 0):
        return from_start(*args)
    out, over, code, got = short_way(*args)

    def again(carry):
        over, _ = carry
        over, code_now, turned, *held = lax.optimization_barrier((over, code, got, *args[3:]))
        turned = turned.reshape(n, 2, BLK_DEV, EDGE * EDGE).swapaxes(1, 2).reshape(n * BLK_DEV, 2, EDGE * EDGE)
        code_now = jnp.max(code_now, axis=2).reshape(n * BLK_DEV)
        ids = jnp.maximum(code_now, 0)
        pairs = jnp.stack([ids // shells, ids % shells], axis=1)
        return over - 1, long_way(turned, pairs, code_now >= 0, *held)

    return lax.while_loop(lambda carry: carry[0] > 0, again, (over, out))[1]


def solution(mesh):
    placed = (
        P(("groups", "shell"), None, None),
        P(("groups", "shell"), None),
        P(("groups", "shell")),
        P("groups"),
        P(("groups", "shell"), None),
        P(("groups", "shell"), None),
    )
    return jax.shard_map(
        per_device,
        mesh=mesh,
        in_specs=placed,
        out_specs=P(("groups", "shell"), None, None),
        check_vma=False,
    )
```

```python
import functools
import math

import jax
import jax.numpy as jnp
from jax import lax
from jax.experimental import pallas as pl
from jax.experimental.pallas import tpu as pltpu
from jax.sharding import PartitionSpec as P

EDGE = 16
NOCC = 256
BLK_DEV = 8
LIVE_DEV = 4
CAP = 128
Z, Y, CORES = 4, 2, 2
F32 = jnp.float32
BF16 = jnp.bfloat16


def padded_rows(matrix, starts, shell_size):
    offsets = jnp.arange(EDGE, dtype=jnp.int32)
    rows = jnp.minimum(starts[:, None] + offsets[None, :], matrix.shape[0] - 1)
    inside = offsets[None, :] < shell_size[:, None]
    return jnp.where(inside[:, :, None], matrix[rows], jnp.zeros((), matrix.dtype))


def half_transform(slot_rows, pairs, keep, occ_blocks):
    count = slot_rows.shape[0]
    vecs_here = slot_rows.shape[1]
    shells = occ_blocks.shape[0]
    group_size = math.gcd(512, count)
    turns = count // group_size
    shaped = slot_rows.reshape(count, vecs_here, EDGE, EDGE)

    def advance(total, turn):
        first = turn * group_size
        block = lax.dynamic_slice_in_dim(shaped, first, group_size, 0)
        okay = lax.dynamic_slice_in_dim(keep, first, group_size, 0)
        block = jnp.where(okay[:, None, None, None], block, jnp.zeros((), block.dtype))
        row_shell = lax.dynamic_slice_in_dim(pairs[:, 0], first, group_size, 0)
        col_shell = lax.dynamic_slice_in_dim(pairs[:, 1], first, group_size, 0)
        coefs = occ_blocks[row_shell]
        piece = jnp.einsum("kmi,kvmn->kvin", coefs, block, preferred_element_type=jnp.float32)
        return (total.at[col_shell].add(piece), None)

    start_total = jnp.zeros((shells, vecs_here, NOCC, EDGE), jnp.float32)
    half, _ = lax.scan(advance, start_total, jnp.arange(turns, dtype=jnp.int32))
    return half


def long_way(turned, pairs, live, shell_size, occ_coef, vir_coef):
    occ_full = lax.all_gather(occ_coef, "shell", axis=0, tiled=True)
    starts = jnp.cumsum(shell_size) - shell_size
    occ_blocks = padded_rows(occ_full, starts, shell_size)
    half = half_transform(turned, pairs, live, occ_blocks)
    hidden = half.astype(jnp.bfloat16)
    vir_full = lax.all_gather(vir_coef, "shell", axis=0, tiled=True)
    vir_blocks = padded_rows(vir_full, starts, shell_size)
    result = jnp.einsum("svin,sna->via", hidden, vir_blocks, preferred_element_type=jnp.float32)
    return result.astype(jnp.bfloat16)


def from_start(panels, block_pairs, block_count, *rest):
    pairs = lax.all_gather(block_pairs, "shell", axis=0, tiled=True)
    counts = lax.all_gather(block_count, "shell", axis=0, tiled=True)
    turned = lax.all_to_all(panels, "shell", split_axis=1, concat_axis=0, tiled=True)
    position = jnp.arange(turned.shape[0], dtype=jnp.int32)
    live = position % BLK_DEV < counts[position // BLK_DEV]
    return long_way(turned, pairs, live, *rest)


def iota(shape, dim):
    return lax.broadcasted_iota(jnp.int32, shape, dim)


def column_of(row, mask):
    return jnp.sum(jnp.where(mask, row, 0.0), axis=1, keepdims=True)


def row_of(column, mask):
    return jnp.sum(jnp.where(mask, column, 0.0), axis=0, keepdims=True)


def zero_one(mask):
    return jnp.where(mask, 1.0, 0.0)


def lane_value(row, index):
    return jnp.sum(jnp.where(iota(row.shape, 1) == index, row, 0.0), axis=1, keepdims=True)


def one_hots(ids, shells):
    lanes = iota(ids.shape, 1).astype(F32)
    return jnp.concatenate([zero_one(ids == lanes + 128.0 * k) for k in range(shells // 128)], axis=1)


def slot_hots(code, shells):
    code = code.reshape(-1, 128)
    kept = code >= 0
    columns = jnp.where(kept, code % shells, -1).astype(F32)
    return one_hots(columns, shells), one_hots(jnp.where(kept, code // shells, -1).astype(F32), shells)


class Shells:
    def __init__(self, size_row):
        shells = size_row.shape[1]
        sub, lane = iota((shells, shells), 0), iota((shells, shells), 1)
        self.before, self.same = lane < sub, lane == sub
        self.starts = column_of(size_row, self.before)
        self.size = column_of(size_row, self.same)
        self.odd = self.starts - 2.0 * jnp.floor(self.starts * 0.5)


class Used:
    def __init__(self, shells, hot, window):
        self.used = column_of(jnp.max(hot, axis=0, keepdims=True), shells.same)
        self.extra, self.ahead, self.edges = [], [], []
        edge = (iota((hot.shape[1], 128), 1) * window).astype(F32)
        reach = jnp.clip(edge - shells.starts, 0.0, shells.size)
        for parity in range(2):
            extra = 1.0 - shells.odd if parity == 0 else shells.odd
            count = self.used * jnp.floor((shells.size + extra) * 0.5)
            count_row = row_of(count, shells.same)
            self.extra.append(extra)
            self.ahead.append(column_of(count_row, shells.before))
            self.edges.append(jnp.sum(self.used * jnp.floor((reach + extra) * 0.5), axis=0, keepdims=True))


def pack_kernel(vir_ref, occ_ref, panels_ref, *refs):
    outs, (turned_ref,) = refs[:4], refs[4:]
    me = lax.axis_index("shell")
    core, y = lax.rem(me, 2), lax.rem(lax.div(me, 2), 2)
    here, nvir = vir_ref.shape
    rows = here // 2
    width, thin = nvir // CORES, occ_ref.shape[1] // CORES
    turned_ref[...] = jnp.swapaxes(panels_ref[...].astype(F32), 0, 1)
    block = EDGE * EDGE
    for dy in range(2):
        parity = lax.rem(y + dy, 2)
        pick = zero_one(iota((rows, here), 1) == 2 * iota((rows, here), 0) + parity).astype(BF16)
        for dc in range(2):
            half = lax.rem(core + dc, 2)
            out = outs[2 * dy + dc]
            part = vir_ref[:, pl.ds(pl.multiple_of(half * width, 128), width)]
            out[:rows, :width] = jnp.dot(pick, part, preferred_element_type=F32).astype(BF16)
            part = occ_ref[:, pl.ds(pl.multiple_of(half * thin, 128), thin)]
            out[:rows, width:] = jnp.dot(pick, part, preferred_element_type=F32).astype(BF16)
            for z in range(Z):
                device = (z * Y + parity) * CORES + half
                pair = turned_ref[pl.ds(2 * device, 2)].reshape(2 * BLK_DEV, block)
                out[rows:, z * block : (z + 1) * block] = pair.astype(BF16)
            out[rows:, Z * block :] = jnp.zeros((2 * BLK_DEV, out.shape[1] - Z * block), BF16)


def ids_kernel(shells, pairs_ref, count_ref, code_ref):
    code = pairs_ref[1:2, :] + shells * pairs_ref[0:1, :]
    code = jnp.where(iota((1, BLK_DEV), 1) < count_ref[...], code, -1).astype(F32)
    square = (BLK_DEV, BLK_DEV)
    code = column_of(code, iota(square, 0) == iota(square, 1)).astype(jnp.int32)
    code_ref[...] = jnp.broadcast_to(jnp.broadcast_to(code, (BLK_DEV, 128))[None], code_ref.shape)


def pick_kernel(here, code_ref, size_ref, *refs):
    sources, (out_ref, over_ref, me_ref), panel_refs = refs[:4], refs[4:7], refs[7:]
    me = lax.axis_index("shell")
    me_ref[0] = me
    core, y, z = lax.rem(me, 2), lax.rem(lax.div(me, 2), 2), lax.div(me, 4)
    window = CORES * Y * here
    shell_count = size_ref.shape[1]
    shells = Shells(size_ref[...].astype(F32))
    lists = [Used(shells, hot, window) for hot in slot_hots(code_ref[...], shell_count)]
    most = jnp.zeros((1, 1), F32)
    lane = iota((1, 128), 1)
    for chosen in lists:
        for edges in chosen.edges:
            later = jnp.concatenate([edges[:, 1:], edges[:, :1]], axis=1)
            most = jnp.maximum(most, jnp.max(jnp.where(lane < Z, later - edges, 0.0), axis=1, keepdims=True))
    over_ref[0] = jnp.where(jnp.max(most) > CAP, 1, 0).astype(jnp.int32)

    width = out_ref.shape[1] - 128
    even = y == 0
    totals = [jnp.zeros((CAP, width), F32), jnp.zeros((CAP, 128), F32)]
    columns = [slice(0, width), slice(width, width + 128)]
    extra = jnp.where(even, lists[0].extra[0], lists[0].extra[1])
    rows = here // 2
    for k, source in enumerate(sources):
        member = 2 * lax.rem(y + k // 2, 2) + lax.rem(core + k % 2, 2)
        device = 4 * z + member
        for r, panel_ref in enumerate(panel_refs):
            lanes = pl.ds(pl.multiple_of((z ^ r) * (EDGE * EDGE), 128), EDGE * EDGE)
            panel_ref[member] = source[rows:, lanes]
        row = (2 * iota((shell_count, 128), 1) + device * here + y).astype(F32)
        where = row - shells.starts
        inside = (where >= 0.0) & (where < shells.size)
        within = jnp.floor((where + extra) * 0.5)
        for chosen, total, column in zip(lists, range(2), columns):
            ahead = jnp.where(even, chosen.ahead[0], chosen.ahead[1])
            base = lane_value(jnp.where(even, chosen.edges[0], chosen.edges[1]), z)
            place = jnp.where(inside & (chosen.used > 0.0), ahead + within + 1.0, 0.0)
            place = jnp.sum(place, axis=0, keepdims=True)
            place = jnp.where(place > 0.0, place - 1.0 - base, -1.0)
            hot = zero_one(place == iota((CAP, 128), 0).astype(F32)).astype(BF16)
            totals[total] += jnp.dot(
                hot[:, :rows], source[:rows, column], preferred_element_type=F32
            )
    for total, column in zip(totals, columns):
        out_ref[:, column] = total.astype(BF16)


def slot_of(window, chip):
    rel = window ^ chip
    early = jnp.where((rel == 3) | (rel == 4), rel ^ 7, rel)
    return jnp.where((rel == 5) | (rel == 6), rel ^ 3, early)


def half_kernel(here, early, code_ref, size_ref, *refs):
    panel_refs, pieces, refs = refs[:Z], refs[Z : Z + 2 * early], refs[Z + 2 * early :]
    half_ref, late_ref, all_ref, got_ref, occ_ref, part_ref, hot_ref, placed_ref, sems = refs
    me = lax.axis_index("shell")
    core, chip = lax.rem(me, CORES), lax.div(me, CORES)
    z = lax.div(chip, Y)
    width = pieces[0].shape[1] - 128
    copies = []
    for far in range(2):
        half = lax.rem(core + far, CORES)
        for k in range(early):
            at = far * early + k
            target = occ_ref.at[pl.ds(k * CAP, CAP), pl.ds(pl.multiple_of(half * 128, 128), 128)]
            copies.append(pltpu.make_async_copy(pieces[at].at[:, pl.ds(width, 128)], target, sems.at[at]))
    for copy in copies:
        copy.start()
    for r, panel_ref in enumerate(panel_refs):
        got_ref[pl.ds((z ^ r) * (Y * CORES), Y * CORES)] = panel_ref[...]
    all_ref[...] = got_ref[...]
    window = CORES * Y * here
    shell_count = size_ref.shape[1]
    got = got_ref[...].astype(F32)
    size_row = size_ref[...].astype(F32)
    shells = Shells(size_row)
    got = got_ref[...].astype(F32)
    hots = slot_hots(code_ref[...], shell_count)
    lists = [Used(shells, hot, window) for hot in hots]
    slots = hots[0].shape[0]
    kept = LIVE_DEV * (slots // BLK_DEV)
    alive = jnp.broadcast_to(jnp.sum(hots[0], axis=1, keepdims=True), (slots, slots))
    sub, lane = iota((slots, slots), 0), iota((slots, slots), 1)
    rank = row_of(alive, sub < lane)
    alive_row = row_of(alive, sub == lane)
    take = (rank == iota((kept, slots), 0).astype(F32)) & (alive_row > 0.0)
    take = zero_one(take).astype(BF16)

    def taken(array):
        return jnp.dot(take, array.astype(BF16), preferred_element_type=F32)

    def spread(hot, column):
        value = jnp.sum(hot * row_of(column, shells.same), axis=1, keepdims=True)
        wide = jnp.broadcast_to(value, (kept, 128)).reshape(kept, 1, 128)
        return jnp.broadcast_to(wide, (kept, EDGE, 128)).reshape(kept * EDGE, 128)

    at = iota((kept * EDGE, 128), 0) % EDGE
    step = at.astype(F32)

    def places(hot, chosen):
        hot = taken(hot)
        first, length = spread(hot, shells.starts), spread(hot, shells.size)
        row = first + step
        odd = (row - 2.0 * jnp.floor(row * 0.5)) > 0.0
        place = jnp.where(odd, spread(hot, chosen.ahead[1]), spread(hot, chosen.ahead[0]))
        place += jnp.floor(step * 0.5)
        offsets = [
            [slot_of(w * Y + k, chip).astype(F32) * CAP - lane_value(e, w) for w in range(Z)]
            for k, e in enumerate(chosen.edges)
        ]
        offset = jnp.where(odd, offsets[1][0], offsets[0][0])
        for w in range(1, Z):
            offset = jnp.where(row >= float(window * w), jnp.where(odd, offsets[1][w], offsets[0][w]), offset)
        return jnp.where(step < length, place + offset, -1.0)[:, :1]

    place_c, place_r = places(hots[0], lists[0]), places(hots[1], lists[1])
    span = 16 * EDGE
    s_in, l_in = iota((span, span), 0), iota((span, span), 1)
    keep_m = (l_in // EDGE) == (s_in % EDGE)
    fold = zero_one((s_in % EDGE) == (l_in % EDGE)).astype(BF16)
    same_slot = (s_in // EDGE) == (l_in // EDGE)
    blocks = [taken(got[:, p * BLK_DEV : (p + 1) * BLK_DEV, :].reshape(slots, span)) for p in range(2)]
    lanes = iota((span, half_ref.shape[1]), 1).astype(F32)
    for copy in copies:
        copy.wait()
    occ = occ_ref[...]
    cut = early * CAP
    for g in range(kept // 16):
        rows = slice(g * span, (g + 1) * span)
        r_hot = zero_one(place_r[rows] == lanes).astype(BF16)
        c_hot = zero_one(place_c[rows] == lanes).astype(BF16)
        part_ref[:, rows] = jnp.dot(r_hot[:, :cut], occ, preferred_element_type=F32).T.astype(BF16)
        hot_ref[:, rows] = r_hot[:, cut:].T
        for p in range(2):
            block = blocks[p][g * 16 : (g + 1) * 16].reshape(16, 1, span)
            block = jnp.broadcast_to(block, (16, EDGE, span)).reshape(span, span)
            block = jnp.where(keep_m, block, 0.0).astype(BF16)
            diag = jnp.dot(block, fold, preferred_element_type=F32)
            diag = jnp.where(same_slot, diag, 0.0).astype(BF16)
            placed_ref[p, rows, :] = jnp.dot(diag, c_hot, preferred_element_type=F32).astype(BF16)
    for p in range(2):
        half_ref[p * NOCC : (p + 1) * NOCC, :] = jnp.dot(part_ref[...], placed_ref[p], preferred_element_type=F32)
        late_ref[p] = jnp.dot(hot_ref[...], placed_ref[p], preferred_element_type=F32).astype(BF16)


def gather_kernel(early, me_ref, part_ref, late_ref, *refs):
    count = (len(refs) - 4) // 2
    pieces, (right_ref, half_ref, occ_ref, sems) = refs[: 2 * count], refs[2 * count :]
    width = right_ref.shape[2]
    core = lax.rem(me_ref[0], CORES)
    first, copies = [], []
    for side in range(2):
        half = lax.rem(core + side, CORES)
        for k in range(count):
            at = side * count + k
            if k >= early:
                target = occ_ref.at[pl.ds((k - early) * CAP, CAP), pl.ds(pl.multiple_of(half * 128, 128), 128)]
                source = pieces[at].at[:, pl.ds(width, 128)]
                first.append(pltpu.make_async_copy(source, target, sems.at[2 * count + at]))
            target = right_ref.at[side, pl.ds(k * CAP, CAP), :]
            copies.append(pltpu.make_async_copy(pieces[at].at[:, pl.ds(0, width)], target, sems.at[at]))
    for copy in (*first, *copies):
        copy.start()
    for copy in first:
        copy.wait()
    occ = occ_ref[...].T
    for p in range(2):
        rows = slice(p * NOCC, (p + 1) * NOCC)
        late = jnp.dot(occ, late_ref[p, : occ_ref.shape[0], :], preferred_element_type=F32)
        half_ref[rows, :] = part_ref[rows, :] + late
    for copy in copies:
        copy.wait()


def last_kernel(me_ref, part_ref, right_ref, late_any, *refs):
    pieces, (out_any, late_ref, half_ref, tiles_ref, sems) = (refs[:2], refs[2:4]), refs[4:]
    width = right_ref.shape[2]
    cut = right_ref.shape[1]
    tile = tiles_ref.shape[3]
    per = width // tile
    core = lax.rem(me_ref[0], CORES)
    rows = late_any.shape[1] - 2 * CAP
    copy = pltpu.make_async_copy(late_any.at[:, pl.ds(rows, 2 * CAP), :], late_ref, sems.at[0])
    copy.start()
    copy.wait()
    sides = [jnp.concatenate([ref[:, width:] for ref in side], axis=0).T for side in pieces]
    for p in range(2):
        for side, occ in enumerate(sides):
            half = lax.rem(core + side, CORES)
            rows = pl.ds(pl.multiple_of(p * NOCC + half * 128, 128), 128)
            late = jnp.dot(occ, late_ref[p], preferred_element_type=F32)
            half_ref[rows, :] = (part_ref[rows, :] + late).astype(BF16)
    results = []
    for side, tail in enumerate(pieces):
        base = lax.rem(core + side, CORES) * width
        for t in range(per):
            columns = slice(t * tile, (t + 1) * tile)
            total = jnp.dot(half_ref[:, :cut], right_ref[side, :, columns], preferred_element_type=F32)
            below = jnp.concatenate([ref[:, columns] for ref in tail], axis=0)
            total += jnp.dot(half_ref[:, cut:], below, preferred_element_type=F32)
            at = side * per + t
            tiles_ref[at] = total.astype(BF16).reshape(tiles_ref.shape[1:])
            target = out_any.at[:, :, pl.ds(pl.multiple_of(base + t * tile, 128), tile)]
            results.append(pltpu.make_async_copy(tiles_ref.at[at], target, sems.at[1 + at]))
            results[-1].start()
    for copy in results:
        copy.wait()


VMEM = pl.BlockSpec(memory_space=pltpu.VMEM)
SMEM = pl.BlockSpec(memory_space=pltpu.SMEM)
ANY = pl.BlockSpec(memory_space=pl.ANY)


def shape(*dims, dtype=BF16):
    return jax.ShapeDtypeStruct(dims, dtype)


def params(mib):
    return pltpu.CompilerParams(vmem_limit_bytes=mib << 20)


def cost(flops, nbytes):
    return pl.CostEstimate(flops=int(flops), bytes_accessed=int(nbytes), transcendentals=0)


def short_way(panels, block_pairs, block_count, shell_size, occ_coef, vir_coef):
    n = lax.axis_size("shell")
    here, nvir = vir_coef.shape
    width = nvir // CORES
    packed = width + NOCC // CORES
    room = Z * Y * CAP
    size_row = shell_size.reshape(1, -1)

    def swap(array, bit):
        return lax.ppermute(array, "shell", [(i, i ^ bit) for i in range(n)])

    keep, to_core, to_y, to_both = pl.pallas_call(
        pack_kernel,
        out_shape=[shape(here // 2 + 2 * BLK_DEV, packed)] * 4,
        in_specs=[VMEM] * 3,
        out_specs=[VMEM] * 4,
        scratch_shapes=[pltpu.VMEM((2 * n, BLK_DEV, EDGE * EDGE), F32)],
        compiler_params=params(12),
        cost_estimate=cost(3e8, 3e6),
        name="pack_rows",
    )(vir_coef, occ_coef, panels)
    to_y, to_both, to_core = swap(to_y, 2), swap(to_both, 3), swap(to_core, 1)
    code = pl.pallas_call(
        functools.partial(ids_kernel, size_row.shape[1]),
        out_shape=shape(n, BLK_DEV, 128, dtype=jnp.int32),
        in_specs=[VMEM] * 2,
        out_specs=VMEM,
        compiler_params=params(12),
        cost_estimate=cost(1e4, 1e4),
        name="pack_ids",
    )(block_pairs.T, block_count.reshape(1, 1))
    code = lax.all_to_all(code, "shell", split_axis=0, concat_axis=0, tiled=True)

    mine, over, me, *panel = pl.pallas_call(
        functools.partial(pick_kernel, here),
        out_shape=[shape(CAP, packed), shape(1, dtype=jnp.int32), shape(1, dtype=jnp.int32)]
        + [shape(Y * CORES, 2 * BLK_DEV, EDGE * EDGE)] * Z,
        in_specs=[VMEM] * 6,
        out_specs=[VMEM, SMEM, SMEM] + [VMEM] * Z,
        compiler_params=params(12),
        cost_estimate=cost(3e8, 2e6),
        name="pick_rows",
    )(code, size_row, keep, to_core, to_y, to_both)

    across, mine_y, beside = swap(mine, 8), swap(mine, 2), swap(mine, 4)
    panel = [panel[0]] + [swap(panel[r], 4 * r) for r in range(1, Z)]
    across, mine_y, beside, *panel = lax.optimization_barrier((across, mine_y, beside, *panel))

    corner, beside_y, across_y = swap(across, 4), swap(beside, 2), swap(across, 2)
    near = [mine, mine_y, beside, across]
    far = [swap(piece, 1) for piece in near]
    early = len(near)
    slots = LIVE_DEV * n * EDGE
    half, late, got = pl.pallas_call(
        functools.partial(half_kernel, here, early),
        out_shape=(
            shape(2 * NOCC, room, dtype=F32),
            shape(2, room - early * CAP, room),
            shape(n, 2 * BLK_DEV, EDGE * EDGE),
        ),
        grid=(1,),
        in_specs=[VMEM] * (2 + Z) + [ANY] * (2 * early),
        out_specs=(
            pl.BlockSpec((2 * NOCC, room), lambda i: (0, 0)),
            pl.BlockSpec((2, room - early * CAP, room), lambda i: (0, 0, 0)),
            pl.BlockSpec((n, 2 * BLK_DEV, EDGE * EDGE), lambda i: (0, 0, 0)),
        ),
        scratch_shapes=[
            pltpu.VMEM((n, 2 * BLK_DEV, EDGE * EDGE), BF16),
            pltpu.VMEM((early * CAP, NOCC), BF16),
            pltpu.VMEM((NOCC, slots), BF16),
            pltpu.VMEM((room - early * CAP, slots), BF16),
            pltpu.VMEM((2, slots, room), BF16),
            pltpu.SemaphoreType.DMA((2 * early,)),
        ],
        compiler_params=params(30),
        cost_estimate=cost(7e9, 1),
        name="half_transform",
    )(code, size_row, *panel, *near, *far)
    corner, beside_y, half, late = lax.optimization_barrier((corner, beside_y, half, late))
    corner_y = swap(corner, 2)
    near += [beside_y, corner]
    far += [swap(piece, 1) for piece in near[early:]]
    count = len(near)
    right, half = pl.pallas_call(
        functools.partial(gather_kernel, early),
        out_shape=(shape(CORES, count * CAP, width), shape(2 * NOCC, room, dtype=F32)),
        in_specs=[SMEM] + [VMEM] * 2 + [ANY] * (2 * count),
        out_specs=(VMEM, VMEM),
        scratch_shapes=[pltpu.VMEM(((count - early) * CAP, NOCC), BF16), pltpu.SemaphoreType.DMA((4 * count,))],
        compiler_params=params(20),
        cost_estimate=cost(1, 1),
        name="gather_pieces",
    )(me, half, late, *near, *far)
    corner_y, right, half = lax.optimization_barrier((corner_y, right, half))
    tails = [across_y, corner_y, swap(across_y, 1), swap(corner_y, 1)]

    tile = width // 3
    out = pl.pallas_call(
        last_kernel,
        out_shape=shape(2, NOCC, nvir),
        in_specs=[SMEM] + [VMEM] * 2 + [ANY] + [VMEM] * 4,
        out_specs=ANY,
        scratch_shapes=[
            pltpu.VMEM((2, 2 * CAP, room), BF16),
            pltpu.VMEM((2 * NOCC, room), BF16),
            pltpu.VMEM((nvir // tile, 2, NOCC, tile), BF16),
            pltpu.SemaphoreType.DMA((1 + nvir // tile,)),
        ],
        compiler_params=params(24),
        cost_estimate=cost(2e10, 1),
        name="last_product",
    )(me, half, right, late, *tails)
    return out, over[0], code, got


def per_device(*args):
    n = lax.axis_size("shell")
    here, nvir = args[5].shape
    shells = args[3].shape[0]
    sparse = LIVE_DEV * n * EDGE < n * here
    if not (sparse and n == Z * Y * CORES and here <= 256 and here % 16 == 0 and nvir % 768 == 0):
        return from_start(*args)
    out, over, code, got = short_way(*args)

    def again(carry):
        over, _ = carry
        over, code_now, turned, *held = lax.optimization_barrier((over, code, got, *args[3:]))
        turned = turned.reshape(n, 2, BLK_DEV, EDGE * EDGE).swapaxes(1, 2).reshape(n * BLK_DEV, 2, EDGE * EDGE)
        code_now = jnp.max(code_now, axis=2).reshape(n * BLK_DEV)
        ids = jnp.maximum(code_now, 0)
        pairs = jnp.stack([ids // shells, ids % shells], axis=1)
        return over - 1, long_way(turned, pairs, code_now >= 0, *held)

    return lax.while_loop(lambda carry: carry[0] > 0, again, (over, out))[1]


def solution(mesh):
    placed = (
        P(("groups", "shell"), None, None),
        P(("groups", "shell"), None),
        P(("groups", "shell")),
        P("groups"),
        P(("groups", "shell"), None),
        P(("groups", "shell"), None),
    )
    return jax.shard_map(
        per_device,
        mesh=mesh,
        in_specs=placed,
        out_specs=P(("groups", "shell"), None, None),
        check_vma=False,
    )
```

```python
import functools
import math

import jax
import jax.numpy as jnp
from jax import lax
from jax.experimental import pallas as pl
from jax.experimental.pallas import tpu as pltpu
from jax.sharding import PartitionSpec as P

EDGE = 16
NOCC = 256
BLK_DEV = 8
LIVE_DEV = 4
CAP = 128
Z, Y, CORES = 4, 2, 2
F32 = jnp.float32
BF16 = jnp.bfloat16


def padded_rows(matrix, starts, shell_size):
    offsets = jnp.arange(EDGE, dtype=jnp.int32)
    rows = jnp.minimum(starts[:, None] + offsets[None, :], matrix.shape[0] - 1)
    inside = offsets[None, :] < shell_size[:, None]
    return jnp.where(inside[:, :, None], matrix[rows], jnp.zeros((), matrix.dtype))


def half_transform(slot_rows, pairs, keep, occ_blocks):
    count = slot_rows.shape[0]
    vecs_here = slot_rows.shape[1]
    shells = occ_blocks.shape[0]
    group_size = math.gcd(512, count)
    turns = count // group_size
    shaped = slot_rows.reshape(count, vecs_here, EDGE, EDGE)

    def advance(total, turn):
        first = turn * group_size
        block = lax.dynamic_slice_in_dim(shaped, first, group_size, 0)
        okay = lax.dynamic_slice_in_dim(keep, first, group_size, 0)
        block = jnp.where(okay[:, None, None, None], block, jnp.zeros((), block.dtype))
        row_shell = lax.dynamic_slice_in_dim(pairs[:, 0], first, group_size, 0)
        col_shell = lax.dynamic_slice_in_dim(pairs[:, 1], first, group_size, 0)
        coefs = occ_blocks[row_shell]
        piece = jnp.einsum("kmi,kvmn->kvin", coefs, block, preferred_element_type=jnp.float32)
        return (total.at[col_shell].add(piece), None)

    start_total = jnp.zeros((shells, vecs_here, NOCC, EDGE), jnp.float32)
    half, _ = lax.scan(advance, start_total, jnp.arange(turns, dtype=jnp.int32))
    return half


def long_way(turned, pairs, live, shell_size, occ_coef, vir_coef):
    occ_full = lax.all_gather(occ_coef, "shell", axis=0, tiled=True)
    starts = jnp.cumsum(shell_size) - shell_size
    occ_blocks = padded_rows(occ_full, starts, shell_size)
    half = half_transform(turned, pairs, live, occ_blocks)
    hidden = half.astype(jnp.bfloat16)
    vir_full = lax.all_gather(vir_coef, "shell", axis=0, tiled=True)
    vir_blocks = padded_rows(vir_full, starts, shell_size)
    result = jnp.einsum("svin,sna->via", hidden, vir_blocks, preferred_element_type=jnp.float32)
    return result.astype(jnp.bfloat16)


def from_start(panels, block_pairs, block_count, *rest):
    pairs = lax.all_gather(block_pairs, "shell", axis=0, tiled=True)
    counts = lax.all_gather(block_count, "shell", axis=0, tiled=True)
    turned = lax.all_to_all(panels, "shell", split_axis=1, concat_axis=0, tiled=True)
    position = jnp.arange(turned.shape[0], dtype=jnp.int32)
    live = position % BLK_DEV < counts[position // BLK_DEV]
    return long_way(turned, pairs, live, *rest)


def iota(shape, dim):
    return lax.broadcasted_iota(jnp.int32, shape, dim)


def column_of(row, mask):
    return jnp.sum(jnp.where(mask, row, 0.0), axis=1, keepdims=True)


def row_of(column, mask):
    return jnp.sum(jnp.where(mask, column, 0.0), axis=0, keepdims=True)


def zero_one(mask):
    return jnp.where(mask, 1.0, 0.0)


def lane_value(row, index):
    return jnp.sum(jnp.where(iota(row.shape, 1) == index, row, 0.0), axis=1, keepdims=True)


def one_hots(ids, shells):
    lanes = iota(ids.shape, 1).astype(F32)
    return jnp.concatenate([zero_one(ids == lanes + 128.0 * k) for k in range(shells // 128)], axis=1)


def slot_hots(code, shells):
    code = code.reshape(-1, 128)
    kept = code >= 0
    columns = jnp.where(kept, code % shells, -1).astype(F32)
    return one_hots(columns, shells), one_hots(jnp.where(kept, code // shells, -1).astype(F32), shells)


class Shells:
    def __init__(self, size_row):
        shells = size_row.shape[1]
        sub, lane = iota((shells, shells), 0), iota((shells, shells), 1)
        self.before, self.same = lane < sub, lane == sub
        self.starts = column_of(size_row, self.before)
        self.size = column_of(size_row, self.same)
        self.odd = self.starts - 2.0 * jnp.floor(self.starts * 0.5)


class Used:
    def __init__(self, shells, hot, window):
        self.used = column_of(jnp.max(hot, axis=0, keepdims=True), shells.same)
        self.extra, self.ahead, self.edges = [], [], []
        edge = (iota((hot.shape[1], 128), 1) * window).astype(F32)
        reach = jnp.clip(edge - shells.starts, 0.0, shells.size)
        for parity in range(2):
            extra = 1.0 - shells.odd if parity == 0 else shells.odd
            count = self.used * jnp.floor((shells.size + extra) * 0.5)
            count_row = row_of(count, shells.same)
            self.extra.append(extra)
            self.ahead.append(column_of(count_row, shells.before))
            self.edges.append(jnp.sum(self.used * jnp.floor((reach + extra) * 0.5), axis=0, keepdims=True))


def pack_kernel(vir_ref, occ_ref, panels_ref, *refs):
    outs, (turned_ref,) = refs[:4], refs[4:]
    me = lax.axis_index("shell")
    core, y = lax.rem(me, 2), lax.rem(lax.div(me, 2), 2)
    here, nvir = vir_ref.shape
    rows = here // 2
    width, thin = nvir // CORES, occ_ref.shape[1] // CORES
    turned_ref[...] = jnp.swapaxes(panels_ref[...].astype(F32), 0, 1)
    block = EDGE * EDGE
    for dy in range(2):
        parity = lax.rem(y + dy, 2)
        pick = zero_one(iota((rows, here), 1) == 2 * iota((rows, here), 0) + parity).astype(BF16)
        for dc in range(2):
            half = lax.rem(core + dc, 2)
            out = outs[2 * dy + dc]
            part = vir_ref[:, pl.ds(pl.multiple_of(half * width, 128), width)]
            out[:rows, :width] = jnp.dot(pick, part, preferred_element_type=F32).astype(BF16)
            part = occ_ref[:, pl.ds(pl.multiple_of(half * thin, 128), thin)]
            out[:rows, width:] = jnp.dot(pick, part, preferred_element_type=F32).astype(BF16)
            for z in range(Z):
                device = (z * Y + parity) * CORES + half
                pair = turned_ref[pl.ds(2 * device, 2)].reshape(2 * BLK_DEV, block)
                out[rows:, z * block : (z + 1) * block] = pair.astype(BF16)
            out[rows:, Z * block :] = jnp.zeros((2 * BLK_DEV, out.shape[1] - Z * block), BF16)


def ids_kernel(shells, pairs_ref, count_ref, code_ref):
    code = pairs_ref[1:2, :] + shells * pairs_ref[0:1, :]
    code = jnp.where(iota((1, BLK_DEV), 1) < count_ref[...], code, -1).astype(F32)
    square = (BLK_DEV, BLK_DEV)
    code = column_of(code, iota(square, 0) == iota(square, 1)).astype(jnp.int32)
    code_ref[...] = jnp.broadcast_to(jnp.broadcast_to(code, (BLK_DEV, 128))[None], code_ref.shape)


def pick_kernel(here, code_ref, size_ref, *refs):
    sources, (out_ref, over_ref, me_ref, panel_ref) = refs[:4], refs[4:]
    me = lax.axis_index("shell")
    me_ref[0] = me
    core, y, z = lax.rem(me, 2), lax.rem(lax.div(me, 2), 2), lax.div(me, 4)
    window = CORES * Y * here
    shell_count = size_ref.shape[1]
    shells = Shells(size_ref[...].astype(F32))
    lists = [Used(shells, hot, window) for hot in slot_hots(code_ref[...], shell_count)]
    most = jnp.zeros((1, 1), F32)
    lane = iota((1, 128), 1)
    for chosen in lists:
        for edges in chosen.edges:
            later = jnp.concatenate([edges[:, 1:], edges[:, :1]], axis=1)
            most = jnp.maximum(most, jnp.max(jnp.where(lane < Z, later - edges, 0.0), axis=1, keepdims=True))
    over_ref[...] = jnp.broadcast_to(jnp.where(most > CAP, 1, 0).astype(jnp.int32), over_ref.shape)

    width = out_ref.shape[1] - 128
    even = y == 0
    totals = [jnp.zeros((CAP, width), F32), jnp.zeros((CAP, 128), F32)]
    columns = [slice(0, width), slice(width, width + 128)]
    extra = jnp.where(even, lists[0].extra[0], lists[0].extra[1])
    rows = here // 2
    for k, source in enumerate(sources):
        member = 2 * lax.rem(y + k // 2, 2) + lax.rem(core + k % 2, 2)
        device = 4 * z + member
        for to_z in range(Z):
            panel_ref[to_z, member] = source[rows:, to_z * EDGE * EDGE : (to_z + 1) * EDGE * EDGE]
        row = (2 * iota((shell_count, 128), 1) + device * here + y).astype(F32)
        where = row - shells.starts
        inside = (where >= 0.0) & (where < shells.size)
        within = jnp.floor((where + extra) * 0.5)
        for chosen, total, column in zip(lists, range(2), columns):
            ahead = jnp.where(even, chosen.ahead[0], chosen.ahead[1])
            base = lane_value(jnp.where(even, chosen.edges[0], chosen.edges[1]), z)
            place = jnp.where(inside & (chosen.used > 0.0), ahead + within + 1.0, 0.0)
            place = jnp.sum(place, axis=0, keepdims=True)
            place = jnp.where(place > 0.0, place - 1.0 - base, -1.0)
            hot = zero_one(place == iota((CAP, 128), 0).astype(F32)).astype(BF16)
            totals[total] += jnp.dot(
                hot[:, :rows], source[:rows, column], preferred_element_type=F32
            )
    for total, column in zip(totals, columns):
        out_ref[:, column] = total.astype(BF16)


def slot_of(window, chip):
    rel = window ^ chip
    early = jnp.where((rel == 3) | (rel == 4), rel ^ 7, rel)
    return jnp.where((rel == 5) | (rel == 6), rel ^ 3, early)


def half_kernel(here, early, code_ref, got_ref, size_ref, *refs):
    pieces, refs = refs[: 2 * early], refs[2 * early :]
    half_ref, late_ref, occ_ref, part_ref, hot_ref, placed_ref, sems = refs
    me = lax.axis_index("shell")
    core, chip = lax.rem(me, CORES), lax.div(me, CORES)
    width = pieces[0].shape[1] - 128
    copies = []
    for far in range(2):
        half = lax.rem(core + far, CORES)
        for k in range(early):
            at = far * early + k
            target = occ_ref.at[pl.ds(k * CAP, CAP), pl.ds(pl.multiple_of(half * 128, 128), 128)]
            copies.append(pltpu.make_async_copy(pieces[at].at[:, pl.ds(width, 128)], target, sems.at[at]))
    for copy in copies:
        copy.start()
    window = CORES * Y * here
    shell_count = size_ref.shape[1]
    got = got_ref[...].astype(F32)
    size_row = size_ref[...].astype(F32)
    shells = Shells(size_row)
    got = got_ref[...].astype(F32)
    hots = slot_hots(code_ref[...], shell_count)
    lists = [Used(shells, hot, window) for hot in hots]
    slots = hots[0].shape[0]
    kept = LIVE_DEV * (slots // BLK_DEV)
    alive = jnp.broadcast_to(jnp.sum(hots[0], axis=1, keepdims=True), (slots, slots))
    sub, lane = iota((slots, slots), 0), iota((slots, slots), 1)
    rank = row_of(alive, sub < lane)
    alive_row = row_of(alive, sub == lane)
    take = (rank == iota((kept, slots), 0).astype(F32)) & (alive_row > 0.0)
    take = zero_one(take).astype(BF16)

    def taken(array):
        return jnp.dot(take, array.astype(BF16), preferred_element_type=F32)

    def spread(hot, column):
        value = jnp.sum(hot * row_of(column, shells.same), axis=1, keepdims=True)
        wide = jnp.broadcast_to(value, (kept, 128)).reshape(kept, 1, 128)
        return jnp.broadcast_to(wide, (kept, EDGE, 128)).reshape(kept * EDGE, 128)

    at = iota((kept * EDGE, 128), 0) % EDGE
    step = at.astype(F32)

    def places(hot, chosen):
        hot = taken(hot)
        first, length = spread(hot, shells.starts), spread(hot, shells.size)
        row = first + step
        odd = (row - 2.0 * jnp.floor(row * 0.5)) > 0.0
        place = jnp.where(odd, spread(hot, chosen.ahead[1]), spread(hot, chosen.ahead[0]))
        place += jnp.floor(step * 0.5)
        offsets = [
            [slot_of(w * Y + k, chip).astype(F32) * CAP - lane_value(e, w) for w in range(Z)]
            for k, e in enumerate(chosen.edges)
        ]
        offset = jnp.where(odd, offsets[1][0], offsets[0][0])
        for w in range(1, Z):
            offset = jnp.where(row >= float(window * w), jnp.where(odd, offsets[1][w], offsets[0][w]), offset)
        return jnp.where(step < length, place + offset, -1.0)[:, :1]

    place_c, place_r = places(hots[0], lists[0]), places(hots[1], lists[1])
    span = 16 * EDGE
    s_in, l_in = iota((span, span), 0), iota((span, span), 1)
    keep_m = (l_in // EDGE) == (s_in % EDGE)
    fold = zero_one((s_in % EDGE) == (l_in % EDGE)).astype(BF16)
    same_slot = (s_in // EDGE) == (l_in // EDGE)
    blocks = [taken(got[:, p * BLK_DEV : (p + 1) * BLK_DEV, :].reshape(slots, span)) for p in range(2)]
    lanes = iota((span, half_ref.shape[1]), 1).astype(F32)
    for copy in copies:
        copy.wait()
    occ = occ_ref[...]
    cut = early * CAP
    for g in range(kept // 16):
        rows = slice(g * span, (g + 1) * span)
        r_hot = zero_one(place_r[rows] == lanes).astype(BF16)
        c_hot = zero_one(place_c[rows] == lanes).astype(BF16)
        part_ref[:, rows] = jnp.dot(r_hot[:, :cut], occ, preferred_element_type=F32).T.astype(BF16)
        hot_ref[:, rows] = r_hot[:, cut:].T
        for p in range(2):
            block = blocks[p][g * 16 : (g + 1) * 16].reshape(16, 1, span)
            block = jnp.broadcast_to(block, (16, EDGE, span)).reshape(span, span)
            block = jnp.where(keep_m, block, 0.0).astype(BF16)
            diag = jnp.dot(block, fold, preferred_element_type=F32)
            diag = jnp.where(same_slot, diag, 0.0).astype(BF16)
            placed_ref[p, rows, :] = jnp.dot(diag, c_hot, preferred_element_type=F32).astype(BF16)
    for p in range(2):
        half_ref[p * NOCC : (p + 1) * NOCC, :] = jnp.dot(part_ref[...], placed_ref[p], preferred_element_type=F32)
        late_ref[p] = jnp.dot(hot_ref[...], placed_ref[p], preferred_element_type=F32).astype(BF16)


def gather_kernel(early, me_ref, mine_over_ref, their_over_ref, part_ref, late_ref, *refs):
    count = (len(refs) - 5) // 2
    pieces, (right_ref, half_ref, over_ref, occ_ref, sems) = refs[: 2 * count], refs[2 * count :]
    over = jnp.max(jnp.maximum(mine_over_ref[...], their_over_ref[...]).astype(F32))
    over_ref[0] = jnp.where(over > 0.0, 1, 0).astype(jnp.int32)
    width = right_ref.shape[2]
    core = lax.rem(me_ref[0], CORES)
    first, copies = [], []
    for side in range(2):
        half = lax.rem(core + side, CORES)
        for k in range(count):
            at = side * count + k
            if k >= early:
                target = occ_ref.at[pl.ds((k - early) * CAP, CAP), pl.ds(pl.multiple_of(half * 128, 128), 128)]
                source = pieces[at].at[:, pl.ds(width, 128)]
                first.append(pltpu.make_async_copy(source, target, sems.at[2 * count + at]))
            target = right_ref.at[side, pl.ds(k * CAP, CAP), :]
            copies.append(pltpu.make_async_copy(pieces[at].at[:, pl.ds(0, width)], target, sems.at[at]))
    for copy in (*first, *copies):
        copy.start()
    for copy in first:
        copy.wait()
    occ = occ_ref[...].T
    for p in range(2):
        rows = slice(p * NOCC, (p + 1) * NOCC)
        late = jnp.dot(occ, late_ref[p, : occ_ref.shape[0], :], preferred_element_type=F32)
        half_ref[rows, :] = part_ref[rows, :] + late
    for copy in copies:
        copy.wait()


def last_kernel(me_ref, part_ref, right_ref, late_any, *refs):
    pieces, (out_any, late_ref, half_ref, tiles_ref, sems) = (refs[:2], refs[2:4]), refs[4:]
    width = right_ref.shape[2]
    cut = right_ref.shape[1]
    tile = tiles_ref.shape[3]
    per = width // tile
    core = lax.rem(me_ref[0], CORES)
    rows = late_any.shape[1] - 2 * CAP
    copy = pltpu.make_async_copy(late_any.at[:, pl.ds(rows, 2 * CAP), :], late_ref, sems.at[0])
    copy.start()
    copy.wait()
    sides = [jnp.concatenate([ref[:, width:] for ref in side], axis=0).T for side in pieces]
    for p in range(2):
        for side, occ in enumerate(sides):
            half = lax.rem(core + side, CORES)
            rows = pl.ds(pl.multiple_of(p * NOCC + half * 128, 128), 128)
            late = jnp.dot(occ, late_ref[p], preferred_element_type=F32)
            half_ref[rows, :] = (part_ref[rows, :] + late).astype(BF16)
    results = []
    for side, tail in enumerate(pieces):
        base = lax.rem(core + side, CORES) * width
        for t in range(per):
            columns = slice(t * tile, (t + 1) * tile)
            total = jnp.dot(half_ref[:, :cut], right_ref[side, :, columns], preferred_element_type=F32)
            below = jnp.concatenate([ref[:, columns] for ref in tail], axis=0)
            total += jnp.dot(half_ref[:, cut:], below, preferred_element_type=F32)
            at = side * per + t
            tiles_ref[at] = total.astype(BF16).reshape(tiles_ref.shape[1:])
            target = out_any.at[:, :, pl.ds(pl.multiple_of(base + t * tile, 128), tile)]
            results.append(pltpu.make_async_copy(tiles_ref.at[at], target, sems.at[1 + at]))
            results[-1].start()
    for copy in results:
        copy.wait()


VMEM = pl.BlockSpec(memory_space=pltpu.VMEM)
SMEM = pl.BlockSpec(memory_space=pltpu.SMEM)
ANY = pl.BlockSpec(memory_space=pl.ANY)


def shape(*dims, dtype=BF16):
    return jax.ShapeDtypeStruct(dims, dtype)


def params(mib):
    return pltpu.CompilerParams(vmem_limit_bytes=mib << 20)


def cost(flops, nbytes):
    return pl.CostEstimate(flops=int(flops), bytes_accessed=int(nbytes), transcendentals=0)


def short_way(panels, block_pairs, block_count, shell_size, occ_coef, vir_coef):
    n = lax.axis_size("shell")
    here, nvir = vir_coef.shape
    width = nvir // CORES
    packed = width + NOCC // CORES
    room = Z * Y * CAP
    size_row = shell_size.reshape(1, -1)

    def swap(array, bit):
        return lax.ppermute(array, "shell", [(i, i ^ bit) for i in range(n)])

    keep, to_core, to_y, to_both = pl.pallas_call(
        pack_kernel,
        out_shape=[shape(here // 2 + 2 * BLK_DEV, packed)] * 4,
        in_specs=[VMEM] * 3,
        out_specs=[VMEM] * 4,
        scratch_shapes=[pltpu.VMEM((2 * n, BLK_DEV, EDGE * EDGE), F32)],
        compiler_params=params(12),
        cost_estimate=cost(3e8, 3e6),
        name="pack_rows",
    )(vir_coef, occ_coef, panels)
    to_y, to_both, to_core = swap(to_y, 2), swap(to_both, 3), swap(to_core, 1)
    code = pl.pallas_call(
        functools.partial(ids_kernel, size_row.shape[1]),
        out_shape=shape(n, BLK_DEV, 128, dtype=jnp.int32),
        in_specs=[VMEM] * 2,
        out_specs=VMEM,
        compiler_params=params(12),
        cost_estimate=cost(1e4, 1e4),
        name="pack_ids",
    )(block_pairs.T, block_count.reshape(1, 1))
    code = lax.all_to_all(code, "shell", split_axis=0, concat_axis=0, tiled=True)

    mine, over, me, panel = pl.pallas_call(
        functools.partial(pick_kernel, here),
        out_shape=[shape(CAP, packed), shape(8, 128, dtype=jnp.int32), shape(1, dtype=jnp.int32)]
        + [shape(Z, Y * CORES, 2 * BLK_DEV, EDGE * EDGE)],
        in_specs=[VMEM] * 6,
        out_specs=[VMEM, VMEM, SMEM, VMEM],
        compiler_params=params(12),
        cost_estimate=cost(3e8, 2e6),
        name="pick_rows",
    )(code, size_row, keep, to_core, to_y, to_both)

    across, mine_y, beside = swap(mine, 8), swap(mine, 2), swap(mine, 4)
    lines = [[Y * CORES * z + k for z in range(Z)] for k in range(Y * CORES)]
    got = lax.all_to_all(panel, "shell", split_axis=0, concat_axis=0, axis_index_groups=lines, tiled=True)
    got = got.reshape(n, 2 * BLK_DEV, EDGE * EDGE)
    far = [swap(mine, 1)]
    across, mine_y, beside, got, *far = lax.optimization_barrier((across, mine_y, beside, got, *far))

    corner, beside_y, across_y = swap(across, 4), swap(beside, 2), swap(across, 2)
    near = [mine, mine_y, beside, across]
    far += [swap(piece, 1) for piece in near[1:]]
    early = len(near)
    slots = LIVE_DEV * n * EDGE
    half, late = pl.pallas_call(
        functools.partial(half_kernel, here, early),
        out_shape=(shape(2 * NOCC, room, dtype=F32), shape(2, room - early * CAP, room)),
        grid=(1,),
        in_specs=[VMEM] * 3 + [ANY] * (2 * early),
        out_specs=(
            pl.BlockSpec((2 * NOCC, room), lambda i: (0, 0)),
            pl.BlockSpec((2, room - early * CAP, room), lambda i: (0, 0, 0)),
        ),
        scratch_shapes=[
            pltpu.VMEM((early * CAP, NOCC), BF16),
            pltpu.VMEM((NOCC, slots), BF16),
            pltpu.VMEM((room - early * CAP, slots), BF16),
            pltpu.VMEM((2, slots, room), BF16),
            pltpu.SemaphoreType.DMA((2 * early,)),
        ],
        compiler_params=params(30),
        cost_estimate=cost(7e9, 1),
        name="half_transform",
    )(code, got, size_row, *near, *far)
    corner, beside_y, half, late = lax.optimization_barrier((corner, beside_y, half, late))
    corner_y = swap(corner, 2)
    near += [beside_y, corner]
    far += [swap(piece, 1) for piece in near[early:]]
    count = len(near)
    over_other = lax.ppermute(over, "groups", [(0, 1), (1, 0)])
    right, half, over = pl.pallas_call(
        functools.partial(gather_kernel, early),
        out_shape=(
            shape(CORES, count * CAP, width),
            shape(2 * NOCC, room, dtype=F32),
            shape(1, dtype=jnp.int32),
        ),
        in_specs=[SMEM] + [VMEM] * 4 + [ANY] * (2 * count),
        out_specs=(VMEM, VMEM, SMEM),
        scratch_shapes=[pltpu.VMEM(((count - early) * CAP, NOCC), BF16), pltpu.SemaphoreType.DMA((4 * count,))],
        compiler_params=params(20),
        cost_estimate=cost(1, 1),
        name="gather_pieces",
    )(me, over, over_other, half, late, *near, *far)
    corner_y, right, half = lax.optimization_barrier((corner_y, right, half))
    tails = [across_y, corner_y, swap(across_y, 1), swap(corner_y, 1)]

    tile = width // 3
    out = pl.pallas_call(
        last_kernel,
        out_shape=shape(2, NOCC, nvir),
        in_specs=[SMEM] + [VMEM] * 2 + [ANY] + [VMEM] * 4,
        out_specs=ANY,
        scratch_shapes=[
            pltpu.VMEM((2, 2 * CAP, room), BF16),
            pltpu.VMEM((2 * NOCC, room), BF16),
            pltpu.VMEM((nvir // tile, 2, NOCC, tile), BF16),
            pltpu.SemaphoreType.DMA((1 + nvir // tile,)),
        ],
        compiler_params=params(24),
        cost_estimate=cost(2e10, 1),
        name="last_product",
    )(me, half, right, late, *tails)
    return out, over[0], code, got


def per_device(*args):
    n = lax.axis_size("shell")
    here, nvir = args[5].shape
    shells = args[3].shape[0]
    sparse = LIVE_DEV * n * EDGE < n * here
    if not (sparse and lax.axis_size("groups") == 2 and n == Z * Y * CORES and here <= 256 and here % 16 == 0 and nvir % 768 == 0):
        return from_start(*args)
    out, over, code, got = short_way(*args)

    def again(carry):
        over, _ = carry
        over, code_now, turned, *held = lax.optimization_barrier((over, code, got, *args[3:]))
        turned = turned.reshape(n, 2, BLK_DEV, EDGE * EDGE).swapaxes(1, 2).reshape(n * BLK_DEV, 2, EDGE * EDGE)
        code_now = jnp.max(code_now, axis=2).reshape(n * BLK_DEV)
        ids = jnp.maximum(code_now, 0)
        pairs = jnp.stack([ids // shells, ids % shells], axis=1)
        return over - 1, long_way(turned, pairs, code_now >= 0, *held)

    return lax.while_loop(lambda carry: carry[0] > 0, again, (over, out))[1]


def solution(mesh):
    placed = (
        P(("groups", "shell"), None, None),
        P(("groups", "shell"), None),
        P(("groups", "shell")),
        P("groups"),
        P(("groups", "shell"), None),
        P(("groups", "shell"), None),
    )
    return jax.shard_map(
        per_device,
        mesh=mesh,
        in_specs=placed,
        out_specs=P(("groups", "shell"), None, None),
        check_vma=False,
    )
```

```python
import functools
import math

import jax
import jax.numpy as jnp
from jax import lax
from jax.experimental import pallas as pl
from jax.experimental.pallas import tpu as pltpu
from jax.sharding import PartitionSpec as P

EDGE = 16
NOCC = 256
BLK_DEV = 8
LIVE_DEV = 4
CAP = 128
Z, Y, CORES = 4, 2, 2
F32 = jnp.float32
BF16 = jnp.bfloat16


def padded_rows(matrix, starts, shell_size):
    offsets = jnp.arange(EDGE, dtype=jnp.int32)
    rows = jnp.minimum(starts[:, None] + offsets[None, :], matrix.shape[0] - 1)
    inside = offsets[None, :] < shell_size[:, None]
    return jnp.where(inside[:, :, None], matrix[rows], jnp.zeros((), matrix.dtype))


def half_transform(slot_rows, pairs, keep, occ_blocks):
    count = slot_rows.shape[0]
    vecs_here = slot_rows.shape[1]
    shells = occ_blocks.shape[0]
    group_size = math.gcd(512, count)
    turns = count // group_size
    shaped = slot_rows.reshape(count, vecs_here, EDGE, EDGE)

    def advance(total, turn):
        first = turn * group_size
        block = lax.dynamic_slice_in_dim(shaped, first, group_size, 0)
        okay = lax.dynamic_slice_in_dim(keep, first, group_size, 0)
        block = jnp.where(okay[:, None, None, None], block, jnp.zeros((), block.dtype))
        row_shell = lax.dynamic_slice_in_dim(pairs[:, 0], first, group_size, 0)
        col_shell = lax.dynamic_slice_in_dim(pairs[:, 1], first, group_size, 0)
        coefs = occ_blocks[row_shell]
        piece = jnp.einsum("kmi,kvmn->kvin", coefs, block, preferred_element_type=jnp.float32)
        return (total.at[col_shell].add(piece), None)

    start_total = jnp.zeros((shells, vecs_here, NOCC, EDGE), jnp.float32)
    half, _ = lax.scan(advance, start_total, jnp.arange(turns, dtype=jnp.int32))
    return half


def long_way(turned, pairs, live, shell_size, occ_coef, vir_coef):
    occ_full = lax.all_gather(occ_coef, "shell", axis=0, tiled=True)
    starts = jnp.cumsum(shell_size) - shell_size
    occ_blocks = padded_rows(occ_full, starts, shell_size)
    half = half_transform(turned, pairs, live, occ_blocks)
    hidden = half.astype(jnp.bfloat16)
    vir_full = lax.all_gather(vir_coef, "shell", axis=0, tiled=True)
    vir_blocks = padded_rows(vir_full, starts, shell_size)
    result = jnp.einsum("svin,sna->via", hidden, vir_blocks, preferred_element_type=jnp.float32)
    return result.astype(jnp.bfloat16)


def from_start(panels, block_pairs, block_count, *rest):
    pairs = lax.all_gather(block_pairs, "shell", axis=0, tiled=True)
    counts = lax.all_gather(block_count, "shell", axis=0, tiled=True)
    turned = lax.all_to_all(panels, "shell", split_axis=1, concat_axis=0, tiled=True)
    position = jnp.arange(turned.shape[0], dtype=jnp.int32)
    live = position % BLK_DEV < counts[position // BLK_DEV]
    return long_way(turned, pairs, live, *rest)


def iota(shape, dim):
    return lax.broadcasted_iota(jnp.int32, shape, dim)


def column_of(row, mask):
    return jnp.sum(jnp.where(mask, row, 0.0), axis=1, keepdims=True)


def row_of(column, mask):
    return jnp.sum(jnp.where(mask, column, 0.0), axis=0, keepdims=True)


def zero_one(mask):
    return jnp.where(mask, 1.0, 0.0)


def lane_value(row, index):
    return jnp.sum(jnp.where(iota(row.shape, 1) == index, row, 0.0), axis=1, keepdims=True)


def one_hots(ids, shells):
    lanes = iota(ids.shape, 1).astype(F32)
    return jnp.concatenate([zero_one(ids == lanes + 128.0 * k) for k in range(shells // 128)], axis=1)


def slot_hots(code, shells):
    code = code.reshape(-1, 128)
    kept = code >= 0
    columns = jnp.where(kept, code % shells, -1).astype(F32)
    return one_hots(columns, shells), one_hots(jnp.where(kept, code // shells, -1).astype(F32), shells)


class Shells:
    def __init__(self, size_row):
        shells = size_row.shape[1]
        sub, lane = iota((shells, shells), 0), iota((shells, shells), 1)
        self.before, self.same = lane < sub, lane == sub
        self.starts = column_of(size_row, self.before)
        self.size = column_of(size_row, self.same)
        self.odd = self.starts - 2.0 * jnp.floor(self.starts * 0.5)


class Used:
    def __init__(self, shells, hot, window):
        self.used = column_of(jnp.max(hot, axis=0, keepdims=True), shells.same)
        self.extra, self.ahead, self.edges = [], [], []
        edge = (iota((hot.shape[1], 128), 1) * window).astype(F32)
        reach = jnp.clip(edge - shells.starts, 0.0, shells.size)
        for parity in range(2):
            extra = 1.0 - shells.odd if parity == 0 else shells.odd
            count = self.used * jnp.floor((shells.size + extra) * 0.5)
            count_row = row_of(count, shells.same)
            self.extra.append(extra)
            self.ahead.append(column_of(count_row, shells.before))
            self.edges.append(jnp.sum(self.used * jnp.floor((reach + extra) * 0.5), axis=0, keepdims=True))


def pack_kernel(vir_ref, occ_ref, panels_ref, *refs):
    outs, (turned_ref,) = refs[:4], refs[4:]
    me = lax.axis_index("shell")
    core, y = lax.rem(me, 2), lax.rem(lax.div(me, 2), 2)
    here, nvir = vir_ref.shape
    rows = here // 2
    width, thin = nvir // CORES, occ_ref.shape[1] // CORES
    turned_ref[...] = jnp.swapaxes(panels_ref[...].astype(F32), 0, 1)
    block = EDGE * EDGE
    for dy in range(2):
        parity = lax.rem(y + dy, 2)
        pick = zero_one(iota((rows, here), 1) == 2 * iota((rows, here), 0) + parity).astype(BF16)
        for dc in range(2):
            half = lax.rem(core + dc, 2)
            out = outs[2 * dy + dc]
            part = vir_ref[:, pl.ds(pl.multiple_of(half * width, 128), width)]
            out[:rows, :width] = jnp.dot(pick, part, preferred_element_type=F32).astype(BF16)
            part = occ_ref[:, pl.ds(pl.multiple_of(half * thin, 128), thin)]
            out[:rows, width:] = jnp.dot(pick, part, preferred_element_type=F32).astype(BF16)
            for z in range(Z):
                device = (z * Y + parity) * CORES + half
                pair = turned_ref[pl.ds(2 * device, 2)].reshape(2 * BLK_DEV, block)
                out[rows:, z * block : (z + 1) * block] = pair.astype(BF16)
            out[rows:, Z * block :] = jnp.zeros((2 * BLK_DEV, out.shape[1] - Z * block), BF16)


def ids_kernel(shells, pairs_ref, count_ref, code_ref):
    code = pairs_ref[1:2, :] + shells * pairs_ref[0:1, :]
    code = jnp.where(iota((1, BLK_DEV), 1) < count_ref[...], code, -1).astype(F32)
    square = (BLK_DEV, BLK_DEV)
    code = column_of(code, iota(square, 0) == iota(square, 1)).astype(jnp.int32)
    code_ref[...] = jnp.broadcast_to(jnp.broadcast_to(code, (BLK_DEV, 128))[None], code_ref.shape)


def pick_kernel(here, code_ref, size_ref, *refs):
    sources, (out_ref, over_ref, me_ref, panel_ref) = refs[:4], refs[4:]
    me = lax.axis_index("shell")
    me_ref[0] = me
    core, y, z = lax.rem(me, 2), lax.rem(lax.div(me, 2), 2), lax.div(me, 4)
    window = CORES * Y * here
    shell_count = size_ref.shape[1]
    shells = Shells(size_ref[...].astype(F32))
    lists = [Used(shells, hot, window) for hot in slot_hots(code_ref[...], shell_count)]
    most = jnp.zeros((1, 1), F32)
    lane = iota((1, 128), 1)
    for chosen in lists:
        for edges in chosen.edges:
            later = jnp.concatenate([edges[:, 1:], edges[:, :1]], axis=1)
            most = jnp.maximum(most, jnp.max(jnp.where(lane < Z, later - edges, 0.0), axis=1, keepdims=True))
    over_ref[...] = jnp.broadcast_to(jnp.where(most > CAP, 1, 0).astype(jnp.int32), over_ref.shape)

    width = out_ref.shape[1] - 128
    even = y == 0
    totals = [jnp.zeros((CAP, width), F32), jnp.zeros((CAP, 128), F32)]
    columns = [slice(0, width), slice(width, width + 128)]
    extra = jnp.where(even, lists[0].extra[0], lists[0].extra[1])
    rows = here // 2
    for k, source in enumerate(sources):
        member = 2 * lax.rem(y + k // 2, 2) + lax.rem(core + k % 2, 2)
        device = 4 * z + member
        for to_z in range(Z):
            panel_ref[to_z, member] = source[rows:, to_z * EDGE * EDGE : (to_z + 1) * EDGE * EDGE]
        row = (2 * iota((shell_count, 128), 1) + device * here + y).astype(F32)
        where = row - shells.starts
        inside = (where >= 0.0) & (where < shells.size)
        within = jnp.floor((where + extra) * 0.5)
        for chosen, total, column in zip(lists, range(2), columns):
            ahead = jnp.where(even, chosen.ahead[0], chosen.ahead[1])
            base = lane_value(jnp.where(even, chosen.edges[0], chosen.edges[1]), z)
            place = jnp.where(inside & (chosen.used > 0.0), ahead + within + 1.0, 0.0)
            place = jnp.sum(place, axis=0, keepdims=True)
            place = jnp.where(place > 0.0, place - 1.0 - base, -1.0)
            hot = zero_one(place == iota((CAP, 128), 0).astype(F32)).astype(BF16)
            totals[total] += jnp.dot(
                hot[:, :rows], source[:rows, column], preferred_element_type=F32
            )
    for total, column in zip(totals, columns):
        out_ref[:, column] = total.astype(BF16)


def slot_of(window, chip):
    rel = window ^ chip
    early = jnp.where((rel == 3) | (rel == 4), rel ^ 7, rel)
    return jnp.where((rel == 5) | (rel == 6), rel ^ 3, early)


def half_kernel(here, early, code_ref, got_ref, size_ref, *refs):
    pieces, refs = refs[: 2 * early], refs[2 * early :]
    half_ref, late_ref, occ_ref, part_ref, hot_ref, placed_ref, sems = refs
    me = lax.axis_index("shell")
    core, chip = lax.rem(me, CORES), lax.div(me, CORES)
    width = pieces[0].shape[1] - 128
    copies = []
    for far in range(2):
        half = lax.rem(core + far, CORES)
        for k in range(early):
            at = far * early + k
            target = occ_ref.at[pl.ds(k * CAP, CAP), pl.ds(pl.multiple_of(half * 128, 128), 128)]
            copies.append(pltpu.make_async_copy(pieces[at].at[:, pl.ds(width, 128)], target, sems.at[at]))
    for copy in copies:
        copy.start()
    window = CORES * Y * here
    shell_count = size_ref.shape[1]
    got = got_ref[...].astype(F32)
    size_row = size_ref[...].astype(F32)
    shells = Shells(size_row)
    got = got_ref[...].astype(F32)
    hots = slot_hots(code_ref[...], shell_count)
    lists = [Used(shells, hot, window) for hot in hots]
    slots = hots[0].shape[0]
    kept = LIVE_DEV * (slots // BLK_DEV)
    alive = jnp.broadcast_to(jnp.sum(hots[0], axis=1, keepdims=True), (slots, slots))
    sub, lane = iota((slots, slots), 0), iota((slots, slots), 1)
    rank = row_of(alive, sub < lane)
    alive_row = row_of(alive, sub == lane)
    take = (rank == iota((kept, slots), 0).astype(F32)) & (alive_row > 0.0)
    take = zero_one(take).astype(BF16)

    def taken(array):
        return jnp.dot(take, array.astype(BF16), preferred_element_type=F32)

    def spread(hot, column):
        value = jnp.sum(hot * row_of(column, shells.same), axis=1, keepdims=True)
        wide = jnp.broadcast_to(value, (kept, 128)).reshape(kept, 1, 128)
        return jnp.broadcast_to(wide, (kept, EDGE, 128)).reshape(kept * EDGE, 128)

    at = iota((kept * EDGE, 128), 0) % EDGE
    step = at.astype(F32)

    def places(hot, chosen):
        hot = taken(hot)
        first, length = spread(hot, shells.starts), spread(hot, shells.size)
        row = first + step
        odd = (row - 2.0 * jnp.floor(row * 0.5)) > 0.0
        place = jnp.where(odd, spread(hot, chosen.ahead[1]), spread(hot, chosen.ahead[0]))
        place += jnp.floor(step * 0.5)
        offsets = [
            [slot_of(w * Y + k, chip).astype(F32) * CAP - lane_value(e, w) for w in range(Z)]
            for k, e in enumerate(chosen.edges)
        ]
        offset = jnp.where(odd, offsets[1][0], offsets[0][0])
        for w in range(1, Z):
            offset = jnp.where(row >= float(window * w), jnp.where(odd, offsets[1][w], offsets[0][w]), offset)
        return jnp.where(step < length, place + offset, -1.0)[:, :1]

    place_c, place_r = places(hots[0], lists[0]), places(hots[1], lists[1])
    span = 16 * EDGE
    s_in, l_in = iota((span, span), 0), iota((span, span), 1)
    keep_m = (l_in // EDGE) == (s_in % EDGE)
    fold = zero_one((s_in % EDGE) == (l_in % EDGE)).astype(BF16)
    same_slot = (s_in // EDGE) == (l_in // EDGE)
    blocks = [taken(got[:, p * BLK_DEV : (p + 1) * BLK_DEV, :].reshape(slots, span)) for p in range(2)]
    lanes = iota((span, half_ref.shape[1]), 1).astype(F32)
    for copy in copies:
        copy.wait()
    occ = occ_ref[...]
    cut = early * CAP
    for g in range(kept // 16):
        rows = slice(g * span, (g + 1) * span)
        r_hot = zero_one(place_r[rows] == lanes).astype(BF16)
        c_hot = zero_one(place_c[rows] == lanes).astype(BF16)
        part_ref[:, rows] = jnp.dot(r_hot[:, :cut], occ, preferred_element_type=F32).T.astype(BF16)
        hot_ref[:, rows] = r_hot[:, cut:].T
        for p in range(2):
            block = blocks[p][g * 16 : (g + 1) * 16].reshape(16, 1, span)
            block = jnp.broadcast_to(block, (16, EDGE, span)).reshape(span, span)
            block = jnp.where(keep_m, block, 0.0).astype(BF16)
            diag = jnp.dot(block, fold, preferred_element_type=F32)
            diag = jnp.where(same_slot, diag, 0.0).astype(BF16)
            placed_ref[p, rows, :] = jnp.dot(diag, c_hot, preferred_element_type=F32).astype(BF16)
    for p in range(2):
        half_ref[p * NOCC : (p + 1) * NOCC, :] = jnp.dot(part_ref[...], placed_ref[p], preferred_element_type=F32)
        late_ref[p] = jnp.dot(hot_ref[...], placed_ref[p], preferred_element_type=F32).astype(BF16)


def gather_kernel(early, me_ref, mine_over_ref, their_over_ref, part_ref, late_ref, *refs):
    count = (len(refs) - 5) // 2
    pieces, (right_ref, half_ref, over_ref, occ_ref, sems) = refs[: 2 * count], refs[2 * count :]
    over = jnp.max(jnp.maximum(mine_over_ref[...], their_over_ref[...]).astype(F32))
    over_ref[0] = jnp.where(over > 0.0, 1, 0).astype(jnp.int32)
    width = right_ref.shape[2]
    core = lax.rem(me_ref[0], CORES)
    first, copies = [], []
    for side in range(2):
        half = lax.rem(core + side, CORES)
        for k in range(count):
            at = side * count + k
            if k >= early:
                target = occ_ref.at[pl.ds((k - early) * CAP, CAP), pl.ds(pl.multiple_of(half * 128, 128), 128)]
                source = pieces[at].at[:, pl.ds(width, 128)]
                first.append(pltpu.make_async_copy(source, target, sems.at[2 * count + at]))
            target = right_ref.at[side, pl.ds(k * CAP, CAP), :]
            copies.append(pltpu.make_async_copy(pieces[at].at[:, pl.ds(0, width)], target, sems.at[at]))
    for copy in (*first, *copies):
        copy.start()
    for copy in first:
        copy.wait()
    occ = occ_ref[...].T
    for p in range(2):
        rows = slice(p * NOCC, (p + 1) * NOCC)
        late = jnp.dot(occ, late_ref[p, : occ_ref.shape[0], :], preferred_element_type=F32)
        half_ref[rows, :] = part_ref[rows, :] + late
    for copy in copies:
        copy.wait()


def last_kernel(me_ref, part_ref, right_ref, late_any, *refs):
    pieces, (out_any, late_ref, half_ref, tiles_ref, sems) = (refs[:2], refs[2:4]), refs[4:]
    width = right_ref.shape[2]
    cut = right_ref.shape[1]
    tile = tiles_ref.shape[3]
    per = width // tile
    core = lax.rem(me_ref[0], CORES)
    rows = late_any.shape[1] - 2 * CAP
    copy = pltpu.make_async_copy(late_any.at[:, pl.ds(rows, 2 * CAP), :], late_ref, sems.at[0])
    copy.start()
    copy.wait()
    sides = [jnp.concatenate([ref[:, width:] for ref in side], axis=0).T for side in pieces]
    for p in range(2):
        for side, occ in enumerate(sides):
            half = lax.rem(core + side, CORES)
            rows = pl.ds(pl.multiple_of(p * NOCC + half * 128, 128), 128)
            late = jnp.dot(occ, late_ref[p], preferred_element_type=F32)
            half_ref[rows, :] = (part_ref[rows, :] + late).astype(BF16)
    results = []
    for side, tail in enumerate(pieces):
        base = lax.rem(core + side, CORES) * width
        for t in range(per):
            columns = slice(t * tile, (t + 1) * tile)
            total = jnp.dot(half_ref[:, :cut], right_ref[side, :, columns], preferred_element_type=F32)
            below = jnp.concatenate([ref[:, columns] for ref in tail], axis=0)
            total += jnp.dot(half_ref[:, cut:], below, preferred_element_type=F32)
            at = side * per + t
            tiles_ref[at] = total.astype(BF16).reshape(tiles_ref.shape[1:])
            target = out_any.at[:, :, pl.ds(pl.multiple_of(base + t * tile, 128), tile)]
            results.append(pltpu.make_async_copy(tiles_ref.at[at], target, sems.at[1 + at]))
            results[-1].start()
    for copy in results:
        copy.wait()


VMEM = pl.BlockSpec(memory_space=pltpu.VMEM)
SMEM = pl.BlockSpec(memory_space=pltpu.SMEM)
ANY = pl.BlockSpec(memory_space=pl.ANY)


def shape(*dims, dtype=BF16):
    return jax.ShapeDtypeStruct(dims, dtype)


def params(mib):
    return pltpu.CompilerParams(vmem_limit_bytes=mib << 20)


def cost(flops, nbytes):
    return pl.CostEstimate(flops=int(flops), bytes_accessed=int(nbytes), transcendentals=0)


def short_way(panels, block_pairs, block_count, shell_size, occ_coef, vir_coef):
    n = lax.axis_size("shell")
    here, nvir = vir_coef.shape
    width = nvir // CORES
    packed = width + NOCC // CORES
    room = Z * Y * CAP
    size_row = shell_size.reshape(1, -1)

    def swap(array, bit):
        return lax.ppermute(array, "shell", [(i, i ^ bit) for i in range(n)])

    keep, to_core, to_y, to_both = pl.pallas_call(
        pack_kernel,
        out_shape=[shape(here // 2 + 2 * BLK_DEV, packed)] * 4,
        in_specs=[VMEM] * 3,
        out_specs=[VMEM] * 4,
        scratch_shapes=[pltpu.VMEM((2 * n, BLK_DEV, EDGE * EDGE), F32)],
        compiler_params=params(12),
        cost_estimate=cost(3e8, 3e6),
        name="pack_rows",
    )(vir_coef, occ_coef, panels)
    to_y, to_both, to_core = swap(to_y, 2), swap(to_both, 3), swap(to_core, 1)
    code = pl.pallas_call(
        functools.partial(ids_kernel, size_row.shape[1]),
        out_shape=shape(n, BLK_DEV, 128, dtype=jnp.int32),
        in_specs=[VMEM] * 2,
        out_specs=VMEM,
        compiler_params=params(12),
        cost_estimate=cost(1e4, 1e4),
        name="pack_ids",
    )(block_pairs.T, block_count.reshape(1, 1))
    code = lax.all_to_all(code, "shell", split_axis=0, concat_axis=0, tiled=True)

    mine, over, me, panel = pl.pallas_call(
        functools.partial(pick_kernel, here),
        out_shape=[shape(CAP, packed), shape(8, 128, dtype=jnp.int32), shape(1, dtype=jnp.int32)]
        + [shape(Z, Y * CORES, 2 * BLK_DEV, EDGE * EDGE)],
        in_specs=[VMEM] * 6,
        out_specs=[VMEM, VMEM, SMEM, VMEM],
        compiler_params=params(12),
        cost_estimate=cost(3e8, 2e6),
        name="pick_rows",
    )(code, size_row, keep, to_core, to_y, to_both)

    across, mine_y, beside = swap(mine, 8), swap(mine, 2), swap(mine, 4)
    lines = [[Y * CORES * z + k for z in range(Z)] for k in range(Y * CORES)]
    got = lax.all_to_all(panel, "shell", split_axis=0, concat_axis=0, axis_index_groups=lines, tiled=True)
    got = got.reshape(n, 2 * BLK_DEV, EDGE * EDGE)
    far = [swap(mine, 1)]
    across, mine_y, beside, got, *far = lax.optimization_barrier((across, mine_y, beside, got, *far))

    corner, beside_y, across_y = swap(across, 4), swap(beside, 2), swap(across, 2)
    near = [mine, mine_y, beside]
    far += [swap(piece, 1) for piece in near[1:]]
    early = len(near)
    slots = LIVE_DEV * n * EDGE
    half, late = pl.pallas_call(
        functools.partial(half_kernel, here, early),
        out_shape=(shape(2 * NOCC, room, dtype=F32), shape(2, room - early * CAP, room)),
        grid=(1,),
        in_specs=[VMEM] * 3 + [ANY] * (2 * early),
        out_specs=(
            pl.BlockSpec((2 * NOCC, room), lambda i: (0, 0)),
            pl.BlockSpec((2, room - early * CAP, room), lambda i: (0, 0, 0)),
        ),
        scratch_shapes=[
            pltpu.VMEM((early * CAP, NOCC), BF16),
            pltpu.VMEM((NOCC, slots), BF16),
            pltpu.VMEM((room - early * CAP, slots), BF16),
            pltpu.VMEM((2, slots, room), BF16),
            pltpu.SemaphoreType.DMA((2 * early,)),
        ],
        compiler_params=params(30),
        cost_estimate=cost(7e9, 1),
        name="half_transform",
    )(code, got, size_row, *near, *far)
    corner, beside_y, half, late = lax.optimization_barrier((corner, beside_y, half, late))
    corner_y = swap(corner, 2)
    near += [across, beside_y, corner]
    far += [swap(piece, 1) for piece in near[early:]]
    count = len(near)
    over_other = lax.ppermute(over, "groups", [(0, 1), (1, 0)])
    right, half, over = pl.pallas_call(
        functools.partial(gather_kernel, early),
        out_shape=(
            shape(CORES, count * CAP, width),
            shape(2 * NOCC, room, dtype=F32),
            shape(1, dtype=jnp.int32),
        ),
        in_specs=[SMEM] + [VMEM] * 4 + [ANY] * (2 * count),
        out_specs=(VMEM, VMEM, SMEM),
        scratch_shapes=[pltpu.VMEM(((count - early) * CAP, NOCC), BF16), pltpu.SemaphoreType.DMA((4 * count,))],
        compiler_params=params(20),
        cost_estimate=cost(1, 1),
        name="gather_pieces",
    )(me, over, over_other, half, late, *near, *far)
    corner_y, right, half = lax.optimization_barrier((corner_y, right, half))
    tails = [across_y, corner_y, swap(across_y, 1), swap(corner_y, 1)]

    tile = width // 3
    out = pl.pallas_call(
        last_kernel,
        out_shape=shape(2, NOCC, nvir),
        in_specs=[SMEM] + [VMEM] * 2 + [ANY] + [VMEM] * 4,
        out_specs=ANY,
        scratch_shapes=[
            pltpu.VMEM((2, 2 * CAP, room), BF16),
            pltpu.VMEM((2 * NOCC, room), BF16),
            pltpu.VMEM((nvir // tile, 2, NOCC, tile), BF16),
            pltpu.SemaphoreType.DMA((1 + nvir // tile,)),
        ],
        compiler_params=params(24),
        cost_estimate=cost(2e10, 1),
        name="last_product",
    )(me, half, right, late, *tails)
    return out, over[0], code, got


def per_device(*args):
    n = lax.axis_size("shell")
    here, nvir = args[5].shape
    shells = args[3].shape[0]
    sparse = LIVE_DEV * n * EDGE < n * here
    if not (sparse and lax.axis_size("groups") == 2 and n == Z * Y * CORES and here <= 256 and here % 16 == 0 and nvir % 768 == 0):
        return from_start(*args)
    out, over, code, got = short_way(*args)

    def again(carry):
        over, _ = carry
        over, code_now, turned, *held = lax.optimization_barrier((over, code, got, *args[3:]))
        turned = turned.reshape(n, 2, BLK_DEV, EDGE * EDGE).swapaxes(1, 2).reshape(n * BLK_DEV, 2, EDGE * EDGE)
        code_now = jnp.max(code_now, axis=2).reshape(n * BLK_DEV)
        ids = jnp.maximum(code_now, 0)
        pairs = jnp.stack([ids // shells, ids % shells], axis=1)
        return over - 1, long_way(turned, pairs, code_now >= 0, *held)

    return lax.while_loop(lambda carry: carry[0] > 0, again, (over, out))[1]


def solution(mesh):
    placed = (
        P(("groups", "shell"), None, None),
        P(("groups", "shell"), None),
        P(("groups", "shell")),
        P("groups"),
        P(("groups", "shell"), None),
        P(("groups", "shell"), None),
    )
    return jax.shard_map(
        per_device,
        mesh=mesh,
        in_specs=placed,
        out_specs=P(("groups", "shell"), None, None),
        check_vma=False,
    )
```
